32 devices in a mesh: req: 8 (over z, y), tp: 4 (over x, core).
Axes of the slice: x: 2, y: 2, z: 4, core: 2. Of those that a mesh axis runs over, the one named last changes fastest.
Arguments:
- hidden: bfloat16 [64, 4096], P('req'), may hold values from -512 to 512
- norm_gain: bfloat16 [4096], replicated, may hold values from 1 to 3
- lm_head: bfloat16 [4096, 8192], P(None, ('req', 'tp'))
- targets: int32 [64], P('req'), may hold values from 0 to 8191
- segments: int32 [64], P('req'), may hold values from 0 to 3, never falling along the last dimension, each value on 1 to 32 neighbouring positions
- scored: int32 [64], P('req'), may hold values from 0 to 1, as said below
Outputs:
- token_logprob: float32 [64], P('req')
- token_entropy: float32 [64], P('req')
- seq_logprob: float32 [4], replicated
The draws below stay inside these ranges and needn't reach their ends.
Inputs may be any that keep to these rules, and one draw needn't show every extreme that they name: At most 4 of the 8 rows of one index of req are scored, and exactly 4 on some index in every draw.
All inputs are finite; a program needn't handle non-finite values.
Results may differ from the reference program's by a relative error of at most 0.0061.
Values may be sent and summed in bfloat16 or wider, within the bound.
No kernel may reach another device: no remote copies, remote signals or barrier semaphores. Data moves between devices by JAX's collectives and lax.ppermute only.
A program may use at most 64 MiB of HBM per device.

```python
import math
import jax
import jax.numpy as jnp
import numpy as np
from jax import lax

D = 4096
VOCAB = 8192
TOK_REQ = 8
SCORE_MOST = 4
TOKENS = 64
SEQS = 4


def head_block(key, block_index):
    return jax.random.normal(jax.random.fold_in(key, block_index), (D, 128), jnp.float32) * (3.0 / math.sqrt(D))


def drawn_plan(key):
    base = jax.random.fold_in(key, 11)
    keys = jax.random.split(jax.random.fold_in(key, 53), 5)
    count = min(16, TOKENS)
    pairs = jax.random.permutation(keys[0], VOCAB // 2)[:count].astype(jnp.int32)
    first_cols = pairs * 2
    ladder = jnp.exp(jnp.arange(count, dtype=jnp.float32) * (math.log(24.0) / max(count - 1, 1)))
    power = ladder[jax.random.permutation(keys[3], count)]
    factor = power * (9.5 / math.sqrt(D))

    def raw_column(column):
        block_data = head_block(base, column // 128)
        return lax.dynamic_slice_in_dim(block_data, column % 128, 1, 1)[:, 0]
    raw_cols = jax.vmap(raw_column)(first_cols)
    fresh = jax.random.normal(keys[1], (count, D), jnp.float32) * (0.5 * 3.0 / math.sqrt(D))
    first_new = raw_cols * factor[:, None]
    second_new = first_new + fresh
    positions = jax.random.permutation(keys[4], TOKENS)[:count].astype(jnp.int32)
    return (first_cols, raw_cols, first_new, second_new, keys[2], count, positions)


def draw_lm_head(key, part):
    base = jax.random.fold_in(key, 11)
    blocks = jax.vmap(lambda block_index: head_block(base, block_index))(jnp.arange(VOCAB // 128))
    whole = jnp.transpose(blocks, (1, 0, 2)).reshape(D, VOCAB)
    first_cols, raw_cols, first_new, second_new, unused_key, count, unused_rows = drawn_plan(key)
    whole = whole.at[:, first_cols].set(jnp.transpose(first_new))
    whole = whole.at[:, first_cols + 1].set(jnp.transpose(second_new))
    return whole.astype(jnp.bfloat16)


def draw_hidden(key, part):
    keys = jax.random.split(jax.random.fold_in(key, 23), 3)
    row_scale = jnp.exp(jax.random.uniform(keys[0], (TOKENS, 1)) * math.log(10.0))
    col_scale = jnp.exp(jax.random.uniform(keys[1], (1, D)) * math.log(10.0))
    values = jnp.clip(jax.random.normal(keys[2], (TOKENS, D)), -4.0, 4.0) * row_scale * col_scale
    first_cols, raw_cols, first_new, second_new, noise_key, count, positions = drawn_plan(key)
    new_rows = raw_cols * (math.sqrt(D) / 3.0) + 0.3 * jax.random.normal(noise_key, (count, D), jnp.float32)
    values = values.at[positions].set(new_rows)
    return jnp.clip(values, -512.0, 512.0).astype(jnp.bfloat16)


def draw_scored(key, part):
    keys = jax.random.split(jax.random.fold_in(key, 37), 3)
    groups = TOKENS // TOK_REQ
    counts = jax.random.randint(keys[0], (groups,), 1, SCORE_MOST + 1)
    fullest = jax.random.randint(keys[1], (), 0, groups)
    counts = jnp.where(jnp.arange(groups) == fullest, SCORE_MOST, counts)
    ranks = jax.vmap(lambda row_key: jax.random.permutation(row_key, TOK_REQ))(jax.random.split(keys[2], groups))
    return (ranks < counts[:, None]).astype(jnp.int32).reshape(TOKENS)


def place_ends(result, own_key, low, high):
    shape = result.shape
    index_at = [jax.random.randint(jax.random.fold_in(own_key, axis), (), 0, shape[axis]) for axis in range(len(shape))]
    result = result.at[tuple(index_at)].set(low)
    longest = shape.index(max(shape))
    index_at[longest] = (index_at[longest] + 1) % shape[longest]
    return result.at[tuple(index_at)].set(high)


def cumulative_ranks(number_of, slope):
    portions = [(1 << 20) // math.isqrt(grade ** slope) + 1 for grade in range(1, number_of + 1)]
    scale = 1 + sum(portions) // (1 << 30)
    return np.cumsum(np.array([max(1, weight // scale) for weight in portions]))


def ranked(rng, dims, amount, slope):
    grid = cumulative_ranks(amount, slope)
    ticket = jax.random.randint(jax.random.fold_in(rng, 1), dims, 0, int(grid[amount - 1]))
    grade = jnp.searchsorted(jnp.asarray(grid, jnp.int32), ticket, side="right")
    return jax.random.permutation(jax.random.fold_in(rng, 2), amount)[grade].astype(jnp.int32)


def profile(amount, total, reach, slope):
    loads = [(1 << 20) // math.isqrt(standing ** slope) + 1 for standing in range(2, amount + 1)]
    spare, given = total - reach - (amount - 1), [1] * (amount - 1)
    while spare > 0:
        movable = [i for i in range(amount - 1) if given[i] < reach]
        pool, left = sum([loads[i] for i in movable]), spare
        for i in movable:
            more = min(reach - given[i], max(1, left * loads[i] // pool), spare)
            given[i] = given[i] + more
            spare = spare - more
    return np.array([reach] + given)


def ragged_sizes(stream_key, number_of, total, bound, slope):
    if number_of == 2:
        one = jax.random.randint(stream_key, (), max(1, total - bound), min(bound, total - 1) + 1)
        return jnp.stack([one, total - one])
    tallies = jnp.asarray(profile(number_of, total, bound, slope), jnp.int32)
    twos = (number_of - 1) // 2
    giver, sink = tallies[1:1 + 2 * twos:2], tallies[2:2 + 2 * twos:2]
    room = jnp.minimum(giver - 1, bound - sink)
    shifted = jax.random.randint(jax.random.fold_in(stream_key, 1), (twos,), 0, 1 << 20) % (room + 1)
    tallies = tallies.at[1:1 + 2 * twos:2].set(giver - shifted).at[2:2 + 2 * twos:2].set(sink + shifted)
    return tallies[jax.random.permutation(jax.random.fold_in(stream_key, 2), number_of)]


def setup_inputs(seed: int = 0) -> dict:
    seeds = jax.random.split(jax.random.key(seed), 7)
    hidden = draw_hidden(jax.random.fold_in(seeds[6], 71), 0)
    norm_gain = jnp.clip(jnp.exp(jax.random.uniform(seeds[1], (D,), jnp.float32, math.log(1.0), math.log(3.0))), 1.0, 3.0).astype(jnp.bfloat16)
    lm_head = draw_lm_head(jax.random.fold_in(seeds[6], 71), 0)
    targets = place_ends(ranked(seeds[3], (TOKENS,), VOCAB, 2), jax.random.fold_in(seeds[3], 3), 0, VOCAB - 1).astype(jnp.int32)
    segments = jnp.searchsorted(jnp.cumsum(ragged_sizes(seeds[4], SEQS, TOKENS, TOKENS // 2, 2)), jnp.arange(TOKENS), side="right").astype(jnp.int32)
    scored = draw_scored(jax.random.fold_in(seeds[6], 71), 0)
    return dict(hidden=hidden, norm_gain=norm_gain, lm_head=lm_head, targets=targets, segments=segments, scored=scored)


def reference(hidden, norm_gain, lm_head, targets, segments, scored):
    values = hidden.astype(jnp.float32)
    row_scale = lax.rsqrt(lax.optimization_barrier(jnp.mean(values * values, axis=1, keepdims=True)) + 1e-05)
    normed = (values * row_scale * norm_gain.astype(jnp.float32)[None, :]).astype(jnp.bfloat16)
    col_width = lm_head.shape[1]
    block_width = math.gcd(col_width, 8192)
    block_count = col_width // block_width
    row_count = hidden.shape[0]

    def advance(running, block_index):
        row_top, row_total, row_weighted, picked = running
        first_col = (block_index * block_width).astype(jnp.int32)
        weights = lax.dynamic_slice_in_dim(lm_head, first_col, block_width, 1)
        logits = jnp.dot(normed, weights, preferred_element_type=jnp.float32)
        new_top = jnp.maximum(row_top, lax.optimization_barrier(jnp.max(logits, axis=1)))
        old_scale = jnp.exp(row_top - new_top)
        scaled = jnp.exp(logits - new_top[:, None])
        row_total = row_total * old_scale + lax.optimization_barrier(jnp.sum(scaled, axis=1))
        row_weighted = row_weighted * old_scale + lax.optimization_barrier(jnp.sum(scaled * logits, axis=1))
        columns = first_col + jnp.arange(block_width, dtype=jnp.int32)
        picked = picked + lax.optimization_barrier(jnp.sum(jnp.where(columns[None, :] == targets[:, None], logits, jnp.float32(0.0)), axis=1))
        return ((new_top, row_total, row_weighted, picked), None)
    start_state = (jnp.full((row_count,), -jnp.inf, jnp.float32), jnp.zeros((row_count,), jnp.float32), jnp.zeros((row_count,), jnp.float32), jnp.zeros((row_count,), jnp.float32))
    final_state, unused = lax.scan(advance, start_state, jnp.arange(block_count, dtype=jnp.int32))
    row_top, row_total, row_weighted, picked = final_state
    log_norm = row_top + jnp.log(row_total)
    row_flags = scored.astype(jnp.float32)
    token_logprob = row_flags * (picked - log_norm)
    token_entropy = row_flags * (log_norm - row_weighted / row_total)
    seq_ids = jnp.arange(SEQS, dtype=jnp.int32)
    seq_logprob = lax.optimization_barrier(jnp.sum(jnp.where(segments[None, :] == seq_ids[:, None], token_logprob[None, :], jnp.float32(0.0)), axis=1))
    return (token_logprob, token_entropy, seq_logprob)
```

```python
import functools

import jax
import jax.numpy as jnp
from jax import lax
from jax.experimental import pallas as pl
from jax.experimental.pallas import tpu as pltpu
from jax.sharding import PartitionSpec as P

SEQS = 4
PICK = 4
LANES = 128
STATS = 4

VMEM = pltpu.VMEM
SMEM = pltpu.SMEM


def ranks_of(scored_ref, row_count):
    ranks, so_far = [], jnp.int32(0)
    for row in range(row_count):
        ranks.append(so_far)
        so_far = so_far + scored_ref[row]
    return ranks, so_far


def pack_kernel(hidden_ref, gain_ref, targets_ref, segments_ref, scored_ref, out_ref, wide_ref, halves_ref):
    row_count, width = hidden_ref.shape
    half = width // 2
    wide_ref[...] = hidden_ref[...].astype(jnp.float32)
    ranks, count = ranks_of(scored_ref, row_count)
    source = [jnp.int32(0)] * PICK
    for row in range(row_count):
        for r in range(PICK):
            hit = jnp.logical_and(scored_ref[row] == 1, ranks[row] == r)
            source[r] = jnp.where(hit, row, source[r])
    for r in range(PICK):
        halves_ref[r : r + 1, :] = wide_ref[pl.ds(source[r], 1), :half]
        halves_ref[PICK + r : PICK + r + 1, :] = wide_ref[pl.ds(source[r], 1), half:]
    values = halves_ref[...]
    part = jnp.sum(values * values, axis=1, keepdims=True)
    part = jnp.broadcast_to(part, (2 * PICK, LANES))
    total = (part + pltpu.roll(part, PICK, 0))[:, :1]
    row_scale = lax.rsqrt(total / width + 1e-05)
    upper = lax.broadcasted_iota(jnp.int32, (2 * PICK, 1), 0) < PICK
    gain = jnp.where(upper, gain_ref[:, :half].astype(jnp.float32), gain_ref[:, half:].astype(jnp.float32))
    out_ref[:, :half] = (values * row_scale * gain).astype(jnp.bfloat16)
    sub = lax.broadcasted_iota(jnp.int32, (2 * PICK, LANES), 0)
    sub = jnp.where(sub >= PICK, sub - PICK, sub)
    lane = lax.broadcasted_iota(jnp.int32, (2 * PICK, LANES), 1)
    side = jnp.zeros((2 * PICK, LANES), jnp.int32)
    for r in range(PICK):
        target = targets_ref[source[r]]
        fields = (target % 256, (target // 256) % 256, target // 65536, segments_ref[source[r]], (count > r).astype(jnp.int32))
        line = jnp.zeros((2 * PICK, LANES), jnp.int32)
        for at, field in enumerate(fields):
            line = jnp.where(lane == at, field, line)
        side = jnp.where(sub == r, line, side)
    out_ref[:, half:] = side.astype(jnp.float32).astype(jnp.bfloat16)


def score_kernel(place_ref, rows_ref, head_ref, stats_ref, meta_ref):
    width, cols = head_ref.shape
    half = width // 2
    groups = rows_ref.shape[0] // (2 * PICK)
    used = groups * PICK
    rows = rows_ref[:, :half]
    early = jnp.dot(rows, head_ref[:half, :], preferred_element_type=jnp.float32)
    late = jnp.dot(rows, head_ref[half:, :], preferred_element_type=jnp.float32)
    early = early.reshape(groups // 2, 2, 2 * PICK, cols)
    late = late.reshape(groups // 2, 2, 2 * PICK, cols)
    upper = lax.broadcasted_iota(jnp.int32, (1, 2 * PICK, 1), 1) < PICK

    def swap(block):
        flat = block.reshape(groups // 2 * 2 * PICK, block.shape[-1])
        return jnp.concatenate(
            [pltpu.roll(flat[i * 2 * PICK : (i + 1) * 2 * PICK], PICK, 0) for i in range(groups // 2)], axis=0
        ).reshape(block.shape)

    logits = jnp.where(upper, early[:, 0] + swap(late[:, 0]), swap(early[:, 1]) + late[:, 1])
    logits = logits.reshape(used, cols)
    side = rows_ref[:, half:].astype(jnp.float32).reshape(groups // 2, 2, 2 * PICK, LANES)
    side = jnp.where(upper, side[:, 0], side[:, 1]).reshape(used, LANES)
    copies = max(1, LANES // used)
    if copies > 1:
        logits = jnp.concatenate([logits] * copies, axis=0)
        side = jnp.concatenate([side] * copies, axis=0)
    logits = logits.T
    side = side.T
    ids = (side[0:1] + 256.0 * side[1:2] + 65536.0 * side[2:3]).astype(jnp.int32)
    row_top = jnp.max(logits, axis=0, keepdims=True)
    scaled = jnp.exp(logits - row_top)
    row_total = jnp.sum(scaled, axis=0, keepdims=True)
    row_weighted = jnp.sum(scaled * logits, axis=0, keepdims=True)
    columns = place_ref[0] * cols + lax.broadcasted_iota(jnp.int32, logits.shape, 0)
    picked = jnp.sum(jnp.where(columns == ids, logits, 0.0), axis=0, keepdims=True)
    stats = (row_top, row_total, row_weighted, picked)
    if copies > 1:
        lane = lax.broadcasted_iota(jnp.int32, (1, LANES), 1)
        joined = picked
        for at in range(STATS - 1):
            joined = jnp.where(lane // used == at, stats[at], joined)
        stats_ref[...] = joined
    else:
        for at in range(STATS):
            stats_ref[:, at * used : (at + 1) * used] = stats[at]
    meta_ref[...] = side[0:8, :]


def finish_kernel(used, place_ref, scored_ref, stats_ref, meta_ref, logprob_ref, entropy_ref, seq_ref):
    row_count = scored_ref.shape[0]
    lanes = max(used, LANES)

    def stat(at):
        if used >= LANES:
            return stats_ref[:, at * used : (at + 1) * used]
        return stats_ref[...] if at == 0 else pltpu.roll(stats_ref[...], LANES - at * used, 1)

    tops = stat(0)
    row_top = jnp.max(tops, axis=0, keepdims=True)
    weight = jnp.exp(tops - row_top)
    row_total = jnp.sum(stat(1) * weight, axis=0, keepdims=True)
    row_weighted = jnp.sum(stat(2) * weight, axis=0, keepdims=True)
    picked = jnp.sum(stat(3), axis=0, keepdims=True)
    log_norm = row_top + jnp.log(row_total)
    lane = lax.broadcasted_iota(jnp.int32, (1, lanes), 1)
    in_use = jnp.logical_and(meta_ref[4:5, :] > 0.5, lane < used)
    logprob = jnp.where(in_use, picked - log_norm, 0.0)
    entropy = jnp.where(in_use, log_norm - row_weighted / row_total, 0.0)
    segment = meta_ref[3:4, :].astype(jnp.int32)
    for s in range(SEQS):
        seq_ref[s] = jnp.sum(jnp.where(segment == s, logprob, 0.0))
    ranks, _ = ranks_of(scored_ref, row_count)
    first = place_ref[1] * PICK
    for row in range(row_count):
        own = jnp.logical_and(lane == first + ranks[row], scored_ref[row] == 1)
        logprob_ref[row] = jnp.sum(jnp.where(own, logprob, 0.0))
        entropy_ref[row] = jnp.sum(jnp.where(own, entropy, 0.0))


def local(hidden, norm_gain, lm_head, targets, segments, scored):
    row_count, width = hidden.shape
    groups, tp_count = lax.axis_size("req"), lax.axis_size("tp")
    own = lax.axis_index("req")
    place = jnp.stack([own * tp_count + lax.axis_index("tp"), own]).astype(jnp.int32)
    half = width // 2
    used = groups * PICK
    lanes = max(used, LANES)

    def spec(space):
        return pl.BlockSpec(memory_space=space)

    packed = pl.pallas_call(
        pack_kernel,
        out_shape=jax.ShapeDtypeStruct((2 * PICK, half + LANES), jnp.bfloat16),
        in_specs=[spec(VMEM)] * 2 + [spec(SMEM)] * 3,
        out_specs=spec(VMEM),
        scratch_shapes=[VMEM((row_count, width), jnp.float32), VMEM((2 * PICK, half), jnp.float32)],
    )(hidden, norm_gain.reshape(1, width), targets, segments, scored)
    rows = lax.all_gather(packed, "req", axis=0, tiled=True)
    stats, meta = pl.pallas_call(
        score_kernel,
        out_shape=(
            jax.ShapeDtypeStruct((1, STATS * used), jnp.float32),
            jax.ShapeDtypeStruct((8, lanes), jnp.float32),
        ),
        in_specs=[spec(SMEM), spec(VMEM), spec(VMEM)],
        out_specs=(spec(VMEM), spec(VMEM)),
        compiler_params=pltpu.CompilerParams(vmem_limit_bytes=40 * 1024 * 1024),
    )(place, rows, lm_head)
    gathered = lax.all_gather(stats, ("req", "tp"), axis=0, tiled=True)
    return pl.pallas_call(
        functools.partial(finish_kernel, used),
        out_shape=(
            jax.ShapeDtypeStruct((row_count,), jnp.float32),
            jax.ShapeDtypeStruct((row_count,), jnp.float32),
            jax.ShapeDtypeStruct((SEQS,), jnp.float32),
        ),
        in_specs=[spec(SMEM), spec(SMEM), spec(VMEM), spec(VMEM)],
        out_specs=(spec(SMEM), spec(SMEM), spec(SMEM)),
    )(place, scored, gathered, meta)


def solution(mesh):
    return jax.shard_map(
        local,
        mesh=mesh,
        in_specs=(P("req", None), P(), P(None, ("req", "tp")), P("req"), P("req"), P("req")),
        out_specs=(P("req"), P("req"), P()),
        check_vma=False,
    )
```

```python
import functools

import jax
import jax.numpy as jnp
from jax import lax
from jax.experimental import pallas as pl
from jax.experimental.pallas import tpu as pltpu
from jax.sharding import PartitionSpec as P

SEQS = 4
PICK = 4
LANES = 128
STATS = 4

VMEM = pltpu.VMEM
SMEM = pltpu.SMEM


def ranks_of(scored_ref, row_count):
    ranks, so_far = [], jnp.int32(0)
    for row in range(row_count):
        ranks.append(so_far)
        so_far = so_far + scored_ref[row]
    return ranks, so_far


def pack_kernel(hidden_ref, gain_ref, targets_ref, segments_ref, scored_ref, out_ref, wide_ref, halves_ref):
    row_count, width = hidden_ref.shape
    half = width // 2
    wide_ref[...] = hidden_ref[...].astype(jnp.float32)
    ranks, count = ranks_of(scored_ref, row_count)
    source = [jnp.int32(0)] * PICK
    for row in range(row_count):
        for r in range(PICK):
            hit = jnp.logical_and(scored_ref[row] == 1, ranks[row] == r)
            source[r] = jnp.where(hit, row, source[r])
    for r in range(PICK):
        halves_ref[r : r + 1, :] = wide_ref[pl.ds(source[r], 1), :half]
        halves_ref[PICK + r : PICK + r + 1, :] = wide_ref[pl.ds(source[r], 1), half:]
    values = halves_ref[...]
    part = jnp.sum(values * values, axis=1, keepdims=True)
    part = jnp.broadcast_to(part, (2 * PICK, LANES))
    total = (part + pltpu.roll(part, PICK, 0))[:, :1]
    row_scale = lax.rsqrt(total / width + 1e-05)
    upper = lax.broadcasted_iota(jnp.int32, (2 * PICK, 1), 0) < PICK
    gain = jnp.where(upper, gain_ref[:, :half].astype(jnp.float32), gain_ref[:, half:].astype(jnp.float32))
    out_ref[:, :half] = (values * row_scale * gain).astype(jnp.bfloat16)
    sub = lax.broadcasted_iota(jnp.int32, (2 * PICK, LANES), 0)
    sub = jnp.where(sub >= PICK, sub - PICK, sub)
    lane = lax.broadcasted_iota(jnp.int32, (2 * PICK, LANES), 1)
    side = jnp.zeros((2 * PICK, LANES), jnp.int32)
    for r in range(PICK):
        target = targets_ref[source[r]]
        fields = (target % 256, (target // 256) % 256, target // 65536, segments_ref[source[r]], (count > r).astype(jnp.int32))
        line = jnp.zeros((2 * PICK, LANES), jnp.int32)
        for at, field in enumerate(fields):
            line = jnp.where(lane == at, field, line)
        side = jnp.where(sub == r, line, side)
    out_ref[:, half:] = side.astype(jnp.float32).astype(jnp.bfloat16)


def score_kernel(place_ref, rows_ref, head_ref, stats_ref, meta_ref):
    width, cols = head_ref.shape
    half = width // 2
    groups = rows_ref.shape[0] // (2 * PICK)
    used = groups * PICK
    rows = rows_ref[:, :half]
    early = jnp.dot(rows, head_ref[:half, :], preferred_element_type=jnp.float32)
    late = jnp.dot(rows, head_ref[half:, :], preferred_element_type=jnp.float32)
    early = early.reshape(groups // 2, 2, 2 * PICK, cols)
    late = late.reshape(groups // 2, 2, 2 * PICK, cols)
    upper = lax.broadcasted_iota(jnp.int32, (1, 2 * PICK, 1), 1) < PICK

    def swap(block):
        flat = block.reshape(groups // 2 * 2 * PICK, block.shape[-1])
        return jnp.concatenate(
            [pltpu.roll(flat[i * 2 * PICK : (i + 1) * 2 * PICK], PICK, 0) for i in range(groups // 2)], axis=0
        ).reshape(block.shape)

    logits = jnp.where(upper, early[:, 0] + swap(late[:, 0]), swap(early[:, 1]) + late[:, 1])
    logits = logits.reshape(used, cols)
    side = rows_ref[:, half:].astype(jnp.float32).reshape(groups // 2, 2, 2 * PICK, LANES)
    side = jnp.where(upper, side[:, 0], side[:, 1]).reshape(used, LANES)
    copies = max(1, LANES // used)
    if copies > 1:
        logits = jnp.concatenate([logits] * copies, axis=0)
        side = jnp.concatenate([side] * copies, axis=0)
    logits = logits.T
    side = side.T
    ids = (side[0:1] + 256.0 * side[1:2] + 65536.0 * side[2:3]).astype(jnp.int32)
    row_top = jnp.max(logits, axis=0, keepdims=True)
    scaled = jnp.exp(logits - row_top)
    row_total = jnp.sum(scaled, axis=0, keepdims=True)
    row_weighted = jnp.sum(scaled * logits, axis=0, keepdims=True)
    columns = place_ref[0] * cols + lax.broadcasted_iota(jnp.int32, logits.shape, 0)
    picked = jnp.sum(jnp.where(columns == ids, logits, 0.0), axis=0, keepdims=True)
    stats = (row_top, row_total, row_weighted, picked)
    if copies > 1:
        lane = lax.broadcasted_iota(jnp.int32, (1, LANES), 1)
        joined = picked
        for at in range(STATS - 1):
            joined = jnp.where(lane // used == at, stats[at], joined)
        stats_ref[...] = joined
    else:
        for at in range(STATS):
            stats_ref[:, at * used : (at + 1) * used] = stats[at]
    meta_ref[...] = side[0:8, :]


def finish_kernel(used, place_ref, scored_ref, stats_ref, meta_ref, logprob_ref, entropy_ref, seq_ref):
    row_count = scored_ref.shape[0]
    lanes = max(used, LANES)

    def stat(at):
        if used >= LANES:
            return stats_ref[:, at * used : (at + 1) * used]
        return stats_ref[...] if at == 0 else pltpu.roll(stats_ref[...], LANES - at * used, 1)

    tops = stat(0)
    row_top = jnp.max(tops, axis=0, keepdims=True)
    weight = jnp.exp(tops - row_top)
    row_total = jnp.sum(stat(1) * weight, axis=0, keepdims=True)
    row_weighted = jnp.sum(stat(2) * weight, axis=0, keepdims=True)
    picked = jnp.sum(stat(3), axis=0, keepdims=True)
    log_norm = row_top + jnp.log(row_total)
    lane = lax.broadcasted_iota(jnp.int32, (1, lanes), 1)
    in_use = jnp.logical_and(meta_ref[4:5, :] > 0.5, lane < used)
    logprob = jnp.where(in_use, picked - log_norm, 0.0)
    entropy = jnp.where(in_use, log_norm - row_weighted / row_total, 0.0)
    segment = meta_ref[3:4, :].astype(jnp.int32)
    for s in range(SEQS):
        seq_ref[s] = jnp.sum(jnp.where(segment == s, logprob, 0.0))
    ranks, _ = ranks_of(scored_ref, row_count)
    first = place_ref[1] * PICK
    for row in range(row_count):
        own = jnp.logical_and(lane == first + ranks[row], scored_ref[row] == 1)
        logprob_ref[row] = jnp.sum(jnp.where(own, logprob, 0.0))
        entropy_ref[row] = jnp.sum(jnp.where(own, entropy, 0.0))


def sent_to_all(block, axis):
    copies = jnp.broadcast_to(block[None], (lax.axis_size(axis),) + block.shape)
    return lax.all_to_all(copies, axis, 0, 0).reshape((-1,) + block.shape[1:])


def local(hidden, norm_gain, lm_head, targets, segments, scored):
    row_count, width = hidden.shape
    groups, tp_count = lax.axis_size("req"), lax.axis_size("tp")
    own = lax.axis_index("req")
    place = jnp.stack([own * tp_count + lax.axis_index("tp"), own]).astype(jnp.int32)
    half = width // 2
    used = groups * PICK
    lanes = max(used, LANES)

    def spec(space):
        return pl.BlockSpec(memory_space=space)

    packed = pl.pallas_call(
        pack_kernel,
        out_shape=jax.ShapeDtypeStruct((2 * PICK, half + LANES), jnp.bfloat16),
        in_specs=[spec(VMEM)] * 2 + [spec(SMEM)] * 3,
        out_specs=spec(VMEM),
        scratch_shapes=[VMEM((row_count, width), jnp.float32), VMEM((2 * PICK, half), jnp.float32)],
    )(hidden, norm_gain.reshape(1, width), targets, segments, scored)
    rows = sent_to_all(packed, "req")
    stats, meta = pl.pallas_call(
        score_kernel,
        out_shape=(
            jax.ShapeDtypeStruct((1, STATS * used), jnp.float32),
            jax.ShapeDtypeStruct((8, lanes), jnp.float32),
        ),
        in_specs=[spec(SMEM), spec(VMEM), spec(VMEM)],
        out_specs=(spec(VMEM), spec(VMEM)),
        compiler_params=pltpu.CompilerParams(vmem_limit_bytes=40 * 1024 * 1024),
    )(place, rows, lm_head)
    gathered = sent_to_all(stats, ("req", "tp"))
    return pl.pallas_call(
        functools.partial(finish_kernel, used),
        out_shape=(
            jax.ShapeDtypeStruct((row_count,), jnp.float32),
            jax.ShapeDtypeStruct((row_count,), jnp.float32),
            jax.ShapeDtypeStruct((SEQS,), jnp.float32),
        ),
        in_specs=[spec(SMEM), spec(SMEM), spec(VMEM), spec(VMEM)],
        out_specs=(spec(SMEM), spec(SMEM), spec(SMEM)),
    )(place, scored, gathered, meta)


def solution(mesh):
    return jax.shard_map(
        local,
        mesh=mesh,
        in_specs=(P("req", None), P(), P(None, ("req", "tp")), P("req"), P("req"), P("req")),
        out_specs=(P("req"), P("req"), P()),
        check_vma=False,
    )
```

```python
import functools

import jax
import jax.numpy as jnp
from jax import lax
from jax.experimental import pallas as pl
from jax.experimental.pallas import tpu as pltpu
from jax.sharding import PartitionSpec as P

SEQS = 4
PICK = 4
LANES = 128
STATS = 4

VMEM = pltpu.VMEM
SMEM = pltpu.SMEM


def ranks_of(scored_ref, row_count):
    ranks, so_far = [], jnp.int32(0)
    for row in range(row_count):
        ranks.append(so_far)
        so_far = so_far + scored_ref[row]
    return ranks, so_far


def pack_kernel(hidden_ref, gain_ref, targets_ref, segments_ref, scored_ref, out_ref, wide_ref, halves_ref, gains_ref):
    row_count, width = hidden_ref.shape
    half = width // 2
    wide_ref[...] = hidden_ref[...].astype(jnp.float32)
    gains_ref[...] = gain_ref[...].astype(jnp.float32)
    ranks, count = ranks_of(scored_ref, row_count)
    source = [jnp.int32(0)] * PICK
    for row in range(row_count):
        for r in range(PICK):
            hit = jnp.logical_and(scored_ref[row] == 1, ranks[row] == r)
            source[r] = jnp.where(hit, row, source[r])
    for r in range(PICK):
        halves_ref[r : r + 1, :] = wide_ref[pl.ds(source[r], 1), :half]
        halves_ref[PICK + r : PICK + r + 1, :] = wide_ref[pl.ds(source[r], 1), half:]
    values = halves_ref[...]
    part = jnp.sum(values * values, axis=1, keepdims=True)
    part = jnp.broadcast_to(part, (2 * PICK, LANES))
    row_scale = lax.rsqrt((part + pltpu.roll(part, PICK, 0)) / width + 1e-05)
    sub = lax.broadcasted_iota(jnp.int32, (2 * PICK, LANES), 0)
    lane = lax.broadcasted_iota(jnp.int32, (2 * PICK, LANES), 1)
    upper = sub < PICK
    chunks = half // LANES
    for at in range(chunks):
        gain = jnp.where(upper, gains_ref[at : at + 1, :], gains_ref[chunks + at : chunks + at + 1, :])
        piece = halves_ref[:, at * LANES : (at + 1) * LANES]
        piece = (piece * row_scale * gain).astype(jnp.bfloat16)
        for to in range(out_ref.shape[0]):
            out_ref[to, :, at * LANES : (at + 1) * LANES] = piece
    row_of = jnp.where(upper, sub, sub - PICK)
    side = jnp.zeros((2 * PICK, LANES), jnp.int32)
    for r in range(PICK):
        target = targets_ref[source[r]]
        digits = jnp.where(lane == 0, target & 255, jnp.where(lane == 1, (target >> 8) & 255, target >> 16))
        line = jnp.where(lane < 3, digits, jnp.where(lane == 3, segments_ref[source[r]], (count > r).astype(jnp.int32)))
        side = jnp.where(row_of == r, line, side)
    side = side.astype(jnp.float32).astype(jnp.bfloat16)
    for to in range(out_ref.shape[0]):
        out_ref[to, :, half:] = side


def stage_kernel(head_ref, out_ref, sems):
    parts = sems.shape[0]
    depth = head_ref.shape[0] // parts
    copies = [
        pltpu.make_async_copy(head_ref.at[pl.ds(i * depth, depth)], out_ref.at[pl.ds(i * depth, depth)], sems.at[i])
        for i in range(parts)
    ]
    for copy in copies:
        copy.start()
    for copy in copies:
        copy.wait()


def score_kernel(place_ref, rows_ref, head_ref, stats_ref, meta_ref):
    width, cols = head_ref.shape
    half = width // 2
    groups = rows_ref.shape[0] // (2 * PICK)
    used = groups * PICK
    rows = rows_ref[:, :half]
    early = jnp.dot(rows, head_ref[:half, :], preferred_element_type=jnp.float32)
    late = jnp.dot(rows, head_ref[half:, :], preferred_element_type=jnp.float32)
    early = early.reshape(groups // 2, 2, 2 * PICK, cols)
    late = late.reshape(groups // 2, 2, 2 * PICK, cols)
    upper = lax.broadcasted_iota(jnp.int32, (1, 2 * PICK, 1), 1) < PICK

    def swap(block):
        flat = block.reshape(groups // 2 * 2 * PICK, block.shape[-1])
        return jnp.concatenate(
            [pltpu.roll(flat[i * 2 * PICK : (i + 1) * 2 * PICK], PICK, 0) for i in range(groups // 2)], axis=0
        ).reshape(block.shape)

    logits = jnp.where(upper, early[:, 0] + swap(late[:, 0]), swap(early[:, 1]) + late[:, 1])
    logits = logits.reshape(used, cols)
    side = rows_ref[:, half:].astype(jnp.float32).reshape(groups // 2, 2, 2 * PICK, LANES)
    side = jnp.where(upper, side[:, 0], side[:, 1]).reshape(used, LANES)
    copies = max(1, LANES // used)
    if copies > 1:
        logits = jnp.concatenate([logits] * copies, axis=0)
        side = jnp.concatenate([side] * copies, axis=0)
    logits = logits.T
    side = side.T
    ids = (side[0:1] + 256.0 * side[1:2] + 65536.0 * side[2:3]).astype(jnp.int32)
    row_top = jnp.max(logits, axis=0, keepdims=True)
    scaled = jnp.exp(logits - row_top)
    row_total = jnp.sum(scaled, axis=0, keepdims=True)
    row_weighted = jnp.sum(scaled * logits, axis=0, keepdims=True)
    columns = place_ref[0] * cols + lax.broadcasted_iota(jnp.int32, logits.shape, 0)
    picked = jnp.sum(jnp.where(columns == ids, logits, 0.0), axis=0, keepdims=True)
    stats = (row_top, row_total, row_weighted, picked)
    if copies > 1:
        lane = lax.broadcasted_iota(jnp.int32, (1, LANES), 1)
        joined = picked
        for at in range(STATS - 1):
            joined = jnp.where(lane // used == at, stats[at], joined)
        stats_ref[...] = joined
    else:
        for at in range(STATS):
            stats_ref[:, at * used : (at + 1) * used] = stats[at]
    meta_ref[...] = side[0:8, :]


def finish_kernel(used, place_ref, scored_ref, stats_ref, meta_ref, logprob_ref, entropy_ref, seq_ref):
    row_count = scored_ref.shape[0]
    lanes = max(used, LANES)

    def stat(at):
        if used >= LANES:
            return stats_ref[:, at * used : (at + 1) * used]
        return stats_ref[...] if at == 0 else pltpu.roll(stats_ref[...], LANES - at * used, 1)

    tops = stat(0)
    row_top = jnp.max(tops, axis=0, keepdims=True)
    weight = jnp.exp(tops - row_top)
    row_total = jnp.sum(stat(1) * weight, axis=0, keepdims=True)
    row_weighted = jnp.sum(stat(2) * weight, axis=0, keepdims=True)
    picked = jnp.sum(stat(3), axis=0, keepdims=True)
    log_norm = row_top + jnp.log(row_total)
    lane = lax.broadcasted_iota(jnp.int32, (1, lanes), 1)
    in_use = jnp.logical_and(meta_ref[4:5, :] > 0.5, lane < used)
    logprob = jnp.where(in_use, picked - log_norm, 0.0)
    entropy = jnp.where(in_use, log_norm - row_weighted / row_total, 0.0)
    sub = lax.broadcasted_iota(jnp.int32, (8, LANES), 0)
    own_lane = lax.broadcasted_iota(jnp.int32, (8, LANES), 1)
    rows_of = lax.broadcasted_iota(jnp.int32, (8, lanes), 0)
    segment = meta_ref[3:4, :].astype(jnp.int32)
    sums = jnp.sum(jnp.where(segment == rows_of, logprob, 0.0), axis=1, keepdims=True)
    seqs = jnp.sum(jnp.where(sub == own_lane, sums, 0.0), axis=0, keepdims=True)
    seq_ref[...] = seqs[0, :SEQS]
    first = place_ref[1] * PICK
    block = first // LANES
    own_logprob, own_entropy = logprob[:, :LANES], entropy[:, :LANES]
    for at in range(1, lanes // LANES):
        piece = slice(at * LANES, (at + 1) * LANES)
        own_logprob = jnp.where(block == at, logprob[:, piece], own_logprob)
        own_entropy = jnp.where(block == at, entropy[:, piece], own_entropy)
    ranks, _ = ranks_of(scored_ref, row_count)
    at = jnp.zeros((8, LANES), jnp.int32)
    keep = jnp.zeros((8, LANES), jnp.int32)
    for row in range(row_count):
        at = jnp.where(own_lane == row, first - block * LANES + ranks[row], at)
        keep = jnp.where(own_lane == row, scored_ref[row], keep)
    at = jnp.minimum(at, LANES - 1)
    both = jnp.where(sub == 0, own_logprob, own_entropy)
    both = jnp.take_along_axis(both, at, axis=1)
    both = jnp.where(keep == 1, both, 0.0)
    logprob_ref[...] = both[0, :row_count]
    entropy_ref[...] = both[1, :row_count]


def sent_to_all(block, axis):
    copies = jnp.broadcast_to(block[None], (lax.axis_size(axis),) + block.shape)
    return lax.all_to_all(copies, axis, 0, 0).reshape((-1,) + block.shape[1:])


def local(hidden, norm_gain, lm_head, targets, segments, scored):
    row_count, width = hidden.shape
    groups, tp_count = lax.axis_size("req"), lax.axis_size("tp")
    own = lax.axis_index("req")
    place = jnp.stack([own * tp_count + lax.axis_index("tp"), own]).astype(jnp.int32)
    half = width // 2
    used = groups * PICK
    lanes = max(used, LANES)

    def spec(space):
        return pl.BlockSpec(memory_space=space)

    packed = pl.pallas_call(
        pack_kernel,
        out_shape=jax.ShapeDtypeStruct((groups, 2 * PICK, half + LANES), jnp.bfloat16),
        in_specs=[spec(VMEM)] * 2 + [spec(SMEM)] * 3,
        out_specs=spec(VMEM),
        scratch_shapes=[
            VMEM((row_count, width), jnp.float32),
            VMEM((2 * PICK, half), jnp.float32),
            VMEM((width // LANES, LANES), jnp.float32),
        ],
    )(hidden, norm_gain.reshape(width // LANES, LANES), targets, segments, scored)
    rows = lax.all_to_all(packed, "req", 0, 0).reshape(groups * 2 * PICK, half + LANES)
    head = pl.pallas_call(
        stage_kernel,
        out_shape=VMEM(lm_head.shape, lm_head.dtype),
        in_specs=[spec(pltpu.HBM)],
        out_specs=spec(VMEM),
        scratch_shapes=[pltpu.SemaphoreType.DMA((4,))],
        cost_estimate=pl.CostEstimate(flops=0, bytes_accessed=2 * lm_head.size * 2, transcendentals=0),
    )(pltpu.with_memory_space_constraint(lm_head, pltpu.HBM))
    stats, meta = pl.pallas_call(
        score_kernel,
        out_shape=(
            jax.ShapeDtypeStruct((1, STATS * used), jnp.float32),
            VMEM((8, lanes), jnp.float32),
        ),
        in_specs=[spec(SMEM), spec(VMEM), spec(VMEM)],
        out_specs=(spec(VMEM), spec(VMEM)),
        compiler_params=pltpu.CompilerParams(vmem_limit_bytes=40 * 1024 * 1024),
    )(place, rows, pltpu.with_memory_space_constraint(head, VMEM))
    gathered = sent_to_all(stats, ("req", "tp"))
    return pl.pallas_call(
        functools.partial(finish_kernel, used),
        out_shape=(
            jax.ShapeDtypeStruct((row_count,), jnp.float32),
            jax.ShapeDtypeStruct((row_count,), jnp.float32),
            jax.ShapeDtypeStruct((SEQS,), jnp.float32),
        ),
        in_specs=[spec(SMEM), spec(SMEM), spec(VMEM), spec(VMEM)],
        out_specs=(spec(VMEM), spec(VMEM), spec(VMEM)),
    )(place, scored, gathered, pltpu.with_memory_space_constraint(meta, VMEM))


def solution(mesh):
    return jax.shard_map(
        local,
        mesh=mesh,
        in_specs=(P("req", None), P(), P(None, ("req", "tp")), P("req"), P("req"), P("req")),
        out_specs=(P("req"), P("req"), P()),
        check_vma=False,
    )
```

```python
import functools

import jax
import jax.numpy as jnp
from jax import lax
from jax.experimental import pallas as pl
from jax.experimental.pallas import tpu as pltpu
from jax.sharding import PartitionSpec as P

SEQS = 4
PICK = 4
LANES = 128
STATS = 4

VMEM = pltpu.VMEM
SMEM = pltpu.SMEM


def ranks_of(scored_ref, row_count):
    ranks, so_far = [], jnp.int32(0)
    for row in range(row_count):
        ranks.append(so_far)
        so_far = so_far + scored_ref[row]
    return ranks, so_far


def pack_kernel(hidden_ref, gain_ref, targets_ref, segments_ref, scored_ref, out_ref, wide_ref, halves_ref, gains_ref):
    row_count, width = hidden_ref.shape
    half = width // 2
    wide_ref[...] = hidden_ref[...].astype(jnp.float32)
    gains_ref[...] = gain_ref[...].astype(jnp.float32)
    ranks, count = ranks_of(scored_ref, row_count)
    source = [jnp.int32(0)] * PICK
    for row in range(row_count):
        for r in range(PICK):
            hit = jnp.logical_and(scored_ref[row] == 1, ranks[row] == r)
            source[r] = jnp.where(hit, row, source[r])
    for r in range(PICK):
        halves_ref[r : r + 1, :] = wide_ref[pl.ds(source[r], 1), :half]
        halves_ref[PICK + r : PICK + r + 1, :] = wide_ref[pl.ds(source[r], 1), half:]
    values = halves_ref[...]
    part = jnp.sum(values * values, axis=1, keepdims=True)
    part = jnp.broadcast_to(part, (2 * PICK, LANES))
    row_scale = lax.rsqrt((part + pltpu.roll(part, PICK, 0)) / width + 1e-05)
    sub = lax.broadcasted_iota(jnp.int32, (2 * PICK, LANES), 0)
    lane = lax.broadcasted_iota(jnp.int32, (2 * PICK, LANES), 1)
    upper = sub < PICK
    chunks = half // LANES
    for at in range(chunks):
        gain = jnp.where(upper, gains_ref[at : at + 1, :], gains_ref[chunks + at : chunks + at + 1, :])
        piece = halves_ref[:, at * LANES : (at + 1) * LANES]
        piece = (piece * row_scale * gain).astype(jnp.bfloat16)
        out_ref[:, at * LANES : (at + 1) * LANES] = piece
    row_of = jnp.where(upper, sub, sub - PICK)
    side = jnp.zeros((2 * PICK, LANES), jnp.int32)
    for r in range(PICK):
        target = targets_ref[source[r]]
        digits = jnp.where(lane == 0, target & 255, jnp.where(lane == 1, (target >> 8) & 255, target >> 16))
        line = jnp.where(lane < 3, digits, jnp.where(lane == 3, segments_ref[source[r]], (count > r).astype(jnp.int32)))
        side = jnp.where(row_of == r, line, side)
    side = side.astype(jnp.float32).astype(jnp.bfloat16)
    out_ref[:, half:] = side


def stage_kernel(head_ref, out_ref, sems):
    parts = sems.shape[0]
    depth = head_ref.shape[0] // parts
    copies = [
        pltpu.make_async_copy(head_ref.at[pl.ds(i * depth, depth)], out_ref.at[pl.ds(i * depth, depth)], sems.at[i])
        for i in range(parts)
    ]
    for copy in copies:
        copy.start()
    for copy in copies:
        copy.wait()


def score_kernel(groups, place_ref, head_ref, *refs):
    blocks, (stats_ref, meta_ref, rows_ref) = refs[:groups], refs[groups:]
    width, cols = head_ref.shape
    half = width // 2
    used = groups * PICK
    for step, block in enumerate(blocks):
        sender = place_ref[1] - step
        rows_ref[jnp.where(sender < 0, sender + groups, sender)] = block[...]
    rows = rows_ref[:, :, :half].reshape(groups * 2 * PICK, half)
    early = jnp.dot(rows, head_ref[:half, :], preferred_element_type=jnp.float32)
    late = jnp.dot(rows, head_ref[half:, :], preferred_element_type=jnp.float32)
    early = early.reshape(groups // 2, 2, 2 * PICK, cols)
    late = late.reshape(groups // 2, 2, 2 * PICK, cols)
    upper = lax.broadcasted_iota(jnp.int32, (1, 2 * PICK, 1), 1) < PICK

    def swap(block):
        flat = block.reshape(groups // 2 * 2 * PICK, block.shape[-1])
        return jnp.concatenate(
            [pltpu.roll(flat[i * 2 * PICK : (i + 1) * 2 * PICK], PICK, 0) for i in range(groups // 2)], axis=0
        ).reshape(block.shape)

    logits = jnp.where(upper, early[:, 0] + swap(late[:, 0]), swap(early[:, 1]) + late[:, 1])
    logits = logits.reshape(used, cols)
    side = rows_ref[:, :, half:].astype(jnp.float32).reshape(groups // 2, 2, 2 * PICK, LANES)
    side = jnp.where(upper, side[:, 0], side[:, 1]).reshape(used, LANES)
    copies = max(1, LANES // used)
    if copies > 1:
        logits = jnp.concatenate([logits] * copies, axis=0)
        side = jnp.concatenate([side] * copies, axis=0)
    logits = logits.T
    side = side.T
    ids = (side[0:1] + 256.0 * side[1:2] + 65536.0 * side[2:3]).astype(jnp.int32)
    row_top = jnp.max(logits, axis=0, keepdims=True)
    scaled = jnp.exp(logits - row_top)
    row_total = jnp.sum(scaled, axis=0, keepdims=True)
    row_weighted = jnp.sum(scaled * logits, axis=0, keepdims=True)
    columns = place_ref[0] * cols + lax.broadcasted_iota(jnp.int32, logits.shape, 0)
    picked = jnp.sum(jnp.where(columns == ids, logits, 0.0), axis=0, keepdims=True)
    stats = (row_top, row_total, row_weighted, picked)
    if copies > 1:
        lane = lax.broadcasted_iota(jnp.int32, (1, LANES), 1)
        joined = picked
        for at in range(STATS - 1):
            joined = jnp.where(lane // used == at, stats[at], joined)
        stats_ref[...] = joined
    else:
        for at in range(STATS):
            stats_ref[:, at * used : (at + 1) * used] = stats[at]
    meta_ref[...] = side[0:8, :]


def finish_kernel(used, place_ref, scored_ref, stats_ref, meta_ref, logprob_ref, entropy_ref, seq_ref):
    row_count = scored_ref.shape[0]
    lanes = max(used, LANES)

    def stat(at):
        if used >= LANES:
            return stats_ref[:, at * used : (at + 1) * used]
        return stats_ref[...] if at == 0 else pltpu.roll(stats_ref[...], LANES - at * used, 1)

    tops = stat(0)
    row_top = jnp.max(tops, axis=0, keepdims=True)
    weight = jnp.exp(tops - row_top)
    row_total = jnp.sum(stat(1) * weight, axis=0, keepdims=True)
    row_weighted = jnp.sum(stat(2) * weight, axis=0, keepdims=True)
    picked = jnp.sum(stat(3), axis=0, keepdims=True)
    log_norm = row_top + jnp.log(row_total)
    lane = lax.broadcasted_iota(jnp.int32, (1, lanes), 1)
    in_use = jnp.logical_and(meta_ref[4:5, :] > 0.5, lane < used)
    logprob = jnp.where(in_use, picked - log_norm, 0.0)
    entropy = jnp.where(in_use, log_norm - row_weighted / row_total, 0.0)
    sub = lax.broadcasted_iota(jnp.int32, (8, LANES), 0)
    own_lane = lax.broadcasted_iota(jnp.int32, (8, LANES), 1)
    rows_of = lax.broadcasted_iota(jnp.int32, (8, lanes), 0)
    segment = meta_ref[3:4, :].astype(jnp.int32)
    sums = jnp.sum(jnp.where(segment == rows_of, logprob, 0.0), axis=1, keepdims=True)
    seqs = jnp.sum(jnp.where(sub == own_lane, sums, 0.0), axis=0, keepdims=True)
    seq_ref[...] = seqs[0, :SEQS]
    first = place_ref[1] * PICK
    block = first // LANES
    own_logprob, own_entropy = logprob[:, :LANES], entropy[:, :LANES]
    for at in range(1, lanes // LANES):
        piece = slice(at * LANES, (at + 1) * LANES)
        own_logprob = jnp.where(block == at, logprob[:, piece], own_logprob)
        own_entropy = jnp.where(block == at, entropy[:, piece], own_entropy)
    ranks, _ = ranks_of(scored_ref, row_count)
    at = jnp.zeros((8, LANES), jnp.int32)
    keep = jnp.zeros((8, LANES), jnp.int32)
    for row in range(row_count):
        at = jnp.where(own_lane == row, first - block * LANES + ranks[row], at)
        keep = jnp.where(own_lane == row, scored_ref[row], keep)
    at = jnp.minimum(at, LANES - 1)
    both = jnp.where(sub == 0, own_logprob, own_entropy)
    both = jnp.take_along_axis(both, at, axis=1)
    both = jnp.where(keep == 1, both, 0.0)
    logprob_ref[...] = both[0, :row_count]
    entropy_ref[...] = both[1, :row_count]


def sent_to_all(block, axis):
    copies = jnp.broadcast_to(block[None], (lax.axis_size(axis),) + block.shape)
    return lax.all_to_all(copies, axis, 0, 0).reshape((-1,) + block.shape[1:])


def local(hidden, norm_gain, lm_head, targets, segments, scored):
    row_count, width = hidden.shape
    groups, tp_count = lax.axis_size("req"), lax.axis_size("tp")
    own = lax.axis_index("req")
    place = jnp.stack([own * tp_count + lax.axis_index("tp"), own]).astype(jnp.int32)
    half = width // 2
    used = groups * PICK
    lanes = max(used, LANES)

    def spec(space):
        return pl.BlockSpec(memory_space=space)

    packed = pl.pallas_call(
        pack_kernel,
        out_shape=jax.ShapeDtypeStruct((2 * PICK, half + LANES), jnp.bfloat16),
        in_specs=[spec(VMEM)] * 2 + [spec(SMEM)] * 3,
        out_specs=spec(VMEM),
        scratch_shapes=[
            VMEM((row_count, width), jnp.float32),
            VMEM((2 * PICK, half), jnp.float32),
            VMEM((width // LANES, LANES), jnp.float32),
        ],
    )(hidden, norm_gain.reshape(width // LANES, LANES), targets, segments, scored)
    blocks = [packed] + [
        lax.ppermute(packed, "req", [(i, (i + step) % groups) for i in range(groups)]) for step in range(1, groups)
    ]
    head = pl.pallas_call(
        stage_kernel,
        out_shape=VMEM(lm_head.shape, lm_head.dtype),
        in_specs=[spec(pltpu.HBM)],
        out_specs=spec(VMEM),
        scratch_shapes=[pltpu.SemaphoreType.DMA((4,))],
        cost_estimate=pl.CostEstimate(flops=0, bytes_accessed=2 * lm_head.size * 2, transcendentals=0),
    )(pltpu.with_memory_space_constraint(lm_head, pltpu.HBM))
    stats, meta = pl.pallas_call(
        functools.partial(score_kernel, groups),
        out_shape=(
            jax.ShapeDtypeStruct((1, STATS * used), jnp.float32),
            VMEM((8, lanes), jnp.float32),
        ),
        in_specs=[spec(SMEM)] + [spec(VMEM)] * (1 + groups),
        out_specs=(spec(VMEM), spec(VMEM)),
        scratch_shapes=[VMEM((groups, 2 * PICK, half + LANES), jnp.bfloat16)],
        compiler_params=pltpu.CompilerParams(vmem_limit_bytes=40 * 1024 * 1024),
    )(place, pltpu.with_memory_space_constraint(head, VMEM), *blocks)
    gathered = sent_to_all(stats, ("req", "tp"))
    return pl.pallas_call(
        functools.partial(finish_kernel, used),
        out_shape=(
            jax.ShapeDtypeStruct((row_count,), jnp.float32),
            jax.ShapeDtypeStruct((row_count,), jnp.float32),
            jax.ShapeDtypeStruct((SEQS,), jnp.float32),
        ),
        in_specs=[spec(SMEM), spec(SMEM), spec(VMEM), spec(VMEM)],
        out_specs=(spec(VMEM), spec(VMEM), spec(VMEM)),
    )(place, scored, gathered, pltpu.with_memory_space_constraint(meta, VMEM))


def solution(mesh):
    return jax.shard_map(
        local,
        mesh=mesh,
        in_specs=(P("req", None), P(), P(None, ("req", "tp")), P("req"), P("req"), P("req")),
        out_specs=(P("req"), P("req"), P()),
        check_vma=False,
    )
```

```python
import functools

import jax
import jax.numpy as jnp
from jax import lax
from jax.experimental import pallas as pl
from jax.experimental.pallas import tpu as pltpu
from jax.sharding import PartitionSpec as P

SEQS = 4
PICK = 4
PAIR = 2
MINE = PICK // PAIR
SUBS = 8
LANES = 128
STATS = 4

VMEM = pltpu.VMEM
SMEM = pltpu.SMEM


def ranks_of(scored_ref, row_count):
    ranks, so_far = [], jnp.int32(0)
    for row in range(row_count):
        ranks.append(so_far)
        so_far = so_far + scored_ref[row]
    return ranks, so_far


def iota(shape, axis):
    return lax.broadcasted_iota(jnp.int32, shape, axis)


def pack_kernel(share, hidden_ref, gain_ref, targets_ref, segments_ref, scored_ref, out_ref, wide_ref, parts_ref, gains_ref):
    row_count, width = hidden_ref.shape
    parts = SUBS // MINE
    span = width // parts
    own, half = lax.axis_index("req"), lax.axis_index("tp") % PAIR
    wide_ref[...] = hidden_ref[...].astype(jnp.float32)
    gains_ref[...] = gain_ref[...].astype(jnp.float32)
    ranks, count = ranks_of(scored_ref, row_count)
    source = [jnp.int32(0)] * PICK
    for row in range(row_count):
        for r in range(PICK):
            hit = jnp.logical_and(scored_ref[row] == 1, ranks[row] == r)
            source[r] = jnp.where(hit, row, source[r])
    mine = [source[i] for i in range(MINE)]
    for h in range(1, PAIR):
        mine = [jnp.where(half == h, source[h * MINE + i], mine[i]) for i in range(MINE)]
    for i in range(MINE):
        for k in range(parts):
            parts_ref[k * MINE + i : k * MINE + i + 1, :] = wide_ref[pl.ds(mine[i], 1), k * span : (k + 1) * span]
    values = parts_ref[...]
    part = jnp.broadcast_to(jnp.sum(values * values, axis=1, keepdims=True), (SUBS, LANES))
    total = part
    for k in range(1, parts):
        total = total + pltpu.roll(part, k * MINE, 0)
    row_scale = lax.rsqrt(total / width + 1e-05)
    sub, lane = iota((SUBS, LANES), 0), iota((SUBS, LANES), 1)
    chunks = span // LANES
    for at in range(chunks):
        gain = gains_ref[at : at + 1, :]
        for k in range(1, parts):
            gain = jnp.where(sub >= k * MINE, gains_ref[k * chunks + at : k * chunks + at + 1, :], gain)
        piece = parts_ref[:, at * LANES : (at + 1) * LANES]
        piece = (piece * row_scale * gain).astype(jnp.bfloat16)
        for to in range(out_ref.shape[0]):
            out_ref[to, :, at * LANES : (at + 1) * LANES] = piece
    width_side = out_ref.shape[2] - span
    sub, lane = iota((SUBS, width_side), 0), iota((SUBS, width_side), 1)
    at_row, at_half = lane % share - own * MINE, lane // share
    side = jnp.zeros((SUBS, width_side), jnp.int32)
    for i in range(MINE):
        target = targets_ref[mine[i]]
        digits = jnp.where(sub == 0, target & 255, jnp.where(sub == 1, (target >> 8) & 255, target >> 16))
        fields = jnp.zeros((SUBS, width_side), jnp.int32)
        for h in range(PAIR):
            r = h * MINE + i
            field = jnp.where(sub == 3, segments_ref[source[r]], (count > r).astype(jnp.int32))
            fields = jnp.where(at_half == h, field, fields)
        side = jnp.where(at_row == i, jnp.where(sub < 3, digits, jnp.where(sub < 5, fields, 0)), side)
    side = side.astype(jnp.float32).astype(jnp.bfloat16)
    for to in range(out_ref.shape[0]):
        out_ref[to, :, span:] = side


def stage_kernel(head_ref, out_ref, sems):
    parts = sems.shape[0]
    depth = head_ref.shape[0] // parts
    copies = [
        pltpu.make_async_copy(head_ref.at[pl.ds(i * depth, depth)], out_ref.at[pl.ds(i * depth, depth)], sems.at[i])
        for i in range(parts)
    ]
    for copy in copies:
        copy.start()
    for copy in copies:
        copy.wait()


def score_kernel(rows_ref, own_ref, other_ref, stats_ref, meta_ref):
    width, cols = own_ref.shape
    groups = rows_ref.shape[0]
    parts = SUBS // MINE
    span = width // parts
    share = groups * MINE
    tp, tp_count = lax.axis_index("tp"), lax.axis_size("tp")
    half = tp % PAIR
    place = lax.axis_index("req") * tp_count + tp
    meta = rows_ref[0, :, span:].astype(jnp.float32)
    for q in range(1, groups):
        meta = meta + rows_ref[q, :, span:].astype(jnp.float32)
    meta_ref[...] = meta
    rows = rows_ref[:, :, :span].reshape(groups * SUBS, span)
    bundle = iota((1, SUBS, 1), 1) // MINE

    def logits_of(head_ref):
        pieces = [
            jnp.dot(rows, head_ref[k * span : (k + 1) * span, :], preferred_element_type=jnp.float32).reshape(
                groups // parts, parts, SUBS, cols
            )
            for k in range(parts)
        ]
        total = None
        for shift in range(parts):
            picked = None
            for k in range(parts):
                piece = pieces[k][:, (k + shift) % parts]
                picked = piece if picked is None else jnp.where(bundle == k, piece, picked)
            if shift:
                picked = jnp.concatenate(
                    [pltpu.roll(picked[a], shift * MINE, 0)[None] for a in range(groups // parts)], axis=0
                )
            total = picked if total is None else total + picked
        return total.reshape(share, cols)

    logits = jnp.concatenate([logits_of(own_ref), logits_of(other_ref)], axis=1)
    copies = max(1, LANES // share)
    if copies > 1:
        logits = jnp.concatenate([logits] * copies, axis=0)
    logits = logits.T
    lanes = logits.shape[1]
    ids = (meta[0:1, :lanes] + 256.0 * meta[1:2, :lanes] + 65536.0 * meta[2:3, :lanes]).astype(jnp.int32)
    row_top = jnp.max(logits, axis=0, keepdims=True)
    scaled = jnp.exp(logits - row_top)
    row_total = jnp.sum(scaled, axis=0, keepdims=True)
    row_weighted = jnp.sum(scaled * logits, axis=0, keepdims=True)
    column = iota(logits.shape, 0)
    other = place - half + (half + 1) % PAIR
    columns = jnp.where(column < cols, place * cols, (other - 1) * cols) + column
    picked = jnp.sum(jnp.where(columns == ids, logits, 0.0), axis=0, keepdims=True)
    stats = (row_top, row_total, row_weighted, picked)
    if copies > 1:
        lane = iota((1, LANES), 1)
        joined = picked
        for at in range(STATS - 1):
            joined = jnp.where(lane // (PAIR * share) == at, stats[at], joined)
        neutral = jnp.where(lane < PAIR * share, -jnp.inf, 0.0)
        stats_ref[...] = jnp.where(lane // share % PAIR == half, joined, neutral)
    else:
        for at in range(STATS):
            for h in range(PAIR):
                first = (at * PAIR + h) * share
                stats_ref[:, first : first + share] = jnp.where(half == h, stats[at], 0.0 if at else -jnp.inf)


def finish_kernel(share, scored_ref, stats_ref, meta_ref, logprob_ref, entropy_ref, seq_ref):
    row_count = scored_ref.shape[0]
    used = PAIR * share
    lanes = max(used, LANES)

    def stat(at):
        if used >= LANES:
            return stats_ref[:, at * used : (at + 1) * used]
        return stats_ref[...] if at == 0 else pltpu.roll(stats_ref[...], LANES - at * used, 1)

    tops = stat(0)
    row_top = jnp.max(tops, axis=0, keepdims=True)
    weight = jnp.exp(tops - row_top)
    row_total = jnp.sum(stat(1) * weight, axis=0, keepdims=True)
    row_weighted = jnp.sum(stat(2) * weight, axis=0, keepdims=True)
    picked = jnp.sum(stat(3), axis=0, keepdims=True)
    log_norm = row_top + jnp.log(row_total)
    in_use = jnp.logical_and(meta_ref[4:5, :] > 0.5, iota((1, lanes), 1) < used)
    logprob = jnp.where(in_use, picked - log_norm, 0.0)
    entropy = jnp.where(in_use, log_norm - row_weighted / row_total, 0.0)
    sub, lane = iota((SUBS, LANES), 0), iota((SUBS, LANES), 1)
    segment = meta_ref[3:4, :].astype(jnp.int32)
    sums = jnp.sum(jnp.where(segment == iota((SUBS, lanes), 0), logprob, 0.0), axis=1, keepdims=True)
    seqs = jnp.sum(jnp.where(sub == lane, sums, 0.0), axis=0, keepdims=True)
    seq_ref[...] = seqs[0, :SEQS]
    ranks, _ = ranks_of(scored_ref, row_count)
    rank = jnp.zeros((SUBS, LANES), jnp.int32)
    keep = jnp.zeros((SUBS, LANES), jnp.int32)
    for row in range(row_count):
        rank = jnp.where(lane == row, ranks[row], rank)
        keep = jnp.where(lane == row, scored_ref[row], keep)
    mine = jnp.zeros((SUBS, LANES), jnp.float32)
    for h in range(PAIR):
        first = h * share + lax.axis_index("req") * MINE
        block = first // LANES
        own_logprob, own_entropy = logprob[:, :LANES], entropy[:, :LANES]
        for at in range(1, lanes // LANES):
            piece = slice(at * LANES, (at + 1) * LANES)
            own_logprob = jnp.where(block == at, logprob[:, piece], own_logprob)
            own_entropy = jnp.where(block == at, entropy[:, piece], own_entropy)
        both = jnp.where(sub == 0, own_logprob, own_entropy)
        both = jnp.take_along_axis(both, first - block * LANES + rank % MINE, axis=1)
        mine = jnp.where(jnp.logical_and(rank // MINE == h, keep == 1), both, mine)
    logprob_ref[...] = mine[0, :row_count]
    entropy_ref[...] = mine[1, :row_count]


def local(hidden, norm_gain, lm_head, targets, segments, scored):
    row_count, width = hidden.shape
    groups, tp_count = lax.axis_size("req"), lax.axis_size("tp")
    span = width * MINE // SUBS
    share = groups * MINE
    lanes = max(PAIR * share, LANES)

    def spec(space):
        return pl.BlockSpec(memory_space=space)

    other = lax.ppermute(lm_head, "tp", [(i, i + 1 - 2 * (i % PAIR)) for i in range(tp_count)])
    packed = pl.pallas_call(
        functools.partial(pack_kernel, share),
        out_shape=jax.ShapeDtypeStruct((groups, SUBS, span + lanes), jnp.bfloat16),
        in_specs=[spec(VMEM)] * 2 + [spec(SMEM)] * 3,
        out_specs=spec(VMEM),
        scratch_shapes=[
            VMEM((row_count, width), jnp.float32),
            VMEM((SUBS, span), jnp.float32),
            VMEM((width // LANES, LANES), jnp.float32),
        ],
    )(hidden, norm_gain.reshape(width // LANES, LANES), targets, segments, scored)
    rows = lax.all_to_all(packed, "req", 0, 0)
    head = pl.pallas_call(
        stage_kernel,
        out_shape=VMEM(lm_head.shape, lm_head.dtype),
        in_specs=[spec(pltpu.HBM)],
        out_specs=spec(VMEM),
        scratch_shapes=[pltpu.SemaphoreType.DMA((4,))],
        cost_estimate=pl.CostEstimate(flops=0, bytes_accessed=2 * lm_head.size * 2, transcendentals=0),
    )(pltpu.with_memory_space_constraint(lm_head, pltpu.HBM))
    stats, meta = pl.pallas_call(
        score_kernel,
        out_shape=(
            jax.ShapeDtypeStruct((1, STATS * PAIR * share), jnp.float32),
            VMEM((SUBS, lanes), jnp.float32),
        ),
        in_specs=[spec(VMEM)] * 3,
        out_specs=(spec(VMEM), spec(VMEM)),
        compiler_params=pltpu.CompilerParams(vmem_limit_bytes=40 * 1024 * 1024),
    )(rows, pltpu.with_memory_space_constraint(head, VMEM), other)
    gathered = sent_to_all(stats, ("req", "tp"))
    return pl.pallas_call(
        functools.partial(finish_kernel, share),
        out_shape=(
            jax.ShapeDtypeStruct((row_count,), jnp.float32),
            jax.ShapeDtypeStruct((row_count,), jnp.float32),
            jax.ShapeDtypeStruct((SEQS,), jnp.float32),
        ),
        in_specs=[spec(SMEM), spec(VMEM), spec(VMEM)],
        out_specs=(spec(VMEM), spec(VMEM), spec(VMEM)),
    )(scored, gathered, pltpu.with_memory_space_constraint(meta, VMEM))


def sent_to_all(block, axis):
    copies = jnp.broadcast_to(block[None], (lax.axis_size(axis),) + block.shape)
    return lax.all_to_all(copies, axis, 0, 0).reshape((-1,) + block.shape[1:])


def solution(mesh):
    return jax.shard_map(
        local,
        mesh=mesh,
        in_specs=(P("req", None), P(), P(None, ("req", "tp")), P("req"), P("req"), P("req")),
        out_specs=(P("req"), P("req"), P()),
        check_vma=False,
    )
```

```python
import functools

import jax
import jax.numpy as jnp
from jax import lax
from jax.experimental import pallas as pl
from jax.experimental.pallas import tpu as pltpu
from jax.sharding import PartitionSpec as P

SEQS = 4
PICK = 4
PAIR = 2
MINE = PICK // PAIR
SUBS = 8
LANES = 128
STATS = 4

VMEM = pltpu.VMEM
SMEM = pltpu.SMEM


def ranks_of(scored_ref, row_count):
    ranks, so_far = [], jnp.int32(0)
    for row in range(row_count):
        ranks.append(so_far)
        so_far = so_far + scored_ref[row]
    return ranks, so_far


def iota(shape, axis):
    return lax.broadcasted_iota(jnp.int32, shape, axis)


def pack_kernel(share, hidden_ref, gain_ref, targets_ref, segments_ref, scored_ref, out_ref, wide_ref, parts_ref, gains_ref):
    row_count, width = hidden_ref.shape
    parts = SUBS // MINE
    span = width // parts
    own, half = lax.axis_index("req"), lax.axis_index("tp") % PAIR
    wide_ref[...] = hidden_ref[...].astype(jnp.float32)
    gains_ref[...] = gain_ref[...].astype(jnp.float32)
    ranks, count = ranks_of(scored_ref, row_count)
    source = [jnp.int32(0)] * PICK
    for row in range(row_count):
        for r in range(PICK):
            hit = jnp.logical_and(scored_ref[row] == 1, ranks[row] == r)
            source[r] = jnp.where(hit, row, source[r])
    mine = [source[i] for i in range(MINE)]
    for h in range(1, PAIR):
        mine = [jnp.where(half == h, source[h * MINE + i], mine[i]) for i in range(MINE)]
    for i in range(MINE):
        for k in range(parts):
            parts_ref[k * MINE + i : k * MINE + i + 1, :] = wide_ref[pl.ds(mine[i], 1), k * span : (k + 1) * span]
    values = parts_ref[...]
    part = jnp.broadcast_to(jnp.sum(values * values, axis=1, keepdims=True), (SUBS, LANES))
    total = part
    for k in range(1, parts):
        total = total + pltpu.roll(part, k * MINE, 0)
    row_scale = lax.rsqrt(total / width + 1e-05)
    sub, lane = iota((SUBS, LANES), 0), iota((SUBS, LANES), 1)
    chunks = span // LANES
    for at in range(chunks):
        gain = gains_ref[at : at + 1, :]
        for k in range(1, parts):
            gain = jnp.where(sub >= k * MINE, gains_ref[k * chunks + at : k * chunks + at + 1, :], gain)
        piece = parts_ref[:, at * LANES : (at + 1) * LANES]
        piece = (piece * row_scale * gain).astype(jnp.bfloat16)
        for to in range(out_ref.shape[0]):
            out_ref[to, :, at * LANES : (at + 1) * LANES] = piece
    width_side = out_ref.shape[2] - span
    sub, lane = iota((SUBS, width_side), 0), iota((SUBS, width_side), 1)
    at_row, at_half = lane % share - own * MINE, lane // share
    side = jnp.zeros((SUBS, width_side), jnp.int32)
    for i in range(MINE):
        target = targets_ref[mine[i]]
        digits = jnp.where(sub == 0, target & 255, jnp.where(sub == 1, (target >> 8) & 255, target >> 16))
        fields = jnp.zeros((SUBS, width_side), jnp.int32)
        for h in range(PAIR):
            r = h * MINE + i
            field = jnp.where(sub == 3, segments_ref[source[r]], (count > r).astype(jnp.int32))
            fields = jnp.where(at_half == h, field, fields)
        side = jnp.where(at_row == i, jnp.where(sub < 3, digits, jnp.where(sub < 5, fields, 0)), side)
    side = side.astype(jnp.float32).astype(jnp.bfloat16)
    for to in range(out_ref.shape[0]):
        out_ref[to, :, span:] = side


def stage_kernel(head_ref, out_ref, sems):
    parts = sems.shape[0]
    depth = head_ref.shape[0] // parts
    copies = [
        pltpu.make_async_copy(head_ref.at[pl.ds(i * depth, depth)], out_ref.at[pl.ds(i * depth, depth)], sems.at[i])
        for i in range(parts)
    ]
    for copy in copies:
        copy.start()
    for copy in copies:
        copy.wait()


def score_kernel(rows_ref, own_ref, other_ref, stats_ref, meta_ref, ordered_ref):
    width, cols = own_ref.shape
    groups = rows_ref.shape[0]
    parts = SUBS // MINE
    span = width // parts
    share = groups * MINE
    tp, tp_count = lax.axis_index("tp"), lax.axis_size("tp")
    half = tp % PAIR
    place = lax.axis_index("req") * tp_count + tp
    count = groups * SUBS
    into, out_of = iota((count, count), 0), iota((count, count), 1)
    wanted = into % share // MINE * SUBS + into // share * MINE + into % MINE
    order = jnp.where(out_of == wanted, 1.0, 0.0).astype(jnp.bfloat16)
    rows = rows_ref[:, :, :span].reshape(count, span)
    ordered = jnp.dot(order, rows, preferred_element_type=jnp.float32).astype(jnp.bfloat16)
    for k in range(parts):
        ordered_ref[:, k * span : (k + 1) * span] = ordered[k * share : (k + 1) * share]
    meta = rows_ref[0, :, span:].astype(jnp.float32)
    for q in range(1, groups):
        meta = meta + rows_ref[q, :, span:].astype(jnp.float32)
    meta_ref[...] = meta
    logits = jnp.concatenate(
        [jnp.dot(ordered_ref[...], head[...], preferred_element_type=jnp.float32) for head in (own_ref, other_ref)],
        axis=1,
    )
    lanes = max(share, LANES)
    sub, lane = iota((share, lanes), 0), iota((share, lanes), 1)
    ids = meta[0:1, :lanes] + 256.0 * meta[1:2, :lanes] + 65536.0 * meta[2:3, :lanes]
    ids = jnp.sum(jnp.where(lane == sub, ids, 0.0), axis=1, keepdims=True).astype(jnp.int32)
    row_top = jnp.max(logits, axis=1, keepdims=True)
    scaled = jnp.exp(logits - row_top)
    row_total = jnp.sum(scaled, axis=1, keepdims=True)
    row_weighted = jnp.sum(scaled * logits, axis=1, keepdims=True)
    column = iota(logits.shape, 1)
    other = place + 1 - 2 * half
    columns = jnp.where(column < cols, place * cols, (other - 1) * cols) + column
    picked = jnp.sum(jnp.where(columns == ids, logits, 0.0), axis=1, keepdims=True)
    stats = (row_top, row_total, row_weighted, picked)
    if PAIR * share * STATS == LANES:
        joined = picked
        for at in range(STATS - 1):
            joined = jnp.where(lane // (PAIR * share) == at, stats[at], joined)
        joined = jnp.sum(jnp.where(lane % share == sub, joined, 0.0), axis=0, keepdims=True)
        lane = iota((1, LANES), 1)
        neutral = jnp.where(lane < PAIR * share, -jnp.inf, 0.0)
        stats_ref[...] = jnp.where(lane // share % PAIR == half, joined, neutral)
    else:
        for at in range(STATS):
            line = jnp.sum(jnp.where(lane == sub, stats[at], 0.0), axis=0, keepdims=True)
            for h in range(PAIR):
                first = (at * PAIR + h) * share
                stats_ref[:, first : first + share] = jnp.where(half == h, line, 0.0 if at else -jnp.inf)


def finish_kernel(share, scored_ref, stats_ref, meta_ref, logprob_ref, entropy_ref, seq_ref):
    row_count = scored_ref.shape[0]
    used = PAIR * share
    lanes = max(used, LANES)

    def stat(at):
        if used >= LANES:
            return stats_ref[:, at * used : (at + 1) * used]
        return stats_ref[...] if at == 0 else pltpu.roll(stats_ref[...], LANES - at * used, 1)

    tops = stat(0)
    row_top = jnp.max(tops, axis=0, keepdims=True)
    weight = jnp.exp(tops - row_top)
    row_total = jnp.sum(stat(1) * weight, axis=0, keepdims=True)
    row_weighted = jnp.sum(stat(2) * weight, axis=0, keepdims=True)
    picked = jnp.sum(stat(3), axis=0, keepdims=True)
    log_norm = row_top + jnp.log(row_total)
    in_use = jnp.logical_and(meta_ref[4:5, :] > 0.5, iota((1, lanes), 1) < used)
    logprob = jnp.where(in_use, picked - log_norm, 0.0)
    entropy = jnp.where(in_use, log_norm - row_weighted / row_total, 0.0)
    sub, lane = iota((SUBS, LANES), 0), iota((SUBS, LANES), 1)
    segment = meta_ref[3:4, :].astype(jnp.int32)
    sums = jnp.sum(jnp.where(segment == iota((SUBS, lanes), 0), logprob, 0.0), axis=1, keepdims=True)
    seqs = jnp.sum(jnp.where(sub == lane, sums, 0.0), axis=0, keepdims=True)
    seq_ref[...] = seqs[0, :SEQS]
    ranks, _ = ranks_of(scored_ref, row_count)
    rank = jnp.zeros((SUBS, LANES), jnp.int32)
    keep = jnp.zeros((SUBS, LANES), jnp.int32)
    for row in range(row_count):
        rank = jnp.where(lane == row, ranks[row], rank)
        keep = jnp.where(lane == row, scored_ref[row], keep)
    mine = jnp.zeros((SUBS, LANES), jnp.float32)
    for h in range(PAIR):
        first = h * share + lax.axis_index("req") * MINE
        block = first // LANES
        own_logprob, own_entropy = logprob[:, :LANES], entropy[:, :LANES]
        for at in range(1, lanes // LANES):
            piece = slice(at * LANES, (at + 1) * LANES)
            own_logprob = jnp.where(block == at, logprob[:, piece], own_logprob)
            own_entropy = jnp.where(block == at, entropy[:, piece], own_entropy)
        both = jnp.where(sub == 0, own_logprob, own_entropy)
        both = jnp.take_along_axis(both, first - block * LANES + rank % MINE, axis=1)
        mine = jnp.where(jnp.logical_and(rank // MINE == h, keep == 1), both, mine)
    logprob_ref[...] = mine[0, :row_count]
    entropy_ref[...] = mine[1, :row_count]


def local(hidden, norm_gain, lm_head, targets, segments, scored):
    row_count, width = hidden.shape
    groups, tp_count = lax.axis_size("req"), lax.axis_size("tp")
    span = width * MINE // SUBS
    share = groups * MINE
    lanes = max(PAIR * share, LANES)

    def spec(space):
        return pl.BlockSpec(memory_space=space)

    other = lax.ppermute(lm_head, "tp", [(i, i + 1 - 2 * (i % PAIR)) for i in range(tp_count)])
    packed = pl.pallas_call(
        functools.partial(pack_kernel, share),
        out_shape=VMEM((groups, SUBS, span + lanes), jnp.bfloat16),
        in_specs=[spec(VMEM)] * 2 + [spec(SMEM)] * 3,
        out_specs=spec(VMEM),
        scratch_shapes=[
            VMEM((row_count, width), jnp.float32),
            VMEM((SUBS, span), jnp.float32),
            VMEM((width // LANES, LANES), jnp.float32),
        ],
    )(hidden, norm_gain.reshape(width // LANES, LANES), targets, segments, scored)
    rows = lax.all_to_all(packed, "req", 0, 0)
    head = pl.pallas_call(
        stage_kernel,
        out_shape=VMEM(lm_head.shape, lm_head.dtype),
        in_specs=[spec(pltpu.HBM)],
        out_specs=spec(VMEM),
        scratch_shapes=[pltpu.SemaphoreType.DMA((4,))],
        cost_estimate=pl.CostEstimate(flops=0, bytes_accessed=2 * lm_head.size * 2, transcendentals=0),
    )(pltpu.with_memory_space_constraint(lm_head, pltpu.HBM))
    stats, meta = pl.pallas_call(
        score_kernel,
        out_shape=(
            jax.ShapeDtypeStruct((1, STATS * PAIR * share), jnp.float32),
            VMEM((SUBS, lanes), jnp.float32),
        ),
        in_specs=[spec(VMEM)] * 3,
        out_specs=(spec(VMEM), spec(VMEM)),
        scratch_shapes=[VMEM((share, width), jnp.bfloat16)],
        compiler_params=pltpu.CompilerParams(vmem_limit_bytes=40 * 1024 * 1024),
    )(rows, pltpu.with_memory_space_constraint(head, VMEM), other)
    gathered = sent_to_all(stats, ("req", "tp"))
    return pl.pallas_call(
        functools.partial(finish_kernel, share),
        out_shape=(
            jax.ShapeDtypeStruct((row_count,), jnp.float32),
            jax.ShapeDtypeStruct((row_count,), jnp.float32),
            jax.ShapeDtypeStruct((SEQS,), jnp.float32),
        ),
        in_specs=[spec(SMEM), spec(VMEM), spec(VMEM)],
        out_specs=(spec(VMEM), spec(VMEM), spec(VMEM)),
    )(scored, pltpu.with_memory_space_constraint(gathered, VMEM), pltpu.with_memory_space_constraint(meta, VMEM))


def sent_to_all(block, axis):
    copies = jnp.broadcast_to(block[None], (lax.axis_size(axis),) + block.shape)
    return lax.all_to_all(copies, axis, 0, 0).reshape((-1,) + block.shape[1:])


def solution(mesh):
    return jax.shard_map(
        local,
        mesh=mesh,
        in_specs=(P("req", None), P(), P(None, ("req", "tp")), P("req"), P("req"), P("req")),
        out_specs=(P("req"), P("req"), P()),
        check_vma=False,
    )
```

```python
import functools

import jax
import jax.numpy as jnp
from jax import lax
from jax.experimental import pallas as pl
from jax.experimental.pallas import tpu as pltpu
from jax.sharding import PartitionSpec as P

SEQS = 4
PICK = 4
PAIR = 2
MINE = PICK // PAIR
SUBS = 8
LANES = 128
STATS = 4

VMEM = pltpu.VMEM
SMEM = pltpu.SMEM


def ranks_of(scored_ref, row_count):
    ranks, so_far = [], jnp.int32(0)
    for row in range(row_count):
        ranks.append(so_far)
        so_far = so_far + scored_ref[row]
    return ranks, so_far


def iota(shape, axis):
    return lax.broadcasted_iota(jnp.int32, shape, axis)


def pack_kernel(share, hidden_ref, gain_ref, targets_ref, segments_ref, scored_ref, out_ref, wide_ref, parts_ref, gains_ref):
    row_count, width = hidden_ref.shape
    parts = SUBS // MINE
    span = width // parts
    own, half = lax.axis_index("req"), lax.axis_index("tp") % PAIR
    wide_ref[...] = hidden_ref[...].astype(jnp.float32)
    gains_ref[...] = gain_ref[...].astype(jnp.float32)
    ranks, count = ranks_of(scored_ref, row_count)
    source = [jnp.int32(0)] * PICK
    for row in range(row_count):
        for r in range(PICK):
            hit = jnp.logical_and(scored_ref[row] == 1, ranks[row] == r)
            source[r] = jnp.where(hit, row, source[r])
    mine = [source[i] for i in range(MINE)]
    for h in range(1, PAIR):
        mine = [jnp.where(half == h, source[h * MINE + i], mine[i]) for i in range(MINE)]
    for i in range(MINE):
        for k in range(parts):
            parts_ref[k * MINE + i : k * MINE + i + 1, :] = wide_ref[pl.ds(mine[i], 1), k * span : (k + 1) * span]
    values = parts_ref[...]
    part = jnp.broadcast_to(jnp.sum(values * values, axis=1, keepdims=True), (SUBS, LANES))
    total = part
    for k in range(1, parts):
        total = total + pltpu.roll(part, k * MINE, 0)
    row_scale = lax.rsqrt(total / width + 1e-05)
    sub, lane = iota((SUBS, LANES), 0), iota((SUBS, LANES), 1)
    chunks = span // LANES
    for at in range(chunks):
        gain = gains_ref[at : at + 1, :]
        for k in range(1, parts):
            gain = jnp.where(sub >= k * MINE, gains_ref[k * chunks + at : k * chunks + at + 1, :], gain)
        piece = parts_ref[:, at * LANES : (at + 1) * LANES]
        piece = (piece * row_scale * gain).astype(jnp.bfloat16)
        for to in range(out_ref.shape[0]):
            out_ref[to, :, at * LANES : (at + 1) * LANES] = piece
    width_side = out_ref.shape[2] - span
    sub, lane = iota((SUBS, width_side), 0), iota((SUBS, width_side), 1)
    at_row, at_half = lane % share - own * MINE, lane // share
    side = jnp.zeros((SUBS, width_side), jnp.int32)
    for i in range(MINE):
        target = targets_ref[mine[i]]
        digits = jnp.where(sub == 0, target & 255, jnp.where(sub == 1, (target >> 8) & 255, target >> 16))
        fields = jnp.zeros((SUBS, width_side), jnp.int32)
        for h in range(PAIR):
            r = h * MINE + i
            field = jnp.where(sub == 3, segments_ref[source[r]], (count > r).astype(jnp.int32))
            fields = jnp.where(at_half == h, field, fields)
        side = jnp.where(at_row == i, jnp.where(sub < 3, digits, jnp.where(sub < 5, fields, 0)), side)
    side = side.astype(jnp.float32).astype(jnp.bfloat16)
    for to in range(out_ref.shape[0]):
        out_ref[to, :, span:] = side


def stage_kernel(own_ref, other_ref, own_out, other_out, sems):
    copies = []
    for at, (source, out) in enumerate(((own_ref, own_out), (other_ref, other_out))):
        depth = out.shape[0] // sems.shape[1]
        for i in range(sems.shape[1]):
            piece = pl.ds(i * depth, depth)
            copies.append(pltpu.make_async_copy(source.at[piece], out.at[piece], sems.at[at, i]))
    for copy in copies:
        copy.start()
    for copy in copies:
        copy.wait()


def score_kernel(rows_ref, own_ref, upper_ref, other_ref, stats_ref, meta_ref, ordered_ref, lower_ref, sems):
    width, cols = own_ref.shape
    staged = upper_ref.shape[0]
    depth = lower_ref.shape[0] // sems.shape[0]
    copies = [
        pltpu.make_async_copy(
            other_ref.at[pl.ds(staged + i * depth, depth)], lower_ref.at[pl.ds(i * depth, depth)], sems.at[i]
        )
        for i in range(sems.shape[0])
    ]
    for copy in copies:
        copy.start()
    groups = rows_ref.shape[0]
    parts = SUBS // MINE
    span = width // parts
    share = groups * MINE
    tp, tp_count = lax.axis_index("tp"), lax.axis_size("tp")
    half = tp % PAIR
    place = lax.axis_index("req") * tp_count + tp
    count = groups * SUBS
    into, out_of = iota((count, count), 0), iota((count, count), 1)
    wanted = into % share // MINE * SUBS + into // share * MINE + into % MINE
    order = jnp.where(out_of == wanted, 1.0, 0.0).astype(jnp.bfloat16)
    rows = rows_ref[:, :, :span].reshape(count, span)
    ordered = jnp.dot(order, rows, preferred_element_type=jnp.float32).astype(jnp.bfloat16)
    for k in range(parts):
        ordered_ref[:, k * span : (k + 1) * span] = ordered[k * share : (k + 1) * share]
    meta = rows_ref[0, :, span:].astype(jnp.float32)
    for q in range(1, groups):
        meta = meta + rows_ref[q, :, span:].astype(jnp.float32)
    meta_ref[...] = meta
    own_logits = jnp.dot(ordered_ref[...], own_ref[...], preferred_element_type=jnp.float32)
    other_logits = jnp.dot(ordered_ref[:, :staged], upper_ref[...], preferred_element_type=jnp.float32)
    for copy in copies:
        copy.wait()
    other_logits += jnp.dot(ordered_ref[:, staged:], lower_ref[...], preferred_element_type=jnp.float32)
    logits = jnp.concatenate([own_logits, other_logits], axis=1)
    lanes = max(share, LANES)
    sub, lane = iota((share, lanes), 0), iota((share, lanes), 1)
    ids = meta[0:1, :lanes] + 256.0 * meta[1:2, :lanes] + 65536.0 * meta[2:3, :lanes]
    ids = jnp.sum(jnp.where(lane == sub, ids, 0.0), axis=1, keepdims=True).astype(jnp.int32)
    row_top = jnp.max(logits, axis=1, keepdims=True)
    scaled = jnp.exp(logits - row_top)
    row_total = jnp.sum(scaled, axis=1, keepdims=True)
    row_weighted = jnp.sum(scaled * logits, axis=1, keepdims=True)
    column = iota(logits.shape, 1)
    other = place + 1 - 2 * half
    columns = jnp.where(column < cols, place * cols, (other - 1) * cols) + column
    picked = jnp.sum(jnp.where(columns == ids, logits, 0.0), axis=1, keepdims=True)
    stats = (row_top, row_total, row_weighted, picked)
    if PAIR * share * STATS == LANES:
        joined = picked
        for at in range(STATS - 1):
            joined = jnp.where(lane // (PAIR * share) == at, stats[at], joined)
        joined = jnp.sum(jnp.where(lane % share == sub, joined, 0.0), axis=0, keepdims=True)
        lane = iota((1, LANES), 1)
        neutral = jnp.where(lane < PAIR * share, -jnp.inf, 0.0)
        stats_ref[...] = jnp.where(lane // share % PAIR == half, joined, neutral)
    else:
        for at in range(STATS):
            line = jnp.sum(jnp.where(lane == sub, stats[at], 0.0), axis=0, keepdims=True)
            for h in range(PAIR):
                first = (at * PAIR + h) * share
                stats_ref[:, first : first + share] = jnp.where(half == h, line, 0.0 if at else -jnp.inf)


def finish_kernel(share, scored_ref, stats_ref, meta_ref, logprob_ref, entropy_ref, seq_ref):
    row_count = scored_ref.shape[0]
    used = PAIR * share
    lanes = max(used, LANES)

    def stat(at):
        if used >= LANES:
            return stats_ref[:, at * used : (at + 1) * used]
        return stats_ref[...] if at == 0 else pltpu.roll(stats_ref[...], LANES - at * used, 1)

    tops = stat(0)
    row_top = jnp.max(tops, axis=0, keepdims=True)
    weight = jnp.exp(tops - row_top)
    row_total = jnp.sum(stat(1) * weight, axis=0, keepdims=True)
    row_weighted = jnp.sum(stat(2) * weight, axis=0, keepdims=True)
    picked = jnp.sum(stat(3), axis=0, keepdims=True)
    log_norm = row_top + jnp.log(row_total)
    in_use = jnp.logical_and(meta_ref[4:5, :] > 0.5, iota((1, lanes), 1) < used)
    logprob = jnp.where(in_use, picked - log_norm, 0.0)
    entropy = jnp.where(in_use, log_norm - row_weighted / row_total, 0.0)
    sub, lane = iota((SUBS, LANES), 0), iota((SUBS, LANES), 1)
    segment = meta_ref[3:4, :].astype(jnp.int32)
    sums = jnp.sum(jnp.where(segment == iota((SUBS, lanes), 0), logprob, 0.0), axis=1, keepdims=True)
    seqs = jnp.sum(jnp.where(sub == lane, sums, 0.0), axis=0, keepdims=True)
    seq_ref[...] = seqs[0, :SEQS]
    ranks, _ = ranks_of(scored_ref, row_count)
    rank = jnp.zeros((SUBS, LANES), jnp.int32)
    keep = jnp.zeros((SUBS, LANES), jnp.int32)
    for row in range(row_count):
        rank = jnp.where(lane == row, ranks[row], rank)
        keep = jnp.where(lane == row, scored_ref[row], keep)
    mine = jnp.zeros((SUBS, LANES), jnp.float32)
    for h in range(PAIR):
        first = h * share + lax.axis_index("req") * MINE
        block = first // LANES
        own_logprob, own_entropy = logprob[:, :LANES], entropy[:, :LANES]
        for at in range(1, lanes // LANES):
            piece = slice(at * LANES, (at + 1) * LANES)
            own_logprob = jnp.where(block == at, logprob[:, piece], own_logprob)
            own_entropy = jnp.where(block == at, entropy[:, piece], own_entropy)
        both = jnp.where(sub == 0, own_logprob, own_entropy)
        both = jnp.take_along_axis(both, first - block * LANES + rank % MINE, axis=1)
        mine = jnp.where(jnp.logical_and(rank // MINE == h, keep == 1), both, mine)
    logprob_ref[...] = mine[0, :row_count]
    entropy_ref[...] = mine[1, :row_count]


def grant(mebibytes):
    return pltpu.CompilerParams(vmem_limit_bytes=mebibytes * 1024 * 1024)


def local(hidden, norm_gain, lm_head, targets, segments, scored):
    row_count, width = hidden.shape
    groups, tp_count = lax.axis_size("req"), lax.axis_size("tp")
    span = width * MINE // SUBS
    share = groups * MINE
    lanes = max(PAIR * share, LANES)

    def spec(space):
        return pl.BlockSpec(memory_space=space)

    other = lax.ppermute(lm_head, "tp", [(i, i + 1 - 2 * (i % PAIR)) for i in range(tp_count)])
    packed = pl.pallas_call(
        functools.partial(pack_kernel, share),
        out_shape=VMEM((groups, SUBS, span + lanes), jnp.bfloat16),
        in_specs=[spec(VMEM)] * 2 + [spec(SMEM)] * 3,
        out_specs=spec(VMEM),
        scratch_shapes=[
            VMEM((row_count, width), jnp.float32),
            VMEM((SUBS, span), jnp.float32),
            VMEM((width // LANES, LANES), jnp.float32),
        ],
    )(hidden, norm_gain.reshape(width // LANES, LANES), targets, segments, scored)
    rows = lax.all_to_all(packed, "req", 0, 0)
    other = pltpu.with_memory_space_constraint(other, pltpu.HBM)
    staged = width // 2
    slices = pl.pallas_call(
        stage_kernel,
        out_shape=(VMEM(lm_head.shape, lm_head.dtype), VMEM((staged, lm_head.shape[1]), lm_head.dtype)),
        in_specs=[spec(pltpu.HBM)] * 2,
        out_specs=(spec(VMEM),) * 2,
        scratch_shapes=[pltpu.SemaphoreType.DMA((2, 4))],
        compiler_params=grant(4),
        cost_estimate=pl.CostEstimate(flops=0, bytes_accessed=3 * 2 * lm_head.size, transcendentals=0),
    )(pltpu.with_memory_space_constraint(lm_head, pltpu.HBM), other)
    stats, meta = pl.pallas_call(
        score_kernel,
        out_shape=(
            jax.ShapeDtypeStruct((1, STATS * PAIR * share), jnp.float32),
            VMEM((SUBS, lanes), jnp.float32),
        ),
        in_specs=[spec(VMEM)] * 3 + [spec(pltpu.HBM)],
        out_specs=(spec(VMEM), spec(VMEM)),
        scratch_shapes=[
            VMEM((share, width), jnp.bfloat16),
            VMEM((width - staged, lm_head.shape[1]), jnp.bfloat16),
            pltpu.SemaphoreType.DMA((4,)),
        ],
        compiler_params=grant(24),
    )(rows, *(pltpu.with_memory_space_constraint(part, VMEM) for part in slices), other)
    gathered = sent_to_all(stats, ("req", "tp"))
    return pl.pallas_call(
        functools.partial(finish_kernel, share),
        out_shape=(
            jax.ShapeDtypeStruct((row_count,), jnp.float32),
            jax.ShapeDtypeStruct((row_count,), jnp.float32),
            jax.ShapeDtypeStruct((SEQS,), jnp.float32),
        ),
        in_specs=[spec(SMEM), spec(VMEM), spec(VMEM)],
        out_specs=(spec(VMEM), spec(VMEM), spec(VMEM)),
    )(scored, pltpu.with_memory_space_constraint(gathered, VMEM), pltpu.with_memory_space_constraint(meta, VMEM))


def sent_to_all(block, axis):
    copies = jnp.broadcast_to(block[None], (lax.axis_size(axis),) + block.shape)
    return lax.all_to_all(copies, axis, 0, 0).reshape((-1,) + block.shape[1:])


def solution(mesh):
    return jax.shard_map(
        local,
        mesh=mesh,
        in_specs=(P("req", None), P(), P(None, ("req", "tp")), P("req"), P("req"), P("req")),
        out_specs=(P("req"), P("req"), P()),
        check_vma=False,
    )
```

```python
import functools

import jax
import jax.numpy as jnp
from jax import lax
from jax.experimental import pallas as pl
from jax.experimental.pallas import tpu as pltpu
from jax.sharding import PartitionSpec as P

SEQS = 4
PICK = 4
PAIR = 2
MINE = PICK // PAIR
SUBS = 8
LANES = 128
STATS = 4

VMEM = pltpu.VMEM
SMEM = pltpu.SMEM


def ranks_of(scored_ref, row_count):
    ranks, so_far = [], jnp.int32(0)
    for row in range(row_count):
        ranks.append(so_far)
        so_far = so_far + scored_ref[row]
    return ranks, so_far


def iota(shape, axis):
    return lax.broadcasted_iota(jnp.int32, shape, axis)


def pack_kernel(share, hidden_ref, gain_ref, targets_ref, segments_ref, scored_ref, out_ref, wide_ref, scale_ref, gains_ref, parts_ref):
    row_count, width = hidden_ref.shape
    receivers, _, length = out_ref.shape
    span = length - max(PAIR * share, LANES)
    pieces = SUBS // MINE
    own, part = lax.axis_index("req"), lax.axis_index("tp")
    wide = hidden_ref[...].astype(jnp.float32)
    for chunk in range(width // LANES):
        wide_ref[chunk] = wide[:, chunk * LANES : (chunk + 1) * LANES]
    total = jnp.broadcast_to(jnp.sum(wide * wide, axis=1, keepdims=True), (row_count, LANES))
    scale_ref[...] = lax.rsqrt(total / width + 1e-05)
    gains_ref[...] = gain_ref[...].astype(jnp.float32)
    ranks, count = ranks_of(scored_ref, row_count)
    source = [jnp.int32(0)] * PICK
    for row in range(row_count):
        for r in range(PICK):
            hit = jnp.logical_and(scored_ref[row] == 1, ranks[row] == r)
            source[r] = jnp.where(hit, row, source[r])
    for r in range(PICK):
        scale = scale_ref[pl.ds(source[r], 1), :]
        for j in range(pieces):
            at = j * MINE + r % MINE
            for chunk in range(span // LANES):
                column = (part * pieces + j) * (span // LANES) + chunk
                values = wide_ref[column, pl.ds(source[r], 1), :]
                gain = gains_ref[pl.ds(column, 1), :]
                parts_ref[r // MINE, at : at + 1, chunk * LANES : (chunk + 1) * LANES] = values * scale * gain
    for to in range(receivers):
        out_ref[to, :, :span] = parts_ref[to % PAIR].astype(jnp.bfloat16)
    sub, lane = iota((SUBS, length - span), 0), iota((SUBS, length - span), 1)
    side = jnp.zeros((SUBS, length - span), jnp.int32)
    for r in range(PICK):
        target = targets_ref[source[r]]
        field = jnp.where(sub == 0, target & 255, jnp.where(sub == 1, (target >> 8) & 255, target >> 16))
        field = jnp.where(sub < 3, field, jnp.where(sub == 3, segments_ref[source[r]], (count > r).astype(jnp.int32)))
        side = jnp.where(lane == r // MINE * share + own * MINE + r % MINE, field, side)
    side = side.astype(jnp.float32).astype(jnp.bfloat16)
    for to in range(receivers):
        out_ref[to, :, span:] = side


def stage_kernel(own_ref, other_ref, own_out, other_out, sems):
    copies = []
    for at, (source, out) in enumerate(((own_ref, own_out), (other_ref, other_out))):
        depth = out.shape[0] // sems.shape[1]
        for i in range(sems.shape[1]):
            piece = pl.ds(i * depth, depth)
            copies.append(pltpu.make_async_copy(source.at[piece], out.at[piece], sems.at[at, i]))
    for copy in copies:
        copy.start()
    for copy in copies:
        copy.wait()


def score_kernel(rows_ref, own_ref, upper_ref, other_ref, stats_ref, meta_ref, ordered_ref, lower_ref, sems):
    width, cols = own_ref.shape
    staged = upper_ref.shape[0]
    depth = lower_ref.shape[0] // sems.shape[0]
    copies = [
        pltpu.make_async_copy(
            other_ref.at[pl.ds(staged + i * depth, depth)], lower_ref.at[pl.ds(i * depth, depth)], sems.at[i]
        )
        for i in range(sems.shape[0])
    ]
    for copy in copies:
        copy.start()
    tp, tp_count = lax.axis_index("tp"), lax.axis_size("tp")
    groups = rows_ref.shape[0] // tp_count
    pieces = SUBS // MINE
    span = width // (tp_count * pieces)
    share = groups * MINE
    half = tp % PAIR
    place = lax.axis_index("req") * tp_count + tp
    batch = min(groups, 8)
    count, rows_of = batch * tp_count * SUBS, batch * MINE
    into, out_of = iota((count, count), 0), iota((count, count), 1)
    wanted = into % rows_of // MINE * (tp_count * SUBS) + into // rows_of * MINE + into % MINE
    order = jnp.where(out_of == wanted, 1.0, 0.0).astype(jnp.bfloat16)
    for first in range(0, groups, batch):
        rows = rows_ref[first * tp_count : (first + batch) * tp_count, :, :span].reshape(count, span)
        ordered = jnp.dot(order, rows, preferred_element_type=jnp.float32).astype(jnp.bfloat16)
        for k in range(tp_count * pieces):
            ordered_ref[first * MINE : first * MINE + rows_of, k * span : (k + 1) * span] = ordered[
                k * rows_of : (k + 1) * rows_of
            ]
    meta = rows_ref[0, :, span:].astype(jnp.float32)
    for q in range(1, groups):
        meta = meta + rows_ref[q * tp_count, :, span:].astype(jnp.float32)
    meta_ref[...] = meta
    own_logits = jnp.dot(ordered_ref[...], own_ref[...], preferred_element_type=jnp.float32)
    other_logits = jnp.dot(ordered_ref[:, :staged], upper_ref[...], preferred_element_type=jnp.float32)
    for copy in copies:
        copy.wait()
    other_logits += jnp.dot(ordered_ref[:, staged:], lower_ref[...], preferred_element_type=jnp.float32)
    logits = jnp.concatenate([own_logits, other_logits], axis=1)
    lanes = max(share, LANES)
    sub, lane = iota((share, lanes), 0), iota((share, lanes), 1)
    ids = meta[0:1, :] + 256.0 * meta[1:2, :] + 65536.0 * meta[2:3, :]
    wanted = iota((share, meta.shape[1]), 1) == half * share + iota((share, meta.shape[1]), 0)
    ids = jnp.sum(jnp.where(wanted, ids, 0.0), axis=1, keepdims=True).astype(jnp.int32)
    row_top = jnp.max(logits, axis=1, keepdims=True)
    scaled = jnp.exp(logits - row_top)
    row_total = jnp.sum(scaled, axis=1, keepdims=True)
    row_weighted = jnp.sum(scaled * logits, axis=1, keepdims=True)
    column = iota(logits.shape, 1)
    other = place + 1 - 2 * half
    columns = jnp.where(column < cols, place * cols, (other - 1) * cols) + column
    picked = jnp.sum(jnp.where(columns == ids, logits, 0.0), axis=1, keepdims=True)
    stats = (row_top, row_total, row_weighted, picked)
    if PAIR * share * STATS == LANES:
        joined = picked
        for at in range(STATS - 1):
            joined = jnp.where(lane // (PAIR * share) == at, stats[at], joined)
        joined = jnp.sum(jnp.where(lane % share == sub, joined, 0.0), axis=0, keepdims=True)
        lane = iota((1, LANES), 1)
        neutral = jnp.where(lane < PAIR * share, -jnp.inf, 0.0)
        stats_ref[...] = jnp.where(lane // share % PAIR == half, joined, neutral)
    else:
        for at in range(STATS):
            line = jnp.sum(jnp.where(lane == sub, stats[at], 0.0), axis=0, keepdims=True)
            for h in range(PAIR):
                first = (at * PAIR + h) * share
                stats_ref[:, first : first + share] = jnp.where(half == h, line, 0.0 if at else -jnp.inf)


def finish_kernel(share, scored_ref, stats_ref, meta_ref, logprob_ref, entropy_ref, seq_ref):
    row_count = scored_ref.shape[0]
    used = PAIR * share
    lanes = max(used, LANES)

    def stat(at):
        if used >= LANES:
            return stats_ref[:, at * used : (at + 1) * used]
        return stats_ref[...] if at == 0 else pltpu.roll(stats_ref[...], LANES - at * used, 1)

    tops = stat(0)
    row_top = jnp.max(tops, axis=0, keepdims=True)
    weight = jnp.exp(tops - row_top)
    row_total = jnp.sum(stat(1) * weight, axis=0, keepdims=True)
    row_weighted = jnp.sum(stat(2) * weight, axis=0, keepdims=True)
    picked = jnp.sum(stat(3), axis=0, keepdims=True)
    log_norm = row_top + jnp.log(row_total)
    in_use = jnp.logical_and(meta_ref[4:5, :] > 0.5, iota((1, lanes), 1) < used)
    logprob = jnp.where(in_use, picked - log_norm, 0.0)
    entropy = jnp.where(in_use, log_norm - row_weighted / row_total, 0.0)
    sub, lane = iota((SUBS, LANES), 0), iota((SUBS, LANES), 1)
    segment = meta_ref[3:4, :].astype(jnp.int32)
    sums = jnp.sum(jnp.where(segment == iota((SUBS, lanes), 0), logprob, 0.0), axis=1, keepdims=True)
    seqs = jnp.sum(jnp.where(sub == lane, sums, 0.0), axis=0, keepdims=True)
    seq_ref[...] = seqs[0, :SEQS]
    ranks, _ = ranks_of(scored_ref, row_count)
    rank = jnp.zeros((SUBS, LANES), jnp.int32)
    keep = jnp.zeros((SUBS, LANES), jnp.int32)
    for row in range(row_count):
        rank = jnp.where(lane == row, ranks[row], rank)
        keep = jnp.where(lane == row, scored_ref[row], keep)
    mine = jnp.zeros((SUBS, LANES), jnp.float32)
    for h in range(PAIR):
        first = h * share + lax.axis_index("req") * MINE
        block = first // LANES
        own_logprob, own_entropy = logprob[:, :LANES], entropy[:, :LANES]
        for at in range(1, lanes // LANES):
            piece = slice(at * LANES, (at + 1) * LANES)
            own_logprob = jnp.where(block == at, logprob[:, piece], own_logprob)
            own_entropy = jnp.where(block == at, entropy[:, piece], own_entropy)
        both = jnp.where(sub == 0, own_logprob, own_entropy)
        both = jnp.take_along_axis(both, first - block * LANES + rank % MINE, axis=1)
        mine = jnp.where(jnp.logical_and(rank // MINE == h, keep == 1), both, mine)
    logprob_ref[...] = mine[0, :row_count]
    entropy_ref[...] = mine[1, :row_count]


def grant(mebibytes):
    return pltpu.CompilerParams(vmem_limit_bytes=mebibytes * 1024 * 1024)


def local(hidden, norm_gain, lm_head, targets, segments, scored):
    row_count, width = hidden.shape
    groups, tp_count = lax.axis_size("req"), lax.axis_size("tp")
    span = width * MINE // SUBS // tp_count
    share = groups * MINE
    lanes = max(PAIR * share, LANES)

    def spec(space):
        return pl.BlockSpec(memory_space=space)

    other = lax.ppermute(lm_head, "tp", [(i, i + 1 - 2 * (i % PAIR)) for i in range(tp_count)])
    packed = pl.pallas_call(
        functools.partial(pack_kernel, share),
        out_shape=jax.ShapeDtypeStruct((groups * tp_count, SUBS, span + lanes), jnp.bfloat16),
        in_specs=[spec(VMEM)] * 2 + [spec(SMEM)] * 3,
        out_specs=spec(VMEM),
        scratch_shapes=[
            VMEM((width // LANES, row_count, LANES), jnp.float32),
            VMEM((row_count, LANES), jnp.float32),
            VMEM((width // LANES, LANES), jnp.float32),
            VMEM((PAIR, SUBS, span), jnp.float32),
        ],
    )(hidden, norm_gain.reshape(width // LANES, LANES), targets, segments, scored)
    rows = lax.all_to_all(packed, ("req", "tp"), 0, 0)
    other = pltpu.with_memory_space_constraint(other, pltpu.HBM)
    staged = width // 2
    slices = pl.pallas_call(
        stage_kernel,
        out_shape=(VMEM(lm_head.shape, lm_head.dtype), VMEM((staged, lm_head.shape[1]), lm_head.dtype)),
        in_specs=[spec(pltpu.HBM)] * 2,
        out_specs=(spec(VMEM),) * 2,
        scratch_shapes=[pltpu.SemaphoreType.DMA((2, 4))],
        compiler_params=grant(4),
        cost_estimate=pl.CostEstimate(flops=0, bytes_accessed=3 * 2 * lm_head.size, transcendentals=0),
    )(pltpu.with_memory_space_constraint(lm_head, pltpu.HBM), other)
    stats, meta = pl.pallas_call(
        score_kernel,
        out_shape=(
            jax.ShapeDtypeStruct((1, STATS * PAIR * share), jnp.float32),
            VMEM((SUBS, lanes), jnp.float32),
        ),
        in_specs=[spec(VMEM)] * 3 + [spec(pltpu.HBM)],
        out_specs=(spec(VMEM), spec(VMEM)),
        scratch_shapes=[
            VMEM((share, width), jnp.bfloat16),
            VMEM((width - staged, lm_head.shape[1]), jnp.bfloat16),
            pltpu.SemaphoreType.DMA((4,)),
        ],
        compiler_params=grant(24),
    )(rows, *(pltpu.with_memory_space_constraint(part, VMEM) for part in slices), other)
    gathered = sent_to_all(stats, ("req", "tp"))
    return pl.pallas_call(
        functools.partial(finish_kernel, share),
        out_shape=(
            jax.ShapeDtypeStruct((row_count,), jnp.float32),
            jax.ShapeDtypeStruct((row_count,), jnp.float32),
            jax.ShapeDtypeStruct((SEQS,), jnp.float32),
        ),
        in_specs=[spec(SMEM), spec(VMEM), spec(VMEM)],
        out_specs=(spec(VMEM), spec(VMEM), spec(VMEM)),
    )(scored, pltpu.with_memory_space_constraint(gathered, VMEM), pltpu.with_memory_space_constraint(meta, VMEM))


def sent_to_all(block, axis):
    copies = jnp.broadcast_to(block[None], (lax.axis_size(axis),) + block.shape)
    return lax.all_to_all(copies, axis, 0, 0).reshape((-1,) + block.shape[1:])


def solution(mesh):
    return jax.shard_map(
        local,
        mesh=mesh,
        in_specs=(P("req", None), P(), P(None, ("req", "tp")), P("req"), P("req"), P("req")),
        out_specs=(P("req"), P("req"), P()),
        check_vma=False,
    )
```

```python
import functools

import jax
import jax.numpy as jnp
from jax import lax
from jax.experimental import pallas as pl
from jax.experimental.pallas import tpu as pltpu
from jax.sharding import PartitionSpec as P

SEQS = 4
PICK = 4
PAIR = 2
MINE = PICK // PAIR
SUBS = 8
LANES = 128
STATS = 4

VMEM = pltpu.VMEM
SMEM = pltpu.SMEM


def ranks_of(scored_ref, row_count):
    ranks, so_far = [], jnp.int32(0)
    for row in range(row_count):
        ranks.append(so_far)
        so_far = so_far + scored_ref[row]
    return ranks, so_far


def iota(shape, axis):
    return lax.broadcasted_iota(jnp.int32, shape, axis)


def pack_kernel(share, hidden_ref, gain_ref, targets_ref, segments_ref, scored_ref, out_ref, wide_ref, parts_ref, gains_ref):
    row_count, width = hidden_ref.shape
    parts = SUBS // MINE
    span = width // parts
    own, half = lax.axis_index("req"), lax.axis_index("tp") % PAIR
    wide_ref[...] = hidden_ref[...].astype(jnp.float32)
    gains_ref[...] = gain_ref[...].astype(jnp.float32)
    ranks, count = ranks_of(scored_ref, row_count)
    source = [jnp.int32(0)] * PICK
    for row in range(row_count):
        for r in range(PICK):
            hit = jnp.logical_and(scored_ref[row] == 1, ranks[row] == r)
            source[r] = jnp.where(hit, row, source[r])
    mine = [source[i] for i in range(MINE)]
    for h in range(1, PAIR):
        mine = [jnp.where(half == h, source[h * MINE + i], mine[i]) for i in range(MINE)]
    for i in range(MINE):
        for k in range(parts):
            parts_ref[k * MINE + i : k * MINE + i + 1, :] = wide_ref[pl.ds(mine[i], 1), k * span : (k + 1) * span]
    values = parts_ref[...]
    part = jnp.broadcast_to(jnp.sum(values * values, axis=1, keepdims=True), (SUBS, LANES))
    total = part
    for k in range(1, parts):
        total = total + pltpu.roll(part, k * MINE, 0)
    row_scale = lax.rsqrt(total / width + 1e-05)
    sub, lane = iota((SUBS, LANES), 0), iota((SUBS, LANES), 1)
    chunks = span // LANES
    for at in range(chunks):
        gain = gains_ref[at : at + 1, :]
        for k in range(1, parts):
            gain = jnp.where(sub >= k * MINE, gains_ref[k * chunks + at : k * chunks + at + 1, :], gain)
        piece = parts_ref[:, at * LANES : (at + 1) * LANES]
        piece = (piece * row_scale * gain).astype(jnp.bfloat16)
        for to in range(out_ref.shape[0]):
            out_ref[to, :, at * LANES : (at + 1) * LANES] = piece
    width_side = out_ref.shape[2] - span
    sub, lane = iota((SUBS, width_side), 0), iota((SUBS, width_side), 1)
    at_row, at_half = lane % share - own * MINE, lane // share
    side = jnp.zeros((SUBS, width_side), jnp.int32)
    for i in range(MINE):
        target = targets_ref[mine[i]]
        digits = jnp.where(sub == 0, target & 255, jnp.where(sub == 1, (target >> 8) & 255, target >> 16))
        fields = jnp.zeros((SUBS, width_side), jnp.int32)
        for h in range(PAIR):
            r = h * MINE + i
            field = jnp.where(sub == 4, (count > r).astype(jnp.int32), source[r])
            fields = jnp.where(at_half == h, jnp.where(sub == 3, segments_ref[source[r]], field), fields)
        side = jnp.where(at_row == i, jnp.where(sub < 3, digits, fields), side)
    side = side.astype(jnp.float32).astype(jnp.bfloat16)
    for to in range(out_ref.shape[0]):
        out_ref[to, :, span:] = side


def stage_kernel(own_ref, other_ref, own_out, other_out, sems):
    copies = []
    for at, (source, out) in enumerate(((own_ref, own_out), (other_ref, other_out))):
        depth = out.shape[0] // sems.shape[1]
        for i in range(sems.shape[1]):
            piece = pl.ds(i * depth, depth)
            copies.append(pltpu.make_async_copy(source.at[piece], out.at[piece], sems.at[at, i]))
    for copy in copies:
        copy.start()
    for copy in copies:
        copy.wait()


def score_kernel(rows_ref, own_ref, upper_ref, other_ref, stats_ref, meta_ref, ordered_ref, lower_ref, sems):
    width, cols = own_ref.shape
    staged = upper_ref.shape[0]
    depth = lower_ref.shape[0] // sems.shape[0]
    copies = [
        pltpu.make_async_copy(
            other_ref.at[pl.ds(staged + i * depth, depth)], lower_ref.at[pl.ds(i * depth, depth)], sems.at[i]
        )
        for i in range(sems.shape[0])
    ]
    for copy in copies:
        copy.start()
    groups = rows_ref.shape[0]
    parts = SUBS // MINE
    span = width // parts
    share = groups * MINE
    tp, tp_count = lax.axis_index("tp"), lax.axis_size("tp")
    half = tp % PAIR
    place = lax.axis_index("req") * tp_count + tp
    count = groups * SUBS
    into, out_of = iota((count, count), 0), iota((count, count), 1)
    wanted = into % share // MINE * SUBS + into // share * MINE + into % MINE
    order = jnp.where(out_of == wanted, 1.0, 0.0).astype(jnp.bfloat16)
    rows = rows_ref[:, :, :span].reshape(count, span)
    ordered = jnp.dot(order, rows, preferred_element_type=jnp.float32).astype(jnp.bfloat16)
    for k in range(parts):
        ordered_ref[:, k * span : (k + 1) * span] = ordered[k * share : (k + 1) * share]
    meta = rows_ref[0, :, span:].astype(jnp.float32)
    for q in range(1, groups):
        meta = meta + rows_ref[q, :, span:].astype(jnp.float32)
    meta_ref[...] = meta
    own_logits = jnp.dot(ordered_ref[...], own_ref[...], preferred_element_type=jnp.float32)
    other_logits = jnp.dot(ordered_ref[:, :staged], upper_ref[...], preferred_element_type=jnp.float32)
    for copy in copies:
        copy.wait()
    other_logits += jnp.dot(ordered_ref[:, staged:], lower_ref[...], preferred_element_type=jnp.float32)
    logits = jnp.concatenate([own_logits, other_logits], axis=1)
    lanes = max(share, LANES)
    sub, lane = iota((share, lanes), 0), iota((share, lanes), 1)
    ids = meta[0:1, :lanes] + 256.0 * meta[1:2, :lanes] + 65536.0 * meta[2:3, :lanes]
    ids = jnp.sum(jnp.where(lane == sub, ids, 0.0), axis=1, keepdims=True).astype(jnp.int32)
    row_top = jnp.max(logits, axis=1, keepdims=True)
    scaled = jnp.exp(logits - row_top)
    row_total = jnp.sum(scaled, axis=1, keepdims=True)
    row_weighted = jnp.sum(scaled * logits, axis=1, keepdims=True)
    column = iota(logits.shape, 1)
    other = place + 1 - 2 * half
    columns = jnp.where(column < cols, place * cols, (other - 1) * cols) + column
    picked = jnp.sum(jnp.where(columns == ids, logits, 0.0), axis=1, keepdims=True)
    stats = (row_top, row_total, row_weighted, picked)
    if PAIR * share * STATS == LANES:
        joined = picked
        for at in range(STATS - 1):
            joined = jnp.where(lane // (PAIR * share) == at, stats[at], joined)
        joined = jnp.sum(jnp.where(lane % share == sub, joined, 0.0), axis=0, keepdims=True)
        lane = iota((1, LANES), 1)
        neutral = jnp.where(lane < PAIR * share, -jnp.inf, 0.0)
        stats_ref[...] = jnp.where(lane // share % PAIR == half, joined, neutral)
    else:
        for at in range(STATS):
            line = jnp.sum(jnp.where(lane == sub, stats[at], 0.0), axis=0, keepdims=True)
            for h in range(PAIR):
                first = (at * PAIR + h) * share
                stats_ref[:, first : first + share] = jnp.where(half == h, line, 0.0 if at else -jnp.inf)


def finish_kernel(share, stats_ref, meta_ref, logprob_ref, entropy_ref, seq_ref):
    row_count = logprob_ref.shape[0]
    used = PAIR * share
    lanes = max(used, LANES)

    def stat(at):
        if used >= LANES:
            return stats_ref[:, at * used : (at + 1) * used]
        return stats_ref[...] if at == 0 else pltpu.roll(stats_ref[...], LANES - at * used, 1)

    tops = stat(0)
    row_top = jnp.max(tops, axis=0, keepdims=True)
    weight = jnp.exp(tops - row_top)
    row_total = jnp.sum(stat(1) * weight, axis=0, keepdims=True)
    row_weighted = jnp.sum(stat(2) * weight, axis=0, keepdims=True)
    picked = jnp.sum(stat(3), axis=0, keepdims=True)
    log_norm = row_top + jnp.log(row_total)
    lane, sub = iota((1, lanes), 1), iota((SUBS, lanes), 0)
    in_use = jnp.logical_and(meta_ref[4:5, :] > 0.5, lane < used)
    logprob = jnp.where(in_use, picked - log_norm, 0.0)
    entropy = jnp.where(in_use, log_norm - row_weighted / row_total, 0.0)
    segment, place = meta_ref[3:4, :].astype(jnp.int32), meta_ref[5:6, :].astype(jnp.int32)
    mine = jnp.logical_and(place == sub, lane % share // MINE == lax.axis_index("req"))

    def placed(values, wanted):
        sums = jnp.sum(jnp.where(wanted, values, 0.0), axis=1, keepdims=True)
        diagonal = iota((SUBS, LANES), 0) == iota((SUBS, LANES), 1)
        return jnp.sum(jnp.where(diagonal, sums, 0.0), axis=0)

    logprob_ref[...] = placed(logprob, mine)[:row_count]
    entropy_ref[...] = placed(entropy, mine)[:row_count]
    seq_ref[...] = placed(logprob, segment == sub)[:SEQS]


def grant(mebibytes):
    return pltpu.CompilerParams(vmem_limit_bytes=mebibytes * 1024 * 1024)


def local(hidden, norm_gain, lm_head, targets, segments, scored):
    row_count, width = hidden.shape
    groups, tp_count = lax.axis_size("req"), lax.axis_size("tp")
    span = width * MINE // SUBS
    share = groups * MINE
    lanes = max(PAIR * share, LANES)

    def spec(space):
        return pl.BlockSpec(memory_space=space)

    other = lax.ppermute(lm_head, "tp", [(i, i + 1 - 2 * (i % PAIR)) for i in range(tp_count)])
    packed = pl.pallas_call(
        functools.partial(pack_kernel, share),
        out_shape=VMEM((groups, SUBS, span + lanes), jnp.bfloat16),
        in_specs=[spec(VMEM)] * 2 + [spec(SMEM)] * 3,
        out_specs=spec(VMEM),
        scratch_shapes=[
            VMEM((row_count, width), jnp.float32),
            VMEM((SUBS, span), jnp.float32),
            VMEM((width // LANES, LANES), jnp.float32),
        ],
    )(hidden, norm_gain.reshape(width // LANES, LANES), targets, segments, scored)
    rows = lax.all_to_all(packed, "req", 0, 0)
    other = pltpu.with_memory_space_constraint(other, pltpu.HBM)
    staged = width // 2
    slices = pl.pallas_call(
        stage_kernel,
        out_shape=(VMEM(lm_head.shape, lm_head.dtype), VMEM((staged, lm_head.shape[1]), lm_head.dtype)),
        in_specs=[spec(pltpu.HBM)] * 2,
        out_specs=(spec(VMEM),) * 2,
        scratch_shapes=[pltpu.SemaphoreType.DMA((2, 4))],
        compiler_params=grant(4),
        cost_estimate=pl.CostEstimate(flops=0, bytes_accessed=3 * 2 * lm_head.size, transcendentals=0),
    )(pltpu.with_memory_space_constraint(lm_head, pltpu.HBM), other)
    stats, meta = pl.pallas_call(
        score_kernel,
        out_shape=(
            jax.ShapeDtypeStruct((1, STATS * PAIR * share), jnp.float32),
            VMEM((SUBS, lanes), jnp.float32),
        ),
        in_specs=[spec(VMEM)] * 3 + [spec(pltpu.HBM)],
        out_specs=(spec(VMEM), spec(VMEM)),
        scratch_shapes=[
            VMEM((share, width), jnp.bfloat16),
            VMEM((width - staged, lm_head.shape[1]), jnp.bfloat16),
            pltpu.SemaphoreType.DMA((4,)),
        ],
        compiler_params=grant(24),
    )(rows, *(pltpu.with_memory_space_constraint(part, VMEM) for part in slices), other)
    gathered = sent_to_all(stats, ("req", "tp"))
    return pl.pallas_call(
        functools.partial(finish_kernel, share),
        out_shape=(
            jax.ShapeDtypeStruct((row_count,), jnp.float32),
            jax.ShapeDtypeStruct((row_count,), jnp.float32),
            jax.ShapeDtypeStruct((SEQS,), jnp.float32),
        ),
        in_specs=[spec(VMEM), spec(VMEM)],
        out_specs=(spec(VMEM), spec(VMEM), spec(VMEM)),
    )(pltpu.with_memory_space_constraint(gathered, VMEM), pltpu.with_memory_space_constraint(meta, VMEM))


def sent_to_all(block, axis):
    copies = jnp.broadcast_to(block[None], (lax.axis_size(axis),) + block.shape)
    return lax.all_to_all(copies, axis, 0, 0).reshape((-1,) + block.shape[1:])


def solution(mesh):
    return jax.shard_map(
        local,
        mesh=mesh,
        in_specs=(P("req", None), P(), P(None, ("req", "tp")), P("req"), P("req"), P("req")),
        out_specs=(P("req"), P("req"), P()),
        check_vma=False,
    )
```

```python
import functools

import jax
import jax.numpy as jnp
from jax import lax
from jax.experimental import pallas as pl
from jax.experimental.pallas import tpu as pltpu
from jax.sharding import PartitionSpec as P

SEQS = 4
PICK = 4
PAIR = 2
MINE = PICK // PAIR
SUBS = 8
LANES = 128
STATS = 4

VMEM = pltpu.VMEM


def over(number, by):
    return number >> (by.bit_length() - 1) if by & (by - 1) == 0 else number // by


def left(number, by):
    return number & (by - 1) if by & (by - 1) == 0 else number % by


def iota(shape, axis):
    return lax.broadcasted_iota(jnp.int32, shape, axis)


def pack_kernel(share, hidden_ref, gain_ref, targets_ref, segments_ref, scored_ref, out_ref, gains_ref):
    row_count, width = hidden_ref.shape
    parts = SUBS // MINE
    span = width // parts
    own, half = lax.axis_index("req"), left(lax.axis_index("tp"), PAIR)
    gains_ref[...] = gain_ref[...].astype(jnp.float32)

    def across(ref):
        return jnp.broadcast_to(ref[...].reshape(1, row_count), (row_count, row_count)).astype(jnp.float32)

    sub, lane = iota((row_count, row_count), 0), iota((row_count, row_count), 1)
    scored, targets, segments = across(scored_ref), across(targets_ref), across(segments_ref)

    def down(values, wanted):
        return jnp.sum(jnp.where(wanted, values, 0.0), axis=1, keepdims=True)

    in_use, target, segment = (down(values, lane == sub) for values in (scored, targets, segments))
    rank_down = down(scored, lane < sub)
    rank_across = jnp.sum(jnp.where(sub < lane, in_use, 0.0), axis=0, keepdims=True)
    wanted = (half * MINE + left(iota((SUBS, row_count), 0), MINE)).astype(jnp.float32)
    choice = jnp.where(jnp.logical_and(rank_across == wanted, scored[:1, :] > 0.5), 1.0, 0.0)
    chosen = jnp.dot(choice.astype(jnp.bfloat16), hidden_ref[...], preferred_element_type=jnp.float32)
    bundle = over(iota((SUBS, span), 0), MINE)
    values = chosen[:, :span]
    for k in range(1, parts):
        values = jnp.where(bundle == k, chosen[:, k * span : (k + 1) * span], values)
    part = jnp.broadcast_to(jnp.sum(values * values, axis=1, keepdims=True), (SUBS, LANES))
    total = part
    for k in range(1, parts):
        total = total + pltpu.roll(part, k * MINE, 0)
    row_scale = lax.rsqrt(total / width + 1e-05)
    bundle = over(iota((SUBS, LANES), 0), MINE)
    chunks = span // LANES
    for at in range(chunks):
        gain = gains_ref[at : at + 1, :]
        for k in range(1, parts):
            gain = jnp.where(bundle == k, gains_ref[k * chunks + at : k * chunks + at + 1, :], gain)
        piece = (values[:, at * LANES : (at + 1) * LANES] * row_scale * gain).astype(jnp.bfloat16)
        for to in range(out_ref.shape[0]):
            out_ref[to, :, at * LANES : (at + 1) * LANES] = piece
    width_side = out_ref.shape[2] - span
    lane = iota((row_count, width_side), 1)
    i = left(lane, share) - own * MINE
    mine = jnp.logical_and(jnp.logical_and(i >= 0, i < MINE), in_use > 0.5)
    here = jnp.logical_and(mine, rank_down == (over(lane, share) * MINE + i).astype(jnp.float32))
    same = jnp.logical_and(mine, rank_down == (half * MINE + i).astype(jnp.float32))

    def field(wanted, numbers):
        return jnp.sum(jnp.where(wanted, numbers, 0.0), axis=0, keepdims=True)

    number = field(same, target).astype(jnp.int32)
    place = iota((row_count, 1), 0).astype(jnp.float32)
    fields = [(number >> shift & 255).astype(jnp.float32) for shift in (0, 8, 16)]
    fields += [field(here, segment), field(here, jnp.ones_like(place)), field(here, place)]
    sub = iota((SUBS, width_side), 0)
    side = jnp.zeros((SUBS, width_side), jnp.float32)
    for at, line in enumerate(fields):
        side = jnp.where(sub == at, line, side)
    side = side.astype(jnp.bfloat16)
    for to in range(out_ref.shape[0]):
        out_ref[to, :, span:] = side


def stage_kernel(own_ref, other_ref, own_out, other_out, sems):
    copies = []
    for at, (source, out) in enumerate(((own_ref, own_out), (other_ref, other_out))):
        depth = out.shape[0] // sems.shape[1]
        for i in range(sems.shape[1]):
            piece = pl.ds(i * depth, depth)
            copies.append(pltpu.make_async_copy(source.at[piece], out.at[piece], sems.at[at, i]))
    for copy in copies:
        copy.start()
    for copy in copies:
        copy.wait()


def score_kernel(rows_ref, own_ref, upper_ref, other_ref, stats_ref, meta_ref, ordered_ref, lower_ref, sems):
    width, cols = own_ref.shape
    staged = upper_ref.shape[0]
    depth = lower_ref.shape[0] // sems.shape[0]
    copies = [
        pltpu.make_async_copy(
            other_ref.at[pl.ds(staged + i * depth, depth)], lower_ref.at[pl.ds(i * depth, depth)], sems.at[i]
        )
        for i in range(sems.shape[0])
    ]
    for copy in copies:
        copy.start()
    groups = rows_ref.shape[0]
    parts = SUBS // MINE
    span = width // parts
    share = groups * MINE
    tp, tp_count = lax.axis_index("tp"), lax.axis_size("tp")
    half = left(tp, PAIR)
    place = lax.axis_index("req") * tp_count + tp
    count = groups * SUBS
    into, out_of = iota((count, count), 0), iota((count, count), 1)
    wanted = over(left(into, share), MINE) * SUBS + over(into, share) * MINE + left(into, MINE)
    order = jnp.where(out_of == wanted, 1.0, 0.0).astype(jnp.bfloat16)
    rows = rows_ref[:, :, :span].reshape(count, span)
    ordered = jnp.dot(order, rows, preferred_element_type=jnp.float32).astype(jnp.bfloat16)
    for k in range(parts):
        ordered_ref[:, k * span : (k + 1) * span] = ordered[k * share : (k + 1) * share]
    meta = rows_ref[0, :, span:].astype(jnp.float32)
    for q in range(1, groups):
        meta = meta + rows_ref[q, :, span:].astype(jnp.float32)
    meta_ref[...] = meta
    own_logits = jnp.dot(ordered_ref[...], own_ref[...], preferred_element_type=jnp.float32)
    other_logits = jnp.dot(ordered_ref[:, :staged], upper_ref[...], preferred_element_type=jnp.float32)
    for copy in copies:
        copy.wait()
    other_logits += jnp.dot(ordered_ref[:, staged:], lower_ref[...], preferred_element_type=jnp.float32)
    logits = jnp.concatenate([own_logits, other_logits], axis=1)
    lanes = max(share, LANES)
    sub, lane = iota((share, lanes), 0), iota((share, lanes), 1)
    ids = meta[0:1, :lanes] + 256.0 * meta[1:2, :lanes] + 65536.0 * meta[2:3, :lanes]
    ids = jnp.sum(jnp.where(lane == sub, ids, 0.0), axis=1, keepdims=True).astype(jnp.int32)
    row_top = jnp.max(logits, axis=1, keepdims=True)
    scaled = jnp.exp(logits - row_top)
    row_total = jnp.sum(scaled, axis=1, keepdims=True)
    row_weighted = jnp.sum(scaled * logits, axis=1, keepdims=True)
    column = iota(logits.shape, 1)
    other = place + 1 - 2 * half
    columns = jnp.where(column < cols, place * cols, (other - 1) * cols) + column
    picked = jnp.sum(jnp.where(columns == ids, logits, 0.0), axis=1, keepdims=True)
    stats = (row_top, row_total, row_weighted, picked)
    if PAIR * share * STATS == LANES:
        joined = picked
        for at in range(STATS - 1):
            joined = jnp.where(over(lane, PAIR * share) == at, stats[at], joined)
        joined = jnp.sum(jnp.where(left(lane, share) == sub, joined, 0.0), axis=0, keepdims=True)
        lane = iota((1, LANES), 1)
        neutral = jnp.where(lane < PAIR * share, -jnp.inf, 0.0)
        stats_ref[...] = jnp.where(left(over(lane, share), PAIR) == half, joined, neutral)
    else:
        for at in range(STATS):
            line = jnp.sum(jnp.where(lane == sub, stats[at], 0.0), axis=0, keepdims=True)
            for h in range(PAIR):
                first = (at * PAIR + h) * share
                stats_ref[:, first : first + share] = jnp.where(half == h, line, 0.0 if at else -jnp.inf)


def finish_kernel(share, stats_ref, meta_ref, logprob_ref, entropy_ref, seq_ref):
    row_count = logprob_ref.shape[0]
    used = PAIR * share
    lanes = max(used, LANES)

    def stat(at):
        if used >= LANES:
            return stats_ref[:, at * used : (at + 1) * used]
        return stats_ref[...] if at == 0 else pltpu.roll(stats_ref[...], LANES - at * used, 1)

    tops = stat(0)
    row_top = jnp.max(tops, axis=0, keepdims=True)
    weight = jnp.exp(tops - row_top)
    row_total = jnp.sum(stat(1) * weight, axis=0, keepdims=True)
    row_weighted = jnp.sum(stat(2) * weight, axis=0, keepdims=True)
    picked = jnp.sum(stat(3), axis=0, keepdims=True)
    log_norm = row_top + jnp.log(row_total)
    lane, sub = iota((1, lanes), 1), iota((SUBS, lanes), 0)
    in_use = jnp.logical_and(meta_ref[4:5, :] > 0.5, lane < used)
    logprob = jnp.where(in_use, picked - log_norm, 0.0)
    entropy = jnp.where(in_use, log_norm - row_weighted / row_total, 0.0)
    segment, place = meta_ref[3:4, :].astype(jnp.int32), meta_ref[5:6, :].astype(jnp.int32)
    mine = jnp.logical_and(place == sub, over(left(lane, share), MINE) == lax.axis_index("req"))

    def placed(values, wanted):
        sums = jnp.sum(jnp.where(wanted, values, 0.0), axis=1, keepdims=True)
        diagonal = iota((SUBS, LANES), 0) == iota((SUBS, LANES), 1)
        return jnp.sum(jnp.where(diagonal, sums, 0.0), axis=0)

    logprob_ref[...] = placed(logprob, mine)[:row_count]
    entropy_ref[...] = placed(entropy, mine)[:row_count]
    seq_ref[...] = placed(logprob, segment == sub)[:SEQS]


def grant(mebibytes):
    return pltpu.CompilerParams(vmem_limit_bytes=mebibytes * 1024 * 1024)


def local(hidden, norm_gain, lm_head, targets, segments, scored):
    row_count, width = hidden.shape
    groups, tp_count = lax.axis_size("req"), lax.axis_size("tp")
    span = width * MINE // SUBS
    share = groups * MINE
    lanes = max(PAIR * share, LANES)

    def spec(space):
        return pl.BlockSpec(memory_space=space)

    other = lax.ppermute(lm_head, "tp", [(i, i + 1 - 2 * (i % PAIR)) for i in range(tp_count)])
    packed = pl.pallas_call(
        functools.partial(pack_kernel, share),
        out_shape=VMEM((groups, SUBS, span + lanes), jnp.bfloat16),
        in_specs=[spec(VMEM)] * 5,
        out_specs=spec(VMEM),
        scratch_shapes=[
            VMEM((width // LANES, LANES), jnp.float32),
        ],
    )(hidden, norm_gain.reshape(width // LANES, LANES), targets, segments, scored)
    rows = lax.all_to_all(packed, "req", 0, 0)
    other = pltpu.with_memory_space_constraint(other, pltpu.HBM)
    staged = width // 2
    slices = pl.pallas_call(
        stage_kernel,
        out_shape=(VMEM(lm_head.shape, lm_head.dtype), VMEM((staged, lm_head.shape[1]), lm_head.dtype)),
        in_specs=[spec(pltpu.HBM)] * 2,
        out_specs=(spec(VMEM),) * 2,
        scratch_shapes=[pltpu.SemaphoreType.DMA((2, 4))],
        compiler_params=grant(4),
        cost_estimate=pl.CostEstimate(flops=0, bytes_accessed=3 * 2 * lm_head.size, transcendentals=0),
    )(pltpu.with_memory_space_constraint(lm_head, pltpu.HBM), other)
    stats, meta = pl.pallas_call(
        score_kernel,
        out_shape=(
            jax.ShapeDtypeStruct((1, STATS * PAIR * share), jnp.float32),
            VMEM((SUBS, lanes), jnp.float32),
        ),
        in_specs=[spec(VMEM)] * 3 + [spec(pltpu.HBM)],
        out_specs=(spec(VMEM), spec(VMEM)),
        scratch_shapes=[
            VMEM((share, width), jnp.bfloat16),
            VMEM((width - staged, lm_head.shape[1]), jnp.bfloat16),
            pltpu.SemaphoreType.DMA((4,)),
        ],
        compiler_params=grant(24),
    )(rows, *(pltpu.with_memory_space_constraint(part, VMEM) for part in slices), other)
    gathered = sent_to_all(stats, ("req", "tp"))
    return pl.pallas_call(
        functools.partial(finish_kernel, share),
        out_shape=(
            jax.ShapeDtypeStruct((row_count,), jnp.float32),
            jax.ShapeDtypeStruct((row_count,), jnp.float32),
            jax.ShapeDtypeStruct((SEQS,), jnp.float32),
        ),
        in_specs=[spec(VMEM), spec(VMEM)],
        out_specs=(spec(VMEM), spec(VMEM), spec(VMEM)),
    )(pltpu.with_memory_space_constraint(gathered, VMEM), pltpu.with_memory_space_constraint(meta, VMEM))


def sent_to_all(block, axis):
    copies = jnp.broadcast_to(block[None], (lax.axis_size(axis),) + block.shape)
    return lax.all_to_all(copies, axis, 0, 0).reshape((-1,) + block.shape[1:])


def solution(mesh):
    return jax.shard_map(
        local,
        mesh=mesh,
        in_specs=(P("req", None), P(), P(None, ("req", "tp")), P("req"), P("req"), P("req")),
        out_specs=(P("req"), P("req"), P()),
        check_vma=False,
    )
```

```python
import functools

import jax
import jax.numpy as jnp
from jax import lax
from jax.experimental import pallas as pl
from jax.experimental.pallas import tpu as pltpu
from jax.sharding import PartitionSpec as P

SEQS = 4
PICK = 4
PAIR = 2
MINE = PICK // PAIR
SUBS = 8
LANES = 128
STATS = 4

VMEM = pltpu.VMEM
SMEM = pltpu.SMEM


def ranks_of(scored_ref, row_count):
    ranks, so_far = [], jnp.int32(0)
    for row in range(row_count):
        ranks.append(so_far)
        so_far = so_far + scored_ref[row]
    return ranks, so_far


def iota(shape, axis):
    return lax.broadcasted_iota(jnp.int32, shape, axis)


def pack_kernel(share, hidden_ref, gain_ref, targets_ref, segments_ref, scored_ref, out_ref, wide_ref, parts_ref, gains_ref):
    row_count, width = hidden_ref.shape
    parts = SUBS // MINE
    span = width // parts
    own, half = lax.axis_index("req"), lax.axis_index("tp") % PAIR
    wide_ref[...] = hidden_ref[...].astype(jnp.float32)
    gains_ref[...] = gain_ref[...].astype(jnp.float32)
    ranks, count = ranks_of(scored_ref, row_count)
    source = [jnp.int32(0)] * PICK
    for row in range(row_count):
        for r in range(PICK):
            hit = jnp.logical_and(scored_ref[row] == 1, ranks[row] == r)
            source[r] = jnp.where(hit, row, source[r])
    mine = [source[i] for i in range(MINE)]
    for h in range(1, PAIR):
        mine = [jnp.where(half == h, source[h * MINE + i], mine[i]) for i in range(MINE)]
    for i in range(MINE):
        for k in range(parts):
            parts_ref[k * MINE + i : k * MINE + i + 1, :] = wide_ref[pl.ds(mine[i], 1), k * span : (k + 1) * span]
    values = parts_ref[...]
    part = jnp.broadcast_to(jnp.sum(values * values, axis=1, keepdims=True), (SUBS, LANES))
    total = part
    for k in range(1, parts):
        total = total + pltpu.roll(part, k * MINE, 0)
    row_scale = lax.rsqrt(total / width + 1e-05)
    sub, lane = iota((SUBS, LANES), 0), iota((SUBS, LANES), 1)
    chunks = span // LANES
    for at in range(chunks):
        gain = gains_ref[at : at + 1, :]
        for k in range(1, parts):
            gain = jnp.where(sub >= k * MINE, gains_ref[k * chunks + at : k * chunks + at + 1, :], gain)
        piece = parts_ref[:, at * LANES : (at + 1) * LANES]
        piece = (piece * row_scale * gain).astype(jnp.bfloat16)
        for to in range(out_ref.shape[0]):
            out_ref[to, :, at * LANES : (at + 1) * LANES] = piece
    width_side = out_ref.shape[2] - span
    sub, lane = iota((SUBS, width_side), 0), iota((SUBS, width_side), 1)
    at_row, at_half = lane % share - own * MINE, lane // share
    side = jnp.zeros((SUBS, width_side), jnp.int32)
    for i in range(MINE):
        target = targets_ref[mine[i]]
        digits = jnp.where(sub == 0, target & 255, jnp.where(sub == 1, (target >> 8) & 255, target >> 16))
        fields = jnp.zeros((SUBS, width_side), jnp.int32)
        for h in range(PAIR):
            r = h * MINE + i
            field = jnp.where(sub == 4, (count > r).astype(jnp.int32), source[r])
            fields = jnp.where(at_half == h, jnp.where(sub == 3, segments_ref[source[r]], field), fields)
        side = jnp.where(at_row == i, jnp.where(sub < 3, digits, fields), side)
    side = side.astype(jnp.float32).astype(jnp.bfloat16)
    for to in range(out_ref.shape[0]):
        out_ref[to, :, span:] = side


def stage_kernel(own_ref, other_ref, own_out, other_out, sems):
    copies = []
    for at, (source, out) in enumerate(((own_ref, own_out), (other_ref, other_out))):
        depth = out.shape[0] // sems.shape[1]
        for i in range(sems.shape[1]):
            piece = pl.ds(i * depth, depth)
            copies.append(pltpu.make_async_copy(source.at[piece], out.at[piece], sems.at[at, i]))
    for copy in copies:
        copy.start()
    for copy in copies:
        copy.wait()


def score_kernel(rows_ref, own_ref, upper_ref, other_ref, stats_ref, meta_ref, ordered_ref, lower_ref, sems):
    width, cols = own_ref.shape
    staged = upper_ref.shape[0]
    depth = lower_ref.shape[0] // sems.shape[0]
    copies = [
        pltpu.make_async_copy(
            other_ref.at[pl.ds(staged + i * depth, depth)], lower_ref.at[pl.ds(i * depth, depth)], sems.at[i]
        )
        for i in range(sems.shape[0])
    ]
    for copy in copies:
        copy.start()
    groups = rows_ref.shape[0]
    parts = SUBS // MINE
    span = width // parts
    share = groups * MINE
    tp, tp_count = lax.axis_index("tp"), lax.axis_size("tp")
    half = tp % PAIR
    place = lax.axis_index("req") * tp_count + tp
    count = groups * SUBS
    into, out_of = iota((count, count), 0), iota((count, count), 1)
    wanted = into % share // MINE * SUBS + into // share * MINE + into % MINE
    order = jnp.where(out_of == wanted, 1.0, 0.0).astype(jnp.bfloat16)
    rows = rows_ref[:, :, :span].reshape(count, span)
    ordered = jnp.dot(order, rows, preferred_element_type=jnp.float32).astype(jnp.bfloat16)
    for k in range(parts):
        ordered_ref[:, k * span : (k + 1) * span] = ordered[k * share : (k + 1) * share]
    meta = rows_ref[0, :, span:].astype(jnp.float32)
    for q in range(1, groups):
        meta = meta + rows_ref[q, :, span:].astype(jnp.float32)
    meta_ref[...] = meta
    chunk = 512

    def product(slice_ref, first):
        def step(i, sums):
            at = pl.multiple_of(first + i * chunk, chunk)
            left = ordered_ref[:, pl.ds(at, chunk)]
            own = own_ref[pl.ds(at, chunk), :]
            other = slice_ref[pl.ds(pl.multiple_of(i * chunk, chunk), chunk), :]
            return (
                sums[0] + jnp.dot(left, own, preferred_element_type=jnp.float32),
                sums[1] + jnp.dot(left, other, preferred_element_type=jnp.float32),
            )

        return step

    zeros = jnp.zeros((share, cols), jnp.float32)
    sums = lax.fori_loop(0, staged // chunk, product(upper_ref, 0), (zeros, zeros))
    for copy in copies:
        copy.wait()
    sums = lax.fori_loop(0, (width - staged) // chunk, product(lower_ref, staged), sums)
    logits = jnp.concatenate(sums, axis=1)
    lanes = max(share, LANES)
    sub, lane = iota((share, lanes), 0), iota((share, lanes), 1)
    ids = meta[0:1, :lanes] + 256.0 * meta[1:2, :lanes] + 65536.0 * meta[2:3, :lanes]
    ids = jnp.sum(jnp.where(lane == sub, ids, 0.0), axis=1, keepdims=True).astype(jnp.int32)
    row_top = jnp.max(logits, axis=1, keepdims=True)
    scaled = jnp.exp(logits - row_top)
    row_total = jnp.sum(scaled, axis=1, keepdims=True)
    row_weighted = jnp.sum(scaled * logits, axis=1, keepdims=True)
    column = iota(logits.shape, 1)
    other = place + 1 - 2 * half
    columns = jnp.where(column < cols, place * cols, (other - 1) * cols) + column
    picked = jnp.sum(jnp.where(columns == ids, logits, 0.0), axis=1, keepdims=True)
    stats = (row_top, row_total, row_weighted, picked)
    if PAIR * share * STATS == LANES:
        joined = picked
        for at in range(STATS - 1):
            joined = jnp.where(lane // (PAIR * share) == at, stats[at], joined)
        joined = jnp.sum(jnp.where(lane % share == sub, joined, 0.0), axis=0, keepdims=True)
        lane = iota((1, LANES), 1)
        neutral = jnp.where(lane < PAIR * share, -jnp.inf, 0.0)
        stats_ref[...] = jnp.where(lane // share % PAIR == half, joined, neutral)
    else:
        for at in range(STATS):
            line = jnp.sum(jnp.where(lane == sub, stats[at], 0.0), axis=0, keepdims=True)
            for h in range(PAIR):
                first = (at * PAIR + h) * share
                stats_ref[:, first : first + share] = jnp.where(half == h, line, 0.0 if at else -jnp.inf)


def finish_kernel(share, stats_ref, meta_ref, logprob_ref, entropy_ref, seq_ref):
    row_count = logprob_ref.shape[0]
    used = PAIR * share
    lanes = max(used, LANES)

    def stat(at):
        if used >= LANES:
            return stats_ref[:, at * used : (at + 1) * used]
        return stats_ref[...] if at == 0 else pltpu.roll(stats_ref[...], LANES - at * used, 1)

    tops = stat(0)
    row_top = jnp.max(tops, axis=0, keepdims=True)
    weight = jnp.exp(tops - row_top)
    row_total = jnp.sum(stat(1) * weight, axis=0, keepdims=True)
    row_weighted = jnp.sum(stat(2) * weight, axis=0, keepdims=True)
    picked = jnp.sum(stat(3), axis=0, keepdims=True)
    log_norm = row_top + jnp.log(row_total)
    lane, sub = iota((1, lanes), 1), iota((SUBS, lanes), 0)
    in_use = jnp.logical_and(meta_ref[4:5, :] > 0.5, lane < used)
    logprob = jnp.where(in_use, picked - log_norm, 0.0)
    entropy = jnp.where(in_use, log_norm - row_weighted / row_total, 0.0)
    segment, place = meta_ref[3:4, :].astype(jnp.int32), meta_ref[5:6, :].astype(jnp.int32)
    mine = jnp.logical_and(place == sub, lane % share // MINE == lax.axis_index("req"))

    def placed(values, wanted):
        sums = jnp.sum(jnp.where(wanted, values, 0.0), axis=1, keepdims=True)
        diagonal = iota((SUBS, LANES), 0) == iota((SUBS, LANES), 1)
        return jnp.sum(jnp.where(diagonal, sums, 0.0), axis=0)

    logprob_ref[...] = placed(logprob, mine)[:row_count]
    entropy_ref[...] = placed(entropy, mine)[:row_count]
    seq_ref[...] = placed(logprob, segment == sub)[:SEQS]


def grant(mebibytes):
    return pltpu.CompilerParams(vmem_limit_bytes=mebibytes * 1024 * 1024)


def local(hidden, norm_gain, lm_head, targets, segments, scored):
    row_count, width = hidden.shape
    groups, tp_count = lax.axis_size("req"), lax.axis_size("tp")
    span = width * MINE // SUBS
    share = groups * MINE
    lanes = max(PAIR * share, LANES)

    def spec(space):
        return pl.BlockSpec(memory_space=space)

    other = lax.ppermute(lm_head, "tp", [(i, i + 1 - 2 * (i % PAIR)) for i in range(tp_count)])
    packed = pl.pallas_call(
        functools.partial(pack_kernel, share),
        out_shape=VMEM((groups, SUBS, span + lanes), jnp.bfloat16),
        in_specs=[spec(VMEM)] * 2 + [spec(SMEM)] * 3,
        out_specs=spec(VMEM),
        scratch_shapes=[
            VMEM((row_count, width), jnp.float32),
            VMEM((SUBS, span), jnp.float32),
            VMEM((width // LANES, LANES), jnp.float32),
        ],
    )(hidden, norm_gain.reshape(width // LANES, LANES), targets, segments, scored)
    rows = lax.all_to_all(packed, "req", 0, 0)
    other = pltpu.with_memory_space_constraint(other, pltpu.HBM)
    staged = width // 2
    slices = pl.pallas_call(
        stage_kernel,
        out_shape=(VMEM(lm_head.shape, lm_head.dtype), VMEM((staged, lm_head.shape[1]), lm_head.dtype)),
        in_specs=[spec(pltpu.HBM)] * 2,
        out_specs=(spec(VMEM),) * 2,
        scratch_shapes=[pltpu.SemaphoreType.DMA((2, 4))],
        compiler_params=grant(4),
        cost_estimate=pl.CostEstimate(flops=0, bytes_accessed=3 * 2 * lm_head.size, transcendentals=0),
    )(pltpu.with_memory_space_constraint(lm_head, pltpu.HBM), other)
    stats, meta = pl.pallas_call(
        score_kernel,
        out_shape=(
            jax.ShapeDtypeStruct((1, STATS * PAIR * share), jnp.float32),
            VMEM((SUBS, lanes), jnp.float32),
        ),
        in_specs=[spec(VMEM)] * 3 + [spec(pltpu.HBM)],
        out_specs=(spec(VMEM), spec(VMEM)),
        scratch_shapes=[
            VMEM((share, width), jnp.bfloat16),
            VMEM((width - staged, lm_head.shape[1]), jnp.bfloat16),
            pltpu.SemaphoreType.DMA((4,)),
        ],
        compiler_params=grant(24),
    )(rows, *(pltpu.with_memory_space_constraint(part, VMEM) for part in slices), other)
    gathered = sent_to_all(stats, ("req", "tp"))
    return pl.pallas_call(
        functools.partial(finish_kernel, share),
        out_shape=(
            jax.ShapeDtypeStruct((row_count,), jnp.float32),
            jax.ShapeDtypeStruct((row_count,), jnp.float32),
            jax.ShapeDtypeStruct((SEQS,), jnp.float32),
        ),
        in_specs=[spec(VMEM), spec(VMEM)],
        out_specs=(spec(VMEM), spec(VMEM), spec(VMEM)),
    )(pltpu.with_memory_space_constraint(gathered, VMEM), pltpu.with_memory_space_constraint(meta, VMEM))


def sent_to_all(block, axis):
    copies = jnp.broadcast_to(block[None], (lax.axis_size(axis),) + block.shape)
    return lax.all_to_all(copies, axis, 0, 0).reshape((-1,) + block.shape[1:])


def solution(mesh):
    return jax.shard_map(
        local,
        mesh=mesh,
        in_specs=(P("req", None), P(), P(None, ("req", "tp")), P("req"), P("req"), P("req")),
        out_specs=(P("req"), P("req"), P()),
        check_vma=False,
    )
```

```python
import functools

import jax
import jax.numpy as jnp
from jax import lax
from jax.experimental import pallas as pl
from jax.experimental.pallas import tpu as pltpu
from jax.sharding import PartitionSpec as P

SEQS = 4
PICK = 4
PAIR = 2
MINE = PICK // PAIR
SUBS = 8
LANES = 128
STATS = 4

VMEM = pltpu.VMEM
SMEM = pltpu.SMEM


def ranks_of(scored_ref, row_count):
    ranks, so_far = [], jnp.int32(0)
    for row in range(row_count):
        ranks.append(so_far)
        so_far = so_far + scored_ref[row]
    return ranks, so_far


def iota(shape, axis):
    return lax.broadcasted_iota(jnp.int32, shape, axis)


def middle_first(count):
    quarter = count // 4
    return [*range(quarter, count - quarter), *range(quarter), *range(count - quarter, count)]


def own_slot(count):
    own, quarter = lax.axis_index("req"), count // 4
    return jnp.where(own < quarter, own + count - 2 * quarter, jnp.where(own < count - quarter, own - quarter, own))


def pack_kernel(share, hidden_ref, gain_ref, targets_ref, segments_ref, scored_ref, out_ref, wide_ref, parts_ref, gains_ref):
    row_count, width = hidden_ref.shape
    parts = SUBS // MINE
    span = width // parts
    own, half = own_slot(out_ref.shape[0]), lax.axis_index("tp") % PAIR
    wide_ref[...] = hidden_ref[...].astype(jnp.float32)
    gains_ref[...] = gain_ref[...].astype(jnp.float32)
    ranks, count = ranks_of(scored_ref, row_count)
    source = [jnp.int32(0)] * PICK
    for row in range(row_count):
        for r in range(PICK):
            hit = jnp.logical_and(scored_ref[row] == 1, ranks[row] == r)
            source[r] = jnp.where(hit, row, source[r])
    mine = [source[i] for i in range(MINE)]
    for h in range(1, PAIR):
        mine = [jnp.where(half == h, source[h * MINE + i], mine[i]) for i in range(MINE)]
    for i in range(MINE):
        for k in range(parts):
            parts_ref[k * MINE + i : k * MINE + i + 1, :] = wide_ref[pl.ds(mine[i], 1), k * span : (k + 1) * span]
    values = parts_ref[...]
    part = jnp.broadcast_to(jnp.sum(values * values, axis=1, keepdims=True), (SUBS, LANES))
    total = part
    for k in range(1, parts):
        total = total + pltpu.roll(part, k * MINE, 0)
    row_scale = lax.rsqrt(total / width + 1e-05)
    sub, lane = iota((SUBS, LANES), 0), iota((SUBS, LANES), 1)
    chunks = span // LANES
    for at in range(chunks):
        gain = gains_ref[at : at + 1, :]
        for k in range(1, parts):
            gain = jnp.where(sub >= k * MINE, gains_ref[k * chunks + at : k * chunks + at + 1, :], gain)
        piece = parts_ref[:, at * LANES : (at + 1) * LANES]
        piece = (piece * row_scale * gain).astype(jnp.bfloat16)
        for to in range(out_ref.shape[0]):
            out_ref[to, :, at * LANES : (at + 1) * LANES] = piece
    width_side = out_ref.shape[2] - span
    sub, lane = iota((SUBS, width_side), 0), iota((SUBS, width_side), 1)
    at_row, at_half = lane % share - own * MINE, lane // share
    side = jnp.zeros((SUBS, width_side), jnp.int32)
    for i in range(MINE):
        target = targets_ref[mine[i]]
        digits = jnp.where(sub == 0, target & 255, jnp.where(sub == 1, (target >> 8) & 255, target >> 16))
        fields = jnp.zeros((SUBS, width_side), jnp.int32)
        for h in range(PAIR):
            r = h * MINE + i
            field = jnp.where(sub == 4, (count > r).astype(jnp.int32), source[r])
            fields = jnp.where(at_half == h, jnp.where(sub == 3, segments_ref[source[r]], field), fields)
        side = jnp.where(at_row == i, jnp.where(sub < 3, digits, fields), side)
    side = side.astype(jnp.float32).astype(jnp.bfloat16)
    for to in range(out_ref.shape[0]):
        out_ref[to, :, span:] = side


def stage_kernel(own_ref, other_ref, own_out, other_out, sems):
    copies = []
    for at, (source, out) in enumerate(((own_ref, own_out), (other_ref, other_out))):
        depth = out.shape[0] // sems.shape[1]
        for i in range(sems.shape[1]):
            piece = pl.ds(i * depth, depth)
            copies.append(pltpu.make_async_copy(source.at[piece], out.at[piece], sems.at[at, i]))
    for copy in copies:
        copy.start()
    for copy in copies:
        copy.wait()


def score_kernel(rows_ref, own_ref, upper_ref, other_ref, stats_ref, meta_ref, ordered_ref, lower_ref, sems):
    width, cols = own_ref.shape
    staged = upper_ref.shape[0]
    depth = lower_ref.shape[0] // sems.shape[0]
    copies = [
        pltpu.make_async_copy(
            other_ref.at[pl.ds(staged + i * depth, depth)], lower_ref.at[pl.ds(i * depth, depth)], sems.at[i]
        )
        for i in range(sems.shape[0])
    ]
    for copy in copies:
        copy.start()
    groups = rows_ref.shape[0]
    parts = SUBS // MINE
    span = width // parts
    share = groups * MINE
    tp, tp_count = lax.axis_index("tp"), lax.axis_size("tp")
    half = tp % PAIR
    place = lax.axis_index("req") * tp_count + tp
    count = groups * SUBS
    into, out_of = iota((count, count), 0), iota((count, count), 1)
    wanted = into % share // MINE * SUBS + into // share * MINE + into % MINE
    order = jnp.where(out_of == wanted, 1.0, 0.0).astype(jnp.bfloat16)
    rows = rows_ref[:, :, :span].reshape(count, span)
    ordered = jnp.dot(order, rows, preferred_element_type=jnp.float32).astype(jnp.bfloat16)
    for k in range(parts):
        ordered_ref[:, k * span : (k + 1) * span] = ordered[k * share : (k + 1) * share]
    meta = rows_ref[0, :, span:].astype(jnp.float32)
    for q in range(1, groups):
        meta = meta + rows_ref[q, :, span:].astype(jnp.float32)
    meta_ref[...] = meta
    own_logits = jnp.dot(ordered_ref[...], own_ref[...], preferred_element_type=jnp.float32)
    other_logits = jnp.dot(ordered_ref[:, :staged], upper_ref[...], preferred_element_type=jnp.float32)
    for copy in copies:
        copy.wait()
    other_logits += jnp.dot(ordered_ref[:, staged:], lower_ref[...], preferred_element_type=jnp.float32)
    logits = jnp.concatenate([own_logits, other_logits], axis=1)
    lanes = max(share, LANES)
    sub, lane = iota((share, lanes), 0), iota((share, lanes), 1)
    ids = meta[0:1, :lanes] + 256.0 * meta[1:2, :lanes] + 65536.0 * meta[2:3, :lanes]
    ids = jnp.sum(jnp.where(lane == sub, ids, 0.0), axis=1, keepdims=True).astype(jnp.int32)
    row_top = jnp.max(logits, axis=1, keepdims=True)
    scaled = jnp.exp(logits - row_top)
    row_total = jnp.sum(scaled, axis=1, keepdims=True)
    row_weighted = jnp.sum(scaled * logits, axis=1, keepdims=True)
    column = iota(logits.shape, 1)
    other = place + 1 - 2 * half
    columns = jnp.where(column < cols, place * cols, (other - 1) * cols) + column
    picked = jnp.sum(jnp.where(columns == ids, logits, 0.0), axis=1, keepdims=True)
    stats = (row_top, row_total, row_weighted, picked)
    if PAIR * share * STATS == LANES:
        joined = picked
        for at in range(STATS - 1):
            joined = jnp.where(lane // (PAIR * share) == at, stats[at], joined)
        joined = jnp.sum(jnp.where(lane % share == sub, joined, 0.0), axis=0, keepdims=True)
        lane = iota((1, LANES), 1)
        neutral = jnp.where(lane < PAIR * share, -jnp.inf, 0.0)
        stats_ref[...] = jnp.where(lane // share % PAIR == half, joined, neutral)
    else:
        for at in range(STATS):
            line = jnp.sum(jnp.where(lane == sub, stats[at], 0.0), axis=0, keepdims=True)
            for h in range(PAIR):
                first = (at * PAIR + h) * share
                stats_ref[:, first : first + share] = jnp.where(half == h, line, 0.0 if at else -jnp.inf)


def finish_kernel(share, stats_ref, meta_ref, logprob_ref, entropy_ref, seq_ref):
    row_count = logprob_ref.shape[0]
    used = PAIR * share
    lanes = max(used, LANES)

    def stat(at):
        if used >= LANES:
            return stats_ref[:, at * used : (at + 1) * used]
        return stats_ref[...] if at == 0 else pltpu.roll(stats_ref[...], LANES - at * used, 1)

    tops = stat(0)
    row_top = jnp.max(tops, axis=0, keepdims=True)
    weight = jnp.exp(tops - row_top)
    row_total = jnp.sum(stat(1) * weight, axis=0, keepdims=True)
    row_weighted = jnp.sum(stat(2) * weight, axis=0, keepdims=True)
    picked = jnp.sum(stat(3), axis=0, keepdims=True)
    log_norm = row_top + jnp.log(row_total)
    lane, sub = iota((1, lanes), 1), iota((SUBS, lanes), 0)
    in_use = jnp.logical_and(meta_ref[4:5, :] > 0.5, lane < used)
    logprob = jnp.where(in_use, picked - log_norm, 0.0)
    entropy = jnp.where(in_use, log_norm - row_weighted / row_total, 0.0)
    segment, place = meta_ref[3:4, :].astype(jnp.int32), meta_ref[5:6, :].astype(jnp.int32)
    mine = jnp.logical_and(place == sub, lane % share // MINE == own_slot(share // MINE))

    def placed(values, wanted):
        sums = jnp.sum(jnp.where(wanted, values, 0.0), axis=1, keepdims=True)
        diagonal = iota((SUBS, LANES), 0) == iota((SUBS, LANES), 1)
        return jnp.sum(jnp.where(diagonal, sums, 0.0), axis=0)

    logprob_ref[...] = placed(logprob, mine)[:row_count]
    entropy_ref[...] = placed(entropy, mine)[:row_count]
    seq_ref[...] = placed(logprob, segment == sub)[:SEQS]


def grant(mebibytes):
    return pltpu.CompilerParams(vmem_limit_bytes=mebibytes * 1024 * 1024)


def local(hidden, norm_gain, lm_head, targets, segments, scored):
    row_count, width = hidden.shape
    groups, tp_count = lax.axis_size("req"), lax.axis_size("tp")
    span = width * MINE // SUBS
    share = groups * MINE
    lanes = max(PAIR * share, LANES)

    def spec(space):
        return pl.BlockSpec(memory_space=space)

    other = lax.ppermute(lm_head, "tp", [(i, i + 1 - 2 * (i % PAIR)) for i in range(tp_count)])
    packed = pl.pallas_call(
        functools.partial(pack_kernel, share),
        out_shape=VMEM((groups, SUBS, span + lanes), jnp.bfloat16),
        in_specs=[spec(VMEM)] * 2 + [spec(SMEM)] * 3,
        out_specs=spec(VMEM),
        scratch_shapes=[
            VMEM((row_count, width), jnp.float32),
            VMEM((SUBS, span), jnp.float32),
            VMEM((width // LANES, LANES), jnp.float32),
        ],
    )(hidden, norm_gain.reshape(width // LANES, LANES), targets, segments, scored)
    rows = lax.all_to_all(packed, "req", 0, 0, axis_index_groups=[middle_first(groups)])
    other = pltpu.with_memory_space_constraint(other, pltpu.HBM)
    staged = width // 2
    slices = pl.pallas_call(
        stage_kernel,
        out_shape=(VMEM(lm_head.shape, lm_head.dtype), VMEM((staged, lm_head.shape[1]), lm_head.dtype)),
        in_specs=[spec(pltpu.HBM)] * 2,
        out_specs=(spec(VMEM),) * 2,
        scratch_shapes=[pltpu.SemaphoreType.DMA((2, 4))],
        compiler_params=grant(4),
        cost_estimate=pl.CostEstimate(flops=0, bytes_accessed=3 * 2 * lm_head.size, transcendentals=0),
    )(pltpu.with_memory_space_constraint(lm_head, pltpu.HBM), other)
    stats, meta = pl.pallas_call(
        score_kernel,
        out_shape=(
            jax.ShapeDtypeStruct((1, STATS * PAIR * share), jnp.float32),
            VMEM((SUBS, lanes), jnp.float32),
        ),
        in_specs=[spec(VMEM)] * 3 + [spec(pltpu.HBM)],
        out_specs=(spec(VMEM), spec(VMEM)),
        scratch_shapes=[
            VMEM((share, width), jnp.bfloat16),
            VMEM((width - staged, lm_head.shape[1]), jnp.bfloat16),
            pltpu.SemaphoreType.DMA((4,)),
        ],
        compiler_params=grant(24),
    )(rows, *(pltpu.with_memory_space_constraint(part, VMEM) for part in slices), other)
    copies = jnp.broadcast_to(stats[None], (groups * tp_count,) + stats.shape)
    members = [q * tp_count + t for q in middle_first(groups) for t in range(tp_count)]
    gathered = lax.all_to_all(copies, ("req", "tp"), 0, 0, axis_index_groups=[members])
    gathered = gathered.reshape(groups * tp_count, stats.shape[1])
    return pl.pallas_call(
        functools.partial(finish_kernel, share),
        out_shape=(
            jax.ShapeDtypeStruct((row_count,), jnp.float32),
            jax.ShapeDtypeStruct((row_count,), jnp.float32),
            jax.ShapeDtypeStruct((SEQS,), jnp.float32),
        ),
        in_specs=[spec(VMEM), spec(VMEM)],
        out_specs=(spec(VMEM), spec(VMEM), spec(VMEM)),
    )(pltpu.with_memory_space_constraint(gathered, VMEM), pltpu.with_memory_space_constraint(meta, VMEM))


def solution(mesh):
    return jax.shard_map(
        local,
        mesh=mesh,
        in_specs=(P("req", None), P(), P(None, ("req", "tp")), P("req"), P("req"), P("req")),
        out_specs=(P("req"), P("req"), P()),
        check_vma=False,
    )
```

```python
import functools

import jax
import jax.numpy as jnp
from jax import lax
from jax.experimental import pallas as pl
from jax.experimental.pallas import tpu as pltpu
from jax.sharding import PartitionSpec as P

SEQS = 4
PICK = 4
PAIR = 2
MINE = PICK // PAIR
SUBS = 8
LANES = 128
STATS = 4

VMEM = pltpu.VMEM
SMEM = pltpu.SMEM


def ranks_of(scored_ref, row_count):
    ranks, so_far = [], jnp.int32(0)
    for row in range(row_count):
        ranks.append(so_far)
        so_far = so_far + scored_ref[row]
    return ranks, so_far


def iota(shape, axis):
    return lax.broadcasted_iota(jnp.int32, shape, axis)


def own_slot(count):
    return count - 1 - lax.axis_index("req")


def pack_kernel(share, hidden_ref, gain_ref, targets_ref, segments_ref, scored_ref, out_ref, wide_ref, parts_ref, gains_ref):
    row_count, width = hidden_ref.shape
    parts = SUBS // MINE
    span = width // parts
    own, half = own_slot(out_ref.shape[0]), lax.axis_index("tp") % PAIR
    wide_ref[...] = hidden_ref[...].astype(jnp.float32)
    gains_ref[...] = gain_ref[...].astype(jnp.float32)
    ranks, count = ranks_of(scored_ref, row_count)
    source = [jnp.int32(0)] * PICK
    for row in range(row_count):
        for r in range(PICK):
            hit = jnp.logical_and(scored_ref[row] == 1, ranks[row] == r)
            source[r] = jnp.where(hit, row, source[r])
    mine = [source[i] for i in range(MINE)]
    for h in range(1, PAIR):
        mine = [jnp.where(half == h, source[h * MINE + i], mine[i]) for i in range(MINE)]
    for i in range(MINE):
        for k in range(parts):
            parts_ref[k * MINE + i : k * MINE + i + 1, :] = wide_ref[pl.ds(mine[i], 1), k * span : (k + 1) * span]
    values = parts_ref[...]
    part = jnp.broadcast_to(jnp.sum(values * values, axis=1, keepdims=True), (SUBS, LANES))
    total = part
    for k in range(1, parts):
        total = total + pltpu.roll(part, k * MINE, 0)
    row_scale = lax.rsqrt(total / width + 1e-05)
    sub, lane = iota((SUBS, LANES), 0), iota((SUBS, LANES), 1)
    chunks = span // LANES
    for at in range(chunks):
        gain = gains_ref[at : at + 1, :]
        for k in range(1, parts):
            gain = jnp.where(sub >= k * MINE, gains_ref[k * chunks + at : k * chunks + at + 1, :], gain)
        piece = parts_ref[:, at * LANES : (at + 1) * LANES]
        piece = (piece * row_scale * gain).astype(jnp.bfloat16)
        for to in range(out_ref.shape[0]):
            out_ref[to, :, at * LANES : (at + 1) * LANES] = piece
    width_side = out_ref.shape[2] - span
    sub, lane = iota((SUBS, width_side), 0), iota((SUBS, width_side), 1)
    at_row, at_half = lane % share - own * MINE, lane // share
    side = jnp.zeros((SUBS, width_side), jnp.int32)
    for i in range(MINE):
        target = targets_ref[mine[i]]
        digits = jnp.where(sub == 0, target & 255, jnp.where(sub == 1, (target >> 8) & 255, target >> 16))
        fields = jnp.zeros((SUBS, width_side), jnp.int32)
        for h in range(PAIR):
            r = h * MINE + i
            field = jnp.where(sub == 4, (count > r).astype(jnp.int32), source[r])
            fields = jnp.where(at_half == h, jnp.where(sub == 3, segments_ref[source[r]], field), fields)
        side = jnp.where(at_row == i, jnp.where(sub < 3, digits, fields), side)
    side = side.astype(jnp.float32).astype(jnp.bfloat16)
    for to in range(out_ref.shape[0]):
        out_ref[to, :, span:] = side


def stage_kernel(own_ref, other_ref, own_out, other_out, sems):
    copies = []
    for at, (source, out) in enumerate(((own_ref, own_out), (other_ref, other_out))):
        depth = out.shape[0] // sems.shape[1]
        for i in range(sems.shape[1]):
            piece = pl.ds(i * depth, depth)
            copies.append(pltpu.make_async_copy(source.at[piece], out.at[piece], sems.at[at, i]))
    for copy in copies:
        copy.start()
    for copy in copies:
        copy.wait()


def score_kernel(rows_ref, own_ref, upper_ref, other_ref, stats_ref, meta_ref, ordered_ref, lower_ref, sems):
    width, cols = own_ref.shape
    staged = upper_ref.shape[0]
    depth = lower_ref.shape[0] // sems.shape[0]
    copies = [
        pltpu.make_async_copy(
            other_ref.at[pl.ds(staged + i * depth, depth)], lower_ref.at[pl.ds(i * depth, depth)], sems.at[i]
        )
        for i in range(sems.shape[0])
    ]
    for copy in copies:
        copy.start()
    groups = rows_ref.shape[0]
    parts = SUBS // MINE
    span = width // parts
    share = groups * MINE
    tp, tp_count = lax.axis_index("tp"), lax.axis_size("tp")
    half = tp % PAIR
    place = lax.axis_index("req") * tp_count + tp
    count = groups * SUBS
    into, out_of = iota((count, count), 0), iota((count, count), 1)
    wanted = into % share // MINE * SUBS + into // share * MINE + into % MINE
    order = jnp.where(out_of == wanted, 1.0, 0.0).astype(jnp.bfloat16)
    rows = rows_ref[:, :, :span].reshape(count, span)
    ordered = jnp.dot(order, rows, preferred_element_type=jnp.float32).astype(jnp.bfloat16)
    for k in range(parts):
        ordered_ref[:, k * span : (k + 1) * span] = ordered[k * share : (k + 1) * share]
    meta = rows_ref[0, :, span:].astype(jnp.float32)
    for q in range(1, groups):
        meta = meta + rows_ref[q, :, span:].astype(jnp.float32)
    meta_ref[...] = meta
    own_logits = jnp.dot(ordered_ref[...], own_ref[...], preferred_element_type=jnp.float32)
    other_logits = jnp.dot(ordered_ref[:, :staged], upper_ref[...], preferred_element_type=jnp.float32)
    for copy in copies:
        copy.wait()
    other_logits += jnp.dot(ordered_ref[:, staged:], lower_ref[...], preferred_element_type=jnp.float32)
    logits = jnp.concatenate([own_logits, other_logits], axis=1)
    lanes = max(share, LANES)
    sub, lane = iota((share, lanes), 0), iota((share, lanes), 1)
    ids = meta[0:1, :lanes] + 256.0 * meta[1:2, :lanes] + 65536.0 * meta[2:3, :lanes]
    ids = jnp.sum(jnp.where(lane == sub, ids, 0.0), axis=1, keepdims=True).astype(jnp.int32)
    row_top = jnp.max(logits, axis=1, keepdims=True)
    scaled = jnp.exp(logits - row_top)
    row_total = jnp.sum(scaled, axis=1, keepdims=True)
    row_weighted = jnp.sum(scaled * logits, axis=1, keepdims=True)
    column = iota(logits.shape, 1)
    other = place + 1 - 2 * half
    columns = jnp.where(column < cols, place * cols, (other - 1) * cols) + column
    picked = jnp.sum(jnp.where(columns == ids, logits, 0.0), axis=1, keepdims=True)
    stats = (row_top, row_total, row_weighted, picked)
    if PAIR * share * STATS == LANES:
        joined = picked
        for at in range(STATS - 1):
            joined = jnp.where(lane // (PAIR * share) == at, stats[at], joined)
        joined = jnp.sum(jnp.where(lane % share == sub, joined, 0.0), axis=0, keepdims=True)
        lane = iota((1, LANES), 1)
        neutral = jnp.where(lane < PAIR * share, -jnp.inf, 0.0)
        stats_ref[...] = jnp.where(lane // share % PAIR == half, joined, neutral)
    else:
        for at in range(STATS):
            line = jnp.sum(jnp.where(lane == sub, stats[at], 0.0), axis=0, keepdims=True)
            for h in range(PAIR):
                first = (at * PAIR + h) * share
                stats_ref[:, first : first + share] = jnp.where(half == h, line, 0.0 if at else -jnp.inf)


def finish_kernel(share, stats_ref, meta_ref, logprob_ref, entropy_ref, seq_ref):
    row_count = logprob_ref.shape[0]
    used = PAIR * share
    lanes = max(used, LANES)

    def stat(at):
        if used >= LANES:
            return stats_ref[:, at * used : (at + 1) * used]
        return stats_ref[...] if at == 0 else pltpu.roll(stats_ref[...], LANES - at * used, 1)

    tops = stat(0)
    row_top = jnp.max(tops, axis=0, keepdims=True)
    weight = jnp.exp(tops - row_top)
    row_total = jnp.sum(stat(1) * weight, axis=0, keepdims=True)
    row_weighted = jnp.sum(stat(2) * weight, axis=0, keepdims=True)
    picked = jnp.sum(stat(3), axis=0, keepdims=True)
    log_norm = row_top + jnp.log(row_total)
    lane, sub = iota((1, lanes), 1), iota((SUBS, lanes), 0)
    in_use = jnp.logical_and(meta_ref[4:5, :] > 0.5, lane < used)
    logprob = jnp.where(in_use, picked - log_norm, 0.0)
    entropy = jnp.where(in_use, log_norm - row_weighted / row_total, 0.0)
    segment, place = meta_ref[3:4, :].astype(jnp.int32), meta_ref[5:6, :].astype(jnp.int32)
    mine = jnp.logical_and(place == sub, lane % share // MINE == own_slot(share // MINE))

    def placed(values, wanted):
        sums = jnp.sum(jnp.where(wanted, values, 0.0), axis=1, keepdims=True)
        diagonal = iota((SUBS, LANES), 0) == iota((SUBS, LANES), 1)
        return jnp.sum(jnp.where(diagonal, sums, 0.0), axis=0)

    logprob_ref[...] = placed(logprob, mine)[:row_count]
    entropy_ref[...] = placed(entropy, mine)[:row_count]
    seq_ref[...] = placed(logprob, segment == sub)[:SEQS]


def grant(mebibytes):
    return pltpu.CompilerParams(vmem_limit_bytes=mebibytes * 1024 * 1024)


def local(hidden, norm_gain, lm_head, targets, segments, scored):
    row_count, width = hidden.shape
    groups, tp_count = lax.axis_size("req"), lax.axis_size("tp")
    span = width * MINE // SUBS
    share = groups * MINE
    lanes = max(PAIR * share, LANES)

    def spec(space):
        return pl.BlockSpec(memory_space=space)

    other = lax.ppermute(lm_head, "tp", [(i, i + 1 - 2 * (i % PAIR)) for i in range(tp_count)])
    packed = pl.pallas_call(
        functools.partial(pack_kernel, share),
        out_shape=VMEM((groups, SUBS, span + lanes), jnp.bfloat16),
        in_specs=[spec(VMEM)] * 2 + [spec(SMEM)] * 3,
        out_specs=spec(VMEM),
        scratch_shapes=[
            VMEM((row_count, width), jnp.float32),
            VMEM((SUBS, span), jnp.float32),
            VMEM((width // LANES, LANES), jnp.float32),
        ],
    )(hidden, norm_gain.reshape(width // LANES, LANES), targets, segments, scored)
    rows = lax.all_to_all(packed, "req", 0, 0, axis_index_groups=[[*reversed(range(groups))]])
    other = pltpu.with_memory_space_constraint(other, pltpu.HBM)
    staged = width // 2
    slices = pl.pallas_call(
        stage_kernel,
        out_shape=(VMEM(lm_head.shape, lm_head.dtype), VMEM((staged, lm_head.shape[1]), lm_head.dtype)),
        in_specs=[spec(pltpu.HBM)] * 2,
        out_specs=(spec(VMEM),) * 2,
        scratch_shapes=[pltpu.SemaphoreType.DMA((2, 4))],
        compiler_params=grant(4),
        cost_estimate=pl.CostEstimate(flops=0, bytes_accessed=3 * 2 * lm_head.size, transcendentals=0),
    )(pltpu.with_memory_space_constraint(lm_head, pltpu.HBM), other)
    stats, meta = pl.pallas_call(
        score_kernel,
        out_shape=(
            jax.ShapeDtypeStruct((1, STATS * PAIR * share), jnp.float32),
            VMEM((SUBS, lanes), jnp.float32),
        ),
        in_specs=[spec(VMEM)] * 3 + [spec(pltpu.HBM)],
        out_specs=(spec(VMEM), spec(VMEM)),
        scratch_shapes=[
            VMEM((share, width), jnp.bfloat16),
            VMEM((width - staged, lm_head.shape[1]), jnp.bfloat16),
            pltpu.SemaphoreType.DMA((4,)),
        ],
        compiler_params=grant(24),
    )(rows, *(pltpu.with_memory_space_constraint(part, VMEM) for part in slices), other)
    copies = jnp.broadcast_to(stats[None], (groups * tp_count,) + stats.shape)
    members = [*reversed(range(groups * tp_count))]
    gathered = lax.all_to_all(copies, ("req", "tp"), 0, 0, axis_index_groups=[members])
    gathered = gathered.reshape(groups * tp_count, stats.shape[1])
    return pl.pallas_call(
        functools.partial(finish_kernel, share),
        out_shape=(
            jax.ShapeDtypeStruct((row_count,), jnp.float32),
            jax.ShapeDtypeStruct((row_count,), jnp.float32),
            jax.ShapeDtypeStruct((SEQS,), jnp.float32),
        ),
        in_specs=[spec(VMEM), spec(VMEM)],
        out_specs=(spec(VMEM), spec(VMEM), spec(VMEM)),
    )(pltpu.with_memory_space_constraint(gathered, VMEM), pltpu.with_memory_space_constraint(meta, VMEM))


def solution(mesh):
    return jax.shard_map(
        local,
        mesh=mesh,
        in_specs=(P("req", None), P(), P(None, ("req", "tp")), P("req"), P("req"), P("req")),
        out_specs=(P("req"), P("req"), P()),
        check_vma=False,
    )
```

```python
import functools

import jax
import jax.numpy as jnp
from jax import lax
from jax.experimental import pallas as pl
from jax.experimental.pallas import tpu as pltpu
from jax.sharding import PartitionSpec as P

SEQS = 4
PICK = 4
PAIR = 2
MINE = PICK // PAIR
SUBS = 8
LANES = 128
STATS = 4

VMEM = pltpu.VMEM
SMEM = pltpu.SMEM


def ranks_of(scored_ref, row_count):
    ranks, so_far = [], jnp.int32(0)
    for row in range(row_count):
        ranks.append(so_far)
        so_far = so_far + scored_ref[row]
    return ranks, so_far


def iota(shape, axis):
    return lax.broadcasted_iota(jnp.int32, shape, axis)


def middle_first(count):
    quarter = count // 4
    order = [*range(quarter, count - quarter), *range(quarter), *range(count - quarter, count)]
    return [count - 1 - index for index in order]


def own_slot(count):
    own, quarter = count - 1 - lax.axis_index("req"), count // 4
    return jnp.where(own < quarter, own + count - 2 * quarter, jnp.where(own < count - quarter, own - quarter, own))


def pack_kernel(share, hidden_ref, gain_ref, targets_ref, segments_ref, scored_ref, out_ref, wide_ref, parts_ref, gains_ref):
    row_count, width = hidden_ref.shape
    parts = SUBS // MINE
    span = width // parts
    own, half = own_slot(out_ref.shape[0]), lax.axis_index("tp") % PAIR
    wide_ref[...] = hidden_ref[...].astype(jnp.float32)
    gains_ref[...] = gain_ref[...].astype(jnp.float32)
    ranks, count = ranks_of(scored_ref, row_count)
    source = [jnp.int32(0)] * PICK
    for row in range(row_count):
        for r in range(PICK):
            hit = jnp.logical_and(scored_ref[row] == 1, ranks[row] == r)
            source[r] = jnp.where(hit, row, source[r])
    mine = [source[i] for i in range(MINE)]
    for h in range(1, PAIR):
        mine = [jnp.where(half == h, source[h * MINE + i], mine[i]) for i in range(MINE)]
    for i in range(MINE):
        for k in range(parts):
            parts_ref[k * MINE + i : k * MINE + i + 1, :] = wide_ref[pl.ds(mine[i], 1), k * span : (k + 1) * span]
    values = parts_ref[...]
    part = jnp.broadcast_to(jnp.sum(values * values, axis=1, keepdims=True), (SUBS, LANES))
    total = part
    for k in range(1, parts):
        total = total + pltpu.roll(part, k * MINE, 0)
    row_scale = lax.rsqrt(total / width + 1e-05)
    sub, lane = iota((SUBS, LANES), 0), iota((SUBS, LANES), 1)
    chunks = span // LANES
    for at in range(chunks):
        gain = gains_ref[at : at + 1, :]
        for k in range(1, parts):
            gain = jnp.where(sub >= k * MINE, gains_ref[k * chunks + at : k * chunks + at + 1, :], gain)
        piece = parts_ref[:, at * LANES : (at + 1) * LANES]
        piece = (piece * row_scale * gain).astype(jnp.bfloat16)
        for to in range(out_ref.shape[0]):
            out_ref[to, :, at * LANES : (at + 1) * LANES] = piece
    width_side = out_ref.shape[2] - span
    sub, lane = iota((SUBS, width_side), 0), iota((SUBS, width_side), 1)
    at_row, at_half = lane % share - own * MINE, lane // share
    side = jnp.zeros((SUBS, width_side), jnp.int32)
    for i in range(MINE):
        target = targets_ref[mine[i]]
        digits = jnp.where(sub == 0, target & 255, jnp.where(sub == 1, (target >> 8) & 255, target >> 16))
        fields = jnp.zeros((SUBS, width_side), jnp.int32)
        for h in range(PAIR):
            r = h * MINE + i
            field = jnp.where(sub == 4, (count > r).astype(jnp.int32), source[r])
            fields = jnp.where(at_half == h, jnp.where(sub == 3, segments_ref[source[r]], field), fields)
        side = jnp.where(at_row == i, jnp.where(sub < 3, digits, fields), side)
    side = side.astype(jnp.float32).astype(jnp.bfloat16)
    for to in range(out_ref.shape[0]):
        out_ref[to, :, span:] = side


def stage_kernel(own_ref, other_ref, own_out, other_out, sems):
    copies = []
    for at, (source, out) in enumerate(((own_ref, own_out), (other_ref, other_out))):
        depth = out.shape[0] // sems.shape[1]
        for i in range(sems.shape[1]):
            piece = pl.ds(i * depth, depth)
            copies.append(pltpu.make_async_copy(source.at[piece], out.at[piece], sems.at[at, i]))
    for copy in copies:
        copy.start()
    for copy in copies:
        copy.wait()


def score_kernel(rows_ref, own_ref, upper_ref, other_ref, stats_ref, meta_ref, ordered_ref, lower_ref, sems):
    width, cols = own_ref.shape
    staged = upper_ref.shape[0]
    depth = lower_ref.shape[0] // sems.shape[0]
    copies = [
        pltpu.make_async_copy(
            other_ref.at[pl.ds(staged + i * depth, depth)], lower_ref.at[pl.ds(i * depth, depth)], sems.at[i]
        )
        for i in range(sems.shape[0])
    ]
    for copy in copies:
        copy.start()
    groups = rows_ref.shape[0]
    parts = SUBS // MINE
    span = width // parts
    share = groups * MINE
    tp, tp_count = lax.axis_index("tp"), lax.axis_size("tp")
    half = tp % PAIR
    place = lax.axis_index("req") * tp_count + tp
    count = groups * SUBS
    into, out_of = iota((count, count), 0), iota((count, count), 1)
    wanted = into % share // MINE * SUBS + into // share * MINE + into % MINE
    order = jnp.where(out_of == wanted, 1.0, 0.0).astype(jnp.bfloat16)
    rows = rows_ref[:, :, :span].reshape(count, span)
    ordered = jnp.dot(order, rows, preferred_element_type=jnp.float32).astype(jnp.bfloat16)
    for k in range(parts):
        ordered_ref[:, k * span : (k + 1) * span] = ordered[k * share : (k + 1) * share]
    meta = rows_ref[0, :, span:].astype(jnp.float32)
    for q in range(1, groups):
        meta = meta + rows_ref[q, :, span:].astype(jnp.float32)
    meta_ref[...] = meta
    own_logits = jnp.dot(ordered_ref[...], own_ref[...], preferred_element_type=jnp.float32)
    other_logits = jnp.dot(ordered_ref[:, :staged], upper_ref[...], preferred_element_type=jnp.float32)
    for copy in copies:
        copy.wait()
    other_logits += jnp.dot(ordered_ref[:, staged:], lower_ref[...], preferred_element_type=jnp.float32)
    logits = jnp.concatenate([own_logits, other_logits], axis=1)
    lanes = max(share, LANES)
    sub, lane = iota((share, lanes), 0), iota((share, lanes), 1)
    ids = meta[0:1, :lanes] + 256.0 * meta[1:2, :lanes] + 65536.0 * meta[2:3, :lanes]
    ids = jnp.sum(jnp.where(lane == sub, ids, 0.0), axis=1, keepdims=True).astype(jnp.int32)
    row_top = jnp.max(logits, axis=1, keepdims=True)
    scaled = jnp.exp(logits - row_top)
    row_total = jnp.sum(scaled, axis=1, keepdims=True)
    row_weighted = jnp.sum(scaled * logits, axis=1, keepdims=True)
    column = iota(logits.shape, 1)
    other = place + 1 - 2 * half
    columns = jnp.where(column < cols, place * cols, (other - 1) * cols) + column
    picked = jnp.sum(jnp.where(columns == ids, logits, 0.0), axis=1, keepdims=True)
    stats = (row_top, row_total, row_weighted, picked)
    if PAIR * share * STATS == LANES:
        joined = picked
        for at in range(STATS - 1):
            joined = jnp.where(lane // (PAIR * share) == at, stats[at], joined)
        joined = jnp.sum(jnp.where(lane % share == sub, joined, 0.0), axis=0, keepdims=True)
        lane = iota((1, LANES), 1)
        neutral = jnp.where(lane < PAIR * share, -jnp.inf, 0.0)
        stats_ref[...] = jnp.where(lane // share % PAIR == half, joined, neutral)
    else:
        for at in range(STATS):
            line = jnp.sum(jnp.where(lane == sub, stats[at], 0.0), axis=0, keepdims=True)
            for h in range(PAIR):
                first = (at * PAIR + h) * share
                stats_ref[:, first : first + share] = jnp.where(half == h, line, 0.0 if at else -jnp.inf)


def finish_kernel(share, stats_ref, meta_ref, logprob_ref, entropy_ref, seq_ref):
    row_count = logprob_ref.shape[0]
    used = PAIR * share
    lanes = max(used, LANES)

    def stat(at):
        if used >= LANES:
            return stats_ref[:, at * used : (at + 1) * used]
        return stats_ref[...] if at == 0 else pltpu.roll(stats_ref[...], LANES - at * used, 1)

    tops = stat(0)
    row_top = jnp.max(tops, axis=0, keepdims=True)
    weight = jnp.exp(tops - row_top)
    row_total = jnp.sum(stat(1) * weight, axis=0, keepdims=True)
    row_weighted = jnp.sum(stat(2) * weight, axis=0, keepdims=True)
    picked = jnp.sum(stat(3), axis=0, keepdims=True)
    log_norm = row_top + jnp.log(row_total)
    lane, sub = iota((1, lanes), 1), iota((SUBS, lanes), 0)
    in_use = jnp.logical_and(meta_ref[4:5, :] > 0.5, lane < used)
    logprob = jnp.where(in_use, picked - log_norm, 0.0)
    entropy = jnp.where(in_use, log_norm - row_weighted / row_total, 0.0)
    segment, place = meta_ref[3:4, :].astype(jnp.int32), meta_ref[5:6, :].astype(jnp.int32)
    mine = jnp.logical_and(place == sub, lane % share // MINE == own_slot(share // MINE))

    def placed(values, wanted):
        sums = jnp.sum(jnp.where(wanted, values, 0.0), axis=1, keepdims=True)
        diagonal = iota((SUBS, LANES), 0) == iota((SUBS, LANES), 1)
        return jnp.sum(jnp.where(diagonal, sums, 0.0), axis=0)

    logprob_ref[...] = placed(logprob, mine)[:row_count]
    entropy_ref[...] = placed(entropy, mine)[:row_count]
    seq_ref[...] = placed(logprob, segment == sub)[:SEQS]


def grant(mebibytes):
    return pltpu.CompilerParams(vmem_limit_bytes=mebibytes * 1024 * 1024)


def local(hidden, norm_gain, lm_head, targets, segments, scored):
    row_count, width = hidden.shape
    groups, tp_count = lax.axis_size("req"), lax.axis_size("tp")
    span = width * MINE // SUBS
    share = groups * MINE
    lanes = max(PAIR * share, LANES)

    def spec(space):
        return pl.BlockSpec(memory_space=space)

    other = lax.ppermute(lm_head, "tp", [(i, i + 1 - 2 * (i % PAIR)) for i in range(tp_count)])
    packed = pl.pallas_call(
        functools.partial(pack_kernel, share),
        out_shape=VMEM((groups, SUBS, span + lanes), jnp.bfloat16),
        in_specs=[spec(VMEM)] * 2 + [spec(SMEM)] * 3,
        out_specs=spec(VMEM),
        scratch_shapes=[
            VMEM((row_count, width), jnp.float32),
            VMEM((SUBS, span), jnp.float32),
            VMEM((width // LANES, LANES), jnp.float32),
        ],
    )(hidden, norm_gain.reshape(width // LANES, LANES), targets, segments, scored)
    rows = lax.all_to_all(packed, "req", 0, 0, axis_index_groups=[middle_first(groups)])
    other = pltpu.with_memory_space_constraint(other, pltpu.HBM)
    staged = width // 2
    slices = pl.pallas_call(
        stage_kernel,
        out_shape=(VMEM(lm_head.shape, lm_head.dtype), VMEM((staged, lm_head.shape[1]), lm_head.dtype)),
        in_specs=[spec(pltpu.HBM)] * 2,
        out_specs=(spec(VMEM),) * 2,
        scratch_shapes=[pltpu.SemaphoreType.DMA((2, 4))],
        compiler_params=grant(4),
        cost_estimate=pl.CostEstimate(flops=0, bytes_accessed=3 * 2 * lm_head.size, transcendentals=0),
    )(pltpu.with_memory_space_constraint(lm_head, pltpu.HBM), other)
    stats, meta = pl.pallas_call(
        score_kernel,
        out_shape=(
            jax.ShapeDtypeStruct((1, STATS * PAIR * share), jnp.float32),
            VMEM((SUBS, lanes), jnp.float32),
        ),
        in_specs=[spec(VMEM)] * 3 + [spec(pltpu.HBM)],
        out_specs=(spec(VMEM), spec(VMEM)),
        scratch_shapes=[
            VMEM((share, width), jnp.bfloat16),
            VMEM((width - staged, lm_head.shape[1]), jnp.bfloat16),
            pltpu.SemaphoreType.DMA((4,)),
        ],
        compiler_params=grant(24),
    )(rows, *(pltpu.with_memory_space_constraint(part, VMEM) for part in slices), other)
    copies = jnp.broadcast_to(stats[None], (groups * tp_count,) + stats.shape)
    members = [q * tp_count + t for q in middle_first(groups) for t in range(tp_count)]
    gathered = lax.all_to_all(copies, ("req", "tp"), 0, 0, axis_index_groups=[members])
    gathered = gathered.reshape(groups * tp_count, stats.shape[1])
    return pl.pallas_call(
        functools.partial(finish_kernel, share),
        out_shape=(
            jax.ShapeDtypeStruct((row_count,), jnp.float32),
            jax.ShapeDtypeStruct((row_count,), jnp.float32),
            jax.ShapeDtypeStruct((SEQS,), jnp.float32),
        ),
        in_specs=[spec(VMEM), spec(VMEM)],
        out_specs=(spec(VMEM), spec(VMEM), spec(VMEM)),
    )(pltpu.with_memory_space_constraint(gathered, VMEM), pltpu.with_memory_space_constraint(meta, VMEM))


def solution(mesh):
    return jax.shard_map(
        local,
        mesh=mesh,
        in_specs=(P("req", None), P(), P(None, ("req", "tp")), P("req"), P("req"), P("req")),
        out_specs=(P("req"), P("req"), P()),
        check_vma=False,
    )
```

```python
import functools

import jax
import jax.numpy as jnp
from jax import lax
from jax.experimental import pallas as pl
from jax.experimental.pallas import tpu as pltpu
from jax.sharding import PartitionSpec as P

SEQS = 4
PICK = 4
PAIR = 2
MINE = PICK // PAIR
SUBS = 8
LANES = 128
STATS = 4

VMEM = pltpu.VMEM
SMEM = pltpu.SMEM


def ranks_of(scored_ref, row_count):
    ranks, so_far = [], jnp.int32(0)
    for row in range(row_count):
        ranks.append(so_far)
        so_far = so_far + scored_ref[row]
    return ranks, so_far


def iota(shape, axis):
    return lax.broadcasted_iota(jnp.int32, shape, axis)


def members(count):
    quarter = count // 4
    return [*reversed(range(quarter, count - quarter)), *range(quarter), *range(count - quarter, count)]


def own_slot(count):
    own, quarter = lax.axis_index("req"), count // 4
    middle = count - quarter - 1 - own
    return jnp.where(own < quarter, own + count - 2 * quarter, jnp.where(own < count - quarter, middle, own))


def pack_kernel(share, hidden_ref, gain_ref, targets_ref, segments_ref, scored_ref, out_ref, wide_ref, parts_ref, gains_ref):
    row_count, width = hidden_ref.shape
    parts = SUBS // MINE
    span = width // parts
    own, half = own_slot(out_ref.shape[0]), lax.axis_index("tp") % PAIR
    wide_ref[...] = hidden_ref[...].astype(jnp.float32)
    gains_ref[...] = gain_ref[...].astype(jnp.float32)
    ranks, count = ranks_of(scored_ref, row_count)
    source = [jnp.int32(0)] * PICK
    for row in range(row_count):
        for r in range(PICK):
            hit = jnp.logical_and(scored_ref[row] == 1, ranks[row] == r)
            source[r] = jnp.where(hit, row, source[r])
    mine = [source[i] for i in range(MINE)]
    for h in range(1, PAIR):
        mine = [jnp.where(half == h, source[h * MINE + i], mine[i]) for i in range(MINE)]
    for i in range(MINE):
        for k in range(parts):
            parts_ref[k * MINE + i : k * MINE + i + 1, :] = wide_ref[pl.ds(mine[i], 1), k * span : (k + 1) * span]
    values = parts_ref[...]
    part = jnp.broadcast_to(jnp.sum(values * values, axis=1, keepdims=True), (SUBS, LANES))
    total = part
    for k in range(1, parts):
        total = total + pltpu.roll(part, k * MINE, 0)
    row_scale = lax.rsqrt(total / width + 1e-05)
    sub, lane = iota((SUBS, LANES), 0), iota((SUBS, LANES), 1)
    chunks = span // LANES
    for at in range(chunks):
        gain = gains_ref[at : at + 1, :]
        for k in range(1, parts):
            gain = jnp.where(sub >= k * MINE, gains_ref[k * chunks + at : k * chunks + at + 1, :], gain)
        piece = parts_ref[:, at * LANES : (at + 1) * LANES]
        piece = (piece * row_scale * gain).astype(jnp.bfloat16)
        for to in range(out_ref.shape[0]):
            out_ref[to, :, at * LANES : (at + 1) * LANES] = piece
    width_side = out_ref.shape[2] - span
    sub, lane = iota((SUBS, width_side), 0), iota((SUBS, width_side), 1)
    at_row, at_half = lane % share - own * MINE, lane // share
    side = jnp.zeros((SUBS, width_side), jnp.int32)
    for i in range(MINE):
        target = targets_ref[mine[i]]
        digits = jnp.where(sub == 0, target & 255, jnp.where(sub == 1, (target >> 8) & 255, target >> 16))
        fields = jnp.zeros((SUBS, width_side), jnp.int32)
        for h in range(PAIR):
            r = h * MINE + i
            field = jnp.where(sub == 4, (count > r).astype(jnp.int32), source[r])
            fields = jnp.where(at_half == h, jnp.where(sub == 3, segments_ref[source[r]], field), fields)
        side = jnp.where(at_row == i, jnp.where(sub < 3, digits, fields), side)
    side = side.astype(jnp.float32).astype(jnp.bfloat16)
    for to in range(out_ref.shape[0]):
        out_ref[to, :, span:] = side


def stage_kernel(own_ref, other_ref, own_out, other_out, sems):
    copies = []
    for at, (source, out) in enumerate(((own_ref, own_out), (other_ref, other_out))):
        depth = out.shape[0] // sems.shape[1]
        for i in range(sems.shape[1]):
            piece = pl.ds(i * depth, depth)
            copies.append(pltpu.make_async_copy(source.at[piece], out.at[piece], sems.at[at, i]))
    for copy in copies:
        copy.start()
    for copy in copies:
        copy.wait()


def score_kernel(rows_ref, own_ref, upper_ref, other_ref, stats_ref, meta_ref, ordered_ref, lower_ref, sems):
    width, cols = own_ref.shape
    staged = upper_ref.shape[0]
    depth = lower_ref.shape[0] // sems.shape[0]
    copies = [
        pltpu.make_async_copy(
            other_ref.at[pl.ds(staged + i * depth, depth)], lower_ref.at[pl.ds(i * depth, depth)], sems.at[i]
        )
        for i in range(sems.shape[0])
    ]
    for copy in copies:
        copy.start()
    groups = rows_ref.shape[0]
    parts = SUBS // MINE
    span = width // parts
    share = groups * MINE
    tp, tp_count = lax.axis_index("tp"), lax.axis_size("tp")
    half = tp % PAIR
    place = lax.axis_index("req") * tp_count + tp
    count = groups * SUBS
    into, out_of = iota((count, count), 0), iota((count, count), 1)
    wanted = into % share // MINE * SUBS + into // share * MINE + into % MINE
    order = jnp.where(out_of == wanted, 1.0, 0.0).astype(jnp.bfloat16)
    rows = rows_ref[:, :, :span].reshape(count, span)
    ordered = jnp.dot(order, rows, preferred_element_type=jnp.float32).astype(jnp.bfloat16)
    for k in range(parts):
        ordered_ref[:, k * span : (k + 1) * span] = ordered[k * share : (k + 1) * share]
    meta = rows_ref[0, :, span:].astype(jnp.float32)
    for q in range(1, groups):
        meta = meta + rows_ref[q, :, span:].astype(jnp.float32)
    meta_ref[...] = meta
    own_logits = jnp.dot(ordered_ref[...], own_ref[...], preferred_element_type=jnp.float32)
    other_logits = jnp.dot(ordered_ref[:, :staged], upper_ref[...], preferred_element_type=jnp.float32)
    for copy in copies:
        copy.wait()
    other_logits += jnp.dot(ordered_ref[:, staged:], lower_ref[...], preferred_element_type=jnp.float32)
    logits = jnp.concatenate([own_logits, other_logits], axis=1)
    lanes = max(share, LANES)
    sub, lane = iota((share, lanes), 0), iota((share, lanes), 1)
    ids = meta[0:1, :lanes] + 256.0 * meta[1:2, :lanes] + 65536.0 * meta[2:3, :lanes]
    ids = jnp.sum(jnp.where(lane == sub, ids, 0.0), axis=1, keepdims=True).astype(jnp.int32)
    row_top = jnp.max(logits, axis=1, keepdims=True)
    scaled = jnp.exp(logits - row_top)
    row_total = jnp.sum(scaled, axis=1, keepdims=True)
    row_weighted = jnp.sum(scaled * logits, axis=1, keepdims=True)
    column = iota(logits.shape, 1)
    other = place + 1 - 2 * half
    columns = jnp.where(column < cols, place * cols, (other - 1) * cols) + column
    picked = jnp.sum(jnp.where(columns == ids, logits, 0.0), axis=1, keepdims=True)
    stats = (row_top, row_total, row_weighted, picked)
    if PAIR * share * STATS == LANES:
        joined = picked
        for at in range(STATS - 1):
            joined = jnp.where(lane // (PAIR * share) == at, stats[at], joined)
        joined = jnp.sum(jnp.where(lane % share == sub, joined, 0.0), axis=0, keepdims=True)
        lane = iota((1, LANES), 1)
        neutral = jnp.where(lane < PAIR * share, -jnp.inf, 0.0)
        stats_ref[...] = jnp.where(lane // share % PAIR == half, joined, neutral)
    else:
        for at in range(STATS):
            line = jnp.sum(jnp.where(lane == sub, stats[at], 0.0), axis=0, keepdims=True)
            for h in range(PAIR):
                first = (at * PAIR + h) * share
                stats_ref[:, first : first + share] = jnp.where(half == h, line, 0.0 if at else -jnp.inf)


def finish_kernel(share, stats_ref, meta_ref, logprob_ref, entropy_ref, seq_ref):
    row_count = logprob_ref.shape[0]
    used = PAIR * share
    lanes = max(used, LANES)

    def stat(at):
        if used >= LANES:
            return stats_ref[:, at * used : (at + 1) * used]
        return stats_ref[...] if at == 0 else pltpu.roll(stats_ref[...], LANES - at * used, 1)

    tops = stat(0)
    row_top = jnp.max(tops, axis=0, keepdims=True)
    weight = jnp.exp(tops - row_top)
    row_total = jnp.sum(stat(1) * weight, axis=0, keepdims=True)
    row_weighted = jnp.sum(stat(2) * weight, axis=0, keepdims=True)
    picked = jnp.sum(stat(3), axis=0, keepdims=True)
    log_norm = row_top + jnp.log(row_total)
    lane, sub = iota((1, lanes), 1), iota((SUBS, lanes), 0)
    in_use = jnp.logical_and(meta_ref[4:5, :] > 0.5, lane < used)
    logprob = jnp.where(in_use, picked - log_norm, 0.0)
    entropy = jnp.where(in_use, log_norm - row_weighted / row_total, 0.0)
    segment, place = meta_ref[3:4, :].astype(jnp.int32), meta_ref[5:6, :].astype(jnp.int32)
    mine = jnp.logical_and(place == sub, lane % share // MINE == own_slot(share // MINE))

    def placed(values, wanted):
        sums = jnp.sum(jnp.where(wanted, values, 0.0), axis=1, keepdims=True)
        diagonal = iota((SUBS, LANES), 0) == iota((SUBS, LANES), 1)
        return jnp.sum(jnp.where(diagonal, sums, 0.0), axis=0)

    logprob_ref[...] = placed(logprob, mine)[:row_count]
    entropy_ref[...] = placed(entropy, mine)[:row_count]
    seq_ref[...] = placed(logprob, segment == sub)[:SEQS]


def grant(mebibytes):
    return pltpu.CompilerParams(vmem_limit_bytes=mebibytes * 1024 * 1024)


def local(hidden, norm_gain, lm_head, targets, segments, scored):
    row_count, width = hidden.shape
    groups, tp_count = lax.axis_size("req"), lax.axis_size("tp")
    span = width * MINE // SUBS
    share = groups * MINE
    lanes = max(PAIR * share, LANES)

    def spec(space):
        return pl.BlockSpec(memory_space=space)

    other = lax.ppermute(lm_head, "tp", [(i, i + 1 - 2 * (i % PAIR)) for i in range(tp_count)])
    packed = pl.pallas_call(
        functools.partial(pack_kernel, share),
        out_shape=VMEM((groups, SUBS, span + lanes), jnp.bfloat16),
        in_specs=[spec(VMEM)] * 2 + [spec(SMEM)] * 3,
        out_specs=spec(VMEM),
        scratch_shapes=[
            VMEM((row_count, width), jnp.float32),
            VMEM((SUBS, span), jnp.float32),
            VMEM((width // LANES, LANES), jnp.float32),
        ],
    )(hidden, norm_gain.reshape(width // LANES, LANES), targets, segments, scored)
    rows = lax.all_to_all(packed, "req", 0, 0, axis_index_groups=[members(groups)])
    other = pltpu.with_memory_space_constraint(other, pltpu.HBM)
    staged = width // 2
    slices = pl.pallas_call(
        stage_kernel,
        out_shape=(VMEM(lm_head.shape, lm_head.dtype), VMEM((staged, lm_head.shape[1]), lm_head.dtype)),
        in_specs=[spec(pltpu.HBM)] * 2,
        out_specs=(spec(VMEM),) * 2,
        scratch_shapes=[pltpu.SemaphoreType.DMA((2, 4))],
        compiler_params=grant(4),
        cost_estimate=pl.CostEstimate(flops=0, bytes_accessed=3 * 2 * lm_head.size, transcendentals=0),
    )(pltpu.with_memory_space_constraint(lm_head, pltpu.HBM), other)
    stats, meta = pl.pallas_call(
        score_kernel,
        out_shape=(
            jax.ShapeDtypeStruct((1, STATS * PAIR * share), jnp.float32),
            VMEM((SUBS, lanes), jnp.float32),
        ),
        in_specs=[spec(VMEM)] * 3 + [spec(pltpu.HBM)],
        out_specs=(spec(VMEM), spec(VMEM)),
        scratch_shapes=[
            VMEM((share, width), jnp.bfloat16),
            VMEM((width - staged, lm_head.shape[1]), jnp.bfloat16),
            pltpu.SemaphoreType.DMA((4,)),
        ],
        compiler_params=grant(24),
    )(rows, *(pltpu.with_memory_space_constraint(part, VMEM) for part in slices), other)
    copies = jnp.broadcast_to(stats[None], (groups * tp_count,) + stats.shape)
    gathered = lax.all_to_all(copies, ("req", "tp"), 0, 0)
    gathered = gathered.reshape(groups * tp_count, stats.shape[1])
    return pl.pallas_call(
        functools.partial(finish_kernel, share),
        out_shape=(
            jax.ShapeDtypeStruct((row_count,), jnp.float32),
            jax.ShapeDtypeStruct((row_count,), jnp.float32),
            jax.ShapeDtypeStruct((SEQS,), jnp.float32),
        ),
        in_specs=[spec(VMEM), spec(VMEM)],
        out_specs=(spec(VMEM), spec(VMEM), spec(VMEM)),
    )(pltpu.with_memory_space_constraint(gathered, VMEM), pltpu.with_memory_space_constraint(meta, VMEM))


def solution(mesh):
    return jax.shard_map(
        local,
        mesh=mesh,
        in_specs=(P("req", None), P(), P(None, ("req", "tp")), P("req"), P("req"), P("req")),
        out_specs=(P("req"), P("req"), P()),
        check_vma=False,
    )
```

```python
import functools

import jax
import jax.numpy as jnp
from jax import lax
from jax.experimental import pallas as pl
from jax.experimental.pallas import tpu as pltpu
from jax.sharding import PartitionSpec as P

SEQS = 4
PICK = 4
PAIR = 2
MINE = PICK // PAIR
SUBS = 8
LANES = 128
STATS = 4

VMEM = pltpu.VMEM
SMEM = pltpu.SMEM


def ranks_of(scored_ref, row_count):
    ranks, so_far = [], jnp.int32(0)
    for row in range(row_count):
        ranks.append(so_far)
        so_far = so_far + scored_ref[row]
    return ranks, so_far


def iota(shape, axis):
    return lax.broadcasted_iota(jnp.int32, shape, axis)


def members(count):
    quarter = count // 4
    return [*reversed(range(quarter, count - quarter)), *range(quarter), *range(count - quarter, count)]


def own_slot(count):
    own, quarter = lax.axis_index("req"), count // 4
    middle = count - quarter - 1 - own
    return jnp.where(own < quarter, own + count - 2 * quarter, jnp.where(own < count - quarter, middle, own))


def pack_kernel(share, hidden_ref, gain_ref, targets_ref, segments_ref, scored_ref, out_ref, wide_ref, parts_ref, gains_ref):
    row_count, width = hidden_ref.shape
    parts = SUBS // MINE
    span = width // parts
    own, half = own_slot(out_ref.shape[0]), lax.axis_index("tp") % PAIR
    wide_ref[...] = hidden_ref[...].astype(jnp.float32)
    gains_ref[...] = gain_ref[...].astype(jnp.float32)
    ranks, count = ranks_of(scored_ref, row_count)
    source = [jnp.int32(0)] * PICK
    for row in range(row_count):
        for r in range(PICK):
            hit = jnp.logical_and(scored_ref[row] == 1, ranks[row] == r)
            source[r] = jnp.where(hit, row, source[r])
    mine = [source[i] for i in range(MINE)]
    for h in range(1, PAIR):
        mine = [jnp.where(half == h, source[h * MINE + i], mine[i]) for i in range(MINE)]
    for i in range(MINE):
        for k in range(parts):
            parts_ref[k * MINE + i : k * MINE + i + 1, :] = wide_ref[pl.ds(mine[i], 1), k * span : (k + 1) * span]
    values = parts_ref[...]
    part = jnp.broadcast_to(jnp.sum(values * values, axis=1, keepdims=True), (SUBS, LANES))
    total = part
    for k in range(1, parts):
        total = total + pltpu.roll(part, k * MINE, 0)
    row_scale = lax.rsqrt(total / width + 1e-05)
    sub, lane = iota((SUBS, LANES), 0), iota((SUBS, LANES), 1)
    chunks = span // LANES
    for at in range(chunks):
        gain = gains_ref[at : at + 1, :]
        for k in range(1, parts):
            gain = jnp.where(sub >= k * MINE, gains_ref[k * chunks + at : k * chunks + at + 1, :], gain)
        piece = parts_ref[:, at * LANES : (at + 1) * LANES]
        piece = (piece * row_scale * gain).astype(jnp.bfloat16)
        for to in range(out_ref.shape[0]):
            out_ref[to, :, at * LANES : (at + 1) * LANES] = piece
    width_side = out_ref.shape[2] - span
    sub, lane = iota((SUBS, width_side), 0), iota((SUBS, width_side), 1)
    at_row, at_half = lane % share - own * MINE, lane // share
    side = jnp.zeros((SUBS, width_side), jnp.int32)
    for i in range(MINE):
        target = targets_ref[mine[i]]
        digits = jnp.where(sub == 0, target & 255, jnp.where(sub == 1, (target >> 8) & 255, target >> 16))
        fields = jnp.zeros((SUBS, width_side), jnp.int32)
        for h in range(PAIR):
            r = h * MINE + i
            field = jnp.where(sub == 4, (count > r).astype(jnp.int32), source[r])
            fields = jnp.where(at_half == h, jnp.where(sub == 3, segments_ref[source[r]], field), fields)
        side = jnp.where(at_row == i, jnp.where(sub < 3, digits, fields), side)
    side = side.astype(jnp.float32).astype(jnp.bfloat16)
    for to in range(out_ref.shape[0]):
        out_ref[to, :, span:] = side


def stage_kernel(own_ref, other_ref, own_out, other_out, sems):
    copies = []
    for at, (source, out) in enumerate(((own_ref, own_out), (other_ref, other_out))):
        depth = out.shape[0] // sems.shape[1]
        for i in range(sems.shape[1]):
            piece = pl.ds(i * depth, depth)
            copies.append(pltpu.make_async_copy(source.at[piece], out.at[piece], sems.at[at, i]))
    for copy in copies:
        copy.start()
    for copy in copies:
        copy.wait()


def score_kernel(rows_ref, own_ref, upper_ref, other_ref, stats_ref, meta_ref, ordered_ref, lower_ref, sems):
    width, cols = own_ref.shape
    staged = upper_ref.shape[0]
    depth = lower_ref.shape[0] // sems.shape[0]
    copies = [
        pltpu.make_async_copy(
            other_ref.at[pl.ds(staged + i * depth, depth)], lower_ref.at[pl.ds(i * depth, depth)], sems.at[i]
        )
        for i in range(sems.shape[0])
    ]
    for copy in copies:
        copy.start()
    groups = rows_ref.shape[0]
    parts = SUBS // MINE
    span = width // parts
    share = groups * MINE
    tp, tp_count = lax.axis_index("tp"), lax.axis_size("tp")
    half = tp % PAIR
    place = lax.axis_index("req") * tp_count + tp
    count = groups * SUBS
    into, out_of = iota((count, count), 0), iota((count, count), 1)
    wanted = into % share // MINE * SUBS + into // share * MINE + into % MINE
    order = jnp.where(out_of == wanted, 1.0, 0.0).astype(jnp.bfloat16)
    rows = rows_ref[:, :, :span].reshape(count, span)
    ordered = jnp.dot(order, rows, preferred_element_type=jnp.float32).astype(jnp.bfloat16)
    for k in range(parts):
        ordered_ref[:, k * span : (k + 1) * span] = ordered[k * share : (k + 1) * share]
    meta = rows_ref[0, :, span:].astype(jnp.float32)
    for q in range(1, groups):
        meta = meta + rows_ref[q, :, span:].astype(jnp.float32)
    meta_ref[...] = meta
    own_logits = jnp.dot(ordered_ref[...], own_ref[...], preferred_element_type=jnp.float32)
    other_logits = jnp.dot(ordered_ref[:, :staged], upper_ref[...], preferred_element_type=jnp.float32)
    for copy in copies:
        copy.wait()
    other_logits += jnp.dot(ordered_ref[:, staged:], lower_ref[...], preferred_element_type=jnp.float32)
    logits = jnp.concatenate([own_logits, other_logits], axis=1)
    lanes = max(share, LANES)
    sub, lane = iota((share, lanes), 0), iota((share, lanes), 1)
    ids = meta[0:1, :lanes] + 256.0 * meta[1:2, :lanes] + 65536.0 * meta[2:3, :lanes]
    ids = jnp.sum(jnp.where(lane == sub, ids, 0.0), axis=1, keepdims=True).astype(jnp.int32)
    row_top = jnp.max(logits, axis=1, keepdims=True)
    scaled = jnp.exp(logits - row_top)
    row_total = jnp.sum(scaled, axis=1, keepdims=True)
    row_weighted = jnp.sum(scaled * logits, axis=1, keepdims=True)
    column = iota(logits.shape, 1)
    other = place + 1 - 2 * half
    columns = jnp.where(column < cols, place * cols, (other - 1) * cols) + column
    picked = jnp.sum(jnp.where(columns == ids, logits, 0.0), axis=1, keepdims=True)
    stats = (row_top, row_total, row_weighted, picked)
    if PAIR * share * STATS == LANES:
        joined = picked
        for at in range(STATS - 1):
            joined = jnp.where(lane // (PAIR * share) == at, stats[at], joined)
        joined = jnp.sum(jnp.where(lane % share == sub, joined, 0.0), axis=0, keepdims=True)
        lane = iota((1, LANES), 1)
        neutral = jnp.where(lane < PAIR * share, -jnp.inf, 0.0)
        stats_ref[...] = jnp.where(lane // share % PAIR == half, joined, neutral)
    else:
        for at in range(STATS):
            line = jnp.sum(jnp.where(lane == sub, stats[at], 0.0), axis=0, keepdims=True)
            for h in range(PAIR):
                first = (at * PAIR + h) * share
                stats_ref[:, first : first + share] = jnp.where(half == h, line, 0.0 if at else -jnp.inf)


def finish_kernel(share, stats_ref, meta_ref, logprob_ref, entropy_ref, seq_ref):
    row_count = logprob_ref.shape[0]
    used = PAIR * share
    lanes = max(used, LANES)

    def stat(at):
        if used >= LANES:
            return stats_ref[:, at * used : (at + 1) * used]
        return stats_ref[...] if at == 0 else pltpu.roll(stats_ref[...], LANES - at * used, 1)

    tops = stat(0)
    row_top = jnp.max(tops, axis=0, keepdims=True)
    weight = jnp.exp(tops - row_top)
    row_total = jnp.sum(stat(1) * weight, axis=0, keepdims=True)
    row_weighted = jnp.sum(stat(2) * weight, axis=0, keepdims=True)
    picked = jnp.sum(stat(3), axis=0, keepdims=True)
    log_norm = row_top + jnp.log(row_total)
    lane, sub = iota((1, lanes), 1), iota((SUBS, lanes), 0)
    in_use = jnp.logical_and(meta_ref[4:5, :] > 0.5, lane < used)
    logprob = jnp.where(in_use, picked - log_norm, 0.0)
    entropy = jnp.where(in_use, log_norm - row_weighted / row_total, 0.0)
    segment, place = meta_ref[3:4, :].astype(jnp.int32), meta_ref[5:6, :].astype(jnp.int32)
    mine = jnp.logical_and(place == sub, lane % share // MINE == own_slot(share // MINE))

    def placed(values, wanted):
        sums = jnp.sum(jnp.where(wanted, values, 0.0), axis=1, keepdims=True)
        diagonal = iota((SUBS, LANES), 0) == iota((SUBS, LANES), 1)
        return jnp.sum(jnp.where(diagonal, sums, 0.0), axis=0)

    logprob_ref[...] = placed(logprob, mine)[:row_count]
    entropy_ref[...] = placed(entropy, mine)[:row_count]
    seq_ref[...] = placed(logprob, segment == sub)[:SEQS]


def grant(mebibytes):
    return pltpu.CompilerParams(vmem_limit_bytes=mebibytes * 1024 * 1024)


def local(hidden, norm_gain, lm_head, targets, segments, scored):
    row_count, width = hidden.shape
    groups, tp_count = lax.axis_size("req"), lax.axis_size("tp")
    span = width * MINE // SUBS
    share = groups * MINE
    lanes = max(PAIR * share, LANES)

    def spec(space):
        return pl.BlockSpec(memory_space=space)

    swap = [(i, i + 1 - 2 * (i % PAIR)) for i in range(tp_count)]
    other = lax.ppermute(lm_head, "tp", swap)
    packed = pl.pallas_call(
        functools.partial(pack_kernel, share),
        out_shape=VMEM((groups, SUBS, span + lanes), jnp.bfloat16),
        in_specs=[spec(VMEM)] * 2 + [spec(SMEM)] * 3,
        out_specs=spec(VMEM),
        scratch_shapes=[
            VMEM((row_count, width), jnp.float32),
            VMEM((SUBS, span), jnp.float32),
            VMEM((width // LANES, LANES), jnp.float32),
        ],
    )(hidden, norm_gain.reshape(width // LANES, LANES), targets, segments, scored)
    rows = lax.all_to_all(packed, "req", 0, 0, axis_index_groups=[members(groups)])
    other = pltpu.with_memory_space_constraint(other, pltpu.HBM)
    staged = width // 2
    slices = pl.pallas_call(
        stage_kernel,
        out_shape=(VMEM(lm_head.shape, lm_head.dtype), VMEM((staged, lm_head.shape[1]), lm_head.dtype)),
        in_specs=[spec(pltpu.HBM)] * 2,
        out_specs=(spec(VMEM),) * 2,
        scratch_shapes=[pltpu.SemaphoreType.DMA((2, 4))],
        compiler_params=grant(4),
        cost_estimate=pl.CostEstimate(flops=0, bytes_accessed=3 * 2 * lm_head.size, transcendentals=0),
    )(pltpu.with_memory_space_constraint(lm_head, pltpu.HBM), other)
    stats, meta = pl.pallas_call(
        score_kernel,
        out_shape=(
            jax.ShapeDtypeStruct((1, STATS * PAIR * share), jnp.float32),
            VMEM((SUBS, lanes), jnp.float32),
        ),
        in_specs=[spec(VMEM)] * 3 + [spec(pltpu.HBM)],
        out_specs=(spec(VMEM), spec(VMEM)),
        scratch_shapes=[
            VMEM((share, width), jnp.bfloat16),
            VMEM((width - staged, lm_head.shape[1]), jnp.bfloat16),
            pltpu.SemaphoreType.DMA((4,)),
        ],
        compiler_params=grant(24),
    )(rows, *(pltpu.with_memory_space_constraint(part, VMEM) for part in slices), other)
    swapped = lax.ppermute(stats, "tp", swap)
    stats = jnp.where(iota(stats.shape, 1) < PAIR * share, jnp.maximum(stats, swapped), stats + swapped)
    chips = groups * tp_count // PAIR
    copies = jnp.broadcast_to(stats[None], (chips,) + stats.shape)
    listed = [[q * tp_count + t for q in members(groups) for t in range(at, tp_count, PAIR)] for at in range(PAIR)]
    gathered = lax.all_to_all(copies, ("req", "tp"), 0, 0, axis_index_groups=listed).reshape(chips, stats.shape[1])
    return pl.pallas_call(
        functools.partial(finish_kernel, share),
        out_shape=(
            jax.ShapeDtypeStruct((row_count,), jnp.float32),
            jax.ShapeDtypeStruct((row_count,), jnp.float32),
            jax.ShapeDtypeStruct((SEQS,), jnp.float32),
        ),
        in_specs=[spec(VMEM), spec(VMEM)],
        out_specs=(spec(VMEM), spec(VMEM), spec(VMEM)),
    )(pltpu.with_memory_space_constraint(gathered, VMEM), pltpu.with_memory_space_constraint(meta, VMEM))


def solution(mesh):
    return jax.shard_map(
        local,
        mesh=mesh,
        in_specs=(P("req", None), P(), P(None, ("req", "tp")), P("req"), P("req"), P("req")),
        out_specs=(P("req"), P("req"), P()),
        check_vma=False,
    )
```

```python
import functools

import jax
import jax.numpy as jnp
from jax import lax
from jax.experimental import pallas as pl
from jax.experimental.pallas import tpu as pltpu
from jax.sharding import PartitionSpec as P

SEQS = 4
PICK = 4
PAIR = 2
MINE = PICK // PAIR
SUBS = 8
LANES = 128
STATS = 4

VMEM = pltpu.VMEM
SMEM = pltpu.SMEM


def ranks_of(scored_ref, row_count):
    ranks, so_far = [], jnp.int32(0)
    for row in range(row_count):
        ranks.append(so_far)
        so_far = so_far + scored_ref[row]
    return ranks, so_far


def iota(shape, axis):
    return lax.broadcasted_iota(jnp.int32, shape, axis)


def members(count):
    ring = [*range(0, count, 2), *reversed(range(1, count, 2))]
    return ring[5 * count // 8 :] + ring[: 5 * count // 8]


def own_slot(count):
    own = lax.axis_index("req")
    at = jnp.where(own % 2 == 0, own // 2, count - 1 - own // 2) - 5 * count // 8
    return jnp.where(at < 0, at + count, at)


def pack_kernel(share, hidden_ref, gain_ref, targets_ref, segments_ref, scored_ref, out_ref, wide_ref, parts_ref, gains_ref):
    row_count, width = hidden_ref.shape
    parts = SUBS // MINE
    span = width // parts
    own, half = own_slot(out_ref.shape[0]), lax.axis_index("tp") % PAIR
    wide_ref[...] = hidden_ref[...].astype(jnp.float32)
    gains_ref[...] = gain_ref[...].astype(jnp.float32)
    ranks, count = ranks_of(scored_ref, row_count)
    source = [jnp.int32(0)] * PICK
    for row in range(row_count):
        for r in range(PICK):
            hit = jnp.logical_and(scored_ref[row] == 1, ranks[row] == r)
            source[r] = jnp.where(hit, row, source[r])
    mine = [source[i] for i in range(MINE)]
    for h in range(1, PAIR):
        mine = [jnp.where(half == h, source[h * MINE + i], mine[i]) for i in range(MINE)]
    for i in range(MINE):
        for k in range(parts):
            parts_ref[k * MINE + i : k * MINE + i + 1, :] = wide_ref[pl.ds(mine[i], 1), k * span : (k + 1) * span]
    values = parts_ref[...]
    part = jnp.broadcast_to(jnp.sum(values * values, axis=1, keepdims=True), (SUBS, LANES))
    total = part
    for k in range(1, parts):
        total = total + pltpu.roll(part, k * MINE, 0)
    row_scale = lax.rsqrt(total / width + 1e-05)
    sub, lane = iota((SUBS, LANES), 0), iota((SUBS, LANES), 1)
    chunks = span // LANES
    for at in range(chunks):
        gain = gains_ref[at : at + 1, :]
        for k in range(1, parts):
            gain = jnp.where(sub >= k * MINE, gains_ref[k * chunks + at : k * chunks + at + 1, :], gain)
        piece = parts_ref[:, at * LANES : (at + 1) * LANES]
        piece = (piece * row_scale * gain).astype(jnp.bfloat16)
        for to in range(out_ref.shape[0]):
            out_ref[to, :, at * LANES : (at + 1) * LANES] = piece
    width_side = out_ref.shape[2] - span
    sub, lane = iota((SUBS, width_side), 0), iota((SUBS, width_side), 1)
    at_row, at_half = lane % share - own * MINE, lane // share
    side = jnp.zeros((SUBS, width_side), jnp.int32)
    for i in range(MINE):
        target = targets_ref[mine[i]]
        digits = jnp.where(sub == 0, target & 255, jnp.where(sub == 1, (target >> 8) & 255, target >> 16))
        fields = jnp.zeros((SUBS, width_side), jnp.int32)
        for h in range(PAIR):
            r = h * MINE + i
            field = jnp.where(sub == 4, (count > r).astype(jnp.int32), source[r])
            fields = jnp.where(at_half == h, jnp.where(sub == 3, segments_ref[source[r]], field), fields)
        side = jnp.where(at_row == i, jnp.where(sub < 3, digits, fields), side)
    side = side.astype(jnp.float32).astype(jnp.bfloat16)
    for to in range(out_ref.shape[0]):
        out_ref[to, :, span:] = side


def stage_kernel(own_ref, other_ref, own_out, other_out, sems):
    copies = []
    for at, (source, out) in enumerate(((own_ref, own_out), (other_ref, other_out))):
        depth = out.shape[0] // sems.shape[1]
        for i in range(sems.shape[1]):
            piece = pl.ds(i * depth, depth)
            copies.append(pltpu.make_async_copy(source.at[piece], out.at[piece], sems.at[at, i]))
    for copy in copies:
        copy.start()
    for copy in copies:
        copy.wait()


def score_kernel(rows_ref, own_ref, upper_ref, other_ref, stats_ref, meta_ref, ordered_ref, lower_ref, sems):
    width, cols = own_ref.shape
    staged = upper_ref.shape[0]
    depth = lower_ref.shape[0] // sems.shape[0]
    copies = [
        pltpu.make_async_copy(
            other_ref.at[pl.ds(staged + i * depth, depth)], lower_ref.at[pl.ds(i * depth, depth)], sems.at[i]
        )
        for i in range(sems.shape[0])
    ]
    for copy in copies:
        copy.start()
    groups = rows_ref.shape[0]
    parts = SUBS // MINE
    span = width // parts
    share = groups * MINE
    tp, tp_count = lax.axis_index("tp"), lax.axis_size("tp")
    half = tp % PAIR
    place = lax.axis_index("req") * tp_count + tp
    count = groups * SUBS
    into, out_of = iota((count, count), 0), iota((count, count), 1)
    wanted = into % share // MINE * SUBS + into // share * MINE + into % MINE
    order = jnp.where(out_of == wanted, 1.0, 0.0).astype(jnp.bfloat16)
    rows = rows_ref[:, :, :span].reshape(count, span)
    ordered = jnp.dot(order, rows, preferred_element_type=jnp.float32).astype(jnp.bfloat16)
    for k in range(parts):
        ordered_ref[:, k * span : (k + 1) * span] = ordered[k * share : (k + 1) * share]
    meta = rows_ref[0, :, span:].astype(jnp.float32)
    for q in range(1, groups):
        meta = meta + rows_ref[q, :, span:].astype(jnp.float32)
    meta_ref[...] = meta
    own_logits = jnp.dot(ordered_ref[...], own_ref[...], preferred_element_type=jnp.float32)
    other_logits = jnp.dot(ordered_ref[:, :staged], upper_ref[...], preferred_element_type=jnp.float32)
    for copy in copies:
        copy.wait()
    other_logits += jnp.dot(ordered_ref[:, staged:], lower_ref[...], preferred_element_type=jnp.float32)
    logits = jnp.concatenate([own_logits, other_logits], axis=1)
    lanes = max(share, LANES)
    sub, lane = iota((share, lanes), 0), iota((share, lanes), 1)
    ids = meta[0:1, :lanes] + 256.0 * meta[1:2, :lanes] + 65536.0 * meta[2:3, :lanes]
    ids = jnp.sum(jnp.where(lane == sub, ids, 0.0), axis=1, keepdims=True).astype(jnp.int32)
    row_top = jnp.max(logits, axis=1, keepdims=True)
    scaled = jnp.exp(logits - row_top)
    row_total = jnp.sum(scaled, axis=1, keepdims=True)
    row_weighted = jnp.sum(scaled * logits, axis=1, keepdims=True)
    column = iota(logits.shape, 1)
    other = place + 1 - 2 * half
    columns = jnp.where(column < cols, place * cols, (other - 1) * cols) + column
    picked = jnp.sum(jnp.where(columns == ids, logits, 0.0), axis=1, keepdims=True)
    stats = (row_top, row_total, row_weighted, picked)
    if PAIR * share * STATS == LANES:
        joined = picked
        for at in range(STATS - 1):
            joined = jnp.where(lane // (PAIR * share) == at, stats[at], joined)
        joined = jnp.sum(jnp.where(lane % share == sub, joined, 0.0), axis=0, keepdims=True)
        lane = iota((1, LANES), 1)
        neutral = jnp.where(lane < PAIR * share, -jnp.inf, 0.0)
        stats_ref[...] = jnp.where(lane // share % PAIR == half, joined, neutral)
    else:
        for at in range(STATS):
            line = jnp.sum(jnp.where(lane == sub, stats[at], 0.0), axis=0, keepdims=True)
            for h in range(PAIR):
                first = (at * PAIR + h) * share
                stats_ref[:, first : first + share] = jnp.where(half == h, line, 0.0 if at else -jnp.inf)


def finish_kernel(share, stats_ref, meta_ref, logprob_ref, entropy_ref, seq_ref):
    row_count = logprob_ref.shape[0]
    used = PAIR * share
    lanes = max(used, LANES)

    def stat(at):
        if used >= LANES:
            return stats_ref[:, at * used : (at + 1) * used]
        return stats_ref[...] if at == 0 else pltpu.roll(stats_ref[...], LANES - at * used, 1)

    tops = stat(0)
    row_top = jnp.max(tops, axis=0, keepdims=True)
    weight = jnp.exp(tops - row_top)
    row_total = jnp.sum(stat(1) * weight, axis=0, keepdims=True)
    row_weighted = jnp.sum(stat(2) * weight, axis=0, keepdims=True)
    picked = jnp.sum(stat(3), axis=0, keepdims=True)
    log_norm = row_top + jnp.log(row_total)
    lane, sub = iota((1, lanes), 1), iota((SUBS, lanes), 0)
    in_use = jnp.logical_and(meta_ref[4:5, :] > 0.5, lane < used)
    logprob = jnp.where(in_use, picked - log_norm, 0.0)
    entropy = jnp.where(in_use, log_norm - row_weighted / row_total, 0.0)
    segment, place = meta_ref[3:4, :].astype(jnp.int32), meta_ref[5:6, :].astype(jnp.int32)
    mine = jnp.logical_and(place == sub, lane % share // MINE == own_slot(share // MINE))

    def placed(values, wanted):
        sums = jnp.sum(jnp.where(wanted, values, 0.0), axis=1, keepdims=True)
        diagonal = iota((SUBS, LANES), 0) == iota((SUBS, LANES), 1)
        return jnp.sum(jnp.where(diagonal, sums, 0.0), axis=0)

    logprob_ref[...] = placed(logprob, mine)[:row_count]
    entropy_ref[...] = placed(entropy, mine)[:row_count]
    seq_ref[...] = placed(logprob, segment == sub)[:SEQS]


def grant(mebibytes):
    return pltpu.CompilerParams(vmem_limit_bytes=mebibytes * 1024 * 1024)


def local(hidden, norm_gain, lm_head, targets, segments, scored):
    row_count, width = hidden.shape
    groups, tp_count = lax.axis_size("req"), lax.axis_size("tp")
    span = width * MINE // SUBS
    share = groups * MINE
    lanes = max(PAIR * share, LANES)

    def spec(space):
        return pl.BlockSpec(memory_space=space)

    other = lax.ppermute(lm_head, "tp", [(i, i + 1 - 2 * (i % PAIR)) for i in range(tp_count)])
    packed = pl.pallas_call(
        functools.partial(pack_kernel, share),
        out_shape=VMEM((groups, SUBS, span + lanes), jnp.bfloat16),
        in_specs=[spec(VMEM)] * 2 + [spec(SMEM)] * 3,
        out_specs=spec(VMEM),
        scratch_shapes=[
            VMEM((row_count, width), jnp.float32),
            VMEM((SUBS, span), jnp.float32),
            VMEM((width // LANES, LANES), jnp.float32),
        ],
    )(hidden, norm_gain.reshape(width // LANES, LANES), targets, segments, scored)
    rows = lax.all_to_all(packed, "req", 0, 0, axis_index_groups=[members(groups)])
    other = pltpu.with_memory_space_constraint(other, pltpu.HBM)
    staged = width // 2
    slices = pl.pallas_call(
        stage_kernel,
        out_shape=(VMEM(lm_head.shape, lm_head.dtype), VMEM((staged, lm_head.shape[1]), lm_head.dtype)),
        in_specs=[spec(pltpu.HBM)] * 2,
        out_specs=(spec(VMEM),) * 2,
        scratch_shapes=[pltpu.SemaphoreType.DMA((2, 4))],
        compiler_params=grant(4),
        cost_estimate=pl.CostEstimate(flops=0, bytes_accessed=3 * 2 * lm_head.size, transcendentals=0),
    )(pltpu.with_memory_space_constraint(lm_head, pltpu.HBM), other)
    stats, meta = pl.pallas_call(
        score_kernel,
        out_shape=(
            jax.ShapeDtypeStruct((1, STATS * PAIR * share), jnp.float32),
            VMEM((SUBS, lanes), jnp.float32),
        ),
        in_specs=[spec(VMEM)] * 3 + [spec(pltpu.HBM)],
        out_specs=(spec(VMEM), spec(VMEM)),
        scratch_shapes=[
            VMEM((share, width), jnp.bfloat16),
            VMEM((width - staged, lm_head.shape[1]), jnp.bfloat16),
            pltpu.SemaphoreType.DMA((4,)),
        ],
        compiler_params=grant(24),
    )(rows, *(pltpu.with_memory_space_constraint(part, VMEM) for part in slices), other)
    copies = jnp.broadcast_to(stats[None], (groups * tp_count,) + stats.shape)
    gathered = lax.all_to_all(copies, ("req", "tp"), 0, 0)
    gathered = gathered.reshape(groups * tp_count, stats.shape[1])
    return pl.pallas_call(
        functools.partial(finish_kernel, share),
        out_shape=(
            jax.ShapeDtypeStruct((row_count,), jnp.float32),
            jax.ShapeDtypeStruct((row_count,), jnp.float32),
            jax.ShapeDtypeStruct((SEQS,), jnp.float32),
        ),
        in_specs=[spec(VMEM), spec(VMEM)],
        out_specs=(spec(VMEM), spec(VMEM), spec(VMEM)),
    )(pltpu.with_memory_space_constraint(gathered, VMEM), pltpu.with_memory_space_constraint(meta, VMEM))


def solution(mesh):
    return jax.shard_map(
        local,
        mesh=mesh,
        in_specs=(P("req", None), P(), P(None, ("req", "tp")), P("req"), P("req"), P("req")),
        out_specs=(P("req"), P("req"), P()),
        check_vma=False,
    )
```

```python
import functools

import jax
import jax.numpy as jnp
from jax import lax
from jax.experimental import pallas as pl
from jax.experimental.pallas import tpu as pltpu
from jax.sharding import PartitionSpec as P

SEQS = 4
PICK = 4
PAIR = 2
MINE = PICK // PAIR
SUBS = 8
LANES = 128
STATS = 4

VMEM = pltpu.VMEM
SMEM = pltpu.SMEM


def ranks_of(scored_ref, row_count):
    ranks, so_far = [], jnp.int32(0)
    for row in range(row_count):
        ranks.append(so_far)
        so_far = so_far + scored_ref[row]
    return ranks, so_far


def iota(shape, axis):
    return lax.broadcasted_iota(jnp.int32, shape, axis)


def members(count, half):
    quarter = count // 4
    middle = range(quarter, count - quarter)
    return [*(middle if half else reversed(middle)), *range(quarter), *range(count - quarter, count)]


def own_slot(count, half):
    own, quarter = lax.axis_index("req"), count // 4
    middle = jnp.where(half == 1, own - quarter, count - quarter - 1 - own)
    return jnp.where(own < quarter, own + count - 2 * quarter, jnp.where(own < count - quarter, middle, own))


def pack_kernel(share, hidden_ref, gain_ref, targets_ref, segments_ref, scored_ref, out_ref, wide_ref, parts_ref, gains_ref):
    row_count, width = hidden_ref.shape
    parts = SUBS // MINE
    span = width // parts
    half = lax.axis_index("tp") % PAIR
    wide_ref[...] = hidden_ref[...].astype(jnp.float32)
    gains_ref[...] = gain_ref[...].astype(jnp.float32)
    ranks, count = ranks_of(scored_ref, row_count)
    source = [jnp.int32(0)] * PICK
    for row in range(row_count):
        for r in range(PICK):
            hit = jnp.logical_and(scored_ref[row] == 1, ranks[row] == r)
            source[r] = jnp.where(hit, row, source[r])
    mine = [source[i] for i in range(MINE)]
    for h in range(1, PAIR):
        mine = [jnp.where(half == h, source[h * MINE + i], mine[i]) for i in range(MINE)]
    for i in range(MINE):
        for k in range(parts):
            parts_ref[k * MINE + i : k * MINE + i + 1, :] = wide_ref[pl.ds(mine[i], 1), k * span : (k + 1) * span]
    values = parts_ref[...]
    part = jnp.broadcast_to(jnp.sum(values * values, axis=1, keepdims=True), (SUBS, LANES))
    total = part
    for k in range(1, parts):
        total = total + pltpu.roll(part, k * MINE, 0)
    row_scale = lax.rsqrt(total / width + 1e-05)
    sub, lane = iota((SUBS, LANES), 0), iota((SUBS, LANES), 1)
    chunks = span // LANES
    for at in range(chunks):
        gain = gains_ref[at : at + 1, :]
        for k in range(1, parts):
            gain = jnp.where(sub >= k * MINE, gains_ref[k * chunks + at : k * chunks + at + 1, :], gain)
        piece = parts_ref[:, at * LANES : (at + 1) * LANES]
        piece = (piece * row_scale * gain).astype(jnp.bfloat16)
        for to in range(out_ref.shape[0]):
            out_ref[to, :, at * LANES : (at + 1) * LANES] = piece
    width_side = out_ref.shape[2] - span
    sub, lane = iota((SUBS, width_side), 0), iota((SUBS, width_side), 1)
    count_to, at_half = out_ref.shape[0], lane // share
    at_mine = lane % share - own_slot(count_to, half) * MINE
    at_row = lane % share - jnp.where(at_half == 1, own_slot(count_to, 1), own_slot(count_to, 0)) * MINE
    side = jnp.zeros((SUBS, width_side), jnp.int32)
    for i in range(MINE):
        target = targets_ref[mine[i]]
        digits = jnp.where(sub == 0, target & 255, jnp.where(sub == 1, (target >> 8) & 255, target >> 16))
        fields = jnp.zeros((SUBS, width_side), jnp.int32)
        for h in range(PAIR):
            r = h * MINE + i
            field = jnp.where(sub == 4, (count > r).astype(jnp.int32), source[r])
            fields = jnp.where(at_half == h, jnp.where(sub == 3, segments_ref[source[r]], field), fields)
        side = jnp.where(jnp.logical_and(sub < 3, at_mine == i), digits, side)
        side = jnp.where(jnp.logical_and(sub >= 3, at_row == i), fields, side)
    side = side.astype(jnp.float32).astype(jnp.bfloat16)
    for to in range(out_ref.shape[0]):
        out_ref[to, :, span:] = side


def stage_kernel(own_ref, other_ref, own_out, other_out, sems):
    copies = []
    for at, (source, out) in enumerate(((own_ref, own_out), (other_ref, other_out))):
        depth = out.shape[0] // sems.shape[1]
        for i in range(sems.shape[1]):
            piece = pl.ds(i * depth, depth)
            copies.append(pltpu.make_async_copy(source.at[piece], out.at[piece], sems.at[at, i]))
    for copy in copies:
        copy.start()
    for copy in copies:
        copy.wait()


def score_kernel(rows_ref, own_ref, upper_ref, other_ref, stats_ref, meta_ref, ordered_ref, lower_ref, sems):
    width, cols = own_ref.shape
    staged = upper_ref.shape[0]
    depth = lower_ref.shape[0] // sems.shape[0]
    copies = [
        pltpu.make_async_copy(
            other_ref.at[pl.ds(staged + i * depth, depth)], lower_ref.at[pl.ds(i * depth, depth)], sems.at[i]
        )
        for i in range(sems.shape[0])
    ]
    for copy in copies:
        copy.start()
    groups = rows_ref.shape[0]
    parts = SUBS // MINE
    span = width // parts
    share = groups * MINE
    tp, tp_count = lax.axis_index("tp"), lax.axis_size("tp")
    half = tp % PAIR
    place = lax.axis_index("req") * tp_count + tp
    count = groups * SUBS
    into, out_of = iota((count, count), 0), iota((count, count), 1)
    wanted = into % share // MINE * SUBS + into // share * MINE + into % MINE
    order = jnp.where(out_of == wanted, 1.0, 0.0).astype(jnp.bfloat16)
    rows = rows_ref[:, :, :span].reshape(count, span)
    ordered = jnp.dot(order, rows, preferred_element_type=jnp.float32).astype(jnp.bfloat16)
    for k in range(parts):
        ordered_ref[:, k * span : (k + 1) * span] = ordered[k * share : (k + 1) * share]
    meta = rows_ref[0, :, span:].astype(jnp.float32)
    for q in range(1, groups):
        meta = meta + rows_ref[q, :, span:].astype(jnp.float32)
    meta_ref[...] = meta
    own_logits = jnp.dot(ordered_ref[...], own_ref[...], preferred_element_type=jnp.float32)
    other_logits = jnp.dot(ordered_ref[:, :staged], upper_ref[...], preferred_element_type=jnp.float32)
    for copy in copies:
        copy.wait()
    other_logits += jnp.dot(ordered_ref[:, staged:], lower_ref[...], preferred_element_type=jnp.float32)
    logits = jnp.concatenate([own_logits, other_logits], axis=1)
    lanes = max(share, LANES)
    sub, lane = iota((share, lanes), 0), iota((share, lanes), 1)
    ids = meta[0:1, :lanes] + 256.0 * meta[1:2, :lanes] + 65536.0 * meta[2:3, :lanes]
    ids = jnp.sum(jnp.where(lane == sub, ids, 0.0), axis=1, keepdims=True).astype(jnp.int32)
    row_top = jnp.max(logits, axis=1, keepdims=True)
    scaled = jnp.exp(logits - row_top)
    row_total = jnp.sum(scaled, axis=1, keepdims=True)
    row_weighted = jnp.sum(scaled * logits, axis=1, keepdims=True)
    column = iota(logits.shape, 1)
    other = place + 1 - 2 * half
    columns = jnp.where(column < cols, place * cols, (other - 1) * cols) + column
    picked = jnp.sum(jnp.where(columns == ids, logits, 0.0), axis=1, keepdims=True)
    stats = (row_top, row_total, row_weighted, picked)
    if PAIR * share * STATS == LANES:
        joined = picked
        for at in range(STATS - 1):
            joined = jnp.where(lane // (PAIR * share) == at, stats[at], joined)
        joined = jnp.sum(jnp.where(lane % share == sub, joined, 0.0), axis=0, keepdims=True)
        lane = iota((1, LANES), 1)
        neutral = jnp.where(lane < PAIR * share, -jnp.inf, 0.0)
        stats_ref[...] = jnp.where(lane // share % PAIR == half, joined, neutral)
    else:
        for at in range(STATS):
            line = jnp.sum(jnp.where(lane == sub, stats[at], 0.0), axis=0, keepdims=True)
            for h in range(PAIR):
                first = (at * PAIR + h) * share
                stats_ref[:, first : first + share] = jnp.where(half == h, line, 0.0 if at else -jnp.inf)


def finish_kernel(share, stats_ref, meta_ref, logprob_ref, entropy_ref, seq_ref):
    row_count = logprob_ref.shape[0]
    used = PAIR * share
    lanes = max(used, LANES)

    def stat(at):
        if used >= LANES:
            return stats_ref[:, at * used : (at + 1) * used]
        return stats_ref[...] if at == 0 else pltpu.roll(stats_ref[...], LANES - at * used, 1)

    tops = stat(0)
    row_top = jnp.max(tops, axis=0, keepdims=True)
    weight = jnp.exp(tops - row_top)
    row_total = jnp.sum(stat(1) * weight, axis=0, keepdims=True)
    row_weighted = jnp.sum(stat(2) * weight, axis=0, keepdims=True)
    picked = jnp.sum(stat(3), axis=0, keepdims=True)
    log_norm = row_top + jnp.log(row_total)
    lane, sub = iota((1, lanes), 1), iota((SUBS, lanes), 0)
    in_use = jnp.logical_and(meta_ref[4:5, :] > 0.5, lane < used)
    logprob = jnp.where(in_use, picked - log_norm, 0.0)
    entropy = jnp.where(in_use, log_norm - row_weighted / row_total, 0.0)
    segment, place = meta_ref[3:4, :].astype(jnp.int32), meta_ref[5:6, :].astype(jnp.int32)
    slot = jnp.where(lane // share == 1, own_slot(share // MINE, 1), own_slot(share // MINE, 0))
    mine = jnp.logical_and(place == sub, lane % share // MINE == slot)

    def placed(values, wanted):
        sums = jnp.sum(jnp.where(wanted, values, 0.0), axis=1, keepdims=True)
        diagonal = iota((SUBS, LANES), 0) == iota((SUBS, LANES), 1)
        return jnp.sum(jnp.where(diagonal, sums, 0.0), axis=0)

    logprob_ref[...] = placed(logprob, mine)[:row_count]
    entropy_ref[...] = placed(entropy, mine)[:row_count]
    seq_ref[...] = placed(logprob, segment == sub)[:SEQS]


def grant(mebibytes):
    return pltpu.CompilerParams(vmem_limit_bytes=mebibytes * 1024 * 1024)


def local(hidden, norm_gain, lm_head, targets, segments, scored):
    row_count, width = hidden.shape
    groups, tp_count = lax.axis_size("req"), lax.axis_size("tp")
    span = width * MINE // SUBS
    share = groups * MINE
    lanes = max(PAIR * share, LANES)

    def spec(space):
        return pl.BlockSpec(memory_space=space)

    other = lax.ppermute(lm_head, "tp", [(i, i + 1 - 2 * (i % PAIR)) for i in range(tp_count)])
    packed = pl.pallas_call(
        functools.partial(pack_kernel, share),
        out_shape=VMEM((groups, SUBS, span + lanes), jnp.bfloat16),
        in_specs=[spec(VMEM)] * 2 + [spec(SMEM)] * 3,
        out_specs=spec(VMEM),
        scratch_shapes=[
            VMEM((row_count, width), jnp.float32),
            VMEM((SUBS, span), jnp.float32),
            VMEM((width // LANES, LANES), jnp.float32),
        ],
    )(hidden, norm_gain.reshape(width // LANES, LANES), targets, segments, scored)
    listed = [[q * tp_count + t for q in members(groups, t % PAIR)] for t in range(tp_count)]
    rows = lax.all_to_all(packed, ("req", "tp"), 0, 0, axis_index_groups=listed)
    other = pltpu.with_memory_space_constraint(other, pltpu.HBM)
    staged = width // 2
    slices = pl.pallas_call(
        stage_kernel,
        out_shape=(VMEM(lm_head.shape, lm_head.dtype), VMEM((staged, lm_head.shape[1]), lm_head.dtype)),
        in_specs=[spec(pltpu.HBM)] * 2,
        out_specs=(spec(VMEM),) * 2,
        scratch_shapes=[pltpu.SemaphoreType.DMA((2, 4))],
        compiler_params=grant(4),
        cost_estimate=pl.CostEstimate(flops=0, bytes_accessed=3 * 2 * lm_head.size, transcendentals=0),
    )(pltpu.with_memory_space_constraint(lm_head, pltpu.HBM), other)
    stats, meta = pl.pallas_call(
        score_kernel,
        out_shape=(
            jax.ShapeDtypeStruct((1, STATS * PAIR * share), jnp.float32),
            VMEM((SUBS, lanes), jnp.float32),
        ),
        in_specs=[spec(VMEM)] * 3 + [spec(pltpu.HBM)],
        out_specs=(spec(VMEM), spec(VMEM)),
        scratch_shapes=[
            VMEM((share, width), jnp.bfloat16),
            VMEM((width - staged, lm_head.shape[1]), jnp.bfloat16),
            pltpu.SemaphoreType.DMA((4,)),
        ],
        compiler_params=grant(24),
    )(rows, *(pltpu.with_memory_space_constraint(part, VMEM) for part in slices), other)
    copies = jnp.broadcast_to(stats[None], (groups * tp_count,) + stats.shape)
    gathered = lax.all_to_all(copies, ("req", "tp"), 0, 0)
    gathered = gathered.reshape(groups * tp_count, stats.shape[1])
    return pl.pallas_call(
        functools.partial(finish_kernel, share),
        out_shape=(
            jax.ShapeDtypeStruct((row_count,), jnp.float32),
            jax.ShapeDtypeStruct((row_count,), jnp.float32),
            jax.ShapeDtypeStruct((SEQS,), jnp.float32),
        ),
        in_specs=[spec(VMEM), spec(VMEM)],
        out_specs=(spec(VMEM), spec(VMEM), spec(VMEM)),
    )(pltpu.with_memory_space_constraint(gathered, VMEM), pltpu.with_memory_space_constraint(meta, VMEM))


def solution(mesh):
    return jax.shard_map(
        local,
        mesh=mesh,
        in_specs=(P("req", None), P(), P(None, ("req", "tp")), P("req"), P("req"), P("req")),
        out_specs=(P("req"), P("req"), P()),
        check_vma=False,
    )
```

```python
import functools

import jax
import jax.numpy as jnp
from jax import lax
from jax.experimental import pallas as pl
from jax.experimental.pallas import tpu as pltpu
from jax.sharding import PartitionSpec as P

SEQS = 4
PICK = 4
PAIR = 2
MINE = PICK // PAIR
SUBS = 8
LANES = 128
STATS = 4

VMEM = pltpu.VMEM
SMEM = pltpu.SMEM


def ranks_of(scored_ref, row_count):
    ranks, so_far = [], jnp.int32(0)
    for row in range(row_count):
        ranks.append(so_far)
        so_far = so_far + scored_ref[row]
    return ranks, so_far


def iota(shape, axis):
    return lax.broadcasted_iota(jnp.int32, shape, axis)


def members(count):
    quarter = count // 4
    return [*reversed(range(quarter, count - quarter)), *range(quarter), *range(count - quarter, count)]


def own_slot(count):
    own, quarter = lax.axis_index("req"), count // 4
    middle = count - quarter - 1 - own
    return jnp.where(own < quarter, own + count - 2 * quarter, jnp.where(own < count - quarter, middle, own))


def pack_kernel(share, hidden_hbm, gain_hbm, targets_hbm, segments_hbm, scored_hbm, out_ref, *scratch):
    hidden_ref, gain_ref, targets_ref, segments_ref, scored_ref, wide_ref, parts_ref, gains_ref, block_ref = scratch[:9]
    in_sems, out_sems = scratch[9:]
    reads = [
        pltpu.make_async_copy(source, to, in_sems.at[at])
        for at, (source, to) in enumerate(
            (
                (scored_hbm, scored_ref),
                (targets_hbm, targets_ref),
                (segments_hbm, segments_ref),
                (hidden_hbm, hidden_ref),
                (gain_hbm, gain_ref),
            )
        )
    ]
    for read in reads:
        read.start()
    row_count, width = hidden_ref.shape
    parts = SUBS // MINE
    span = width // parts
    own, half = own_slot(out_ref.shape[0]), lax.axis_index("tp") % PAIR
    for read in reads:
        read.wait()
    wide_ref[...] = hidden_ref[...].astype(jnp.float32)
    gains_ref[...] = gain_ref[...].astype(jnp.float32)
    ranks, count = ranks_of(scored_ref, row_count)
    source = [jnp.int32(0)] * PICK
    for row in range(row_count):
        for r in range(PICK):
            hit = jnp.logical_and(scored_ref[row] == 1, ranks[row] == r)
            source[r] = jnp.where(hit, row, source[r])
    mine = [source[i] for i in range(MINE)]
    for h in range(1, PAIR):
        mine = [jnp.where(half == h, source[h * MINE + i], mine[i]) for i in range(MINE)]
    for i in range(MINE):
        for k in range(parts):
            parts_ref[k * MINE + i : k * MINE + i + 1, :] = wide_ref[pl.ds(mine[i], 1), k * span : (k + 1) * span]
    values = parts_ref[...]
    part = jnp.broadcast_to(jnp.sum(values * values, axis=1, keepdims=True), (SUBS, LANES))
    total = part
    for k in range(1, parts):
        total = total + pltpu.roll(part, k * MINE, 0)
    row_scale = lax.rsqrt(total / width + 1e-05)
    sub, lane = iota((SUBS, LANES), 0), iota((SUBS, LANES), 1)
    chunks = span // LANES
    for at in range(chunks):
        gain = gains_ref[at : at + 1, :]
        for k in range(1, parts):
            gain = jnp.where(sub >= k * MINE, gains_ref[k * chunks + at : k * chunks + at + 1, :], gain)
        piece = parts_ref[:, at * LANES : (at + 1) * LANES]
        block_ref[:, at * LANES : (at + 1) * LANES] = (piece * row_scale * gain).astype(jnp.bfloat16)
    width_side = out_ref.shape[2] - span
    sub, lane = iota((SUBS, width_side), 0), iota((SUBS, width_side), 1)
    at_row, at_half = lane % share - own * MINE, lane // share
    side = jnp.zeros((SUBS, width_side), jnp.int32)
    for i in range(MINE):
        target = targets_ref[mine[i]]
        digits = jnp.where(sub == 0, target & 255, jnp.where(sub == 1, (target >> 8) & 255, target >> 16))
        fields = jnp.zeros((SUBS, width_side), jnp.int32)
        for h in range(PAIR):
            r = h * MINE + i
            field = jnp.where(sub == 4, (count > r).astype(jnp.int32), source[r])
            fields = jnp.where(at_half == h, jnp.where(sub == 3, segments_ref[source[r]], field), fields)
        side = jnp.where(at_row == i, jnp.where(sub < 3, digits, fields), side)
    block_ref[:, span:] = side.astype(jnp.float32).astype(jnp.bfloat16)
    writes = [pltpu.make_async_copy(block_ref, out_ref.at[to], out_sems.at[to]) for to in range(out_ref.shape[0])]
    for write in writes:
        write.start()
    for write in writes:
        write.wait()


def stage_kernel(share, own_ref, other_ref, own_out, other_out, order_out, sems):
    copies = []
    for at, (source, out) in enumerate(((own_ref, own_out), (other_ref, other_out))):
        depth = out.shape[0] // sems.shape[1]
        for i in range(sems.shape[1]):
            piece = pl.ds(i * depth, depth)
            copies.append(pltpu.make_async_copy(source.at[piece], out.at[piece], sems.at[at, i]))
    for copy in copies:
        copy.start()
    into, out_of = iota(order_out.shape, 0), iota(order_out.shape, 1)
    wanted = into % share // MINE * SUBS + into // share * MINE + into % MINE
    order_out[...] = jnp.where(out_of == wanted, 1.0, 0.0).astype(jnp.bfloat16)
    for copy in copies:
        copy.wait()


def score_kernel(rows_ref, own_ref, upper_ref, order_ref, other_ref, stats_ref, meta_ref, ordered_ref, lower_ref, sems):
    width, cols = own_ref.shape
    staged = upper_ref.shape[0]
    depth = lower_ref.shape[0] // sems.shape[0]
    copies = [
        pltpu.make_async_copy(
            other_ref.at[pl.ds(staged + i * depth, depth)], lower_ref.at[pl.ds(i * depth, depth)], sems.at[i]
        )
        for i in range(sems.shape[0])
    ]
    for copy in copies:
        copy.start()
    groups = rows_ref.shape[0]
    parts = SUBS // MINE
    span = width // parts
    share = groups * MINE
    tp, tp_count = lax.axis_index("tp"), lax.axis_size("tp")
    half = tp % PAIR
    place = lax.axis_index("req") * tp_count + tp
    count = groups * SUBS
    rows = rows_ref[:, :, :span].reshape(count, span)
    ordered = jnp.dot(order_ref[...], rows, preferred_element_type=jnp.float32).astype(jnp.bfloat16)
    for k in range(parts):
        ordered_ref[:, k * span : (k + 1) * span] = ordered[k * share : (k + 1) * share]
    meta = rows_ref[0, :, span:].astype(jnp.float32)
    for q in range(1, groups):
        meta = meta + rows_ref[q, :, span:].astype(jnp.float32)
    meta_ref[...] = meta
    own_logits = jnp.dot(ordered_ref[...], own_ref[...], preferred_element_type=jnp.float32)
    other_logits = jnp.dot(ordered_ref[:, :staged], upper_ref[...], preferred_element_type=jnp.float32)
    for copy in copies:
        copy.wait()
    other_logits += jnp.dot(ordered_ref[:, staged:], lower_ref[...], preferred_element_type=jnp.float32)
    logits = jnp.concatenate([own_logits, other_logits], axis=1)
    lanes = max(share, LANES)
    sub, lane = iota((share, lanes), 0), iota((share, lanes), 1)
    ids = meta[0:1, :lanes] + 256.0 * meta[1:2, :lanes] + 65536.0 * meta[2:3, :lanes]
    ids = jnp.sum(jnp.where(lane == sub, ids, 0.0), axis=1, keepdims=True).astype(jnp.int32)
    row_top = jnp.max(logits, axis=1, keepdims=True)
    scaled = jnp.exp(logits - row_top)
    row_total = jnp.sum(scaled, axis=1, keepdims=True)
    row_weighted = jnp.sum(scaled * logits, axis=1, keepdims=True)
    column = iota(logits.shape, 1)
    other = place + 1 - 2 * half
    columns = jnp.where(column < cols, place * cols, (other - 1) * cols) + column
    picked = jnp.sum(jnp.where(columns == ids, logits, 0.0), axis=1, keepdims=True)
    stats = (row_top, row_total, row_weighted, picked)
    if PAIR * share * STATS == LANES:
        joined = picked
        for at in range(STATS - 1):
            joined = jnp.where(lane // (PAIR * share) == at, stats[at], joined)
        joined = jnp.sum(jnp.where(lane % share == sub, joined, 0.0), axis=0, keepdims=True)
        lane = iota((1, LANES), 1)
        neutral = jnp.where(lane < PAIR * share, -jnp.inf, 0.0)
        stats_ref[...] = jnp.where(lane // share % PAIR == half, joined, neutral)
    else:
        for at in range(STATS):
            line = jnp.sum(jnp.where(lane == sub, stats[at], 0.0), axis=0, keepdims=True)
            for h in range(PAIR):
                first = (at * PAIR + h) * share
                stats_ref[:, first : first + share] = jnp.where(half == h, line, 0.0 if at else -jnp.inf)


def finish_kernel(share, stats_ref, meta_ref, logprob_ref, entropy_ref, seq_ref):
    row_count = logprob_ref.shape[0]
    used = PAIR * share
    lanes = max(used, LANES)

    def stat(at):
        if used >= LANES:
            return stats_ref[:, at * used : (at + 1) * used]
        return stats_ref[...] if at == 0 else pltpu.roll(stats_ref[...], LANES - at * used, 1)

    tops = stat(0)
    row_top = jnp.max(tops, axis=0, keepdims=True)
    weight = jnp.exp(tops - row_top)
    row_total = jnp.sum(stat(1) * weight, axis=0, keepdims=True)
    row_weighted = jnp.sum(stat(2) * weight, axis=0, keepdims=True)
    picked = jnp.sum(stat(3), axis=0, keepdims=True)
    log_norm = row_top + jnp.log(row_total)
    lane, sub = iota((1, lanes), 1), iota((SUBS, lanes), 0)
    in_use = jnp.logical_and(meta_ref[4:5, :] > 0.5, lane < used)
    logprob = jnp.where(in_use, picked - log_norm, 0.0)
    entropy = jnp.where(in_use, log_norm - row_weighted / row_total, 0.0)
    segment, place = meta_ref[3:4, :].astype(jnp.int32), meta_ref[5:6, :].astype(jnp.int32)
    mine = jnp.logical_and(place == sub, lane % share // MINE == own_slot(share // MINE))

    def placed(values, wanted):
        sums = jnp.sum(jnp.where(wanted, values, 0.0), axis=1, keepdims=True)
        diagonal = iota((SUBS, LANES), 0) == iota((SUBS, LANES), 1)
        return jnp.sum(jnp.where(diagonal, sums, 0.0), axis=0)

    logprob_ref[...] = placed(logprob, mine)[:row_count]
    entropy_ref[...] = placed(entropy, mine)[:row_count]
    seq_ref[...] = placed(logprob, segment == sub)[:SEQS]


def grant(mebibytes):
    return pltpu.CompilerParams(vmem_limit_bytes=mebibytes * 1024 * 1024)


def local(hidden, norm_gain, lm_head, targets, segments, scored):
    row_count, width = hidden.shape
    groups, tp_count = lax.axis_size("req"), lax.axis_size("tp")
    span = width * MINE // SUBS
    share = groups * MINE
    lanes = max(PAIR * share, LANES)

    def spec(space):
        return pl.BlockSpec(memory_space=space)

    other = lax.ppermute(lm_head, "tp", [(i, i + 1 - 2 * (i % PAIR)) for i in range(tp_count)])
    packed = pl.pallas_call(
        functools.partial(pack_kernel, share),
        out_shape=jax.ShapeDtypeStruct((groups, SUBS, span + lanes), jnp.bfloat16),
        in_specs=[spec(pltpu.HBM)] * 5,
        out_specs=spec(pltpu.HBM),
        scratch_shapes=[
            VMEM((row_count, width), jnp.bfloat16),
            VMEM((width // LANES, LANES), jnp.bfloat16),
            *[SMEM((row_count,), jnp.int32)] * 3,
            VMEM((row_count, width), jnp.float32),
            VMEM((SUBS, span), jnp.float32),
            VMEM((width // LANES, LANES), jnp.float32),
            VMEM((SUBS, span + lanes), jnp.bfloat16),
            pltpu.SemaphoreType.DMA((5,)),
            pltpu.SemaphoreType.DMA((groups,)),
        ],
    )(hidden, norm_gain.reshape(width // LANES, LANES), targets, segments, scored)
    rows = lax.all_to_all(packed, "req", 0, 0, axis_index_groups=[members(groups)])
    other = pltpu.with_memory_space_constraint(other, pltpu.HBM)
    staged = width * 9 // 16
    slices = pl.pallas_call(
        functools.partial(stage_kernel, share),
        out_shape=(
            VMEM(lm_head.shape, lm_head.dtype),
            VMEM((staged, lm_head.shape[1]), lm_head.dtype),
            VMEM((groups * SUBS, groups * SUBS), jnp.bfloat16),
        ),
        in_specs=[spec(pltpu.HBM)] * 2,
        out_specs=(spec(VMEM),) * 3,
        scratch_shapes=[pltpu.SemaphoreType.DMA((2, 4))],
        compiler_params=grant(4),
        cost_estimate=pl.CostEstimate(flops=0, bytes_accessed=3 * 2 * lm_head.size, transcendentals=0),
    )(pltpu.with_memory_space_constraint(lm_head, pltpu.HBM), other)
    stats, meta = pl.pallas_call(
        score_kernel,
        out_shape=(
            jax.ShapeDtypeStruct((1, STATS * PAIR * share), jnp.float32),
            VMEM((SUBS, lanes), jnp.float32),
        ),
        in_specs=[spec(VMEM)] * 4 + [spec(pltpu.HBM)],
        out_specs=(spec(VMEM), spec(VMEM)),
        scratch_shapes=[
            VMEM((share, width), jnp.bfloat16),
            VMEM((width - staged, lm_head.shape[1]), jnp.bfloat16),
            pltpu.SemaphoreType.DMA((4,)),
        ],
        compiler_params=grant(24),
    )(rows, *(pltpu.with_memory_space_constraint(part, VMEM) for part in slices), other)
    copies = jnp.broadcast_to(stats[None], (groups * tp_count,) + stats.shape)
    gathered = lax.all_to_all(copies, ("req", "tp"), 0, 0)
    gathered = gathered.reshape(groups * tp_count, stats.shape[1])
    return pl.pallas_call(
        functools.partial(finish_kernel, share),
        out_shape=(
            jax.ShapeDtypeStruct((row_count,), jnp.float32),
            jax.ShapeDtypeStruct((row_count,), jnp.float32),
            jax.ShapeDtypeStruct((SEQS,), jnp.float32),
        ),
        in_specs=[spec(VMEM), spec(VMEM)],
        out_specs=(spec(VMEM), spec(VMEM), spec(VMEM)),
    )(pltpu.with_memory_space_constraint(gathered, VMEM), pltpu.with_memory_space_constraint(meta, VMEM))


def solution(mesh):
    return jax.shard_map(
        local,
        mesh=mesh,
        in_specs=(P("req", None), P(), P(None, ("req", "tp")), P("req"), P("req"), P("req")),
        out_specs=(P("req"), P("req"), P()),
        check_vma=False,
    )
```

```python
import functools

import jax
import jax.numpy as jnp
from jax import lax
from jax.experimental import pallas as pl
from jax.experimental.pallas import tpu as pltpu
from jax.sharding import PartitionSpec as P

SEQS = 4
PICK = 4
PAIR = 2
MINE = PICK // PAIR
SUBS = 8
LANES = 128
STATS = 4

VMEM = pltpu.VMEM
SMEM = pltpu.SMEM


def ranks_of(scored_ref, row_count):
    ranks, so_far = [], jnp.int32(0)
    for row in range(row_count):
        ranks.append(so_far)
        so_far = so_far + scored_ref[row]
    return ranks, so_far


def iota(shape, axis):
    return lax.broadcasted_iota(jnp.int32, shape, axis)


def members(count):
    quarter = count // 4
    return [*reversed(range(quarter, count - quarter)), *range(quarter), *range(count - quarter, count)]


def own_slot(count):
    own, quarter = lax.axis_index("req"), count // 4
    middle = count - quarter - 1 - own
    return jnp.where(own < quarter, own + count - 2 * quarter, jnp.where(own < count - quarter, middle, own))


def pack_kernel(share, hidden_ref, gain_ref, targets_ref, segments_ref, scored_ref, out_ref, wide_ref, parts_ref, gains_ref):
    row_count, width = hidden_ref.shape
    parts = SUBS // MINE
    span = width // parts
    own, half = own_slot(out_ref.shape[0]), lax.axis_index("tp") % PAIR
    wide_ref[...] = hidden_ref[...].astype(jnp.float32)
    gains_ref[...] = gain_ref[...].astype(jnp.float32)
    ranks, count = ranks_of(scored_ref, row_count)
    source = [jnp.int32(0)] * PICK
    for row in range(row_count):
        for r in range(PICK):
            hit = jnp.logical_and(scored_ref[row] == 1, ranks[row] == r)
            source[r] = jnp.where(hit, row, source[r])
    mine = [source[i] for i in range(MINE)]
    for h in range(1, PAIR):
        mine = [jnp.where(half == h, source[h * MINE + i], mine[i]) for i in range(MINE)]
    for i in range(MINE):
        for k in range(parts):
            parts_ref[k * MINE + i : k * MINE + i + 1, :] = wide_ref[pl.ds(mine[i], 1), k * span : (k + 1) * span]
    values = parts_ref[...]
    part = jnp.broadcast_to(jnp.sum(values * values, axis=1, keepdims=True), (SUBS, LANES))
    total = part
    for k in range(1, parts):
        total = total + pltpu.roll(part, k * MINE, 0)
    row_scale = lax.rsqrt(total / width + 1e-05)
    sub, lane = iota((SUBS, LANES), 0), iota((SUBS, LANES), 1)
    chunks = span // LANES
    for at in range(chunks):
        gain = gains_ref[at : at + 1, :]
        for k in range(1, parts):
            gain = jnp.where(sub >= k * MINE, gains_ref[k * chunks + at : k * chunks + at + 1, :], gain)
        piece = parts_ref[:, at * LANES : (at + 1) * LANES]
        piece = (piece * row_scale * gain).astype(jnp.bfloat16)
        for to in range(out_ref.shape[0]):
            out_ref[to, :, at * LANES : (at + 1) * LANES] = piece
    width_side = out_ref.shape[2] - span
    sub, lane = iota((SUBS, width_side), 0), iota((SUBS, width_side), 1)
    at_row, at_half = lane % share - own * MINE, lane // share
    side = jnp.zeros((SUBS, width_side), jnp.int32)
    for i in range(MINE):
        target = targets_ref[mine[i]]
        digits = jnp.where(sub == 0, target & 255, jnp.where(sub == 1, (target >> 8) & 255, target >> 16))
        fields = jnp.zeros((SUBS, width_side), jnp.int32)
        for h in range(PAIR):
            r = h * MINE + i
            field = jnp.where(sub == 4, (count > r).astype(jnp.int32), source[r])
            fields = jnp.where(at_half == h, jnp.where(sub == 3, segments_ref[source[r]], field), fields)
        side = jnp.where(at_row == i, jnp.where(sub < 3, digits, fields), side)
    side = side.astype(jnp.float32).astype(jnp.bfloat16)
    for to in range(out_ref.shape[0]):
        out_ref[to, :, span:] = side


def stage_kernel(own_ref, other_ref, own_out, other_out, sems):
    copies = []
    for at, (source, out) in enumerate(((own_ref, own_out), (other_ref, other_out))):
        depth = out.shape[0] // sems.shape[1]
        for i in range(sems.shape[1]):
            piece = pl.ds(i * depth, depth)
            copies.append(pltpu.make_async_copy(source.at[piece], out.at[piece], sems.at[at, i]))
    for copy in copies:
        copy.start()
    for copy in copies:
        copy.wait()


def score_kernel(rows_ref, own_ref, upper_ref, other_ref, stats_ref, meta_ref, ordered_ref, lower_ref, sems):
    width, cols = own_ref.shape
    staged = upper_ref.shape[0]
    depth = lower_ref.shape[0] // sems.shape[0]
    copies = [
        pltpu.make_async_copy(
            other_ref.at[pl.ds(staged + i * depth, depth)], lower_ref.at[pl.ds(i * depth, depth)], sems.at[i]
        )
        for i in range(sems.shape[0])
    ]
    for copy in copies:
        copy.start()
    groups = rows_ref.shape[0]
    parts = SUBS // MINE
    span = width // parts
    share = groups * MINE
    tp, tp_count = lax.axis_index("tp"), lax.axis_size("tp")
    half = tp % PAIR
    place = lax.axis_index("req") * tp_count + tp
    count = groups * SUBS
    into, out_of = iota((count, count), 0), iota((count, count), 1)
    wanted = into % share // MINE * SUBS + into // share * MINE + into % MINE
    order = jnp.where(out_of == wanted, 1.0, 0.0).astype(jnp.bfloat16)
    rows = rows_ref[:, :, :span].reshape(count, span)
    ordered = jnp.dot(order, rows, preferred_element_type=jnp.float32).astype(jnp.bfloat16)
    for k in range(parts):
        ordered_ref[:, k * span : (k + 1) * span] = ordered[k * share : (k + 1) * share]
    meta = rows_ref[0, :, span:].astype(jnp.float32)
    for q in range(1, groups):
        meta = meta + rows_ref[q, :, span:].astype(jnp.float32)
    meta_ref[...] = meta
    chunk = min(1024, width - staged)

    def product(slice_ref, first):
        def step(i, sums):
            at = pl.multiple_of(first + i * chunk, chunk)
            rows = ordered_ref[:, pl.ds(at, chunk)]
            own = own_ref[pl.ds(at, chunk), :]
            other = slice_ref[pl.ds(pl.multiple_of(i * chunk, chunk), chunk), :]
            return (
                sums[0] + jnp.dot(rows, own, preferred_element_type=jnp.float32),
                sums[1] + jnp.dot(rows, other, preferred_element_type=jnp.float32),
            )

        return step

    zeros = jnp.zeros((share, cols), jnp.float32)
    sums = lax.fori_loop(0, staged // chunk, product(upper_ref, 0), (zeros, zeros))
    for copy in copies:
        copy.wait()
    sums = lax.fori_loop(0, (width - staged) // chunk, product(lower_ref, staged), sums)
    logits = jnp.concatenate(sums, axis=1)
    lanes = max(share, LANES)
    sub, lane = iota((share, lanes), 0), iota((share, lanes), 1)
    ids = meta[0:1, :lanes] + 256.0 * meta[1:2, :lanes] + 65536.0 * meta[2:3, :lanes]
    ids = jnp.sum(jnp.where(lane == sub, ids, 0.0), axis=1, keepdims=True).astype(jnp.int32)
    row_top = jnp.max(logits, axis=1, keepdims=True)
    scaled = jnp.exp(logits - row_top)
    row_total = jnp.sum(scaled, axis=1, keepdims=True)
    row_weighted = jnp.sum(scaled * logits, axis=1, keepdims=True)
    column = iota(logits.shape, 1)
    other = place + 1 - 2 * half
    columns = jnp.where(column < cols, place * cols, (other - 1) * cols) + column
    picked = jnp.sum(jnp.where(columns == ids, logits, 0.0), axis=1, keepdims=True)
    stats = (row_top, row_total, row_weighted, picked)
    if PAIR * share * STATS == LANES:
        joined = picked
        for at in range(STATS - 1):
            joined = jnp.where(lane // (PAIR * share) == at, stats[at], joined)
        joined = jnp.sum(jnp.where(lane % share == sub, joined, 0.0), axis=0, keepdims=True)
        lane = iota((1, LANES), 1)
        neutral = jnp.where(lane < PAIR * share, -jnp.inf, 0.0)
        stats_ref[...] = jnp.where(lane // share % PAIR == half, joined, neutral)
    else:
        for at in range(STATS):
            line = jnp.sum(jnp.where(lane == sub, stats[at], 0.0), axis=0, keepdims=True)
            for h in range(PAIR):
                first = (at * PAIR + h) * share
                stats_ref[:, first : first + share] = jnp.where(half == h, line, 0.0 if at else -jnp.inf)


def finish_kernel(share, stats_ref, meta_ref, logprob_ref, entropy_ref, seq_ref):
    row_count = logprob_ref.shape[0]
    used = PAIR * share
    lanes = max(used, LANES)

    def stat(at):
        if used >= LANES:
            return stats_ref[:, at * used : (at + 1) * used]
        return stats_ref[...] if at == 0 else pltpu.roll(stats_ref[...], LANES - at * used, 1)

    tops = stat(0)
    row_top = jnp.max(tops, axis=0, keepdims=True)
    weight = jnp.exp(tops - row_top)
    row_total = jnp.sum(stat(1) * weight, axis=0, keepdims=True)
    row_weighted = jnp.sum(stat(2) * weight, axis=0, keepdims=True)
    picked = jnp.sum(stat(3), axis=0, keepdims=True)
    log_norm = row_top + jnp.log(row_total)
    lane, sub = iota((1, lanes), 1), iota((SUBS, lanes), 0)
    in_use = jnp.logical_and(meta_ref[4:5, :] > 0.5, lane < used)
    logprob = jnp.where(in_use, picked - log_norm, 0.0)
    entropy = jnp.where(in_use, log_norm - row_weighted / row_total, 0.0)
    segment, place = meta_ref[3:4, :].astype(jnp.int32), meta_ref[5:6, :].astype(jnp.int32)
    mine = jnp.logical_and(place == sub, lane % share // MINE == own_slot(share // MINE))

    def placed(values, wanted):
        sums = jnp.sum(jnp.where(wanted, values, 0.0), axis=1, keepdims=True)
        diagonal = iota((SUBS, LANES), 0) == iota((SUBS, LANES), 1)
        return jnp.sum(jnp.where(diagonal, sums, 0.0), axis=0)

    logprob_ref[...] = placed(logprob, mine)[:row_count]
    entropy_ref[...] = placed(entropy, mine)[:row_count]
    seq_ref[...] = placed(logprob, segment == sub)[:SEQS]


def grant(mebibytes):
    return pltpu.CompilerParams(vmem_limit_bytes=mebibytes * 1024 * 1024)


def local(hidden, norm_gain, lm_head, targets, segments, scored):
    row_count, width = hidden.shape
    groups, tp_count = lax.axis_size("req"), lax.axis_size("tp")
    span = width * MINE // SUBS
    share = groups * MINE
    lanes = max(PAIR * share, LANES)

    def spec(space):
        return pl.BlockSpec(memory_space=space)

    other = lax.ppermute(lm_head, "tp", [(i, i + 1 - 2 * (i % PAIR)) for i in range(tp_count)])
    packed = pl.pallas_call(
        functools.partial(pack_kernel, share),
        out_shape=VMEM((groups, SUBS, span + lanes), jnp.bfloat16),
        in_specs=[spec(VMEM)] * 2 + [spec(SMEM)] * 3,
        out_specs=spec(VMEM),
        scratch_shapes=[
            VMEM((row_count, width), jnp.float32),
            VMEM((SUBS, span), jnp.float32),
            VMEM((width // LANES, LANES), jnp.float32),
        ],
    )(hidden, norm_gain.reshape(width // LANES, LANES), targets, segments, scored)
    rows = lax.all_to_all(packed, "req", 0, 0, axis_index_groups=[members(groups)])
    other = pltpu.with_memory_space_constraint(other, pltpu.HBM)
    staged = width // 2
    slices = pl.pallas_call(
        stage_kernel,
        out_shape=(VMEM(lm_head.shape, lm_head.dtype), VMEM((staged, lm_head.shape[1]), lm_head.dtype)),
        in_specs=[spec(pltpu.HBM)] * 2,
        out_specs=(spec(VMEM),) * 2,
        scratch_shapes=[pltpu.SemaphoreType.DMA((2, 4))],
        compiler_params=grant(4),
        cost_estimate=pl.CostEstimate(flops=0, bytes_accessed=3 * 2 * lm_head.size, transcendentals=0),
    )(pltpu.with_memory_space_constraint(lm_head, pltpu.HBM), other)
    stats, meta = pl.pallas_call(
        score_kernel,
        out_shape=(
            jax.ShapeDtypeStruct((1, STATS * PAIR * share), jnp.float32),
            VMEM((SUBS, lanes), jnp.float32),
        ),
        in_specs=[spec(VMEM)] * 3 + [spec(pltpu.HBM)],
        out_specs=(spec(VMEM), spec(VMEM)),
        scratch_shapes=[
            VMEM((share, width), jnp.bfloat16),
            VMEM((width - staged, lm_head.shape[1]), jnp.bfloat16),
            pltpu.SemaphoreType.DMA((4,)),
        ],
        compiler_params=grant(24),
    )(rows, *(pltpu.with_memory_space_constraint(part, VMEM) for part in slices), other)
    copies = jnp.broadcast_to(stats[None], (groups * tp_count,) + stats.shape)
    gathered = lax.all_to_all(copies, ("req", "tp"), 0, 0)
    gathered = gathered.reshape(groups * tp_count, stats.shape[1])
    return pl.pallas_call(
        functools.partial(finish_kernel, share),
        out_shape=(
            jax.ShapeDtypeStruct((row_count,), jnp.float32),
            jax.ShapeDtypeStruct((row_count,), jnp.float32),
            jax.ShapeDtypeStruct((SEQS,), jnp.float32),
        ),
        in_specs=[spec(VMEM), spec(VMEM)],
        out_specs=(spec(VMEM), spec(VMEM), spec(VMEM)),
    )(pltpu.with_memory_space_constraint(gathered, VMEM), pltpu.with_memory_space_constraint(meta, VMEM))


def solution(mesh):
    return jax.shard_map(
        local,
        mesh=mesh,
        in_specs=(P("req", None), P(), P(None, ("req", "tp")), P("req"), P("req"), P("req")),
        out_specs=(P("req"), P("req"), P()),
        check_vma=False,
    )
```

```python
import functools

import jax
import jax.numpy as jnp
from jax import lax
from jax.experimental import pallas as pl
from jax.experimental.pallas import tpu as pltpu
from jax.sharding import PartitionSpec as P

SEQS = 4
PICK = 4
PAIR = 2
MINE = PICK // PAIR
SUBS = 8
LANES = 128
STATS = 4

VMEM = pltpu.VMEM
SMEM = pltpu.SMEM


def ranks_of(scored_ref, row_count):
    ranks, so_far = [], jnp.int32(0)
    for row in range(row_count):
        ranks.append(so_far)
        so_far = so_far + scored_ref[row]
    return ranks, so_far


def iota(shape, axis):
    return lax.broadcasted_iota(jnp.int32, shape, axis)


def members(count):
    quarter = count // 4
    return [*reversed(range(quarter, count - quarter)), *range(quarter), *range(count - quarter, count)]


def own_slot(count):
    own, quarter = lax.axis_index("req"), count // 4
    middle = count - quarter - 1 - own
    return jnp.where(own < quarter, own + count - 2 * quarter, jnp.where(own < count - quarter, middle, own))


def pack_kernel(share, hidden_ref, gain_ref, targets_ref, segments_ref, scored_ref, out_ref, wide_ref, parts_ref, gains_ref):
    row_count, width = hidden_ref.shape
    parts = SUBS // MINE
    span = width // parts
    own, half = own_slot(out_ref.shape[0]), lax.axis_index("tp") % PAIR
    wide_ref[...] = hidden_ref[...].astype(jnp.float32)
    gains_ref[...] = gain_ref[...].astype(jnp.float32)
    ranks, count = ranks_of(scored_ref, row_count)
    source = [jnp.int32(0)] * PICK
    for row in range(row_count):
        for r in range(PICK):
            hit = jnp.logical_and(scored_ref[row] == 1, ranks[row] == r)
            source[r] = jnp.where(hit, row, source[r])
    mine = [source[i] for i in range(MINE)]
    for h in range(1, PAIR):
        mine = [jnp.where(half == h, source[h * MINE + i], mine[i]) for i in range(MINE)]
    for i in range(MINE):
        for k in range(parts):
            parts_ref[k * MINE + i : k * MINE + i + 1, :] = wide_ref[pl.ds(mine[i], 1), k * span : (k + 1) * span]
    values = parts_ref[...]
    part = jnp.broadcast_to(jnp.sum(values * values, axis=1, keepdims=True), (SUBS, LANES))
    total = part
    for k in range(1, parts):
        total = total + pltpu.roll(part, k * MINE, 0)
    row_scale = lax.rsqrt(total / width + 1e-05)
    sub, lane = iota((SUBS, LANES), 0), iota((SUBS, LANES), 1)
    chunks = span // LANES
    for at in range(chunks):
        gain = gains_ref[at : at + 1, :]
        for k in range(1, parts):
            gain = jnp.where(sub >= k * MINE, gains_ref[k * chunks + at : k * chunks + at + 1, :], gain)
        piece = parts_ref[:, at * LANES : (at + 1) * LANES]
        piece = (piece * row_scale * gain).astype(jnp.bfloat16)
        for to in range(out_ref.shape[0]):
            out_ref[to, :, at * LANES : (at + 1) * LANES] = piece
    width_side = out_ref.shape[2] - span
    sub, lane = iota((SUBS, width_side), 0), iota((SUBS, width_side), 1)
    at_row, at_half = lane % share - own * MINE, lane // share
    side = jnp.zeros((SUBS, width_side), jnp.int32)
    for i in range(MINE):
        target = targets_ref[mine[i]]
        digits = jnp.where(sub == 0, target & 255, jnp.where(sub == 1, (target >> 8) & 255, target >> 16))
        fields = jnp.zeros((SUBS, width_side), jnp.int32)
        for h in range(PAIR):
            r = h * MINE + i
            field = jnp.where(sub == 4, (count > r).astype(jnp.int32), source[r])
            fields = jnp.where(at_half == h, jnp.where(sub == 3, segments_ref[source[r]], field), fields)
        side = jnp.where(at_row == i, jnp.where(sub < 3, digits, fields), side)
    side = side.astype(jnp.float32).astype(jnp.bfloat16)
    for to in range(out_ref.shape[0]):
        out_ref[to, :, span:] = side


def stage_kernel(share, own_ref, other_ref, own_out, other_out, order_out, sems):
    copies = []
    for at, (source, out) in enumerate(((own_ref, own_out), (other_ref, other_out))):
        depth = out.shape[0] // sems.shape[1]
        for i in range(sems.shape[1]):
            piece = pl.ds(i * depth, depth)
            copies.append(pltpu.make_async_copy(source.at[piece], out.at[piece], sems.at[at, i]))
    for copy in copies:
        copy.start()
    into, out_of = iota(order_out.shape, 0), iota(order_out.shape, 1)
    wanted = into % share // MINE * SUBS + into // share * MINE + into % MINE
    order_out[...] = jnp.where(out_of == wanted, 1.0, 0.0).astype(jnp.bfloat16)
    for copy in copies:
        copy.wait()


def score_kernel(rows_ref, own_ref, upper_ref, order_ref, other_ref, stats_ref, meta_ref, ordered_ref, whole_ref, sems):
    width, cols = own_ref.shape
    staged, chunk = upper_ref.shape[0], width // sems.shape[0]

    def fetch(source, at):
        piece = pl.ds(at * chunk, chunk)
        return pltpu.make_async_copy(source.at[piece], whole_ref.at[piece], sems.at[at])

    for at in range(sems.shape[0]):
        fetch(upper_ref if at * chunk < staged else other_ref, at).start()
    groups = rows_ref.shape[0]
    parts = SUBS // MINE
    span = width // parts
    share = groups * MINE
    tp, tp_count = lax.axis_index("tp"), lax.axis_size("tp")
    half = tp % PAIR
    place = lax.axis_index("req") * tp_count + tp
    count = groups * SUBS
    rows = rows_ref[:, :, :span].reshape(count, span)
    ordered = jnp.dot(order_ref[...], rows, preferred_element_type=jnp.float32).astype(jnp.bfloat16)
    for k in range(parts):
        ordered_ref[:, k * span : (k + 1) * span] = ordered[k * share : (k + 1) * share]
    meta = rows_ref[0, :, span:].astype(jnp.float32)
    for q in range(1, groups):
        meta = meta + rows_ref[q, :, span:].astype(jnp.float32)
    meta_ref[...] = meta

    def step(at, sums):
        piece = pl.ds(pl.multiple_of(at * chunk, chunk), chunk)
        rows = ordered_ref[:, piece]
        own = sums[0] + jnp.dot(rows, own_ref[piece, :], preferred_element_type=jnp.float32)
        fetch(other_ref, at).wait()
        return own, sums[1] + jnp.dot(rows, whole_ref[piece, :], preferred_element_type=jnp.float32)

    zeros = jnp.zeros((share, cols), jnp.float32)
    logits = jnp.concatenate(lax.fori_loop(0, width // chunk, step, (zeros, zeros)), axis=1)
    lanes = max(share, LANES)
    sub, lane = iota((share, lanes), 0), iota((share, lanes), 1)
    ids = meta[0:1, :lanes] + 256.0 * meta[1:2, :lanes] + 65536.0 * meta[2:3, :lanes]
    ids = jnp.sum(jnp.where(lane == sub, ids, 0.0), axis=1, keepdims=True).astype(jnp.int32)
    row_top = jnp.max(logits, axis=1, keepdims=True)
    scaled = jnp.exp(logits - row_top)
    row_total = jnp.sum(scaled, axis=1, keepdims=True)
    row_weighted = jnp.sum(scaled * logits, axis=1, keepdims=True)
    column = iota(logits.shape, 1)
    other = place + 1 - 2 * half
    columns = jnp.where(column < cols, place * cols, (other - 1) * cols) + column
    picked = jnp.sum(jnp.where(columns == ids, logits, 0.0), axis=1, keepdims=True)
    stats = (row_top, row_total, row_weighted, picked)
    if PAIR * share * STATS == LANES:
        joined = picked
        for at in range(STATS - 1):
            joined = jnp.where(lane // (PAIR * share) == at, stats[at], joined)
        joined = jnp.sum(jnp.where(lane % share == sub, joined, 0.0), axis=0, keepdims=True)
        lane = iota((1, LANES), 1)
        neutral = jnp.where(lane < PAIR * share, -jnp.inf, 0.0)
        stats_ref[...] = jnp.where(lane // share % PAIR == half, joined, neutral)
    else:
        for at in range(STATS):
            line = jnp.sum(jnp.where(lane == sub, stats[at], 0.0), axis=0, keepdims=True)
            for h in range(PAIR):
                first = (at * PAIR + h) * share
                stats_ref[:, first : first + share] = jnp.where(half == h, line, 0.0 if at else -jnp.inf)


def finish_kernel(share, stats_ref, meta_ref, logprob_ref, entropy_ref, seq_ref):
    row_count = logprob_ref.shape[0]
    used = PAIR * share
    lanes = max(used, LANES)

    def stat(at):
        if used >= LANES:
            return stats_ref[:, at * used : (at + 1) * used]
        return stats_ref[...] if at == 0 else pltpu.roll(stats_ref[...], LANES - at * used, 1)

    tops = stat(0)
    row_top = jnp.max(tops, axis=0, keepdims=True)
    weight = jnp.exp(tops - row_top)
    row_total = jnp.sum(stat(1) * weight, axis=0, keepdims=True)
    row_weighted = jnp.sum(stat(2) * weight, axis=0, keepdims=True)
    picked = jnp.sum(stat(3), axis=0, keepdims=True)
    log_norm = row_top + jnp.log(row_total)
    lane, sub = iota((1, lanes), 1), iota((SUBS, lanes), 0)
    in_use = jnp.logical_and(meta_ref[4:5, :] > 0.5, lane < used)
    logprob = jnp.where(in_use, picked - log_norm, 0.0)
    entropy = jnp.where(in_use, log_norm - row_weighted / row_total, 0.0)
    segment, place = meta_ref[3:4, :].astype(jnp.int32), meta_ref[5:6, :].astype(jnp.int32)
    mine = jnp.logical_and(place == sub, lane % share // MINE == own_slot(share // MINE))

    def placed(values, wanted):
        sums = jnp.sum(jnp.where(wanted, values, 0.0), axis=1, keepdims=True)
        diagonal = iota((SUBS, LANES), 0) == iota((SUBS, LANES), 1)
        return jnp.sum(jnp.where(diagonal, sums, 0.0), axis=0)

    logprob_ref[...] = placed(logprob, mine)[:row_count]
    entropy_ref[...] = placed(entropy, mine)[:row_count]
    seq_ref[...] = placed(logprob, segment == sub)[:SEQS]


def grant(mebibytes):
    return pltpu.CompilerParams(vmem_limit_bytes=mebibytes * 1024 * 1024)


def local(hidden, norm_gain, lm_head, targets, segments, scored):
    row_count, width = hidden.shape
    groups, tp_count = lax.axis_size("req"), lax.axis_size("tp")
    span = width * MINE // SUBS
    share = groups * MINE
    lanes = max(PAIR * share, LANES)

    def spec(space):
        return pl.BlockSpec(memory_space=space)

    other = lax.ppermute(lm_head, "tp", [(i, i + 1 - 2 * (i % PAIR)) for i in range(tp_count)])
    packed = pl.pallas_call(
        functools.partial(pack_kernel, share),
        out_shape=VMEM((groups, SUBS, span + lanes), jnp.bfloat16),
        in_specs=[spec(VMEM)] * 2 + [spec(SMEM)] * 3,
        out_specs=spec(VMEM),
        scratch_shapes=[
            VMEM((row_count, width), jnp.float32),
            VMEM((SUBS, span), jnp.float32),
            VMEM((width // LANES, LANES), jnp.float32),
        ],
    )(hidden, norm_gain.reshape(width // LANES, LANES), targets, segments, scored)
    rows = lax.all_to_all(packed, "req", 0, 0, axis_index_groups=[members(groups)])
    other = pltpu.with_memory_space_constraint(other, pltpu.HBM)
    staged = width // 2
    slices = pl.pallas_call(
        functools.partial(stage_kernel, share),
        out_shape=(
            VMEM(lm_head.shape, lm_head.dtype),
            VMEM((staged, lm_head.shape[1]), lm_head.dtype),
            VMEM((groups * SUBS, groups * SUBS), jnp.bfloat16),
        ),
        in_specs=[spec(pltpu.HBM)] * 2,
        out_specs=(spec(VMEM),) * 3,
        scratch_shapes=[pltpu.SemaphoreType.DMA((2, 4))],
        compiler_params=grant(4),
        cost_estimate=pl.CostEstimate(flops=0, bytes_accessed=3 * 2 * lm_head.size, transcendentals=0),
    )(pltpu.with_memory_space_constraint(lm_head, pltpu.HBM), other)
    stats, meta = pl.pallas_call(
        score_kernel,
        out_shape=(
            jax.ShapeDtypeStruct((1, STATS * PAIR * share), jnp.float32),
            VMEM((SUBS, lanes), jnp.float32),
        ),
        in_specs=[spec(VMEM)] * 4 + [spec(pltpu.HBM)],
        out_specs=(spec(VMEM), spec(VMEM)),
        scratch_shapes=[
            VMEM((share, width), jnp.bfloat16),
            VMEM(lm_head.shape, jnp.bfloat16),
            pltpu.SemaphoreType.DMA((4,)),
        ],
        compiler_params=grant(24),
    )(rows, *(pltpu.with_memory_space_constraint(part, VMEM) for part in slices), other)
    copies = jnp.broadcast_to(stats[None], (groups * tp_count,) + stats.shape)
    gathered = lax.all_to_all(copies, ("req", "tp"), 0, 0)
    gathered = gathered.reshape(groups * tp_count, stats.shape[1])
    return pl.pallas_call(
        functools.partial(finish_kernel, share),
        out_shape=(
            jax.ShapeDtypeStruct((row_count,), jnp.float32),
            jax.ShapeDtypeStruct((row_count,), jnp.float32),
            jax.ShapeDtypeStruct((SEQS,), jnp.float32),
        ),
        in_specs=[spec(VMEM), spec(VMEM)],
        out_specs=(spec(VMEM), spec(VMEM), spec(VMEM)),
    )(pltpu.with_memory_space_constraint(gathered, VMEM), pltpu.with_memory_space_constraint(meta, VMEM))


def solution(mesh):
    return jax.shard_map(
        local,
        mesh=mesh,
        in_specs=(P("req", None), P(), P(None, ("req", "tp")), P("req"), P("req"), P("req")),
        out_specs=(P("req"), P("req"), P()),
        check_vma=False,
    )
```

```python
import functools

import jax
import jax.numpy as jnp
from jax import lax
from jax.experimental import pallas as pl
from jax.experimental.pallas import tpu as pltpu
from jax.sharding import PartitionSpec as P

SEQS = 4
PICK = 4
PAIR = 2
MINE = PICK // PAIR
SUBS = 8
LANES = 128
STATS = 4

VMEM = pltpu.VMEM
SMEM = pltpu.SMEM


def ranks_of(scored_ref, row_count):
    ranks, so_far = [], jnp.int32(0)
    for row in range(row_count):
        ranks.append(so_far)
        so_far = so_far + scored_ref[row]
    return ranks, so_far


def iota(shape, axis):
    return lax.broadcasted_iota(jnp.int32, shape, axis)


def members(count):
    quarter = count // 4
    return [*reversed(range(quarter, count - quarter)), *range(quarter), *range(count - quarter, count)]


def own_slot(count):
    own, quarter = lax.axis_index("req"), count // 4
    middle = count - quarter - 1 - own
    return jnp.where(own < quarter, own + count - 2 * quarter, jnp.where(own < count - quarter, middle, own))


def pack_kernel(share, hidden_ref, gain_ref, targets_ref, segments_ref, scored_ref, out_ref, wide_ref, parts_ref, gains_ref):
    row_count, width = hidden_ref.shape
    parts = SUBS // MINE
    span = width // parts
    own, half = own_slot(out_ref.shape[0]), lax.axis_index("tp") % PAIR
    wide_ref[...] = hidden_ref[...].astype(jnp.float32)
    gains_ref[...] = gain_ref[...].astype(jnp.float32)
    ranks, count = ranks_of(scored_ref, row_count)
    source = [jnp.int32(0)] * PICK
    for row in range(row_count):
        for r in range(PICK):
            hit = jnp.logical_and(scored_ref[row] == 1, ranks[row] == r)
            source[r] = jnp.where(hit, row, source[r])
    mine = [source[i] for i in range(MINE)]
    for h in range(1, PAIR):
        mine = [jnp.where(half == h, source[h * MINE + i], mine[i]) for i in range(MINE)]
    for i in range(MINE):
        for k in range(parts):
            parts_ref[k * MINE + i : k * MINE + i + 1, :] = wide_ref[pl.ds(mine[i], 1), k * span : (k + 1) * span]
    values = parts_ref[...]
    part = jnp.broadcast_to(jnp.sum(values * values, axis=1, keepdims=True), (SUBS, LANES))
    total = part
    for k in range(1, parts):
        total = total + pltpu.roll(part, k * MINE, 0)
    row_scale = lax.rsqrt(total / width + 1e-05)
    sub, lane = iota((SUBS, LANES), 0), iota((SUBS, LANES), 1)
    chunks = span // LANES
    for at in range(chunks):
        gain = gains_ref[at : at + 1, :]
        for k in range(1, parts):
            gain = jnp.where(sub >= k * MINE, gains_ref[k * chunks + at : k * chunks + at + 1, :], gain)
        piece = parts_ref[:, at * LANES : (at + 1) * LANES]
        piece = (piece * row_scale * gain).astype(jnp.bfloat16)
        for to in range(out_ref.shape[0]):
            out_ref[to, :, at * LANES : (at + 1) * LANES] = piece
    width_side = out_ref.shape[2] - span
    sub, lane = iota((SUBS, width_side), 0), iota((SUBS, width_side), 1)
    at_row, at_half = lane % share - own * MINE, lane // share
    side = jnp.zeros((SUBS, width_side), jnp.int32)
    for i in range(MINE):
        target = targets_ref[mine[i]]
        digits = jnp.where(sub == 0, target & 255, jnp.where(sub == 1, (target >> 8) & 255, target >> 16))
        fields = jnp.zeros((SUBS, width_side), jnp.int32)
        for h in range(PAIR):
            r = h * MINE + i
            field = jnp.where(sub == 4, (count > r).astype(jnp.int32), source[r])
            fields = jnp.where(at_half == h, jnp.where(sub == 3, segments_ref[source[r]], field), fields)
        side = jnp.where(at_row == i, jnp.where(sub < 3, digits, fields), side)
    side = side.astype(jnp.float32).astype(jnp.bfloat16)
    for to in range(out_ref.shape[0]):
        out_ref[to, :, span:] = side


def stage_kernel(share, own_ref, other_ref, own_out, other_out, order_out, sems):
    copies = []
    for at, (source, out) in enumerate(((own_ref, own_out), (other_ref, other_out))):
        depth = out.shape[0] // sems.shape[1]
        for i in range(sems.shape[1]):
            piece = pl.ds(i * depth, depth)
            copies.append(pltpu.make_async_copy(source.at[piece], out.at[piece], sems.at[at, i]))
    for copy in copies:
        copy.start()
    into, out_of = iota(order_out.shape, 0), iota(order_out.shape, 1)
    wanted = into % share // MINE * SUBS + into // share * MINE + into % MINE
    order_out[...] = jnp.where(out_of == wanted, 1.0, 0.0).astype(jnp.bfloat16)
    for copy in copies:
        copy.wait()


def score_kernel(rows_ref, own_ref, upper_ref, order_ref, other_ref, stats_ref, meta_ref, ordered_ref, lower_ref, sems):
    width, cols = own_ref.shape
    staged = upper_ref.shape[0]
    depth = lower_ref.shape[0] // sems.shape[0]
    copies = [
        pltpu.make_async_copy(
            other_ref.at[pl.ds(staged + i * depth, depth)], lower_ref.at[pl.ds(i * depth, depth)], sems.at[i]
        )
        for i in range(sems.shape[0])
    ]
    for copy in copies:
        copy.start()
    groups = rows_ref.shape[0]
    parts = SUBS // MINE
    span = width // parts
    share = groups * MINE
    tp, tp_count = lax.axis_index("tp"), lax.axis_size("tp")
    half = tp % PAIR
    place = lax.axis_index("req") * tp_count + tp
    count = groups * SUBS
    rows = rows_ref[:, :, :span].reshape(count, span)
    ordered = jnp.dot(order_ref[...], rows, preferred_element_type=jnp.float32).astype(jnp.bfloat16)
    for k in range(parts):
        ordered_ref[:, k * span : (k + 1) * span] = ordered[k * share : (k + 1) * share]
    meta = rows_ref[0, :, span:].astype(jnp.float32)
    for q in range(1, groups):
        meta = meta + rows_ref[q, :, span:].astype(jnp.float32)
    meta_ref[...] = meta

    def product(slice_ref, first, at, depth):
        piece = pl.ds(pl.multiple_of(at * depth, depth), depth)
        rows = ordered_ref[:, pl.ds(pl.multiple_of(first + at * depth, depth), depth)]
        return jnp.dot(rows, slice_ref[piece, :], preferred_element_type=jnp.float32)

    def resident(at, sums):
        return (
            sums[0] + product(own_ref, 0, at, width // 2),
            sums[1] + product(upper_ref, 0, at, staged // 2),
        )

    def fetched(at, total):
        return total + product(lower_ref, staged, at, (width - staged) // 2)

    zeros = jnp.zeros((share, cols), jnp.float32)
    own_logits, other_logits = lax.fori_loop(0, 2, resident, (zeros, zeros))
    for copy in copies:
        copy.wait()
    logits = jnp.concatenate([own_logits, lax.fori_loop(0, 2, fetched, other_logits)], axis=1)
    lanes = max(share, LANES)
    sub, lane = iota((share, lanes), 0), iota((share, lanes), 1)
    ids = meta[0:1, :lanes] + 256.0 * meta[1:2, :lanes] + 65536.0 * meta[2:3, :lanes]
    ids = jnp.sum(jnp.where(lane == sub, ids, 0.0), axis=1, keepdims=True).astype(jnp.int32)
    row_top = jnp.max(logits, axis=1, keepdims=True)
    scaled = jnp.exp(logits - row_top)
    row_total = jnp.sum(scaled, axis=1, keepdims=True)
    row_weighted = jnp.sum(scaled * logits, axis=1, keepdims=True)
    column = iota(logits.shape, 1)
    other = place + 1 - 2 * half
    columns = jnp.where(column < cols, place * cols, (other - 1) * cols) + column
    picked = jnp.sum(jnp.where(columns == ids, logits, 0.0), axis=1, keepdims=True)
    stats = (row_top, row_total, row_weighted, picked)
    if PAIR * share * STATS == LANES:
        joined = picked
        for at in range(STATS - 1):
            joined = jnp.where(lane // (PAIR * share) == at, stats[at], joined)
        joined = jnp.sum(jnp.where(lane % share == sub, joined, 0.0), axis=0, keepdims=True)
        lane = iota((1, LANES), 1)
        neutral = jnp.where(lane < PAIR * share, -jnp.inf, 0.0)
        stats_ref[...] = jnp.where(lane // share % PAIR == half, joined, neutral)
    else:
        for at in range(STATS):
            line = jnp.sum(jnp.where(lane == sub, stats[at], 0.0), axis=0, keepdims=True)
            for h in range(PAIR):
                first = (at * PAIR + h) * share
                stats_ref[:, first : first + share] = jnp.where(half == h, line, 0.0 if at else -jnp.inf)


def finish_kernel(share, stats_ref, meta_ref, logprob_ref, entropy_ref, seq_ref):
    row_count = logprob_ref.shape[0]
    used = PAIR * share
    lanes = max(used, LANES)

    def stat(at):
        if used >= LANES:
            return stats_ref[:, at * used : (at + 1) * used]
        return stats_ref[...] if at == 0 else pltpu.roll(stats_ref[...], LANES - at * used, 1)

    tops = stat(0)
    row_top = jnp.max(tops, axis=0, keepdims=True)
    weight = jnp.exp(tops - row_top)
    row_total = jnp.sum(stat(1) * weight, axis=0, keepdims=True)
    row_weighted = jnp.sum(stat(2) * weight, axis=0, keepdims=True)
    picked = jnp.sum(stat(3), axis=0, keepdims=True)
    log_norm = row_top + jnp.log(row_total)
    lane, sub = iota((1, lanes), 1), iota((SUBS, lanes), 0)
    in_use = jnp.logical_and(meta_ref[4:5, :] > 0.5, lane < used)
    logprob = jnp.where(in_use, picked - log_norm, 0.0)
    entropy = jnp.where(in_use, log_norm - row_weighted / row_total, 0.0)
    segment, place = meta_ref[3:4, :].astype(jnp.int32), meta_ref[5:6, :].astype(jnp.int32)
    mine = jnp.logical_and(place == sub, lane % share // MINE == own_slot(share // MINE))

    def placed(values, wanted):
        sums = jnp.sum(jnp.where(wanted, values, 0.0), axis=1, keepdims=True)
        diagonal = iota((SUBS, LANES), 0) == iota((SUBS, LANES), 1)
        return jnp.sum(jnp.where(diagonal, sums, 0.0), axis=0)

    logprob_ref[...] = placed(logprob, mine)[:row_count]
    entropy_ref[...] = placed(entropy, mine)[:row_count]
    seq_ref[...] = placed(logprob, segment == sub)[:SEQS]


def grant(mebibytes):
    return pltpu.CompilerParams(vmem_limit_bytes=mebibytes * 1024 * 1024)


def local(hidden, norm_gain, lm_head, targets, segments, scored):
    row_count, width = hidden.shape
    groups, tp_count = lax.axis_size("req"), lax.axis_size("tp")
    span = width * MINE // SUBS
    share = groups * MINE
    lanes = max(PAIR * share, LANES)

    def spec(space):
        return pl.BlockSpec(memory_space=space)

    other = lax.ppermute(lm_head, "tp", [(i, i + 1 - 2 * (i % PAIR)) for i in range(tp_count)])
    packed = pl.pallas_call(
        functools.partial(pack_kernel, share),
        out_shape=VMEM((groups, SUBS, span + lanes), jnp.bfloat16),
        in_specs=[spec(VMEM)] * 2 + [spec(SMEM)] * 3,
        out_specs=spec(VMEM),
        scratch_shapes=[
            VMEM((row_count, width), jnp.float32),
            VMEM((SUBS, span), jnp.float32),
            VMEM((width // LANES, LANES), jnp.float32),
        ],
    )(hidden, norm_gain.reshape(width // LANES, LANES), targets, segments, scored)
    rows = lax.all_to_all(packed, "req", 0, 0, axis_index_groups=[members(groups)])
    other = pltpu.with_memory_space_constraint(other, pltpu.HBM)
    staged = width // 2
    slices = pl.pallas_call(
        functools.partial(stage_kernel, share),
        out_shape=(
            VMEM(lm_head.shape, lm_head.dtype),
            VMEM((staged, lm_head.shape[1]), lm_head.dtype),
            VMEM((groups * SUBS, groups * SUBS), jnp.bfloat16),
        ),
        in_specs=[spec(pltpu.HBM)] * 2,
        out_specs=(spec(VMEM),) * 3,
        scratch_shapes=[pltpu.SemaphoreType.DMA((2, 4))],
        compiler_params=grant(4),
        cost_estimate=pl.CostEstimate(flops=0, bytes_accessed=3 * 2 * lm_head.size, transcendentals=0),
    )(pltpu.with_memory_space_constraint(lm_head, pltpu.HBM), other)
    stats, meta = pl.pallas_call(
        score_kernel,
        out_shape=(
            jax.ShapeDtypeStruct((1, STATS * PAIR * share), jnp.float32),
            VMEM((SUBS, lanes), jnp.float32),
        ),
        in_specs=[spec(VMEM)] * 4 + [spec(pltpu.HBM)],
        out_specs=(spec(VMEM), spec(VMEM)),
        scratch_shapes=[
            VMEM((share, width), jnp.bfloat16),
            VMEM((width - staged, lm_head.shape[1]), jnp.bfloat16),
            pltpu.SemaphoreType.DMA((4,)),
        ],
        compiler_params=grant(24),
    )(rows, *(pltpu.with_memory_space_constraint(part, VMEM) for part in slices), other)
    copies = jnp.broadcast_to(stats[None], (groups * tp_count,) + stats.shape)
    gathered = lax.all_to_all(copies, ("req", "tp"), 0, 0)
    gathered = gathered.reshape(groups * tp_count, stats.shape[1])
    return pl.pallas_call(
        functools.partial(finish_kernel, share),
        out_shape=(
            jax.ShapeDtypeStruct((row_count,), jnp.float32),
            jax.ShapeDtypeStruct((row_count,), jnp.float32),
            jax.ShapeDtypeStruct((SEQS,), jnp.float32),
        ),
        in_specs=[spec(VMEM), spec(VMEM)],
        out_specs=(spec(VMEM), spec(VMEM), spec(VMEM)),
    )(pltpu.with_memory_space_constraint(gathered, VMEM), pltpu.with_memory_space_constraint(meta, VMEM))


def solution(mesh):
    return jax.shard_map(
        local,
        mesh=mesh,
        in_specs=(P("req", None), P(), P(None, ("req", "tp")), P("req"), P("req"), P("req")),
        out_specs=(P("req"), P("req"), P()),
        check_vma=False,
    )
```

```python
import functools

import jax
import jax.numpy as jnp
from jax import lax
from jax.experimental import pallas as pl
from jax.experimental.pallas import tpu as pltpu
from jax.sharding import PartitionSpec as P

SEQS = 4
PICK = 4
PAIR = 2
MINE = PICK // PAIR
SUBS = 8
LANES = 128
STATS = 4

VMEM = pltpu.VMEM
SMEM = pltpu.SMEM


def ranks_of(scored_ref, row_count):
    ranks, so_far = [], jnp.int32(0)
    for row in range(row_count):
        ranks.append(so_far)
        so_far = so_far + scored_ref[row]
    return ranks, so_far


def iota(shape, axis):
    return lax.broadcasted_iota(jnp.int32, shape, axis)


def members(count):
    return [(5 * count // 8 + at) % count for at in range(count)]


def own_slot(count):
    at = lax.axis_index("req") - 5 * count // 8
    return jnp.where(at < 0, at + count, at)


def pack_kernel(share, hidden_ref, gain_ref, targets_ref, segments_ref, scored_ref, out_ref, wide_ref, parts_ref, gains_ref):
    row_count, width = hidden_ref.shape
    parts = SUBS // MINE
    span = width // parts
    own, half = own_slot(out_ref.shape[0]), lax.axis_index("tp") % PAIR
    wide_ref[...] = hidden_ref[...].astype(jnp.float32)
    gains_ref[...] = gain_ref[...].astype(jnp.float32)
    ranks, count = ranks_of(scored_ref, row_count)
    source = [jnp.int32(0)] * PICK
    for row in range(row_count):
        for r in range(PICK):
            hit = jnp.logical_and(scored_ref[row] == 1, ranks[row] == r)
            source[r] = jnp.where(hit, row, source[r])
    mine = [source[i] for i in range(MINE)]
    for h in range(1, PAIR):
        mine = [jnp.where(half == h, source[h * MINE + i], mine[i]) for i in range(MINE)]
    for i in range(MINE):
        for k in range(parts):
            parts_ref[k * MINE + i : k * MINE + i + 1, :] = wide_ref[pl.ds(mine[i], 1), k * span : (k + 1) * span]
    values = parts_ref[...]
    part = jnp.broadcast_to(jnp.sum(values * values, axis=1, keepdims=True), (SUBS, LANES))
    total = part
    for k in range(1, parts):
        total = total + pltpu.roll(part, k * MINE, 0)
    row_scale = lax.rsqrt(total / width + 1e-05)
    sub, lane = iota((SUBS, LANES), 0), iota((SUBS, LANES), 1)
    chunks = span // LANES
    for at in range(chunks):
        gain = gains_ref[at : at + 1, :]
        for k in range(1, parts):
            gain = jnp.where(sub >= k * MINE, gains_ref[k * chunks + at : k * chunks + at + 1, :], gain)
        piece = parts_ref[:, at * LANES : (at + 1) * LANES]
        piece = (piece * row_scale * gain).astype(jnp.bfloat16)
        for to in range(out_ref.shape[0]):
            out_ref[to, :, at * LANES : (at + 1) * LANES] = piece
    width_side = out_ref.shape[2] - span
    sub, lane = iota((SUBS, width_side), 0), iota((SUBS, width_side), 1)
    at_row, at_half = lane % share - own * MINE, lane // share
    side = jnp.zeros((SUBS, width_side), jnp.int32)
    for i in range(MINE):
        target = targets_ref[mine[i]]
        digits = jnp.where(sub == 0, target & 255, jnp.where(sub == 1, (target >> 8) & 255, target >> 16))
        fields = jnp.zeros((SUBS, width_side), jnp.int32)
        for h in range(PAIR):
            r = h * MINE + i
            field = jnp.where(sub == 4, (count > r).astype(jnp.int32), source[r])
            fields = jnp.where(at_half == h, jnp.where(sub == 3, segments_ref[source[r]], field), fields)
        side = jnp.where(at_row == i, jnp.where(sub < 3, digits, fields), side)
    side = side.astype(jnp.float32).astype(jnp.bfloat16)
    for to in range(out_ref.shape[0]):
        out_ref[to, :, span:] = side


def stage_kernel(share, own_ref, other_ref, own_out, other_out, order_out, sems):
    copies = []
    for at, (source, out) in enumerate(((own_ref, own_out), (other_ref, other_out))):
        depth = out.shape[0] // sems.shape[1]
        for i in range(sems.shape[1]):
            piece = pl.ds(i * depth, depth)
            copies.append(pltpu.make_async_copy(source.at[piece], out.at[piece], sems.at[at, i]))
    for copy in copies:
        copy.start()
    into, out_of = iota(order_out.shape, 0), iota(order_out.shape, 1)
    wanted = into % share // MINE * SUBS + into // share * MINE + into % MINE
    order_out[...] = jnp.where(out_of == wanted, 1.0, 0.0).astype(jnp.bfloat16)
    for copy in copies:
        copy.wait()


def score_kernel(rows_ref, own_ref, upper_ref, order_ref, other_ref, stats_ref, meta_ref, ordered_ref, lower_ref, sems):
    width, cols = own_ref.shape
    staged = upper_ref.shape[0]
    depth = lower_ref.shape[0] // sems.shape[0]
    copies = [
        pltpu.make_async_copy(
            other_ref.at[pl.ds(staged + i * depth, depth)], lower_ref.at[pl.ds(i * depth, depth)], sems.at[i]
        )
        for i in range(sems.shape[0])
    ]
    for copy in copies:
        copy.start()
    groups = rows_ref.shape[0]
    parts = SUBS // MINE
    span = width // parts
    share = groups * MINE
    tp, tp_count = lax.axis_index("tp"), lax.axis_size("tp")
    half = tp % PAIR
    place = lax.axis_index("req") * tp_count + tp
    count = groups * SUBS
    rows = rows_ref[:, :, :span].reshape(count, span)
    ordered = jnp.dot(order_ref[...], rows, preferred_element_type=jnp.float32).astype(jnp.bfloat16)
    for k in range(parts):
        ordered_ref[:, k * span : (k + 1) * span] = ordered[k * share : (k + 1) * share]
    meta = rows_ref[0, :, span:].astype(jnp.float32)
    for q in range(1, groups):
        meta = meta + rows_ref[q, :, span:].astype(jnp.float32)
    meta_ref[...] = meta

    def product(slice_ref, first, at, depth):
        piece = pl.ds(pl.multiple_of(at * depth, depth), depth)
        rows = ordered_ref[:, pl.ds(pl.multiple_of(first + at * depth, depth), depth)]
        return jnp.dot(rows, slice_ref[piece, :], preferred_element_type=jnp.float32)

    def resident(at, sums):
        return (
            sums[0] + product(own_ref, 0, at, width // 2),
            sums[1] + product(upper_ref, 0, at, staged // 2),
        )

    def fetched(at, total):
        return total + product(lower_ref, staged, at, (width - staged) // 2)

    zeros = jnp.zeros((share, cols), jnp.float32)
    own_logits, other_logits = lax.fori_loop(0, 2, resident, (zeros, zeros))
    for copy in copies:
        copy.wait()
    logits = jnp.concatenate([own_logits, lax.fori_loop(0, 2, fetched, other_logits)], axis=1)
    lanes = max(share, LANES)
    sub, lane = iota((share, lanes), 0), iota((share, lanes), 1)
    ids = meta[0:1, :lanes] + 256.0 * meta[1:2, :lanes] + 65536.0 * meta[2:3, :lanes]
    ids = jnp.sum(jnp.where(lane == sub, ids, 0.0), axis=1, keepdims=True).astype(jnp.int32)
    row_top = jnp.max(logits, axis=1, keepdims=True)
    scaled = jnp.exp(logits - row_top)
    row_total = jnp.sum(scaled, axis=1, keepdims=True)
    row_weighted = jnp.sum(scaled * logits, axis=1, keepdims=True)
    column = iota(logits.shape, 1)
    other = place + 1 - 2 * half
    columns = jnp.where(column < cols, place * cols, (other - 1) * cols) + column
    picked = jnp.sum(jnp.where(columns == ids, logits, 0.0), axis=1, keepdims=True)
    stats = (row_top, row_total, row_weighted, picked)
    if PAIR * share * STATS == LANES:
        joined = picked
        for at in range(STATS - 1):
            joined = jnp.where(lane // (PAIR * share) == at, stats[at], joined)
        joined = jnp.sum(jnp.where(lane % share == sub, joined, 0.0), axis=0, keepdims=True)
        lane = iota((1, LANES), 1)
        neutral = jnp.where(lane < PAIR * share, -jnp.inf, 0.0)
        stats_ref[...] = jnp.where(lane // share % PAIR == half, joined, neutral)
    else:
        for at in range(STATS):
            line = jnp.sum(jnp.where(lane == sub, stats[at], 0.0), axis=0, keepdims=True)
            for h in range(PAIR):
                first = (at * PAIR + h) * share
                stats_ref[:, first : first + share] = jnp.where(half == h, line, 0.0 if at else -jnp.inf)


def finish_kernel(share, stats_ref, meta_ref, logprob_ref, entropy_ref, seq_ref):
    row_count = logprob_ref.shape[0]
    used = PAIR * share
    lanes = max(used, LANES)

    def stat(at):
        if used >= LANES:
            return stats_ref[:, at * used : (at + 1) * used]
        return stats_ref[...] if at == 0 else pltpu.roll(stats_ref[...], LANES - at * used, 1)

    tops = stat(0)
    row_top = jnp.max(tops, axis=0, keepdims=True)
    weight = jnp.exp(tops - row_top)
    row_total = jnp.sum(stat(1) * weight, axis=0, keepdims=True)
    row_weighted = jnp.sum(stat(2) * weight, axis=0, keepdims=True)
    picked = jnp.sum(stat(3), axis=0, keepdims=True)
    log_norm = row_top + jnp.log(row_total)
    lane, sub = iota((1, lanes), 1), iota((SUBS, lanes), 0)
    in_use = jnp.logical_and(meta_ref[4:5, :] > 0.5, lane < used)
    logprob = jnp.where(in_use, picked - log_norm, 0.0)
    entropy = jnp.where(in_use, log_norm - row_weighted / row_total, 0.0)
    segment, place = meta_ref[3:4, :].astype(jnp.int32), meta_ref[5:6, :].astype(jnp.int32)
    mine = jnp.logical_and(place == sub, lane % share // MINE == own_slot(share // MINE))

    def placed(values, wanted):
        sums = jnp.sum(jnp.where(wanted, values, 0.0), axis=1, keepdims=True)
        diagonal = iota((SUBS, LANES), 0) == iota((SUBS, LANES), 1)
        return jnp.sum(jnp.where(diagonal, sums, 0.0), axis=0)

    logprob_ref[...] = placed(logprob, mine)[:row_count]
    entropy_ref[...] = placed(entropy, mine)[:row_count]
    seq_ref[...] = placed(logprob, segment == sub)[:SEQS]


def grant(mebibytes):
    return pltpu.CompilerParams(vmem_limit_bytes=mebibytes * 1024 * 1024)


def local(hidden, norm_gain, lm_head, targets, segments, scored):
    row_count, width = hidden.shape
    groups, tp_count = lax.axis_size("req"), lax.axis_size("tp")
    span = width * MINE // SUBS
    share = groups * MINE
    lanes = max(PAIR * share, LANES)

    def spec(space):
        return pl.BlockSpec(memory_space=space)

    other = lax.ppermute(lm_head, "tp", [(i, i + 1 - 2 * (i % PAIR)) for i in range(tp_count)])
    packed = pl.pallas_call(
        functools.partial(pack_kernel, share),
        out_shape=VMEM((groups, SUBS, span + lanes), jnp.bfloat16),
        in_specs=[spec(VMEM)] * 2 + [spec(SMEM)] * 3,
        out_specs=spec(VMEM),
        scratch_shapes=[
            VMEM((row_count, width), jnp.float32),
            VMEM((SUBS, span), jnp.float32),
            VMEM((width // LANES, LANES), jnp.float32),
        ],
    )(hidden, norm_gain.reshape(width // LANES, LANES), targets, segments, scored)
    rows = lax.all_to_all(packed, "req", 0, 0, axis_index_groups=[members(groups)])
    other = pltpu.with_memory_space_constraint(other, pltpu.HBM)
    staged = width // 2
    slices = pl.pallas_call(
        functools.partial(stage_kernel, share),
        out_shape=(
            VMEM(lm_head.shape, lm_head.dtype),
            VMEM((staged, lm_head.shape[1]), lm_head.dtype),
            VMEM((groups * SUBS, groups * SUBS), jnp.bfloat16),
        ),
        in_specs=[spec(pltpu.HBM)] * 2,
        out_specs=(spec(VMEM),) * 3,
        scratch_shapes=[pltpu.SemaphoreType.DMA((2, 4))],
        compiler_params=grant(4),
        cost_estimate=pl.CostEstimate(flops=0, bytes_accessed=3 * 2 * lm_head.size, transcendentals=0),
    )(pltpu.with_memory_space_constraint(lm_head, pltpu.HBM), other)
    stats, meta = pl.pallas_call(
        score_kernel,
        out_shape=(
            jax.ShapeDtypeStruct((1, STATS * PAIR * share), jnp.float32),
            VMEM((SUBS, lanes), jnp.float32),
        ),
        in_specs=[spec(VMEM)] * 4 + [spec(pltpu.HBM)],
        out_specs=(spec(VMEM), spec(VMEM)),
        scratch_shapes=[
            VMEM((share, width), jnp.bfloat16),
            VMEM((width - staged, lm_head.shape[1]), jnp.bfloat16),
            pltpu.SemaphoreType.DMA((4,)),
        ],
        compiler_params=grant(24),
    )(rows, *(pltpu.with_memory_space_constraint(part, VMEM) for part in slices), other)
    copies = jnp.broadcast_to(stats[None], (groups * tp_count,) + stats.shape)
    gathered = lax.all_to_all(copies, ("req", "tp"), 0, 0)
    gathered = gathered.reshape(groups * tp_count, stats.shape[1])
    return pl.pallas_call(
        functools.partial(finish_kernel, share),
        out_shape=(
            jax.ShapeDtypeStruct((row_count,), jnp.float32),
            jax.ShapeDtypeStruct((row_count,), jnp.float32),
            jax.ShapeDtypeStruct((SEQS,), jnp.float32),
        ),
        in_specs=[spec(VMEM), spec(VMEM)],
        out_specs=(spec(VMEM), spec(VMEM), spec(VMEM)),
    )(pltpu.with_memory_space_constraint(gathered, VMEM), pltpu.with_memory_space_constraint(meta, VMEM))


def solution(mesh):
    return jax.shard_map(
        local,
        mesh=mesh,
        in_specs=(P("req", None), P(), P(None, ("req", "tp")), P("req"), P("req"), P("req")),
        out_specs=(P("req"), P("req"), P()),
        check_vma=False,
    )
```

```python
import functools

import jax
import jax.numpy as jnp
from jax import lax
from jax.experimental import pallas as pl
from jax.experimental.pallas import tpu as pltpu
from jax.sharding import PartitionSpec as P

SEQS = 4
PICK = 4
PAIR = 2
MINE = PICK // PAIR
SUBS = 8
LANES = 128
STATS = 4

VMEM = pltpu.VMEM
SMEM = pltpu.SMEM


def ranks_of(scored_ref, row_count):
    ranks, so_far = [], jnp.int32(0)
    for row in range(row_count):
        ranks.append(so_far)
        so_far = so_far + scored_ref[row]
    return ranks, so_far


def iota(shape, axis):
    return lax.broadcasted_iota(jnp.int32, shape, axis)


def members(count):
    return [(5 * count // 8 + at) % count for at in range(count)]


def own_slot(count):
    at = lax.axis_index("req") - 5 * count // 8
    return jnp.where(at < 0, at + count, at)


def pack_kernel(share, hidden_ref, gain_ref, targets_ref, segments_ref, scored_ref, out_ref, wide_ref, parts_ref, gains_ref):
    row_count, width = hidden_ref.shape
    parts = SUBS // MINE
    span = width // parts
    own, half = own_slot(out_ref.shape[0]), lax.axis_index("tp") % PAIR
    wide_ref[...] = hidden_ref[...].astype(jnp.float32)
    gains_ref[...] = gain_ref[...].astype(jnp.float32)
    ranks, count = ranks_of(scored_ref, row_count)
    source = [jnp.int32(0)] * PICK
    for row in range(row_count):
        for r in range(PICK):
            hit = jnp.logical_and(scored_ref[row] == 1, ranks[row] == r)
            source[r] = jnp.where(hit, row, source[r])
    mine = [source[i] for i in range(MINE)]
    for h in range(1, PAIR):
        mine = [jnp.where(half == h, source[h * MINE + i], mine[i]) for i in range(MINE)]
    for i in range(MINE):
        for k in range(parts):
            parts_ref[k * MINE + i : k * MINE + i + 1, :] = wide_ref[pl.ds(mine[i], 1), k * span : (k + 1) * span]
    values = parts_ref[...]
    part = jnp.broadcast_to(jnp.sum(values * values, axis=1, keepdims=True), (SUBS, LANES))
    total = part
    for k in range(1, parts):
        total = total + pltpu.roll(part, k * MINE, 0)
    row_scale = lax.rsqrt(total / width + 1e-05)
    sub, lane = iota((SUBS, LANES), 0), iota((SUBS, LANES), 1)
    chunks = span // LANES
    for at in range(chunks):
        gain = gains_ref[at : at + 1, :]
        for k in range(1, parts):
            gain = jnp.where(sub >= k * MINE, gains_ref[k * chunks + at : k * chunks + at + 1, :], gain)
        piece = parts_ref[:, at * LANES : (at + 1) * LANES]
        piece = (piece * row_scale * gain).astype(jnp.bfloat16)
        for to in range(out_ref.shape[0]):
            out_ref[to, :, at * LANES : (at + 1) * LANES] = piece
    width_side = out_ref.shape[2] - span
    sub, lane = iota((SUBS, width_side), 0), iota((SUBS, width_side), 1)
    at_row, at_half = lane % share - own * MINE, lane // share
    side = jnp.zeros((SUBS, width_side), jnp.int32)
    for i in range(MINE):
        target = targets_ref[mine[i]]
        digits = jnp.where(sub == 0, target & 255, jnp.where(sub == 1, (target >> 8) & 255, target >> 16))
        fields = jnp.zeros((SUBS, width_side), jnp.int32)
        for h in range(PAIR):
            r = h * MINE + i
            field = jnp.where(sub == 4, (count > r).astype(jnp.int32), source[r])
            fields = jnp.where(at_half == h, jnp.where(sub == 3, segments_ref[source[r]], field), fields)
        side = jnp.where(at_row == i, jnp.where(sub < 3, digits, fields), side)
    side = side.astype(jnp.float32).astype(jnp.bfloat16)
    for to in range(out_ref.shape[0]):
        out_ref[to, :, span:] = side


def stage_kernel(share, own_ref, other_ref, own_out, other_out, order_out, sems):
    copies = []
    for at, (source, out) in enumerate(((own_ref, own_out), (other_ref, other_out))):
        depth = out.shape[0] // sems.shape[1]
        for i in range(sems.shape[1]):
            piece = pl.ds(i * depth, depth)
            copies.append(pltpu.make_async_copy(source.at[piece], out.at[piece], sems.at[at, i]))
    for copy in copies:
        copy.start()
    into, out_of = iota(order_out.shape, 0), iota(order_out.shape, 1)
    wanted = into % share // MINE * SUBS + into // share * MINE + into % MINE
    order_out[...] = jnp.where(out_of == wanted, 1.0, 0.0).astype(jnp.bfloat16)
    for copy in copies:
        copy.wait()


def score_kernel(rows_ref, own_ref, upper_ref, order_ref, other_ref, stats_ref, meta_ref, ordered_ref, lower_ref, sems):
    width, cols = own_ref.shape
    staged = upper_ref.shape[0]
    depth = lower_ref.shape[0] // sems.shape[0]
    copies = [
        pltpu.make_async_copy(
            other_ref.at[pl.ds(staged + i * depth, depth)], lower_ref.at[pl.ds(i * depth, depth)], sems.at[i]
        )
        for i in range(sems.shape[0])
    ]
    for copy in copies:
        copy.start()
    groups = rows_ref.shape[0]
    parts = SUBS // MINE
    span = width // parts
    share = groups * MINE
    tp, tp_count = lax.axis_index("tp"), lax.axis_size("tp")
    half = tp % PAIR
    place = lax.axis_index("req") * tp_count + tp
    count = groups * SUBS
    rows = rows_ref[:, :, :span].reshape(count, span)
    ordered = jnp.dot(order_ref[...], rows, preferred_element_type=jnp.float32).astype(jnp.bfloat16)
    for k in range(parts):
        ordered_ref[:, k * span : (k + 1) * span] = ordered[k * share : (k + 1) * share]
    meta = rows_ref[0, :, span:].astype(jnp.float32)
    for q in range(1, groups):
        meta = meta + rows_ref[q, :, span:].astype(jnp.float32)
    meta_ref[...] = meta

    def product(slice_ref, first, at, depth):
        piece = pl.ds(pl.multiple_of(at * depth, depth), depth)
        rows = ordered_ref[:, pl.ds(pl.multiple_of(first + at * depth, depth), depth)]
        return jnp.dot(rows, slice_ref[piece, :], preferred_element_type=jnp.float32)

    def resident(at, sums):
        return (
            sums[0] + product(own_ref, 0, at, width // 2),
            sums[1] + product(upper_ref, 0, at, staged // 2),
        )

    def fetched(at, total):
        return total + product(lower_ref, staged, at, (width - staged) // 2)

    zeros = jnp.zeros((share, cols), jnp.float32)
    own_logits, other_logits = lax.fori_loop(0, 2, resident, (zeros, zeros))
    for copy in copies:
        copy.wait()
    logits = jnp.concatenate([own_logits, lax.fori_loop(0, 2, fetched, other_logits)], axis=1)
    lanes = max(share, LANES)
    sub, lane = iota((share, lanes), 0), iota((share, lanes), 1)
    ids = meta[0:1, :lanes] + 256.0 * meta[1:2, :lanes] + 65536.0 * meta[2:3, :lanes]
    ids = jnp.sum(jnp.where(lane == sub, ids, 0.0), axis=1, keepdims=True).astype(jnp.int32)
    row_top = jnp.max(logits, axis=1, keepdims=True)
    scaled = jnp.exp(logits - row_top)
    row_total = jnp.sum(scaled, axis=1, keepdims=True)
    row_weighted = jnp.sum(scaled * logits, axis=1, keepdims=True)
    column = iota(logits.shape, 1)
    other = place + 1 - 2 * half
    columns = jnp.where(column < cols, place * cols, (other - 1) * cols) + column
    picked = jnp.sum(jnp.where(columns == ids, logits, 0.0), axis=1, keepdims=True)
    stats = (row_top, row_total, row_weighted, picked)
    if PAIR * share * STATS == LANES:
        joined = picked
        for at in range(STATS - 1):
            joined = jnp.where(lane // (PAIR * share) == at, stats[at], joined)
        joined = jnp.sum(jnp.where(lane % share == sub, joined, 0.0), axis=0, keepdims=True)
        lane = iota((1, LANES), 1)
        neutral = jnp.where(lane < PAIR * share, -jnp.inf, 0.0)
        stats_ref[...] = jnp.where(lane // share % PAIR == half, joined, neutral)
    else:
        for at in range(STATS):
            line = jnp.sum(jnp.where(lane == sub, stats[at], 0.0), axis=0, keepdims=True)
            for h in range(PAIR):
                first = (at * PAIR + h) * share
                stats_ref[:, first : first + share] = jnp.where(half == h, line, 0.0 if at else -jnp.inf)


def finish_kernel(share, stats_ref, meta_ref, logprob_ref, entropy_ref, seq_ref):
    row_count = logprob_ref.shape[0]
    used = PAIR * share
    lanes = max(used, LANES)

    def stat(at):
        if used >= LANES:
            return stats_ref[:, at * used : (at + 1) * used]
        return stats_ref[...] if at == 0 else pltpu.roll(stats_ref[...], LANES - at * used, 1)

    tops = stat(0)
    row_top = jnp.max(tops, axis=0, keepdims=True)
    weight = jnp.exp(tops - row_top)
    row_total = jnp.sum(stat(1) * weight, axis=0, keepdims=True)
    row_weighted = jnp.sum(stat(2) * weight, axis=0, keepdims=True)
    picked = jnp.sum(stat(3), axis=0, keepdims=True)
    log_norm = row_top + jnp.log(row_total)
    lane, sub = iota((1, lanes), 1), iota((SUBS, lanes), 0)
    in_use = jnp.logical_and(meta_ref[4:5, :] > 0.5, lane < used)
    logprob = jnp.where(in_use, picked - log_norm, 0.0)
    entropy = jnp.where(in_use, log_norm - row_weighted / row_total, 0.0)
    segment, place = meta_ref[3:4, :].astype(jnp.int32), meta_ref[5:6, :].astype(jnp.int32)
    mine = jnp.logical_and(place == sub, lane % share // MINE == own_slot(share // MINE))

    def placed(values, wanted):
        sums = jnp.sum(jnp.where(wanted, values, 0.0), axis=1, keepdims=True)
        diagonal = iota((SUBS, LANES), 0) == iota((SUBS, LANES), 1)
        return jnp.sum(jnp.where(diagonal, sums, 0.0), axis=0)

    logprob_ref[...] = placed(logprob, mine)[:row_count]
    entropy_ref[...] = placed(entropy, mine)[:row_count]
    seq_ref[...] = placed(logprob, segment == sub)[:SEQS]


def grant(mebibytes):
    return pltpu.CompilerParams(vmem_limit_bytes=mebibytes * 1024 * 1024)


def local(hidden, norm_gain, lm_head, targets, segments, scored):
    row_count, width = hidden.shape
    groups, tp_count = lax.axis_size("req"), lax.axis_size("tp")
    span = width * MINE // SUBS
    share = groups * MINE
    lanes = max(PAIR * share, LANES)

    def spec(space):
        return pl.BlockSpec(memory_space=space)

    swap = [(i, i + 1 - 2 * (i % PAIR)) for i in range(tp_count)]
    other = lax.ppermute(lm_head, "tp", swap)
    packed = pl.pallas_call(
        functools.partial(pack_kernel, share),
        out_shape=VMEM((groups, SUBS, span + lanes), jnp.bfloat16),
        in_specs=[spec(VMEM)] * 2 + [spec(SMEM)] * 3,
        out_specs=spec(VMEM),
        scratch_shapes=[
            VMEM((row_count, width), jnp.float32),
            VMEM((SUBS, span), jnp.float32),
            VMEM((width // LANES, LANES), jnp.float32),
        ],
    )(hidden, norm_gain.reshape(width // LANES, LANES), targets, segments, scored)
    rows = lax.all_to_all(packed, "req", 0, 0, axis_index_groups=[members(groups)])
    other = pltpu.with_memory_space_constraint(other, pltpu.HBM)
    staged = width // 2
    slices = pl.pallas_call(
        functools.partial(stage_kernel, share),
        out_shape=(
            VMEM(lm_head.shape, lm_head.dtype),
            VMEM((staged, lm_head.shape[1]), lm_head.dtype),
            VMEM((groups * SUBS, groups * SUBS), jnp.bfloat16),
        ),
        in_specs=[spec(pltpu.HBM)] * 2,
        out_specs=(spec(VMEM),) * 3,
        scratch_shapes=[pltpu.SemaphoreType.DMA((2, 4))],
        compiler_params=grant(4),
        cost_estimate=pl.CostEstimate(flops=0, bytes_accessed=3 * 2 * lm_head.size, transcendentals=0),
    )(pltpu.with_memory_space_constraint(lm_head, pltpu.HBM), other)
    stats, meta = pl.pallas_call(
        score_kernel,
        out_shape=(
            jax.ShapeDtypeStruct((1, STATS * PAIR * share), jnp.float32),
            VMEM((SUBS, lanes), jnp.float32),
        ),
        in_specs=[spec(VMEM)] * 4 + [spec(pltpu.HBM)],
        out_specs=(spec(VMEM), spec(VMEM)),
        scratch_shapes=[
            VMEM((share, width), jnp.bfloat16),
            VMEM((width - staged, lm_head.shape[1]), jnp.bfloat16),
            pltpu.SemaphoreType.DMA((4,)),
        ],
        compiler_params=grant(24),
    )(rows, *(pltpu.with_memory_space_constraint(part, VMEM) for part in slices), other)
    swapped = lax.ppermute(stats, "tp", swap)
    stats = jnp.where(iota(stats.shape, 1) < PAIR * share, jnp.maximum(stats, swapped), stats + swapped)
    chips = groups * tp_count // PAIR
    copies = jnp.broadcast_to(stats[None], (chips,) + stats.shape)
    listed = [[*reversed(range(at, groups * tp_count, PAIR))] for at in range(PAIR)]
    gathered = lax.all_to_all(copies, ("req", "tp"), 0, 0, axis_index_groups=listed).reshape(chips, stats.shape[1])
    return pl.pallas_call(
        functools.partial(finish_kernel, share),
        out_shape=(
            jax.ShapeDtypeStruct((row_count,), jnp.float32),
            jax.ShapeDtypeStruct((row_count,), jnp.float32),
            jax.ShapeDtypeStruct((SEQS,), jnp.float32),
        ),
        in_specs=[spec(VMEM), spec(VMEM)],
        out_specs=(spec(VMEM), spec(VMEM), spec(VMEM)),
    )(pltpu.with_memory_space_constraint(gathered, VMEM), pltpu.with_memory_space_constraint(meta, VMEM))


def solution(mesh):
    return jax.shard_map(
        local,
        mesh=mesh,
        in_specs=(P("req", None), P(), P(None, ("req", "tp")), P("req"), P("req"), P("req")),
        out_specs=(P("req"), P("req"), P()),
        check_vma=False,
    )
```

```python
import functools

import jax
import jax.numpy as jnp
from jax import lax
from jax.experimental import pallas as pl
from jax.experimental.pallas import tpu as pltpu
from jax.sharding import PartitionSpec as P

SEQS = 4
PICK = 4
PAIR = 2
MINE = PICK // PAIR
SUBS = 8
LANES = 128
STATS = 4

VMEM = pltpu.VMEM
SMEM = pltpu.SMEM


def ranks_of(scored_ref, row_count):
    ranks, so_far = [], jnp.int32(0)
    for row in range(row_count):
        ranks.append(so_far)
        so_far = so_far + scored_ref[row]
    return ranks, so_far


def over(number, by):
    return number >> (by.bit_length() - 1) if by & (by - 1) == 0 else number // by


def left(number, by):
    return number & (by - 1) if by & (by - 1) == 0 else number % by


def iota(shape, axis):
    return lax.broadcasted_iota(jnp.int32, shape, axis)


def members(count):
    return [(5 * count // 8 + at) % count for at in range(count)]


def own_slot(count):
    at = lax.axis_index("req") - 5 * count // 8
    return jnp.where(at < 0, at + count, at)


def pack_kernel(share, hidden_hbm, gain_hbm, targets_hbm, segments_hbm, scored_hbm, out_ref, *scratch):
    hidden_ref, gain_ref, targets_ref, segments_ref, scored_ref, wide_ref, parts_ref, gains_ref, sems = scratch
    sources = (scored_hbm, targets_hbm, segments_hbm, hidden_hbm, gain_hbm)
    places = (scored_ref, targets_ref, segments_ref, hidden_ref, gain_ref)
    reads = [pltpu.make_async_copy(source, to, sems.at[at]) for at, (source, to) in enumerate(zip(sources, places))]
    for read in reads:
        read.start()
    row_count, width = hidden_ref.shape
    receivers = out_ref.shape[0]
    parts = SUBS // MINE
    span = width // parts
    own, half = own_slot(receivers), lax.axis_index("tp") % PAIR
    width_side = out_ref.shape[2] - span
    sub, lane = iota((SUBS, width_side), 0), iota((SUBS, width_side), 1)
    at_row, at_half = left(lane, share) - own * MINE, over(lane, share)
    for read in reads[:3]:
        read.wait()
    ranks, count = ranks_of(scored_ref, row_count)
    source = [jnp.int32(0)] * PICK
    for row in range(row_count):
        for r in range(PICK):
            hit = jnp.logical_and(scored_ref[row] == 1, ranks[row] == r)
            source[r] = jnp.where(hit, row, source[r])
    mine = [source[i] for i in range(MINE)]
    for h in range(1, PAIR):
        mine = [jnp.where(half == h, source[h * MINE + i], mine[i]) for i in range(MINE)]
    side = jnp.zeros((SUBS, width_side), jnp.int32)
    for i in range(MINE):
        target = targets_ref[mine[i]]
        digits = jnp.where(sub == 0, target & 255, jnp.where(sub == 1, (target >> 8) & 255, target >> 16))
        fields = jnp.zeros((SUBS, width_side), jnp.int32)
        for h in range(PAIR):
            r = h * MINE + i
            field = jnp.where(sub == 4, (count > r).astype(jnp.int32), source[r])
            fields = jnp.where(at_half == h, jnp.where(sub == 3, segments_ref[source[r]], field), fields)
        side = jnp.where(at_row == i, jnp.where(sub < 3, digits, fields), side)
    side = side.astype(jnp.float32).astype(jnp.bfloat16)
    for to in range(receivers):
        out_ref[to, :, span:] = side
    for read in reads[3:]:
        read.wait()
    wide_ref[...] = hidden_ref[...].astype(jnp.float32)
    gains_ref[...] = gain_ref[...].astype(jnp.float32)
    for i in range(MINE):
        for k in range(parts):
            parts_ref[k * MINE + i : k * MINE + i + 1, :] = wide_ref[pl.ds(mine[i], 1), k * span : (k + 1) * span]
    values = parts_ref[...]
    part = jnp.broadcast_to(jnp.sum(values * values, axis=1, keepdims=True), (SUBS, LANES))
    total = part
    for k in range(1, parts):
        total = total + pltpu.roll(part, k * MINE, 0)
    row_scale = lax.rsqrt(total / width + 1e-05)
    sub = iota((SUBS, LANES), 0)
    chunks = span // LANES
    for at in range(chunks):
        gain = gains_ref[at : at + 1, :]
        for k in range(1, parts):
            gain = jnp.where(sub >= k * MINE, gains_ref[k * chunks + at : k * chunks + at + 1, :], gain)
        piece = parts_ref[:, at * LANES : (at + 1) * LANES]
        piece = (piece * row_scale * gain).astype(jnp.bfloat16)
        for to in range(receivers):
            out_ref[to, :, at * LANES : (at + 1) * LANES] = piece


def stage_kernel(share, own_ref, other_ref, own_out, other_out, order_out, sems):
    copies = []
    for at, (source, out) in enumerate(((own_ref, own_out), (other_ref, other_out))):
        depth = out.shape[0] // sems.shape[1]
        for i in range(sems.shape[1]):
            piece = pl.ds(i * depth, depth)
            copies.append(pltpu.make_async_copy(source.at[piece], out.at[piece], sems.at[at, i]))
    for copy in copies:
        copy.start()
    into, out_of = iota(order_out.shape, 0), iota(order_out.shape, 1)
    wanted = into % share // MINE * SUBS + into // share * MINE + into % MINE
    order_out[...] = jnp.where(out_of == wanted, 1.0, 0.0).astype(jnp.bfloat16)
    for copy in copies:
        copy.wait()


def score_kernel(rows_ref, own_ref, upper_ref, order_ref, other_ref, stats_ref, meta_ref, ordered_ref, lower_ref, sems):
    width, cols = own_ref.shape
    staged = upper_ref.shape[0]
    depth = lower_ref.shape[0] // sems.shape[0]
    copies = [
        pltpu.make_async_copy(
            other_ref.at[pl.ds(staged + i * depth, depth)], lower_ref.at[pl.ds(i * depth, depth)], sems.at[i]
        )
        for i in range(sems.shape[0])
    ]
    for copy in copies:
        copy.start()
    groups = rows_ref.shape[0]
    parts = SUBS // MINE
    span = width // parts
    share = groups * MINE
    tp, tp_count = lax.axis_index("tp"), lax.axis_size("tp")
    half = tp % PAIR
    place = lax.axis_index("req") * tp_count + tp
    count = groups * SUBS
    rows = rows_ref[:, :, :span].reshape(count, span)
    ordered = jnp.dot(order_ref[...], rows, preferred_element_type=jnp.float32).astype(jnp.bfloat16)
    for k in range(parts):
        ordered_ref[:, k * span : (k + 1) * span] = ordered[k * share : (k + 1) * share]
    meta = rows_ref[0, :, span:].astype(jnp.float32)
    for q in range(1, groups):
        meta = meta + rows_ref[q, :, span:].astype(jnp.float32)
    meta_ref[...] = meta

    def product(slice_ref, first, at, depth):
        piece = pl.ds(pl.multiple_of(at * depth, depth), depth)
        rows = ordered_ref[:, pl.ds(pl.multiple_of(first + at * depth, depth), depth)]
        return jnp.dot(rows, slice_ref[piece, :], preferred_element_type=jnp.float32)

    def resident(at, sums):
        return (
            sums[0] + product(own_ref, 0, at, width // 2),
            sums[1] + product(upper_ref, 0, at, staged // 2),
        )

    def fetched(at, total):
        return total + product(lower_ref, staged, at, (width - staged) // 2)

    zeros = jnp.zeros((share, cols), jnp.float32)
    own_logits, other_logits = lax.fori_loop(0, 2, resident, (zeros, zeros))
    for copy in copies:
        copy.wait()
    logits = jnp.concatenate([own_logits, lax.fori_loop(0, 2, fetched, other_logits)], axis=1)
    lanes = max(share, LANES)
    sub, lane = iota((share, lanes), 0), iota((share, lanes), 1)
    ids = meta[0:1, :lanes] + 256.0 * meta[1:2, :lanes] + 65536.0 * meta[2:3, :lanes]
    ids = jnp.sum(jnp.where(lane == sub, ids, 0.0), axis=1, keepdims=True).astype(jnp.int32)
    row_top = jnp.max(logits, axis=1, keepdims=True)
    scaled = jnp.exp(logits - row_top)
    row_total = jnp.sum(scaled, axis=1, keepdims=True)
    row_weighted = jnp.sum(scaled * logits, axis=1, keepdims=True)
    column = iota(logits.shape, 1)
    other = place + 1 - 2 * half
    columns = jnp.where(column < cols, place * cols, (other - 1) * cols) + column
    picked = jnp.sum(jnp.where(columns == ids, logits, 0.0), axis=1, keepdims=True)
    stats = (row_top, row_total, row_weighted, picked)
    if PAIR * share * STATS == LANES:
        joined = picked
        for at in range(STATS - 1):
            joined = jnp.where(lane // (PAIR * share) == at, stats[at], joined)
        joined = jnp.sum(jnp.where(lane % share == sub, joined, 0.0), axis=0, keepdims=True)
        lane = iota((1, LANES), 1)
        neutral = jnp.where(lane < PAIR * share, -jnp.inf, 0.0)
        stats_ref[...] = jnp.where(lane // share % PAIR == half, joined, neutral)
    else:
        for at in range(STATS):
            line = jnp.sum(jnp.where(lane == sub, stats[at], 0.0), axis=0, keepdims=True)
            for h in range(PAIR):
                first = (at * PAIR + h) * share
                stats_ref[:, first : first + share] = jnp.where(half == h, line, 0.0 if at else -jnp.inf)


def finish_kernel(share, stats_ref, meta_ref, logprob_ref, entropy_ref, seq_ref):
    row_count = logprob_ref.shape[0]
    used = PAIR * share
    lanes = max(used, LANES)

    def stat(at):
        if used >= LANES:
            return stats_ref[:, at * used : (at + 1) * used]
        return stats_ref[...] if at == 0 else pltpu.roll(stats_ref[...], LANES - at * used, 1)

    tops = stat(0)
    row_top = jnp.max(tops, axis=0, keepdims=True)
    weight = jnp.exp(tops - row_top)
    row_total = jnp.sum(stat(1) * weight, axis=0, keepdims=True)
    row_weighted = jnp.sum(stat(2) * weight, axis=0, keepdims=True)
    picked = jnp.sum(stat(3), axis=0, keepdims=True)
    log_norm = row_top + jnp.log(row_total)
    lane, sub = iota((1, lanes), 1), iota((SUBS, lanes), 0)
    in_use = jnp.logical_and(meta_ref[4:5, :] > 0.5, lane < used)
    logprob = jnp.where(in_use, picked - log_norm, 0.0)
    entropy = jnp.where(in_use, log_norm - row_weighted / row_total, 0.0)
    segment, place = meta_ref[3:4, :].astype(jnp.int32), meta_ref[5:6, :].astype(jnp.int32)
    mine = jnp.logical_and(place == sub, lane % share // MINE == own_slot(share // MINE))

    def placed(values, wanted):
        sums = jnp.sum(jnp.where(wanted, values, 0.0), axis=1, keepdims=True)
        diagonal = iota((SUBS, LANES), 0) == iota((SUBS, LANES), 1)
        return jnp.sum(jnp.where(diagonal, sums, 0.0), axis=0)

    logprob_ref[...] = placed(logprob, mine)[:row_count]
    entropy_ref[...] = placed(entropy, mine)[:row_count]
    seq_ref[...] = placed(logprob, segment == sub)[:SEQS]


def grant(mebibytes):
    return pltpu.CompilerParams(vmem_limit_bytes=mebibytes * 1024 * 1024)


def local(hidden, norm_gain, lm_head, targets, segments, scored):
    row_count, width = hidden.shape
    groups, tp_count = lax.axis_size("req"), lax.axis_size("tp")
    span = width * MINE // SUBS
    share = groups * MINE
    lanes = max(PAIR * share, LANES)

    def spec(space):
        return pl.BlockSpec(memory_space=space)

    swap = [(i, i + 1 - 2 * (i % PAIR)) for i in range(tp_count)]
    other = lax.ppermute(lm_head, "tp", swap)
    packed = pl.pallas_call(
        functools.partial(pack_kernel, share),
        out_shape=jax.ShapeDtypeStruct((groups, SUBS, span + lanes), jnp.bfloat16),
        in_specs=[spec(pltpu.HBM)] * 5,
        out_specs=spec(VMEM),
        scratch_shapes=[
            VMEM((row_count, width), jnp.bfloat16),
            VMEM((width // LANES, LANES), jnp.bfloat16),
            *[SMEM((row_count,), jnp.int32)] * 3,
            VMEM((row_count, width), jnp.float32),
            VMEM((SUBS, span), jnp.float32),
            VMEM((width // LANES, LANES), jnp.float32),
            pltpu.SemaphoreType.DMA((5,)),
        ],
    )(hidden, norm_gain.reshape(width // LANES, LANES), targets, segments, scored)
    rows = lax.all_to_all(packed, "req", 0, 0, axis_index_groups=[members(groups)])
    other = pltpu.with_memory_space_constraint(other, pltpu.HBM)
    staged = width // 2
    slices = pl.pallas_call(
        functools.partial(stage_kernel, share),
        out_shape=(
            VMEM(lm_head.shape, lm_head.dtype),
            VMEM((staged, lm_head.shape[1]), lm_head.dtype),
            VMEM((groups * SUBS, groups * SUBS), jnp.bfloat16),
        ),
        in_specs=[spec(pltpu.HBM)] * 2,
        out_specs=(spec(VMEM),) * 3,
        scratch_shapes=[pltpu.SemaphoreType.DMA((2, 4))],
        compiler_params=grant(4),
        cost_estimate=pl.CostEstimate(flops=0, bytes_accessed=3 * 2 * lm_head.size, transcendentals=0),
    )(pltpu.with_memory_space_constraint(lm_head, pltpu.HBM), other)
    stats, meta = pl.pallas_call(
        score_kernel,
        out_shape=(
            jax.ShapeDtypeStruct((1, STATS * PAIR * share), jnp.float32),
            VMEM((SUBS, lanes), jnp.float32),
        ),
        in_specs=[spec(VMEM)] * 4 + [spec(pltpu.HBM)],
        out_specs=(spec(VMEM), spec(VMEM)),
        scratch_shapes=[
            VMEM((share, width), jnp.bfloat16),
            VMEM((width - staged, lm_head.shape[1]), jnp.bfloat16),
            pltpu.SemaphoreType.DMA((4,)),
        ],
        compiler_params=grant(24),
    )(rows, *(pltpu.with_memory_space_constraint(part, VMEM) for part in slices), other)
    swapped = lax.ppermute(stats, "tp", swap)
    stats = jnp.where(iota(stats.shape, 1) < PAIR * share, jnp.maximum(stats, swapped), stats + swapped)
    chips = groups * tp_count // PAIR
    copies = jnp.broadcast_to(stats[None], (chips,) + stats.shape)
    listed = [[*reversed(range(at, groups * tp_count, PAIR))] for at in range(PAIR)]
    gathered = lax.all_to_all(copies, ("req", "tp"), 0, 0, axis_index_groups=listed).reshape(chips, stats.shape[1])
    return pl.pallas_call(
        functools.partial(finish_kernel, share),
        out_shape=(
            jax.ShapeDtypeStruct((row_count,), jnp.float32),
            jax.ShapeDtypeStruct((row_count,), jnp.float32),
            jax.ShapeDtypeStruct((SEQS,), jnp.float32),
        ),
        in_specs=[spec(VMEM), spec(VMEM)],
        out_specs=(spec(VMEM), spec(VMEM), spec(VMEM)),
    )(pltpu.with_memory_space_constraint(gathered, VMEM), pltpu.with_memory_space_constraint(meta, VMEM))


def solution(mesh):
    return jax.shard_map(
        local,
        mesh=mesh,
        in_specs=(P("req", None), P(), P(None, ("req", "tp")), P("req"), P("req"), P("req")),
        out_specs=(P("req"), P("req"), P()),
        check_vma=False,
    )
```

```python
import functools

import jax
import jax.numpy as jnp
from jax import lax
from jax.experimental import pallas as pl
from jax.experimental.pallas import tpu as pltpu
from jax.sharding import PartitionSpec as P

SEQS = 4
PICK = 4
PAIR = 2
MINE = PICK // PAIR
SUBS = 8
LANES = 128
STATS = 4

VMEM = pltpu.VMEM
SMEM = pltpu.SMEM


def ranks_of(scored_ref, row_count):
    ranks, so_far = [], jnp.int32(0)
    for row in range(row_count):
        ranks.append(so_far)
        so_far = so_far + scored_ref[row]
    return ranks, so_far


def iota(shape, axis):
    return lax.broadcasted_iota(jnp.int32, shape, axis)


def members(count):
    return [(5 * count // 8 + at) % count for at in range(count)]


def own_slot(count):
    at = lax.axis_index("req") - 5 * count // 8
    return jnp.where(at < 0, at + count, at)


def pack_kernel(share, hidden_ref, gain_ref, targets_ref, segments_ref, scored_ref, out_ref, wide_ref, parts_ref, gains_ref):
    row_count, width = hidden_ref.shape
    parts = SUBS // MINE
    span = width // parts
    own, half = own_slot(out_ref.shape[0]), lax.axis_index("tp") % PAIR
    wide_ref[...] = hidden_ref[...].astype(jnp.float32)
    gains_ref[...] = gain_ref[...].astype(jnp.float32)
    ranks, count = ranks_of(scored_ref, row_count)
    source = [jnp.int32(0)] * PICK
    for row in range(row_count):
        for r in range(PICK):
            hit = jnp.logical_and(scored_ref[row] == 1, ranks[row] == r)
            source[r] = jnp.where(hit, row, source[r])
    mine = [source[i] for i in range(MINE)]
    for h in range(1, PAIR):
        mine = [jnp.where(half == h, source[h * MINE + i], mine[i]) for i in range(MINE)]
    for i in range(MINE):
        for k in range(parts):
            parts_ref[k * MINE + i : k * MINE + i + 1, :] = wide_ref[pl.ds(mine[i], 1), k * span : (k + 1) * span]
    values = parts_ref[...]
    part = jnp.broadcast_to(jnp.sum(values * values, axis=1, keepdims=True), (SUBS, LANES))
    total = part
    for k in range(1, parts):
        total = total + pltpu.roll(part, k * MINE, 0)
    row_scale = lax.rsqrt(total / width + 1e-05)
    sub, lane = iota((SUBS, LANES), 0), iota((SUBS, LANES), 1)
    chunks = span // LANES
    for at in range(chunks):
        gain = gains_ref[at : at + 1, :]
        for k in range(1, parts):
            gain = jnp.where(sub >= k * MINE, gains_ref[k * chunks + at : k * chunks + at + 1, :], gain)
        piece = parts_ref[:, at * LANES : (at + 1) * LANES]
        piece = (piece * row_scale * gain).astype(jnp.bfloat16)
        for to in range(out_ref.shape[0]):
            out_ref[to, :, at * LANES : (at + 1) * LANES] = piece
    width_side = out_ref.shape[2] - span
    sub, lane = iota((SUBS, width_side), 0), iota((SUBS, width_side), 1)
    at_row, at_half = lane % share - own * MINE, lane // share
    side = jnp.zeros((SUBS, width_side), jnp.int32)
    for i in range(MINE):
        target = targets_ref[mine[i]]
        digits = jnp.where(sub == 0, target & 255, jnp.where(sub == 1, (target >> 8) & 255, target >> 16))
        fields = jnp.zeros((SUBS, width_side), jnp.int32)
        for h in range(PAIR):
            r = h * MINE + i
            field = jnp.where(sub == 4, (count > r).astype(jnp.int32), source[r])
            fields = jnp.where(at_half == h, jnp.where(sub == 3, segments_ref[source[r]], field), fields)
        side = jnp.where(at_row == i, jnp.where(sub < 3, digits, fields), side)
    side = side.astype(jnp.float32).astype(jnp.bfloat16)
    for to in range(out_ref.shape[0]):
        out_ref[to, :, span:] = side


def stage_kernel(share, own_ref, other_ref, own_out, other_out, order_out, sems):
    copies = []
    for at, (source, out) in enumerate(((own_ref, own_out), (other_ref, other_out))):
        depth = out.shape[0] // sems.shape[1]
        for i in range(sems.shape[1]):
            piece = pl.ds(i * depth, depth)
            copies.append(pltpu.make_async_copy(source.at[piece], out.at[piece], sems.at[at, i]))
    for copy in copies:
        copy.start()
    into, out_of = iota(order_out.shape, 0), iota(order_out.shape, 1)
    wanted = into % share // MINE * SUBS + into // share * MINE + into % MINE
    order_out[...] = jnp.where(out_of == wanted, 1.0, 0.0).astype(jnp.bfloat16)
    for copy in copies:
        copy.wait()


def score_kernel(rows_ref, own_ref, upper_ref, order_ref, other_ref, stats_ref, meta_ref, ordered_ref, lower_ref, sems):
    width, cols = own_ref.shape
    staged = upper_ref.shape[0]
    depth = lower_ref.shape[0] // sems.shape[0]
    copies = [
        pltpu.make_async_copy(
            other_ref.at[pl.ds(staged + i * depth, depth)], lower_ref.at[pl.ds(i * depth, depth)], sems.at[i]
        )
        for i in range(sems.shape[0])
    ]
    for copy in copies:
        copy.start()
    groups = rows_ref.shape[0]
    parts = SUBS // MINE
    span = width // parts
    share = groups * MINE
    tp, tp_count = lax.axis_index("tp"), lax.axis_size("tp")
    half = tp % PAIR
    place = lax.axis_index("req") * tp_count + tp
    count = groups * SUBS
    rows = rows_ref[:, :, :span].reshape(count, span)
    ordered = jnp.dot(order_ref[...], rows, preferred_element_type=jnp.float32).astype(jnp.bfloat16)
    for k in range(parts):
        ordered_ref[:, k * span : (k + 1) * span] = ordered[k * share : (k + 1) * share]
    meta = rows_ref[0, :, span:].astype(jnp.float32)
    for q in range(1, groups):
        meta = meta + rows_ref[q, :, span:].astype(jnp.float32)
    meta_ref[...] = meta

    def product(slice_ref, first, at, depth):
        piece = pl.ds(pl.multiple_of(at * depth, depth), depth)
        rows = ordered_ref[:, pl.ds(pl.multiple_of(first + at * depth, depth), depth)]
        return jnp.dot(rows, slice_ref[piece, :], preferred_element_type=jnp.float32)

    def resident(at, sums):
        return (
            sums[0] + product(own_ref, 0, at, width // 2),
            sums[1] + product(upper_ref, 0, at, staged // 2),
        )

    def fetched(at, total):
        return total + product(lower_ref, staged, at, (width - staged) // 2)

    zeros = jnp.zeros((share, cols), jnp.float32)
    own_logits, other_logits = lax.fori_loop(0, 2, resident, (zeros, zeros))
    for copy in copies:
        copy.wait()
    logits = jnp.concatenate([own_logits, lax.fori_loop(0, 2, fetched, other_logits)], axis=1)
    lanes = max(share, LANES)
    sub, lane = iota((share, lanes), 0), iota((share, lanes), 1)
    ids = meta[0:1, :lanes] + 256.0 * meta[1:2, :lanes] + 65536.0 * meta[2:3, :lanes]
    ids = jnp.sum(jnp.where(lane == sub, ids, 0.0), axis=1, keepdims=True).astype(jnp.int32)
    row_top = jnp.max(logits, axis=1, keepdims=True)
    scaled = jnp.exp(logits - row_top)
    row_total = jnp.sum(scaled, axis=1, keepdims=True)
    row_weighted = jnp.sum(scaled * logits, axis=1, keepdims=True)
    column = iota(logits.shape, 1)
    other = place + 1 - 2 * half
    columns = jnp.where(column < cols, place * cols, (other - 1) * cols) + column
    picked = jnp.sum(jnp.where(columns == ids, logits, 0.0), axis=1, keepdims=True)
    stats = (row_top, row_total, row_weighted, picked)
    if PAIR * share * STATS == LANES:
        joined = picked
        for at in range(STATS - 1):
            joined = jnp.where(lane // (PAIR * share) == at, stats[at], joined)
        joined = jnp.sum(jnp.where(lane % share == sub, joined, 0.0), axis=0, keepdims=True)
        lane = iota((1, LANES), 1)
        neutral = jnp.where(lane < PAIR * share, -jnp.inf, 0.0)
        stats_ref[...] = jnp.where(lane // share % PAIR == half, joined, neutral)
    else:
        for at in range(STATS):
            line = jnp.sum(jnp.where(lane == sub, stats[at], 0.0), axis=0, keepdims=True)
            for h in range(PAIR):
                first = (at * PAIR + h) * share
                stats_ref[:, first : first + share] = jnp.where(half == h, line, 0.0 if at else -jnp.inf)


def finish_kernel(share, stats_ref, meta_ref, logprob_ref, entropy_ref, seq_ref):
    row_count = logprob_ref.shape[0]
    used = PAIR * share
    lanes = max(used, LANES)

    def stat(at):
        if used >= LANES:
            return stats_ref[:, at * used : (at + 1) * used]
        return stats_ref[...] if at == 0 else pltpu.roll(stats_ref[...], LANES - at * used, 1)

    tops = stat(0)
    row_top = jnp.max(tops, axis=0, keepdims=True)
    weight = jnp.exp(tops - row_top)
    row_total = jnp.sum(stat(1) * weight, axis=0, keepdims=True)
    row_weighted = jnp.sum(stat(2) * weight, axis=0, keepdims=True)
    picked = jnp.sum(stat(3), axis=0, keepdims=True)
    log_norm = row_top + jnp.log(row_total)
    lane, sub = iota((1, lanes), 1), iota((SUBS, lanes), 0)
    in_use = jnp.logical_and(meta_ref[4:5, :] > 0.5, lane < used)
    logprob = jnp.where(in_use, picked - log_norm, 0.0)
    entropy = jnp.where(in_use, log_norm - row_weighted / row_total, 0.0)
    segment, place = meta_ref[3:4, :].astype(jnp.int32), meta_ref[5:6, :].astype(jnp.int32)
    mine = jnp.logical_and(place == sub, lane % share // MINE == own_slot(share // MINE))

    def placed(values, wanted):
        sums = jnp.sum(jnp.where(wanted, values, 0.0), axis=1, keepdims=True)
        diagonal = iota((SUBS, LANES), 0) == iota((SUBS, LANES), 1)
        return jnp.sum(jnp.where(diagonal, sums, 0.0), axis=0)

    logprob_ref[...] = placed(logprob, mine)[:row_count]
    entropy_ref[...] = placed(entropy, mine)[:row_count]
    seq_ref[...] = placed(logprob, segment == sub)[:SEQS]


def grant(mebibytes):
    return pltpu.CompilerParams(vmem_limit_bytes=mebibytes * 1024 * 1024)


def local(hidden, norm_gain, lm_head, targets, segments, scored):
    row_count, width = hidden.shape
    groups, tp_count = lax.axis_size("req"), lax.axis_size("tp")
    span = width * MINE // SUBS
    share = groups * MINE
    lanes = max(PAIR * share, LANES)

    def spec(space):
        return pl.BlockSpec(memory_space=space)

    swap = [(i, i + 1 - 2 * (i % PAIR)) for i in range(tp_count)]
    other = lax.ppermute(lm_head, "tp", swap)
    packed = pl.pallas_call(
        functools.partial(pack_kernel, share),
        out_shape=VMEM((groups, SUBS, span + lanes), jnp.bfloat16),
        in_specs=[spec(VMEM)] * 2 + [spec(SMEM)] * 3,
        out_specs=spec(VMEM),
        scratch_shapes=[
            VMEM((row_count, width), jnp.float32),
            VMEM((SUBS, span), jnp.float32),
            VMEM((width // LANES, LANES), jnp.float32),
        ],
    )(hidden, norm_gain.reshape(width // LANES, LANES), targets, segments, scored)
    rows = lax.all_to_all(packed, "req", 0, 0, axis_index_groups=[members(groups)])
    other = pltpu.with_memory_space_constraint(other, pltpu.HBM)
    staged = width // 2
    slices = pl.pallas_call(
        functools.partial(stage_kernel, share),
        out_shape=(
            VMEM(lm_head.shape, lm_head.dtype),
            VMEM((staged, lm_head.shape[1]), lm_head.dtype),
            VMEM((groups * SUBS, groups * SUBS), jnp.bfloat16),
        ),
        in_specs=[spec(pltpu.HBM)] * 2,
        out_specs=(spec(VMEM),) * 3,
        scratch_shapes=[pltpu.SemaphoreType.DMA((2, 4))],
        compiler_params=grant(4),
        cost_estimate=pl.CostEstimate(flops=0, bytes_accessed=3 * 2 * lm_head.size, transcendentals=0),
    )(pltpu.with_memory_space_constraint(lm_head, pltpu.HBM), other)
    stats, meta = pl.pallas_call(
        score_kernel,
        out_shape=(
            jax.ShapeDtypeStruct((1, STATS * PAIR * share), jnp.float32),
            VMEM((SUBS, lanes), jnp.float32),
        ),
        in_specs=[spec(VMEM)] * 4 + [spec(pltpu.HBM)],
        out_specs=(spec(VMEM), spec(VMEM)),
        scratch_shapes=[
            VMEM((share, width), jnp.bfloat16),
            VMEM((width - staged, lm_head.shape[1]), jnp.bfloat16),
            pltpu.SemaphoreType.DMA((4,)),
        ],
        compiler_params=grant(24),
    )(rows, *(pltpu.with_memory_space_constraint(part, VMEM) for part in slices), other)
    swapped = lax.ppermute(stats, "tp", swap)
    stats = jnp.where(iota(stats.shape, 1) < PAIR * share, jnp.maximum(stats, swapped), stats + swapped)
    chips = groups * tp_count // PAIR
    copies = jnp.broadcast_to(stats[None], (chips,) + stats.shape)
    first = 5 * groups // 8
    order = [*reversed(range(first + 1)), *reversed(range(first + 1, groups))]
    listed = [[q * tp_count + t for q in order for t in reversed(range(at, tp_count, PAIR))] for at in range(PAIR)]
    gathered = lax.all_to_all(copies, ("req", "tp"), 0, 0, axis_index_groups=listed).reshape(chips, stats.shape[1])
    return pl.pallas_call(
        functools.partial(finish_kernel, share),
        out_shape=(
            jax.ShapeDtypeStruct((row_count,), jnp.float32),
            jax.ShapeDtypeStruct((row_count,), jnp.float32),
            jax.ShapeDtypeStruct((SEQS,), jnp.float32),
        ),
        in_specs=[spec(VMEM), spec(VMEM)],
        out_specs=(spec(VMEM), spec(VMEM), spec(VMEM)),
    )(pltpu.with_memory_space_constraint(gathered, VMEM), pltpu.with_memory_space_constraint(meta, VMEM))


def solution(mesh):
    return jax.shard_map(
        local,
        mesh=mesh,
        in_specs=(P("req", None), P(), P(None, ("req", "tp")), P("req"), P("req"), P("req")),
        out_specs=(P("req"), P("req"), P()),
        check_vma=False,
    )
```

```python
import functools

import jax
import jax.numpy as jnp
from jax import lax
from jax.experimental import pallas as pl
from jax.experimental.pallas import tpu as pltpu
from jax.sharding import PartitionSpec as P

SEQS = 4
PICK = 4
PAIR = 2
MINE = PICK // PAIR
SUBS = 8
LANES = 128
STATS = 4

VMEM = pltpu.VMEM
SMEM = pltpu.SMEM


def ranks_of(scored_ref, row_count):
    ranks, so_far = [], jnp.int32(0)
    for row in range(row_count):
        ranks.append(so_far)
        so_far = so_far + scored_ref[row]
    return ranks, so_far


def iota(shape, axis):
    return lax.broadcasted_iota(jnp.int32, shape, axis)


def members(count):
    return [(5 * count // 8 + at) % count for at in range(count)]


def own_slot(count):
    at = lax.axis_index("req") - 5 * count // 8
    return jnp.where(at < 0, at + count, at)


def pack_kernel(share, hidden_ref, gain_ref, targets_ref, segments_ref, scored_ref, out_ref, wide_ref, parts_ref, gains_ref):
    row_count, width = hidden_ref.shape
    parts = SUBS // MINE
    span = width // parts
    own, half = own_slot(out_ref.shape[0]), lax.axis_index("tp") % PAIR
    wide_ref[...] = hidden_ref[...].astype(jnp.float32)
    gains_ref[...] = gain_ref[...].astype(jnp.float32)
    ranks, count = ranks_of(scored_ref, row_count)
    source = [jnp.int32(0)] * PICK
    for row in range(row_count):
        for r in range(PICK):
            hit = jnp.logical_and(scored_ref[row] == 1, ranks[row] == r)
            source[r] = jnp.where(hit, row, source[r])
    mine = [source[i] for i in range(MINE)]
    for h in range(1, PAIR):
        mine = [jnp.where(half == h, source[h * MINE + i], mine[i]) for i in range(MINE)]
    for i in range(MINE):
        for k in range(parts):
            parts_ref[k * MINE + i : k * MINE + i + 1, :] = wide_ref[pl.ds(mine[i], 1), k * span : (k + 1) * span]
    values = parts_ref[...]
    part = jnp.broadcast_to(jnp.sum(values * values, axis=1, keepdims=True), (SUBS, LANES))
    total = part
    for k in range(1, parts):
        total = total + pltpu.roll(part, k * MINE, 0)
    row_scale = lax.rsqrt(total / width + 1e-05)
    sub, lane = iota((SUBS, LANES), 0), iota((SUBS, LANES), 1)
    chunks = span // LANES
    for at in range(chunks):
        gain = gains_ref[at : at + 1, :]
        for k in range(1, parts):
            gain = jnp.where(sub >= k * MINE, gains_ref[k * chunks + at : k * chunks + at + 1, :], gain)
        piece = parts_ref[:, at * LANES : (at + 1) * LANES]
        piece = (piece * row_scale * gain).astype(jnp.bfloat16)
        for to in range(out_ref.shape[0]):
            out_ref[to, :, at * LANES : (at + 1) * LANES] = piece
    width_side = out_ref.shape[2] - span
    sub, lane = iota((SUBS, width_side), 0), iota((SUBS, width_side), 1)
    at_row, at_half = lane % share - own * MINE, lane // share
    side = jnp.zeros((SUBS, width_side), jnp.int32)
    for i in range(MINE):
        target = targets_ref[mine[i]]
        digits = jnp.where(sub == 0, target & 255, jnp.where(sub == 1, (target >> 8) & 255, target >> 16))
        fields = jnp.zeros((SUBS, width_side), jnp.int32)
        for h in range(PAIR):
            r = h * MINE + i
            field = jnp.where(sub == 4, (count > r).astype(jnp.int32), source[r])
            fields = jnp.where(at_half == h, jnp.where(sub == 3, segments_ref[source[r]], field), fields)
        side = jnp.where(at_row == i, jnp.where(sub < 3, digits, fields), side)
    side = side.astype(jnp.float32).astype(jnp.bfloat16)
    for to in range(out_ref.shape[0]):
        out_ref[to, :, span:] = side


def stage_kernel(share, own_ref, other_ref, own_out, other_out, order_out, sems):
    copies = []
    for at, (source, out) in enumerate(((own_ref, own_out), (other_ref, other_out))):
        depth = out.shape[0] // sems.shape[1]
        for i in range(sems.shape[1]):
            piece = pl.ds(i * depth, depth)
            copies.append(pltpu.make_async_copy(source.at[piece], out.at[piece], sems.at[at, i]))
    for copy in copies:
        copy.start()
    into, out_of = iota(order_out.shape, 0), iota(order_out.shape, 1)
    wanted = into % share // MINE * SUBS + into // share * MINE + into % MINE
    order_out[...] = jnp.where(out_of == wanted, 1.0, 0.0).astype(jnp.bfloat16)
    for copy in copies:
        copy.wait()


def score_kernel(rows_ref, own_ref, upper_ref, order_ref, other_ref, stats_ref, meta_ref, ordered_ref, lower_ref, sems):
    width, cols = own_ref.shape
    staged = upper_ref.shape[0]
    depth = lower_ref.shape[0] // sems.shape[0]
    copies = [
        pltpu.make_async_copy(
            other_ref.at[pl.ds(staged + i * depth, depth)], lower_ref.at[pl.ds(i * depth, depth)], sems.at[i]
        )
        for i in range(sems.shape[0])
    ]
    for copy in copies:
        copy.start()
    groups = rows_ref.shape[0]
    parts = SUBS // MINE
    span = width // parts
    share = groups * MINE
    tp, tp_count = lax.axis_index("tp"), lax.axis_size("tp")
    half = tp % PAIR
    place = lax.axis_index("req") * tp_count + tp
    count = groups * SUBS
    rows = rows_ref[:, :, :span].reshape(count, span)
    ordered = jnp.dot(order_ref[...], rows, preferred_element_type=jnp.float32).astype(jnp.bfloat16)
    for k in range(parts):
        ordered_ref[:, k * span : (k + 1) * span] = ordered[k * share : (k + 1) * share]
    meta = rows_ref[0, :, span:].astype(jnp.float32)
    for q in range(1, groups):
        meta = meta + rows_ref[q, :, span:].astype(jnp.float32)
    meta_ref[...] = meta

    def product(slice_ref, first, at, depth):
        piece = pl.ds(pl.multiple_of(at * depth, depth), depth)
        rows = ordered_ref[:, pl.ds(pl.multiple_of(first + at * depth, depth), depth)]
        return jnp.dot(rows, slice_ref[piece, :], preferred_element_type=jnp.float32)

    def resident(at, sums):
        return (
            sums[0] + product(own_ref, 0, at, width // 2),
            sums[1] + product(upper_ref, 0, at, staged // 2),
        )

    def fetched(at, total):
        return total + product(lower_ref, staged, at, (width - staged) // 2)

    zeros = jnp.zeros((share, cols), jnp.float32)
    own_logits, other_logits = lax.fori_loop(0, 2, resident, (zeros, zeros))
    for copy in copies:
        copy.wait()
    logits = jnp.concatenate([own_logits, lax.fori_loop(0, 2, fetched, other_logits)], axis=1)
    lanes = max(share, LANES)
    sub, lane = iota((share, lanes), 0), iota((share, lanes), 1)
    ids = meta[0:1, :lanes] + 256.0 * meta[1:2, :lanes] + 65536.0 * meta[2:3, :lanes]
    ids = jnp.sum(jnp.where(lane == sub, ids, 0.0), axis=1, keepdims=True).astype(jnp.int32)
    row_top = jnp.max(logits, axis=1, keepdims=True)
    scaled = jnp.exp(logits - row_top)
    row_total = jnp.sum(scaled, axis=1, keepdims=True)
    row_weighted = jnp.sum(scaled * logits, axis=1, keepdims=True)
    column = iota(logits.shape, 1)
    other = place + 1 - 2 * half
    columns = jnp.where(column < cols, place * cols, (other - 1) * cols) + column
    picked = jnp.sum(jnp.where(columns == ids, logits, 0.0), axis=1, keepdims=True)
    stats = (row_top, row_total, row_weighted, picked)
    if PAIR * share * STATS == LANES:
        joined = picked
        for at in range(STATS - 1):
            joined = jnp.where(lane // (PAIR * share) == at, stats[at], joined)
        joined = jnp.sum(jnp.where(lane % share == sub, joined, 0.0), axis=0, keepdims=True)
        lane = iota((1, LANES), 1)
        neutral = jnp.where(lane < PAIR * share, -jnp.inf, 0.0)
        stats_ref[...] = jnp.where(lane // share % PAIR == half, joined, neutral)
    else:
        for at in range(STATS):
            line = jnp.sum(jnp.where(lane == sub, stats[at], 0.0), axis=0, keepdims=True)
            for h in range(PAIR):
                first = (at * PAIR + h) * share
                stats_ref[:, first : first + share] = jnp.where(half == h, line, 0.0 if at else -jnp.inf)


def finish_kernel(share, stats_ref, meta_ref, logprob_ref, entropy_ref, seq_ref):
    row_count = logprob_ref.shape[0]
    used = PAIR * share
    lanes = max(used, LANES)

    def stat(at):
        if used >= LANES:
            return stats_ref[:, at * used : (at + 1) * used]
        return stats_ref[...] if at == 0 else pltpu.roll(stats_ref[...], LANES - at * used, 1)

    tops = stat(0)
    row_top = jnp.max(tops, axis=0, keepdims=True)
    weight = jnp.exp(tops - row_top)
    row_total = jnp.sum(stat(1) * weight, axis=0, keepdims=True)
    row_weighted = jnp.sum(stat(2) * weight, axis=0, keepdims=True)
    picked = jnp.sum(stat(3), axis=0, keepdims=True)
    log_norm = row_top + jnp.log(row_total)
    lane, sub = iota((1, lanes), 1), iota((SUBS, lanes), 0)
    in_use = jnp.logical_and(meta_ref[4:5, :] > 0.5, lane < used)
    logprob = jnp.where(in_use, picked - log_norm, 0.0)
    entropy = jnp.where(in_use, log_norm - row_weighted / row_total, 0.0)
    segment, place = meta_ref[3:4, :].astype(jnp.int32), meta_ref[5:6, :].astype(jnp.int32)
    mine = jnp.logical_and(place == sub, lane % share // MINE == own_slot(share // MINE))

    def placed(values, wanted):
        sums = jnp.sum(jnp.where(wanted, values, 0.0), axis=1, keepdims=True)
        diagonal = iota((SUBS, LANES), 0) == iota((SUBS, LANES), 1)
        return jnp.sum(jnp.where(diagonal, sums, 0.0), axis=0)

    logprob_ref[...] = placed(logprob, mine)[:row_count]
    entropy_ref[...] = placed(entropy, mine)[:row_count]
    seq_ref[...] = placed(logprob, segment == sub)[:SEQS]


def grant(mebibytes):
    return pltpu.CompilerParams(vmem_limit_bytes=mebibytes * 1024 * 1024)


def local(hidden, norm_gain, lm_head, targets, segments, scored):
    row_count, width = hidden.shape
    groups, tp_count = lax.axis_size("req"), lax.axis_size("tp")
    span = width * MINE // SUBS
    share = groups * MINE
    lanes = max(PAIR * share, LANES)

    def spec(space):
        return pl.BlockSpec(memory_space=space)

    swap = [(i, i + 1 - 2 * (i % PAIR)) for i in range(tp_count)]
    other = lax.ppermute(lm_head, "tp", swap)
    packed = pl.pallas_call(
        functools.partial(pack_kernel, share),
        out_shape=VMEM((groups, SUBS, span + lanes), jnp.bfloat16),
        in_specs=[spec(VMEM)] * 2 + [spec(SMEM)] * 3,
        out_specs=spec(VMEM),
        scratch_shapes=[
            VMEM((row_count, width), jnp.float32),
            VMEM((SUBS, span), jnp.float32),
            VMEM((width // LANES, LANES), jnp.float32),
        ],
    )(hidden, norm_gain.reshape(width // LANES, LANES), targets, segments, scored)
    rows = lax.all_to_all(packed, "req", 0, 0, axis_index_groups=[members(groups)])
    other = pltpu.with_memory_space_constraint(other, pltpu.HBM)
    staged = width // 2
    slices = pl.pallas_call(
        functools.partial(stage_kernel, share),
        out_shape=(
            VMEM(lm_head.shape, lm_head.dtype),
            VMEM((staged, lm_head.shape[1]), lm_head.dtype),
            VMEM((groups * SUBS, groups * SUBS), jnp.bfloat16),
        ),
        in_specs=[spec(pltpu.HBM)] * 2,
        out_specs=(spec(VMEM),) * 3,
        scratch_shapes=[pltpu.SemaphoreType.DMA((2, 4))],
        compiler_params=grant(4),
        cost_estimate=pl.CostEstimate(flops=0, bytes_accessed=3 * 2 * lm_head.size, transcendentals=0),
    )(pltpu.with_memory_space_constraint(lm_head, pltpu.HBM), other)
    stats, meta = pl.pallas_call(
        score_kernel,
        out_shape=(
            jax.ShapeDtypeStruct((1, STATS * PAIR * share), jnp.float32),
            VMEM((SUBS, lanes), jnp.float32),
        ),
        in_specs=[spec(VMEM)] * 4 + [spec(pltpu.HBM)],
        out_specs=(spec(VMEM), spec(VMEM)),
        scratch_shapes=[
            VMEM((share, width), jnp.bfloat16),
            VMEM((width - staged, lm_head.shape[1]), jnp.bfloat16),
            pltpu.SemaphoreType.DMA((4,)),
        ],
        compiler_params=grant(24),
    )(rows, *(pltpu.with_memory_space_constraint(part, VMEM) for part in slices), other)
    swapped = lax.ppermute(stats, "tp", swap)
    stats = jnp.where(iota(stats.shape, 1) < PAIR * share, jnp.maximum(stats, swapped), stats + swapped)
    chips = groups * tp_count // PAIR
    copies = jnp.broadcast_to(stats[None], (chips,) + stats.shape)
    first = 3 * groups // 8
    order = [*reversed(range(first + 1)), *reversed(range(first + 1, groups))]
    listed = [[q * tp_count + t for q in order for t in reversed(range(at, tp_count, PAIR))] for at in range(PAIR)]
    gathered = lax.all_to_all(copies, ("req", "tp"), 0, 0, axis_index_groups=listed).reshape(chips, stats.shape[1])
    return pl.pallas_call(
        functools.partial(finish_kernel, share),
        out_shape=(
            jax.ShapeDtypeStruct((row_count,), jnp.float32),
            jax.ShapeDtypeStruct((row_count,), jnp.float32),
            jax.ShapeDtypeStruct((SEQS,), jnp.float32),
        ),
        in_specs=[spec(VMEM), spec(VMEM)],
        out_specs=(spec(VMEM), spec(VMEM), spec(VMEM)),
    )(pltpu.with_memory_space_constraint(gathered, VMEM), pltpu.with_memory_space_constraint(meta, VMEM))


def solution(mesh):
    return jax.shard_map(
        local,
        mesh=mesh,
        in_specs=(P("req", None), P(), P(None, ("req", "tp")), P("req"), P("req"), P("req")),
        out_specs=(P("req"), P("req"), P()),
        check_vma=False,
    )
```

```python
import functools

import jax
import jax.numpy as jnp
from jax import lax
from jax.experimental import pallas as pl
from jax.experimental.pallas import tpu as pltpu
from jax.sharding import PartitionSpec as P

SEQS = 4
PICK = 4
PAIR = 2
MINE = PICK // PAIR
SUBS = 8
LANES = 128
STATS = 4

VMEM = pltpu.VMEM
SMEM = pltpu.SMEM


def ranks_of(scored_ref, row_count):
    ranks, so_far = [], jnp.int32(0)
    for row in range(row_count):
        ranks.append(so_far)
        so_far = so_far + scored_ref[row]
    return ranks, so_far


def iota(shape, axis):
    return lax.broadcasted_iota(jnp.int32, shape, axis)


def members(count):
    return [(count // 2 + at) % count for at in range(count)]


def own_slot(count):
    at = lax.axis_index("req") - count // 2
    return jnp.where(at < 0, at + count, at)


def pack_kernel(share, hidden_ref, gain_ref, targets_ref, segments_ref, scored_ref, out_ref, wide_ref, parts_ref, gains_ref):
    row_count, width = hidden_ref.shape
    parts = SUBS // MINE
    span = width // parts
    own, half = own_slot(out_ref.shape[0]), lax.axis_index("tp") % PAIR
    wide_ref[...] = hidden_ref[...].astype(jnp.float32)
    gains_ref[...] = gain_ref[...].astype(jnp.float32)
    ranks, count = ranks_of(scored_ref, row_count)
    source = [jnp.int32(0)] * PICK
    for row in range(row_count):
        for r in range(PICK):
            hit = jnp.logical_and(scored_ref[row] == 1, ranks[row] == r)
            source[r] = jnp.where(hit, row, source[r])
    mine = [source[i] for i in range(MINE)]
    for h in range(1, PAIR):
        mine = [jnp.where(half == h, source[h * MINE + i], mine[i]) for i in range(MINE)]
    for i in range(MINE):
        for k in range(parts):
            parts_ref[k * MINE + i : k * MINE + i + 1, :] = wide_ref[pl.ds(mine[i], 1), k * span : (k + 1) * span]
    values = parts_ref[...]
    part = jnp.broadcast_to(jnp.sum(values * values, axis=1, keepdims=True), (SUBS, LANES))
    total = part
    for k in range(1, parts):
        total = total + pltpu.roll(part, k * MINE, 0)
    row_scale = lax.rsqrt(total / width + 1e-05)
    sub, lane = iota((SUBS, LANES), 0), iota((SUBS, LANES), 1)
    chunks = span // LANES
    for at in range(chunks):
        gain = gains_ref[at : at + 1, :]
        for k in range(1, parts):
            gain = jnp.where(sub >= k * MINE, gains_ref[k * chunks + at : k * chunks + at + 1, :], gain)
        piece = parts_ref[:, at * LANES : (at + 1) * LANES]
        piece = (piece * row_scale * gain).astype(jnp.bfloat16)
        for to in range(out_ref.shape[0]):
            out_ref[to, :, at * LANES : (at + 1) * LANES] = piece
    width_side = out_ref.shape[2] - span
    sub, lane = iota((SUBS, width_side), 0), iota((SUBS, width_side), 1)
    at_row, at_half = lane % share - own * MINE, lane // share
    side = jnp.zeros((SUBS, width_side), jnp.int32)
    for i in range(MINE):
        target = targets_ref[mine[i]]
        digits = jnp.where(sub == 0, target & 255, jnp.where(sub == 1, (target >> 8) & 255, target >> 16))
        fields = jnp.zeros((SUBS, width_side), jnp.int32)
        for h in range(PAIR):
            r = h * MINE + i
            field = jnp.where(sub == 4, (count > r).astype(jnp.int32), source[r])
            fields = jnp.where(at_half == h, jnp.where(sub == 3, segments_ref[source[r]], field), fields)
        side = jnp.where(at_row == i, jnp.where(sub < 3, digits, fields), side)
    side = side.astype(jnp.float32).astype(jnp.bfloat16)
    for to in range(out_ref.shape[0]):
        out_ref[to, :, span:] = side


def stage_kernel(share, own_ref, other_ref, own_out, other_out, order_out, sems):
    copies = []
    for at, (source, out) in enumerate(((own_ref, own_out), (other_ref, other_out))):
        depth = out.shape[0] // sems.shape[1]
        for i in range(sems.shape[1]):
            piece = pl.ds(i * depth, depth)
            copies.append(pltpu.make_async_copy(source.at[piece], out.at[piece], sems.at[at, i]))
    for copy in copies:
        copy.start()
    into, out_of = iota(order_out.shape, 0), iota(order_out.shape, 1)
    wanted = into % share // MINE * SUBS + into // share * MINE + into % MINE
    order_out[...] = jnp.where(out_of == wanted, 1.0, 0.0).astype(jnp.bfloat16)
    for copy in copies:
        copy.wait()


def score_kernel(rows_ref, own_ref, upper_ref, order_ref, other_ref, stats_ref, meta_ref, ordered_ref, lower_ref, sems):
    width, cols = own_ref.shape
    staged = upper_ref.shape[0]
    depth = lower_ref.shape[0] // sems.shape[0]
    copies = [
        pltpu.make_async_copy(
            other_ref.at[pl.ds(staged + i * depth, depth)], lower_ref.at[pl.ds(i * depth, depth)], sems.at[i]
        )
        for i in range(sems.shape[0])
    ]
    for copy in copies:
        copy.start()
    groups = rows_ref.shape[0]
    parts = SUBS // MINE
    span = width // parts
    share = groups * MINE
    tp, tp_count = lax.axis_index("tp"), lax.axis_size("tp")
    half = tp % PAIR
    place = lax.axis_index("req") * tp_count + tp
    count = groups * SUBS
    rows = rows_ref[:, :, :span].reshape(count, span)
    ordered = jnp.dot(order_ref[...], rows, preferred_element_type=jnp.float32).astype(jnp.bfloat16)
    for k in range(parts):
        ordered_ref[:, k * span : (k + 1) * span] = ordered[k * share : (k + 1) * share]
    meta = rows_ref[0, :, span:].astype(jnp.float32)
    for q in range(1, groups):
        meta = meta + rows_ref[q, :, span:].astype(jnp.float32)
    meta_ref[...] = meta

    def product(slice_ref, first, at, depth):
        piece = pl.ds(pl.multiple_of(at * depth, depth), depth)
        rows = ordered_ref[:, pl.ds(pl.multiple_of(first + at * depth, depth), depth)]
        return jnp.dot(rows, slice_ref[piece, :], preferred_element_type=jnp.float32)

    def resident(at, sums):
        return (
            sums[0] + product(own_ref, 0, at, width // 2),
            sums[1] + product(upper_ref, 0, at, staged // 2),
        )

    def fetched(at, total):
        return total + product(lower_ref, staged, at, (width - staged) // 2)

    zeros = jnp.zeros((share, cols), jnp.float32)
    own_logits, other_logits = lax.fori_loop(0, 2, resident, (zeros, zeros))
    for copy in copies:
        copy.wait()
    logits = jnp.concatenate([own_logits, lax.fori_loop(0, 2, fetched, other_logits)], axis=1)
    lanes = max(share, LANES)
    sub, lane = iota((share, lanes), 0), iota((share, lanes), 1)
    ids = meta[0:1, :lanes] + 256.0 * meta[1:2, :lanes] + 65536.0 * meta[2:3, :lanes]
    ids = jnp.sum(jnp.where(lane == sub, ids, 0.0), axis=1, keepdims=True).astype(jnp.int32)
    row_top = jnp.max(logits, axis=1, keepdims=True)
    scaled = jnp.exp(logits - row_top)
    row_total = jnp.sum(scaled, axis=1, keepdims=True)
    row_weighted = jnp.sum(scaled * logits, axis=1, keepdims=True)
    column = iota(logits.shape, 1)
    other = place + 1 - 2 * half
    columns = jnp.where(column < cols, place * cols, (other - 1) * cols) + column
    picked = jnp.sum(jnp.where(columns == ids, logits, 0.0), axis=1, keepdims=True)
    stats = (row_top, row_total, row_weighted, picked)
    if PAIR * share * STATS == LANES:
        joined = picked
        for at in range(STATS - 1):
            joined = jnp.where(lane // (PAIR * share) == at, stats[at], joined)
        joined = jnp.sum(jnp.where(lane % share == sub, joined, 0.0), axis=0, keepdims=True)
        lane = iota((1, LANES), 1)
        neutral = jnp.where(lane < PAIR * share, -jnp.inf, 0.0)
        stats_ref[...] = jnp.where(lane // share % PAIR == half, joined, neutral)
    else:
        for at in range(STATS):
            line = jnp.sum(jnp.where(lane == sub, stats[at], 0.0), axis=0, keepdims=True)
            for h in range(PAIR):
                first = (at * PAIR + h) * share
                stats_ref[:, first : first + share] = jnp.where(half == h, line, 0.0 if at else -jnp.inf)


def finish_kernel(share, stats_ref, meta_ref, logprob_ref, entropy_ref, seq_ref):
    row_count = logprob_ref.shape[0]
    used = PAIR * share
    lanes = max(used, LANES)

    def stat(at):
        if used >= LANES:
            return stats_ref[:, at * used : (at + 1) * used]
        return stats_ref[...] if at == 0 else pltpu.roll(stats_ref[...], LANES - at * used, 1)

    tops = stat(0)
    row_top = jnp.max(tops, axis=0, keepdims=True)
    weight = jnp.exp(tops - row_top)
    row_total = jnp.sum(stat(1) * weight, axis=0, keepdims=True)
    row_weighted = jnp.sum(stat(2) * weight, axis=0, keepdims=True)
    picked = jnp.sum(stat(3), axis=0, keepdims=True)
    log_norm = row_top + jnp.log(row_total)
    lane, sub = iota((1, lanes), 1), iota((SUBS, lanes), 0)
    in_use = jnp.logical_and(meta_ref[4:5, :] > 0.5, lane < used)
    logprob = jnp.where(in_use, picked - log_norm, 0.0)
    entropy = jnp.where(in_use, log_norm - row_weighted / row_total, 0.0)
    segment, place = meta_ref[3:4, :].astype(jnp.int32), meta_ref[5:6, :].astype(jnp.int32)
    mine = jnp.logical_and(place == sub, lane % share // MINE == own_slot(share // MINE))

    def placed(values, wanted):
        sums = jnp.sum(jnp.where(wanted, values, 0.0), axis=1, keepdims=True)
        diagonal = iota((SUBS, LANES), 0) == iota((SUBS, LANES), 1)
        return jnp.sum(jnp.where(diagonal, sums, 0.0), axis=0)

    logprob_ref[...] = placed(logprob, mine)[:row_count]
    entropy_ref[...] = placed(entropy, mine)[:row_count]
    seq_ref[...] = placed(logprob, segment == sub)[:SEQS]


def grant(mebibytes):
    return pltpu.CompilerParams(vmem_limit_bytes=mebibytes * 1024 * 1024)


def local(hidden, norm_gain, lm_head, targets, segments, scored):
    row_count, width = hidden.shape
    groups, tp_count = lax.axis_size("req"), lax.axis_size("tp")
    span = width * MINE // SUBS
    share = groups * MINE
    lanes = max(PAIR * share, LANES)

    def spec(space):
        return pl.BlockSpec(memory_space=space)

    swap = [(i, i + 1 - 2 * (i % PAIR)) for i in range(tp_count)]
    other = lax.ppermute(lm_head, "tp", swap)
    packed = pl.pallas_call(
        functools.partial(pack_kernel, share),
        out_shape=VMEM((groups, SUBS, span + lanes), jnp.bfloat16),
        in_specs=[spec(VMEM)] * 2 + [spec(SMEM)] * 3,
        out_specs=spec(VMEM),
        scratch_shapes=[
            VMEM((row_count, width), jnp.float32),
            VMEM((SUBS, span), jnp.float32),
            VMEM((width // LANES, LANES), jnp.float32),
        ],
    )(hidden, norm_gain.reshape(width // LANES, LANES), targets, segments, scored)
    rows = lax.all_to_all(packed, "req", 0, 0, axis_index_groups=[members(groups)])
    other = pltpu.with_memory_space_constraint(other, pltpu.HBM)
    staged = width // 2
    slices = pl.pallas_call(
        functools.partial(stage_kernel, share),
        out_shape=(
            VMEM(lm_head.shape, lm_head.dtype),
            VMEM((staged, lm_head.shape[1]), lm_head.dtype),
            VMEM((groups * SUBS, groups * SUBS), jnp.bfloat16),
        ),
        in_specs=[spec(pltpu.HBM)] * 2,
        out_specs=(spec(VMEM),) * 3,
        scratch_shapes=[pltpu.SemaphoreType.DMA((2, 4))],
        compiler_params=grant(4),
        cost_estimate=pl.CostEstimate(flops=0, bytes_accessed=3 * 2 * lm_head.size, transcendentals=0),
    )(pltpu.with_memory_space_constraint(lm_head, pltpu.HBM), other)
    stats, meta = pl.pallas_call(
        score_kernel,
        out_shape=(
            jax.ShapeDtypeStruct((1, STATS * PAIR * share), jnp.float32),
            VMEM((SUBS, lanes), jnp.float32),
        ),
        in_specs=[spec(VMEM)] * 4 + [spec(pltpu.HBM)],
        out_specs=(spec(VMEM), spec(VMEM)),
        scratch_shapes=[
            VMEM((share, width), jnp.bfloat16),
            VMEM((width - staged, lm_head.shape[1]), jnp.bfloat16),
            pltpu.SemaphoreType.DMA((4,)),
        ],
        compiler_params=grant(24),
    )(rows, *(pltpu.with_memory_space_constraint(part, VMEM) for part in slices), other)
    swapped = lax.ppermute(stats, "tp", swap)
    stats = jnp.where(iota(stats.shape, 1) < PAIR * share, jnp.maximum(stats, swapped), stats + swapped)
    chips = groups * tp_count // PAIR
    copies = jnp.broadcast_to(stats[None], (chips,) + stats.shape)
    listed = [[*reversed(range(at, groups * tp_count, PAIR))] for at in range(PAIR)]
    gathered = lax.all_to_all(copies, ("req", "tp"), 0, 0, axis_index_groups=listed).reshape(chips, stats.shape[1])
    return pl.pallas_call(
        functools.partial(finish_kernel, share),
        out_shape=(
            jax.ShapeDtypeStruct((row_count,), jnp.float32),
            jax.ShapeDtypeStruct((row_count,), jnp.float32),
            jax.ShapeDtypeStruct((SEQS,), jnp.float32),
        ),
        in_specs=[spec(VMEM), spec(VMEM)],
        out_specs=(spec(VMEM), spec(VMEM), spec(VMEM)),
    )(pltpu.with_memory_space_constraint(gathered, VMEM), pltpu.with_memory_space_constraint(meta, VMEM))


def solution(mesh):
    return jax.shard_map(
        local,
        mesh=mesh,
        in_specs=(P("req", None), P(), P(None, ("req", "tp")), P("req"), P("req"), P("req")),
        out_specs=(P("req"), P("req"), P()),
        check_vma=False,
    )
```

```python
import functools

import jax
import jax.numpy as jnp
from jax import lax
from jax.experimental import pallas as pl
from jax.experimental.pallas import tpu as pltpu
from jax.sharding import PartitionSpec as P

SEQS = 4
PICK = 4
PAIR = 2
MINE = PICK // PAIR
SUBS = 8
LANES = 128
STATS = 4

VMEM = pltpu.VMEM
SMEM = pltpu.SMEM


def ranks_of(scored_ref, row_count):
    ranks, so_far = [], jnp.int32(0)
    for row in range(row_count):
        ranks.append(so_far)
        so_far = so_far + scored_ref[row]
    return ranks, so_far


def iota(shape, axis):
    return lax.broadcasted_iota(jnp.int32, shape, axis)


def members(count):
    return [(5 * count // 8 + at) % count for at in range(count)]


def own_slot(count):
    at = lax.axis_index("req") - 5 * count // 8
    return jnp.where(at < 0, at + count, at)


def pack_kernel(share, hidden_ref, gain_ref, targets_ref, segments_ref, scored_ref, out_ref, wide_ref, parts_ref, gains_ref):
    row_count, width = hidden_ref.shape
    parts = SUBS // MINE
    span = width // parts
    own, half = own_slot(out_ref.shape[0]), lax.axis_index("tp") % PAIR
    wide_ref[...] = hidden_ref[...].astype(jnp.float32)
    gains_ref[...] = gain_ref[...].astype(jnp.float32)
    ranks, count = ranks_of(scored_ref, row_count)
    source = [jnp.int32(0)] * PICK
    for row in range(row_count):
        for r in range(PICK):
            hit = jnp.logical_and(scored_ref[row] == 1, ranks[row] == r)
            source[r] = jnp.where(hit, row, source[r])
    mine = [source[i] for i in range(MINE)]
    for h in range(1, PAIR):
        mine = [jnp.where(half == h, source[h * MINE + i], mine[i]) for i in range(MINE)]
    for i in range(MINE):
        for k in range(parts):
            parts_ref[k * MINE + i : k * MINE + i + 1, :] = wide_ref[pl.ds(mine[i], 1), k * span : (k + 1) * span]
    values = parts_ref[...]
    part = jnp.broadcast_to(jnp.sum(values * values, axis=1, keepdims=True), (SUBS, LANES))
    total = part
    for k in range(1, parts):
        total = total + pltpu.roll(part, k * MINE, 0)
    row_scale = lax.rsqrt(total / width + 1e-05)
    sub, lane = iota((SUBS, LANES), 0), iota((SUBS, LANES), 1)
    chunks = span // LANES
    for at in range(chunks):
        gain = gains_ref[at : at + 1, :]
        for k in range(1, parts):
            gain = jnp.where(sub >= k * MINE, gains_ref[k * chunks + at : k * chunks + at + 1, :], gain)
        piece = parts_ref[:, at * LANES : (at + 1) * LANES]
        piece = (piece * row_scale * gain).astype(jnp.bfloat16)
        for to in range(out_ref.shape[0]):
            out_ref[to, :, at * LANES : (at + 1) * LANES] = piece
    width_side = out_ref.shape[2] - span
    sub, lane = iota((SUBS, width_side), 0), iota((SUBS, width_side), 1)
    at_row, at_half = lane % share - own * MINE, lane // share
    side = jnp.zeros((SUBS, width_side), jnp.int32)
    for i in range(MINE):
        target = targets_ref[mine[i]]
        digits = jnp.where(sub == 0, target & 255, jnp.where(sub == 1, (target >> 8) & 255, target >> 16))
        fields = jnp.zeros((SUBS, width_side), jnp.int32)
        for h in range(PAIR):
            r = h * MINE + i
            field = jnp.where(sub == 4, (count > r).astype(jnp.int32), source[r])
            fields = jnp.where(at_half == h, jnp.where(sub == 3, segments_ref[source[r]], field), fields)
        side = jnp.where(at_row == i, jnp.where(sub < 3, digits, fields), side)
    side = side.astype(jnp.float32).astype(jnp.bfloat16)
    for to in range(out_ref.shape[0]):
        out_ref[to, :, span:] = side


def stage_kernel(share, own_ref, other_ref, own_out, other_out, order_out, sems):
    copies = []
    for at, (source, out) in enumerate(((own_ref, own_out), (other_ref, other_out))):
        depth = out.shape[0] // sems.shape[1]
        for i in range(sems.shape[1]):
            piece = pl.ds(i * depth, depth)
            copies.append(pltpu.make_async_copy(source.at[piece], out.at[piece], sems.at[at, i]))
    for copy in copies:
        copy.start()
    into, out_of = iota(order_out.shape, 0), iota(order_out.shape, 1)
    wanted = into % share // MINE * SUBS + into // share * MINE + into % MINE
    order_out[...] = jnp.where(out_of == wanted, 1.0, 0.0).astype(jnp.bfloat16)
    for copy in copies:
        copy.wait()


def score_kernel(rows_ref, own_ref, upper_ref, order_ref, other_ref, stats_ref, meta_ref, ordered_ref, lower_ref, sems):
    width, cols = own_ref.shape
    staged = upper_ref.shape[0]
    depth = lower_ref.shape[0] // sems.shape[0]
    copies = [
        pltpu.make_async_copy(
            other_ref.at[pl.ds(staged + i * depth, depth)], lower_ref.at[pl.ds(i * depth, depth)], sems.at[i]
        )
        for i in range(sems.shape[0])
    ]
    for copy in copies:
        copy.start()
    groups = rows_ref.shape[0]
    parts = SUBS // MINE
    span = width // parts
    share = groups * MINE
    tp, tp_count = lax.axis_index("tp"), lax.axis_size("tp")
    half = tp % PAIR
    place = lax.axis_index("req") * tp_count + tp
    count = groups * SUBS
    rows = rows_ref[:, :, :span].reshape(count, span)
    ordered = jnp.dot(order_ref[...], rows, preferred_element_type=jnp.float32).astype(jnp.bfloat16)
    for k in range(parts):
        ordered_ref[:, k * span : (k + 1) * span] = ordered[k * share : (k + 1) * share]
    meta = rows_ref[0, :, span:].astype(jnp.float32)
    for q in range(1, groups):
        meta = meta + rows_ref[q, :, span:].astype(jnp.float32)
    meta_ref[...] = meta

    def product(slice_ref, first, at, depth):
        piece = pl.ds(pl.multiple_of(at * depth, depth), depth)
        rows = ordered_ref[:, pl.ds(pl.multiple_of(first + at * depth, depth), depth)]
        return jnp.dot(rows, slice_ref[piece, :], preferred_element_type=jnp.float32)

    def resident(at, sums):
        return (
            sums[0] + product(own_ref, 0, at, width // 2),
            sums[1] + product(upper_ref, 0, at, staged // 2),
        )

    def fetched(at, total):
        return total + product(lower_ref, staged, at, (width - staged) // 2)

    zeros = jnp.zeros((share, cols), jnp.float32)
    own_logits, other_logits = lax.fori_loop(0, 2, resident, (zeros, zeros))
    for copy in copies:
        copy.wait()
    logits = jnp.concatenate([own_logits, lax.fori_loop(0, 2, fetched, other_logits)], axis=1)
    lanes = max(share, LANES)
    sub, lane = iota((share, lanes), 0), iota((share, lanes), 1)
    ids = meta[0:1, :lanes] + 256.0 * meta[1:2, :lanes] + 65536.0 * meta[2:3, :lanes]
    ids = jnp.sum(jnp.where(lane == sub, ids, 0.0), axis=1, keepdims=True).astype(jnp.int32)
    row_top = jnp.max(logits, axis=1, keepdims=True)
    scaled = jnp.exp(logits - row_top)
    row_total = jnp.sum(scaled, axis=1, keepdims=True)
    row_weighted = jnp.sum(scaled * logits, axis=1, keepdims=True)
    column = iota(logits.shape, 1)
    other = place + 1 - 2 * half
    columns = jnp.where(column < cols, place * cols, (other - 1) * cols) + column
    picked = jnp.sum(jnp.where(columns == ids, logits, 0.0), axis=1, keepdims=True)
    stats = (row_top, row_total, row_weighted, picked)
    if PAIR * share * STATS == LANES:
        joined = picked
        for at in range(STATS - 1):
            joined = jnp.where(lane // (PAIR * share) == at, stats[at], joined)
        joined = jnp.sum(jnp.where(lane % share == sub, joined, 0.0), axis=0, keepdims=True)
        lane = iota((1, LANES), 1)
        neutral = jnp.where(lane < PAIR * share, -jnp.inf, 0.0)
        stats_ref[...] = jnp.where(lane // share % PAIR == half, joined, neutral)
    else:
        for at in range(STATS):
            line = jnp.sum(jnp.where(lane == sub, stats[at], 0.0), axis=0, keepdims=True)
            for h in range(PAIR):
                first = (at * PAIR + h) * share
                stats_ref[:, first : first + share] = jnp.where(half == h, line, 0.0 if at else -jnp.inf)


def finish_kernel(share, stats_ref, meta_ref, logprob_ref, entropy_ref, seq_ref):
    row_count = logprob_ref.shape[0]
    used = PAIR * share
    lanes = max(used, LANES)

    def stat(at):
        if used >= LANES:
            return stats_ref[:, at * used : (at + 1) * used]
        return stats_ref[...] if at == 0 else pltpu.roll(stats_ref[...], LANES - at * used, 1)

    tops = stat(0)
    row_top = jnp.max(tops, axis=0, keepdims=True)
    weight = jnp.exp(tops - row_top)
    row_total = jnp.sum(stat(1) * weight, axis=0, keepdims=True)
    row_weighted = jnp.sum(stat(2) * weight, axis=0, keepdims=True)
    picked = jnp.sum(stat(3), axis=0, keepdims=True)
    log_norm = row_top + jnp.log(row_total)
    lane, sub = iota((1, lanes), 1), iota((SUBS, lanes), 0)
    in_use = jnp.logical_and(meta_ref[4:5, :] > 0.5, lane < used)
    logprob = jnp.where(in_use, picked - log_norm, 0.0)
    entropy = jnp.where(in_use, log_norm - row_weighted / row_total, 0.0)
    segment, place = meta_ref[3:4, :].astype(jnp.int32), meta_ref[5:6, :].astype(jnp.int32)
    power = share.bit_length() - 1 if share & (share - 1) == 0 else None
    in_share = lane % share if power is None else lane & (share - 1)
    mine = jnp.logical_and(place == sub, in_share >> (MINE.bit_length() - 1) == own_slot(share // MINE))
    stacked = jnp.concatenate(
        [
            jnp.where(mine, logprob, 0.0),
            jnp.where(mine, entropy, 0.0),
            jnp.where(segment == sub, logprob, 0.0),
        ],
        axis=0,
    )
    sums = jnp.sum(stacked, axis=1, keepdims=True)
    diagonal = iota((SUBS, LANES), 0) == iota((SUBS, LANES), 1)
    lines = [
        jnp.sum(jnp.where(diagonal, sums[at * SUBS : (at + 1) * SUBS], 0.0), axis=0) for at in range(3)
    ]
    logprob_ref[...] = lines[0][:row_count]
    entropy_ref[...] = lines[1][:row_count]
    seq_ref[...] = lines[2][:SEQS]


def grant(mebibytes):
    return pltpu.CompilerParams(vmem_limit_bytes=mebibytes * 1024 * 1024)


def local(hidden, norm_gain, lm_head, targets, segments, scored):
    row_count, width = hidden.shape
    groups, tp_count = lax.axis_size("req"), lax.axis_size("tp")
    span = width * MINE // SUBS
    share = groups * MINE
    lanes = max(PAIR * share, LANES)

    def spec(space):
        return pl.BlockSpec(memory_space=space)

    swap = [(i, i + 1 - 2 * (i % PAIR)) for i in range(tp_count)]
    other = lax.ppermute(lm_head, "tp", swap)
    packed = pl.pallas_call(
        functools.partial(pack_kernel, share),
        out_shape=VMEM((groups, SUBS, span + lanes), jnp.bfloat16),
        in_specs=[spec(VMEM)] * 2 + [spec(SMEM)] * 3,
        out_specs=spec(VMEM),
        scratch_shapes=[
            VMEM((row_count, width), jnp.float32),
            VMEM((SUBS, span), jnp.float32),
            VMEM((width // LANES, LANES), jnp.float32),
        ],
    )(hidden, norm_gain.reshape(width // LANES, LANES), targets, segments, scored)
    rows = lax.all_to_all(packed, "req", 0, 0, axis_index_groups=[members(groups)])
    other = pltpu.with_memory_space_constraint(other, pltpu.HBM)
    staged = width // 2
    slices = pl.pallas_call(
        functools.partial(stage_kernel, share),
        out_shape=(
            VMEM(lm_head.shape, lm_head.dtype),
            VMEM((staged, lm_head.shape[1]), lm_head.dtype),
            VMEM((groups * SUBS, groups * SUBS), jnp.bfloat16),
        ),
        in_specs=[spec(pltpu.HBM)] * 2,
        out_specs=(spec(VMEM),) * 3,
        scratch_shapes=[pltpu.SemaphoreType.DMA((2, 4))],
        compiler_params=grant(4),
        cost_estimate=pl.CostEstimate(flops=0, bytes_accessed=3 * 2 * lm_head.size, transcendentals=0),
    )(pltpu.with_memory_space_constraint(lm_head, pltpu.HBM), other)
    stats, meta = pl.pallas_call(
        score_kernel,
        out_shape=(
            jax.ShapeDtypeStruct((1, STATS * PAIR * share), jnp.float32),
            VMEM((SUBS, lanes), jnp.float32),
        ),
        in_specs=[spec(VMEM)] * 4 + [spec(pltpu.HBM)],
        out_specs=(spec(VMEM), spec(VMEM)),
        scratch_shapes=[
            VMEM((share, width), jnp.bfloat16),
            VMEM((width - staged, lm_head.shape[1]), jnp.bfloat16),
            pltpu.SemaphoreType.DMA((4,)),
        ],
        compiler_params=grant(24),
    )(rows, *(pltpu.with_memory_space_constraint(part, VMEM) for part in slices), other)
    swapped = lax.ppermute(stats, "tp", swap)
    stats = jnp.where(iota(stats.shape, 1) < PAIR * share, jnp.maximum(stats, swapped), stats + swapped)
    chips = groups * tp_count // PAIR
    copies = jnp.broadcast_to(stats[None], (chips,) + stats.shape)
    listed = [[*reversed(range(at, groups * tp_count, PAIR))] for at in range(PAIR)]
    gathered = lax.all_to_all(copies, ("req", "tp"), 0, 0, axis_index_groups=listed).reshape(chips, stats.shape[1])
    return pl.pallas_call(
        functools.partial(finish_kernel, share),
        out_shape=(
            jax.ShapeDtypeStruct((row_count,), jnp.float32),
            jax.ShapeDtypeStruct((row_count,), jnp.float32),
            jax.ShapeDtypeStruct((SEQS,), jnp.float32),
        ),
        in_specs=[spec(VMEM), spec(VMEM)],
        out_specs=(spec(VMEM), spec(VMEM), spec(VMEM)),
    )(pltpu.with_memory_space_constraint(gathered, VMEM), pltpu.with_memory_space_constraint(meta, VMEM))


def solution(mesh):
    return jax.shard_map(
        local,
        mesh=mesh,
        in_specs=(P("req", None), P(), P(None, ("req", "tp")), P("req"), P("req"), P("req")),
        out_specs=(P("req"), P("req"), P()),
        check_vma=False,
    )
```

```python
import functools

import jax
import jax.numpy as jnp
from jax import lax
from jax.experimental import pallas as pl
from jax.experimental.pallas import tpu as pltpu
from jax.sharding import PartitionSpec as P

SEQS = 4
PICK = 4
PAIR = 2
MINE = PICK // PAIR
SUBS = 8
LANES = 128
STATS = 4

VMEM = pltpu.VMEM
SMEM = pltpu.SMEM


def ranks_of(scored_ref, row_count):
    ranks, so_far = [], jnp.int32(0)
    for row in range(row_count):
        ranks.append(so_far)
        so_far = so_far + scored_ref[row]
    return ranks, so_far


def iota(shape, axis):
    return lax.broadcasted_iota(jnp.int32, shape, axis)


def members(count):
    return [(5 * count // 8 + at) % count for at in range(count)]


def own_slot(count):
    at = lax.axis_index("req") - 5 * count // 8
    return jnp.where(at < 0, at + count, at)


def pack_kernel(share, hidden_ref, gain_ref, targets_ref, segments_ref, scored_ref, out_ref, wide_ref, parts_ref, gains_ref):
    row_count, width = hidden_ref.shape
    parts = SUBS // MINE
    span = width // parts
    own, half = own_slot(out_ref.shape[0]), lax.axis_index("tp") % PAIR
    wide_ref[...] = hidden_ref[...].astype(jnp.float32)
    gains_ref[...] = gain_ref[...].astype(jnp.float32)
    ranks, count = ranks_of(scored_ref, row_count)
    source = [jnp.int32(0)] * PICK
    for row in range(row_count):
        for r in range(PICK):
            hit = jnp.logical_and(scored_ref[row] == 1, ranks[row] == r)
            source[r] = jnp.where(hit, row, source[r])
    mine = [source[i] for i in range(MINE)]
    for h in range(1, PAIR):
        mine = [jnp.where(half == h, source[h * MINE + i], mine[i]) for i in range(MINE)]
    for i in range(MINE):
        for k in range(parts):
            parts_ref[k * MINE + i : k * MINE + i + 1, :] = wide_ref[pl.ds(mine[i], 1), k * span : (k + 1) * span]
    values = parts_ref[...]
    part = jnp.broadcast_to(jnp.sum(values * values, axis=1, keepdims=True), (SUBS, LANES))
    total = part
    for k in range(1, parts):
        total = total + pltpu.roll(part, k * MINE, 0)
    row_scale = lax.rsqrt(total / width + 1e-05)
    sub, lane = iota((SUBS, LANES), 0), iota((SUBS, LANES), 1)
    chunks = span // LANES
    for at in range(chunks):
        gain = gains_ref[at : at + 1, :]
        for k in range(1, parts):
            gain = jnp.where(sub >= k * MINE, gains_ref[k * chunks + at : k * chunks + at + 1, :], gain)
        piece = parts_ref[:, at * LANES : (at + 1) * LANES]
        piece = (piece * row_scale * gain).astype(jnp.bfloat16)
        for to in range(out_ref.shape[0]):
            out_ref[to, :, at * LANES : (at + 1) * LANES] = piece
    width_side = out_ref.shape[2] - span
    sub, lane = iota((SUBS, width_side), 0), iota((SUBS, width_side), 1)
    at_row, at_half = lane % share - own * MINE, lane // share
    side = jnp.zeros((SUBS, width_side), jnp.int32)
    for i in range(MINE):
        target = targets_ref[mine[i]]
        digits = jnp.where(sub == 0, target & 255, jnp.where(sub == 1, (target >> 8) & 255, target >> 16))
        fields = jnp.zeros((SUBS, width_side), jnp.int32)
        for h in range(PAIR):
            r = h * MINE + i
            field = jnp.where(sub == 4, (count > r).astype(jnp.int32), source[r])
            fields = jnp.where(at_half == h, jnp.where(sub == 3, segments_ref[source[r]], field), fields)
        side = jnp.where(at_row == i, jnp.where(sub < 3, digits, fields), side)
    side = side.astype(jnp.float32).astype(jnp.bfloat16)
    for to in range(out_ref.shape[0]):
        out_ref[to, :, span:] = side


def stage_kernel(share, own_ref, other_ref, own_out, other_out, order_out, sems):
    copies = []
    for at, (source, out) in enumerate(((own_ref, own_out), (other_ref, other_out))):
        depth = out.shape[0] // sems.shape[1]
        for i in range(sems.shape[1]):
            piece = pl.ds(i * depth, depth)
            copies.append(pltpu.make_async_copy(source.at[piece], out.at[piece], sems.at[at, i]))
    for copy in copies:
        copy.start()
    into, out_of = iota(order_out.shape, 0), iota(order_out.shape, 1)
    wanted = into % share // MINE * SUBS + into // share * MINE + into % MINE
    order_out[...] = jnp.where(out_of == wanted, 1.0, 0.0).astype(jnp.bfloat16)
    for copy in copies:
        copy.wait()


def score_kernel(rows_ref, own_ref, upper_ref, order_ref, other_ref, stats_ref, meta_ref, ordered_ref, lower_ref, sems):
    width, cols = own_ref.shape
    staged = upper_ref.shape[0]
    depth = lower_ref.shape[0] // sems.shape[0]
    copies = [
        pltpu.make_async_copy(
            other_ref.at[pl.ds(staged + i * depth, depth)], lower_ref.at[pl.ds(i * depth, depth)], sems.at[i]
        )
        for i in range(sems.shape[0])
    ]
    for copy in copies:
        copy.start()
    groups = rows_ref.shape[0]
    parts = SUBS // MINE
    span = width // parts
    share = groups * MINE
    tp, tp_count = lax.axis_index("tp"), lax.axis_size("tp")
    half = tp % PAIR
    place = lax.axis_index("req") * tp_count + tp
    count = groups * SUBS
    rows = rows_ref[:, :, :span].reshape(count, span)
    ordered = jnp.dot(order_ref[...], rows, preferred_element_type=jnp.float32).astype(jnp.bfloat16)
    for k in range(parts):
        ordered_ref[:, k * span : (k + 1) * span] = ordered[k * share : (k + 1) * share]
    meta = rows_ref[0, :, span:].astype(jnp.float32)
    for q in range(1, groups):
        meta = meta + rows_ref[q, :, span:].astype(jnp.float32)
    meta_ref[...] = meta

    def product(slice_ref, first, at, depth):
        piece = pl.ds(pl.multiple_of(at * depth, depth), depth)
        rows = ordered_ref[:, pl.ds(pl.multiple_of(first + at * depth, depth), depth)]
        return jnp.dot(rows, slice_ref[piece, :], preferred_element_type=jnp.float32)

    def resident(at, sums):
        return (
            sums[0] + product(own_ref, 0, at, width // 2),
            sums[1] + product(upper_ref, 0, at, staged // 2),
        )

    def fetched(at, total):
        pltpu.make_async_copy(
            other_ref.at[pl.ds(staged + at * depth, depth)], lower_ref.at[pl.ds(at * depth, depth)], sems.at[at]
        ).wait()
        return total + product(lower_ref, staged, at, depth)

    zeros = jnp.zeros((share, cols), jnp.float32)
    own_logits, other_logits = lax.fori_loop(0, 2, resident, (zeros, zeros))
    logits = jnp.concatenate([own_logits, lax.fori_loop(0, sems.shape[0], fetched, other_logits)], axis=1)
    lanes = max(share, LANES)
    sub, lane = iota((share, lanes), 0), iota((share, lanes), 1)
    ids = meta[0:1, :lanes] + 256.0 * meta[1:2, :lanes] + 65536.0 * meta[2:3, :lanes]
    ids = jnp.sum(jnp.where(lane == sub, ids, 0.0), axis=1, keepdims=True).astype(jnp.int32)
    row_top = jnp.max(logits, axis=1, keepdims=True)
    scaled = jnp.exp(logits - row_top)
    row_total = jnp.sum(scaled, axis=1, keepdims=True)
    row_weighted = jnp.sum(scaled * logits, axis=1, keepdims=True)
    column = iota(logits.shape, 1)
    other = place + 1 - 2 * half
    columns = jnp.where(column < cols, place * cols, (other - 1) * cols) + column
    picked = jnp.sum(jnp.where(columns == ids, logits, 0.0), axis=1, keepdims=True)
    stats = (row_top, row_total, row_weighted, picked)
    if PAIR * share * STATS == LANES:
        joined = picked
        for at in range(STATS - 1):
            joined = jnp.where(lane // (PAIR * share) == at, stats[at], joined)
        joined = jnp.sum(jnp.where(lane % share == sub, joined, 0.0), axis=0, keepdims=True)
        lane = iota((1, LANES), 1)
        neutral = jnp.where(lane < PAIR * share, -jnp.inf, 0.0)
        stats_ref[...] = jnp.where(lane // share % PAIR == half, joined, neutral)
    else:
        for at in range(STATS):
            line = jnp.sum(jnp.where(lane == sub, stats[at], 0.0), axis=0, keepdims=True)
            for h in range(PAIR):
                first = (at * PAIR + h) * share
                stats_ref[:, first : first + share] = jnp.where(half == h, line, 0.0 if at else -jnp.inf)


def finish_kernel(share, stats_ref, meta_ref, logprob_ref, entropy_ref, seq_ref):
    row_count = logprob_ref.shape[0]
    used = PAIR * share
    lanes = max(used, LANES)

    def stat(at):
        if used >= LANES:
            return stats_ref[:, at * used : (at + 1) * used]
        return stats_ref[...] if at == 0 else pltpu.roll(stats_ref[...], LANES - at * used, 1)

    tops = stat(0)
    row_top = jnp.max(tops, axis=0, keepdims=True)
    weight = jnp.exp(tops - row_top)
    row_total = jnp.sum(stat(1) * weight, axis=0, keepdims=True)
    row_weighted = jnp.sum(stat(2) * weight, axis=0, keepdims=True)
    picked = jnp.sum(stat(3), axis=0, keepdims=True)
    log_norm = row_top + jnp.log(row_total)
    lane, sub = iota((1, lanes), 1), iota((SUBS, lanes), 0)
    in_use = jnp.logical_and(meta_ref[4:5, :] > 0.5, lane < used)
    logprob = jnp.where(in_use, picked - log_norm, 0.0)
    entropy = jnp.where(in_use, log_norm - row_weighted / row_total, 0.0)
    segment, place = meta_ref[3:4, :].astype(jnp.int32), meta_ref[5:6, :].astype(jnp.int32)
    mine = jnp.logical_and(place == sub, lane % share // MINE == own_slot(share // MINE))

    def placed(values, wanted):
        sums = jnp.sum(jnp.where(wanted, values, 0.0), axis=1, keepdims=True)
        diagonal = iota((SUBS, LANES), 0) == iota((SUBS, LANES), 1)
        return jnp.sum(jnp.where(diagonal, sums, 0.0), axis=0)

    logprob_ref[...] = placed(logprob, mine)[:row_count]
    entropy_ref[...] = placed(entropy, mine)[:row_count]
    seq_ref[...] = placed(logprob, segment == sub)[:SEQS]


def grant(mebibytes):
    return pltpu.CompilerParams(vmem_limit_bytes=mebibytes * 1024 * 1024)


def local(hidden, norm_gain, lm_head, targets, segments, scored):
    row_count, width = hidden.shape
    groups, tp_count = lax.axis_size("req"), lax.axis_size("tp")
    span = width * MINE // SUBS
    share = groups * MINE
    lanes = max(PAIR * share, LANES)

    def spec(space):
        return pl.BlockSpec(memory_space=space)

    swap = [(i, i + 1 - 2 * (i % PAIR)) for i in range(tp_count)]
    other = lax.ppermute(lm_head, "tp", swap)
    packed = pl.pallas_call(
        functools.partial(pack_kernel, share),
        out_shape=VMEM((groups, SUBS, span + lanes), jnp.bfloat16),
        in_specs=[spec(VMEM)] * 2 + [spec(SMEM)] * 3,
        out_specs=spec(VMEM),
        scratch_shapes=[
            VMEM((row_count, width), jnp.float32),
            VMEM((SUBS, span), jnp.float32),
            VMEM((width // LANES, LANES), jnp.float32),
        ],
    )(hidden, norm_gain.reshape(width // LANES, LANES), targets, segments, scored)
    rows = lax.all_to_all(packed, "req", 0, 0, axis_index_groups=[members(groups)])
    other = pltpu.with_memory_space_constraint(other, pltpu.HBM)
    staged = width // 2
    slices = pl.pallas_call(
        functools.partial(stage_kernel, share),
        out_shape=(
            VMEM(lm_head.shape, lm_head.dtype),
            VMEM((staged, lm_head.shape[1]), lm_head.dtype),
            VMEM((groups * SUBS, groups * SUBS), jnp.bfloat16),
        ),
        in_specs=[spec(pltpu.HBM)] * 2,
        out_specs=(spec(VMEM),) * 3,
        scratch_shapes=[pltpu.SemaphoreType.DMA((2, 4))],
        compiler_params=grant(4),
        cost_estimate=pl.CostEstimate(flops=0, bytes_accessed=3 * 2 * lm_head.size, transcendentals=0),
    )(pltpu.with_memory_space_constraint(lm_head, pltpu.HBM), other)
    stats, meta = pl.pallas_call(
        score_kernel,
        out_shape=(
            jax.ShapeDtypeStruct((1, STATS * PAIR * share), jnp.float32),
            VMEM((SUBS, lanes), jnp.float32),
        ),
        in_specs=[spec(VMEM)] * 4 + [spec(pltpu.HBM)],
        out_specs=(spec(VMEM), spec(VMEM)),
        scratch_shapes=[
            VMEM((share, width), jnp.bfloat16),
            VMEM((width - staged, lm_head.shape[1]), jnp.bfloat16),
            pltpu.SemaphoreType.DMA((2,)),
        ],
        compiler_params=grant(24),
    )(rows, *(pltpu.with_memory_space_constraint(part, VMEM) for part in slices), other)
    swapped = lax.ppermute(stats, "tp", swap)
    stats = jnp.where(iota(stats.shape, 1) < PAIR * share, jnp.maximum(stats, swapped), stats + swapped)
    chips = groups * tp_count // PAIR
    copies = jnp.broadcast_to(stats[None], (chips,) + stats.shape)
    listed = [[*reversed(range(at, groups * tp_count, PAIR))] for at in range(PAIR)]
    gathered = lax.all_to_all(copies, ("req", "tp"), 0, 0, axis_index_groups=listed).reshape(chips, stats.shape[1])
    return pl.pallas_call(
        functools.partial(finish_kernel, share),
        out_shape=(
            jax.ShapeDtypeStruct((row_count,), jnp.float32),
            jax.ShapeDtypeStruct((row_count,), jnp.float32),
            jax.ShapeDtypeStruct((SEQS,), jnp.float32),
        ),
        in_specs=[spec(VMEM), spec(VMEM)],
        out_specs=(spec(VMEM), spec(VMEM), spec(VMEM)),
    )(pltpu.with_memory_space_constraint(gathered, VMEM), pltpu.with_memory_space_constraint(meta, VMEM))


def solution(mesh):
    return jax.shard_map(
        local,
        mesh=mesh,
        in_specs=(P("req", None), P(), P(None, ("req", "tp")), P("req"), P("req"), P("req")),
        out_specs=(P("req"), P("req"), P()),
        check_vma=False,
    )
```

```python
import functools

import jax
import jax.numpy as jnp
from jax import lax
from jax.experimental import pallas as pl
from jax.experimental.pallas import tpu as pltpu
from jax.sharding import PartitionSpec as P

SEQS = 4
PICK = 4
PAIR = 2
MINE = PICK // PAIR
SUBS = 8
LANES = 128
STATS = 4

VMEM = pltpu.VMEM
SMEM = pltpu.SMEM


def ranks_of(scored_ref, row_count):
    ranks, so_far = [], jnp.int32(0)
    for row in range(row_count):
        ranks.append(so_far)
        so_far = so_far + scored_ref[row]
    return ranks, so_far


def iota(shape, axis):
    return lax.broadcasted_iota(jnp.int32, shape, axis)


def members(count):
    return [(5 * count // 8 + at) % count for at in range(count)]


def own_slot(count):
    at = lax.axis_index("req") - 5 * count // 8
    return jnp.where(at < 0, at + count, at)


def pack_kernel(share, hidden_ref, gain_ref, targets_ref, segments_ref, scored_ref, out_ref, wide_ref, parts_ref, gains_ref):
    row_count, width = hidden_ref.shape
    parts = SUBS // MINE
    span = width // parts
    own, half = own_slot(out_ref.shape[0]), lax.axis_index("tp") % PAIR
    wide_ref[...] = hidden_ref[...].astype(jnp.float32)
    gains_ref[...] = gain_ref[...].astype(jnp.float32)
    ranks, count = ranks_of(scored_ref, row_count)
    source = [jnp.int32(0)] * PICK
    for row in range(row_count):
        for r in range(PICK):
            hit = jnp.logical_and(scored_ref[row] == 1, ranks[row] == r)
            source[r] = jnp.where(hit, row, source[r])
    mine = [source[i] for i in range(MINE)]
    for h in range(1, PAIR):
        mine = [jnp.where(half == h, source[h * MINE + i], mine[i]) for i in range(MINE)]
    for i in range(MINE):
        for k in range(parts):
            parts_ref[k * MINE + i : k * MINE + i + 1, :] = wide_ref[pl.ds(mine[i], 1), k * span : (k + 1) * span]
    values = parts_ref[...]
    part = jnp.broadcast_to(jnp.sum(values * values, axis=1, keepdims=True), (SUBS, LANES))
    total = part
    for k in range(1, parts):
        total = total + pltpu.roll(part, k * MINE, 0)
    row_scale = lax.rsqrt(total / width + 1e-05)
    sub, lane = iota((SUBS, LANES), 0), iota((SUBS, LANES), 1)
    chunks = span // LANES
    for at in range(chunks):
        gain = gains_ref[at : at + 1, :]
        for k in range(1, parts):
            gain = jnp.where(sub >= k * MINE, gains_ref[k * chunks + at : k * chunks + at + 1, :], gain)
        piece = parts_ref[:, at * LANES : (at + 1) * LANES]
        piece = (piece * row_scale * gain).astype(jnp.bfloat16)
        for to in range(out_ref.shape[0]):
            out_ref[to, :, at * LANES : (at + 1) * LANES] = piece
    width_side = out_ref.shape[2] - span
    sub, lane = iota((SUBS, width_side), 0), iota((SUBS, width_side), 1)
    at_row, at_half = lane % share - own * MINE, lane // share
    side = jnp.zeros((SUBS, width_side), jnp.int32)
    for i in range(MINE):
        target = targets_ref[mine[i]]
        digits = jnp.where(sub == 0, target & 255, jnp.where(sub == 1, (target >> 8) & 255, target >> 16))
        fields = jnp.zeros((SUBS, width_side), jnp.int32)
        for h in range(PAIR):
            r = h * MINE + i
            field = jnp.where(sub == 4, (count > r).astype(jnp.int32), source[r])
            fields = jnp.where(at_half == h, jnp.where(sub == 3, segments_ref[source[r]], field), fields)
        side = jnp.where(at_row == i, jnp.where(sub < 3, digits, fields), side)
    side = side.astype(jnp.float32).astype(jnp.bfloat16)
    for to in range(out_ref.shape[0]):
        out_ref[to, :, span:] = side


def stage_kernel(share, own_ref, other_ref, own_out, other_out, order_out, sems):
    copies = []
    for at, (source, out) in enumerate(((own_ref, own_out), (other_ref, other_out))):
        depth = out.shape[0] // sems.shape[1]
        for i in range(sems.shape[1]):
            piece = pl.ds(i * depth, depth)
            copies.append(pltpu.make_async_copy(source.at[piece], out.at[piece], sems.at[at, i]))
    for copy in copies:
        copy.start()
    into, out_of = iota(order_out.shape, 0), iota(order_out.shape, 1)
    wanted = into % share // MINE * SUBS + into // share * MINE + into % MINE
    order_out[...] = jnp.where(out_of == wanted, 1.0, 0.0).astype(jnp.bfloat16)
    for copy in copies:
        copy.wait()


def score_kernel(rows_ref, own_ref, upper_ref, order_ref, other_ref, stats_ref, meta_ref, ordered_ref, lower_ref, sems):
    width, cols = own_ref.shape
    staged = upper_ref.shape[0]
    depth = lower_ref.shape[0] // sems.shape[0]
    part = depth // sems.shape[1]

    def reads(at):
        firsts = [at * depth + i * part for i in range(sems.shape[1])]
        return [
            pltpu.make_async_copy(
                other_ref.at[pl.ds(staged + first, part)], lower_ref.at[pl.ds(first, part)], sems.at[at, i]
            )
            for i, first in enumerate(firsts)
        ]

    for at in range(sems.shape[0]):
        for read in reads(at):
            read.start()
    groups = rows_ref.shape[0]
    parts = SUBS // MINE
    span = width // parts
    share = groups * MINE
    tp, tp_count = lax.axis_index("tp"), lax.axis_size("tp")
    half = tp % PAIR
    place = lax.axis_index("req") * tp_count + tp
    count = groups * SUBS
    rows = rows_ref[:, :, :span].reshape(count, span)
    ordered = jnp.dot(order_ref[...], rows, preferred_element_type=jnp.float32).astype(jnp.bfloat16)
    for k in range(parts):
        ordered_ref[:, k * span : (k + 1) * span] = ordered[k * share : (k + 1) * share]
    meta = rows_ref[0, :, span:].astype(jnp.float32)
    for q in range(1, groups):
        meta = meta + rows_ref[q, :, span:].astype(jnp.float32)
    meta_ref[...] = meta

    def product(slice_ref, first, at, depth):
        piece = pl.ds(pl.multiple_of(at * depth, depth), depth)
        rows = ordered_ref[:, pl.ds(pl.multiple_of(first + at * depth, depth), depth)]
        return jnp.dot(rows, slice_ref[piece, :], preferred_element_type=jnp.float32)

    def resident(at, sums):
        return (
            sums[0] + product(own_ref, 0, at, width // 2),
            sums[1] + product(upper_ref, 0, at, staged // 2),
        )

    def fetched(at, total):
        for read in reads(at):
            read.wait()
        return total + product(lower_ref, staged, at, depth)

    zeros = jnp.zeros((share, cols), jnp.float32)
    own_logits, other_logits = lax.fori_loop(0, 2, resident, (zeros, zeros))
    logits = jnp.concatenate([own_logits, lax.fori_loop(0, sems.shape[0], fetched, other_logits)], axis=1)
    lanes = max(share, LANES)
    sub, lane = iota((share, lanes), 0), iota((share, lanes), 1)
    ids = meta[0:1, :lanes] + 256.0 * meta[1:2, :lanes] + 65536.0 * meta[2:3, :lanes]
    ids = jnp.sum(jnp.where(lane == sub, ids, 0.0), axis=1, keepdims=True).astype(jnp.int32)
    row_top = jnp.max(logits, axis=1, keepdims=True)
    scaled = jnp.exp(logits - row_top)
    row_total = jnp.sum(scaled, axis=1, keepdims=True)
    row_weighted = jnp.sum(scaled * logits, axis=1, keepdims=True)
    column = iota(logits.shape, 1)
    other = place + 1 - 2 * half
    columns = jnp.where(column < cols, place * cols, (other - 1) * cols) + column
    picked = jnp.sum(jnp.where(columns == ids, logits, 0.0), axis=1, keepdims=True)
    stats = (row_top, row_total, row_weighted, picked)
    if PAIR * share * STATS == LANES:
        joined = picked
        for at in range(STATS - 1):
            joined = jnp.where(lane // (PAIR * share) == at, stats[at], joined)
        joined = jnp.sum(jnp.where(lane % share == sub, joined, 0.0), axis=0, keepdims=True)
        lane = iota((1, LANES), 1)
        neutral = jnp.where(lane < PAIR * share, -jnp.inf, 0.0)
        stats_ref[...] = jnp.where(lane // share % PAIR == half, joined, neutral)
    else:
        for at in range(STATS):
            line = jnp.sum(jnp.where(lane == sub, stats[at], 0.0), axis=0, keepdims=True)
            for h in range(PAIR):
                first = (at * PAIR + h) * share
                stats_ref[:, first : first + share] = jnp.where(half == h, line, 0.0 if at else -jnp.inf)


def finish_kernel(share, stats_ref, meta_ref, logprob_ref, entropy_ref, seq_ref):
    row_count = logprob_ref.shape[0]
    used = PAIR * share
    lanes = max(used, LANES)

    def stat(at):
        if used >= LANES:
            return stats_ref[:, at * used : (at + 1) * used]
        return stats_ref[...] if at == 0 else pltpu.roll(stats_ref[...], LANES - at * used, 1)

    tops = stat(0)
    row_top = jnp.max(tops, axis=0, keepdims=True)
    weight = jnp.exp(tops - row_top)
    row_total = jnp.sum(stat(1) * weight, axis=0, keepdims=True)
    row_weighted = jnp.sum(stat(2) * weight, axis=0, keepdims=True)
    picked = jnp.sum(stat(3), axis=0, keepdims=True)
    log_norm = row_top + jnp.log(row_total)
    lane, sub = iota((1, lanes), 1), iota((SUBS, lanes), 0)
    in_use = jnp.logical_and(meta_ref[4:5, :] > 0.5, lane < used)
    logprob = jnp.where(in_use, picked - log_norm, 0.0)
    entropy = jnp.where(in_use, log_norm - row_weighted / row_total, 0.0)
    segment, place = meta_ref[3:4, :].astype(jnp.int32), meta_ref[5:6, :].astype(jnp.int32)
    mine = jnp.logical_and(place == sub, lane % share // MINE == own_slot(share // MINE))

    def placed(values, wanted):
        sums = jnp.sum(jnp.where(wanted, values, 0.0), axis=1, keepdims=True)
        diagonal = iota((SUBS, LANES), 0) == iota((SUBS, LANES), 1)
        return jnp.sum(jnp.where(diagonal, sums, 0.0), axis=0)

    logprob_ref[...] = placed(logprob, mine)[:row_count]
    entropy_ref[...] = placed(entropy, mine)[:row_count]
    seq_ref[...] = placed(logprob, segment == sub)[:SEQS]


def grant(mebibytes):
    return pltpu.CompilerParams(vmem_limit_bytes=mebibytes * 1024 * 1024)


def local(hidden, norm_gain, lm_head, targets, segments, scored):
    row_count, width = hidden.shape
    groups, tp_count = lax.axis_size("req"), lax.axis_size("tp")
    span = width * MINE // SUBS
    share = groups * MINE
    lanes = max(PAIR * share, LANES)

    def spec(space):
        return pl.BlockSpec(memory_space=space)

    swap = [(i, i + 1 - 2 * (i % PAIR)) for i in range(tp_count)]
    other = lax.ppermute(lm_head, "tp", swap)
    packed = pl.pallas_call(
        functools.partial(pack_kernel, share),
        out_shape=VMEM((groups, SUBS, span + lanes), jnp.bfloat16),
        in_specs=[spec(VMEM)] * 2 + [spec(SMEM)] * 3,
        out_specs=spec(VMEM),
        scratch_shapes=[
            VMEM((row_count, width), jnp.float32),
            VMEM((SUBS, span), jnp.float32),
            VMEM((width // LANES, LANES), jnp.float32),
        ],
    )(hidden, norm_gain.reshape(width // LANES, LANES), targets, segments, scored)
    rows = lax.all_to_all(packed, "req", 0, 0, axis_index_groups=[members(groups)])
    other = pltpu.with_memory_space_constraint(other, pltpu.HBM)
    staged = width // 2
    slices = pl.pallas_call(
        functools.partial(stage_kernel, share),
        out_shape=(
            VMEM(lm_head.shape, lm_head.dtype),
            VMEM((staged, lm_head.shape[1]), lm_head.dtype),
            VMEM((groups * SUBS, groups * SUBS), jnp.bfloat16),
        ),
        in_specs=[spec(pltpu.HBM)] * 2,
        out_specs=(spec(VMEM),) * 3,
        scratch_shapes=[pltpu.SemaphoreType.DMA((2, 4))],
        compiler_params=grant(4),
        cost_estimate=pl.CostEstimate(flops=0, bytes_accessed=3 * 2 * lm_head.size, transcendentals=0),
    )(pltpu.with_memory_space_constraint(lm_head, pltpu.HBM), other)
    stats, meta = pl.pallas_call(
        score_kernel,
        out_shape=(
            jax.ShapeDtypeStruct((1, STATS * PAIR * share), jnp.float32),
            VMEM((SUBS, lanes), jnp.float32),
        ),
        in_specs=[spec(VMEM)] * 4 + [spec(pltpu.HBM)],
        out_specs=(spec(VMEM), spec(VMEM)),
        scratch_shapes=[
            VMEM((share, width), jnp.bfloat16),
            VMEM((width - staged, lm_head.shape[1]), jnp.bfloat16),
            pltpu.SemaphoreType.DMA((2, 2)),
        ],
        compiler_params=grant(24),
    )(rows, *(pltpu.with_memory_space_constraint(part, VMEM) for part in slices), other)
    swapped = lax.ppermute(stats, "tp", swap)
    stats = jnp.where(iota(stats.shape, 1) < PAIR * share, jnp.maximum(stats, swapped), stats + swapped)
    chips = groups * tp_count // PAIR
    copies = jnp.broadcast_to(stats[None], (chips,) + stats.shape)
    listed = [[*reversed(range(at, groups * tp_count, PAIR))] for at in range(PAIR)]
    gathered = lax.all_to_all(copies, ("req", "tp"), 0, 0, axis_index_groups=listed).reshape(chips, stats.shape[1])
    return pl.pallas_call(
        functools.partial(finish_kernel, share),
        out_shape=(
            jax.ShapeDtypeStruct((row_count,), jnp.float32),
            jax.ShapeDtypeStruct((row_count,), jnp.float32),
            jax.ShapeDtypeStruct((SEQS,), jnp.float32),
        ),
        in_specs=[spec(VMEM), spec(VMEM)],
        out_specs=(spec(VMEM), spec(VMEM), spec(VMEM)),
    )(pltpu.with_memory_space_constraint(gathered, VMEM), pltpu.with_memory_space_constraint(meta, VMEM))


def solution(mesh):
    return jax.shard_map(
        local,
        mesh=mesh,
        in_specs=(P("req", None), P(), P(None, ("req", "tp")), P("req"), P("req"), P("req")),
        out_specs=(P("req"), P("req"), P()),
        check_vma=False,
    )
```
